32 devices in a mesh: table: 4 (over y, core), rows: 8 (over z, x).
Axes of the slice: x: 2, y: 2, z: 4, core: 2. Of those that a mesh axis runs over, the one named last changes fastest.
Arguments:
- cells: bfloat16 [4, 512, 119, 192], P('table', 'rows'), may hold values from -6 to 6
- cotangent: bfloat16 [4, 512, 119, 192], P('table', 'rows'), may hold values from -6 to 6
- train_count: int32 [4], P('table'), may hold values from 8 to 32
- key_mask: int32 [4, 32], P('table', 'rows'), may hold values 0 or 1
- train_order: int32 [4, 32], P('table', 'rows'), may hold values from 0 to 31, each once within a row
- proj_weights: float32 [6, 192, 192], replicated, may hold values from -0.4375 to 0.4375
- out_weights: float32 [2, 192, 192], replicated
- mlp_in: float32 [192, 768], replicated, may hold values from -0.4375 to 0.4375
- mlp_out: float32 [768, 192], replicated, may hold values from -0.21875 to 0.21875
- norm_params: float32 [6, 192], replicated
- square_rows: float32 [8, 192], replicated, may hold values from 2437.12 to 9748.48
- square_cols: float32 [8, 192], replicated, may hold values from 2437.12 to 9748.48
- mlp_model_stats: float32 [2, 192], replicated, may hold values from 24371.2 to 97484.8
- mlp_hidden_stats: float32 [2, 768], replicated, may hold values from 24371.2 to 97484.8
- norm_second: float32 [6, 192], replicated, may hold values from 24371.2 to 97484.8
Outputs:
- out_cells: bfloat16 [4, 512, 119, 192], P('table', 'rows')
- cells_grad: float32 [4, 512, 119, 192], P('table', 'rows')
- proj_grad: float32 [6, 192, 192], replicated
- out_grad: float32 [2, 192, 192], replicated
- mlp_in_grad: float32 [192, 768], replicated
- mlp_out_grad: float32 [768, 192], replicated
- norm_grad: float32 [6, 192], replicated
- proj_new: float32 [6, 192, 192], replicated
- out_new: float32 [2, 192, 192], replicated
- mlp_in_new: float32 [192, 768], replicated
- mlp_out_new: float32 [768, 192], replicated
- norm_new: float32 [6, 192], replicated
- square_rows_new: float32 [8, 192], replicated
- square_cols_new: float32 [8, 192], replicated
- mlp_model_new: float32 [2, 192], replicated
- mlp_hidden_new: float32 [2, 768], replicated
- norm_second_new: float32 [6, 192], replicated
The draws below stay inside these ranges and needn't reach their ends.
All inputs are finite; a program needn't handle non-finite values. No bound on the sum of `key_mask` on one device may be relied on, other than what follows from the above.
Results may differ from the reference program's by a relative error of at most 0.024.
Values may be sent and summed in bfloat16 or wider, within the bound.
No kernel may reach another device: no remote copies, remote signals or barrier semaphores. Data moves between devices by JAX's collectives and lax.ppermute only.
A program may use at most 768 MiB of HBM per device.

```python
import math
import jax
import jax.numpy as jnp
from jax import lax

D = 192
HEADS = 6
HEAD = 32
FF = 768
F = 119
ROW_DEV = 64
KEY_DEV = 4
STEP = 3
TABLES = 4
ROWS = 512
KEYS = 32


def draw_out_weights(key, part):
    key = jax.random.fold_in(key, 5)
    feature_scale = max(1, 4 * D // F) ** (-0.5)
    item_scale = max(1, 4 * D // KEYS) ** (-0.5)
    scales = jnp.array([feature_scale, item_scale], jnp.float32)
    normal_draw = jax.random.normal(key, (2, D, D), jnp.float32)
    return normal_draw * scales[:, None, None]


def draw_norm_params(key, part):
    key = jax.random.fold_in(key, 9)
    gain_key, shift_key = jax.random.split(key)
    gains = jax.random.uniform(gain_key, (6, D), jnp.float32, 0.7, 1.3)
    shifts = 0.3 * jax.random.normal(shift_key, (6, D), jnp.float32)
    gain_rows = (jnp.arange(6) % 2 == 0)[:, None]
    return jnp.where(gain_rows, gains, shifts)


def with_ends(values, stream_key, smallest, high):
    dims = values.shape
    place = [jax.random.randint(jax.random.fold_in(stream_key, axis), (), 0, dims[axis]) for axis in range(len(dims))]
    values = values.at[tuple(place)].set(smallest)
    longest = dims.index(max(dims))
    place[longest] = (place[longest] + 1) % dims[longest]
    return values.at[tuple(place)].set(high)


def block_levels(key, shape, cuts, smallest, largest):
    loudness = 1.0
    for dim, blocks in cuts:
        heights = jax.random.uniform(jax.random.fold_in(jax.random.fold_in(key, 6), dim), (blocks,), jnp.float32, smallest / len(cuts), largest / len(cuts))
        loudness = loudness * jnp.repeat(jnp.exp(heights), shape[dim] // blocks).reshape((-1,) + (1,) * (len(shape) - 1 - dim))
    return loudness


def gaussian(stream_key, extent, scale, bound, shards=(), held_as=jnp.bfloat16):
    factor_of = block_levels(stream_key, extent, shards, -0.22, 0.18) if shards else 1.0
    entries = jax.random.normal(stream_key, extent, jnp.float32) * scale * factor_of
    return jnp.minimum(jnp.maximum(entries, -bound), bound).astype(held_as)


def setup_inputs(seed: int = 0) -> dict:
    key_list = jax.random.split(jax.random.key(seed), 16)
    cells = gaussian(key_list[0], (TABLES, ROWS, F, D), 1.0, 6.0, ((0, 4), (1, 8)))
    cotangent = gaussian(key_list[1], (TABLES, ROWS, F, D), 1.0, 6.0, ((0, 4), (1, 8)))
    train_count = with_ends(jax.random.randint(key_list[2], (TABLES,), KEYS // 4, KEYS + 1), jax.random.fold_in(key_list[2], 1), KEYS // 4, KEYS).astype(jnp.int32)
    key_mask = with_ends((jax.random.randint(key_list[3], (TABLES, KEYS), 0, 4) < 3).astype(jnp.int32), jax.random.fold_in(key_list[3], 1), 0, 1)
    train_order = jax.vmap(lambda own: jax.random.permutation(own, KEYS))(jax.random.split(key_list[4], TABLES)).reshape((TABLES, KEYS)).astype(jnp.int32)
    proj_weights = gaussian(key_list[5], (6, D, D), D ** -0.5, 0.4375, (), jnp.float32)
    out_weights = draw_out_weights(jax.random.fold_in(key_list[15], 71), 0)
    mlp_in = gaussian(key_list[7], (D, FF), D ** -0.5, 0.4375, (), jnp.float32)
    mlp_out = gaussian(key_list[8], (FF, D), FF ** -0.5, 0.21875, (), jnp.float32)
    norm_params = draw_norm_params(jax.random.fold_in(key_list[15], 71), 0)
    square_rows = jnp.clip(jnp.exp(jax.random.uniform(key_list[10], (8, D), jnp.float32, math.log(2437.12), math.log(9748.48))), 2437.12, 9748.48)
    square_cols = jnp.clip(jnp.exp(jax.random.uniform(key_list[11], (8, D), jnp.float32, math.log(2437.12), math.log(9748.48))), 2437.12, 9748.48)
    mlp_model_stats = jnp.clip(jnp.exp(jax.random.uniform(key_list[12], (2, D), jnp.float32, math.log(24371.2), math.log(97484.8))), 24371.2, 97484.8)
    mlp_hidden_stats = jnp.clip(jnp.exp(jax.random.uniform(key_list[13], (2, FF), jnp.float32, math.log(24371.2), math.log(97484.8))), 24371.2, 97484.8)
    norm_second = jnp.clip(jnp.exp(jax.random.uniform(key_list[14], (6, D), jnp.float32, math.log(24371.2), math.log(97484.8))), 24371.2, 97484.8)
    return {"cells": cells, "cotangent": cotangent, "train_count": train_count, "key_mask": key_mask, "train_order": train_order, "proj_weights": proj_weights, "out_weights": out_weights, "mlp_in": mlp_in, "mlp_out": mlp_out, "norm_params": norm_params, "square_rows": square_rows, "square_cols": square_cols, "mlp_model_stats": mlp_model_stats, "mlp_hidden_stats": mlp_hidden_stats, "norm_second": norm_second}


@jax.custom_vjp
def low(v):
    return lax.optimization_barrier(v.astype(jnp.bfloat16)).astype(jnp.float32)

@jax.custom_vjp
def low_back(v):
    return v

def low_keep(v):
    return (low(v), None)

def low_pass(kept, grad):
    return (grad,)

def back_keep(v):
    return (v, None)

def back_low(kept, grad):
    return (low(grad),)
low.defvjp(low_keep, low_pass)
low_back.defvjp(back_keep, back_low)
HIGHEST = lax.Precision.HIGHEST
CLIP = 0.3
RATE = 0.5

def rounded_both(value):
    return low_back(low(value))

def split_heads(value):
    return value.reshape(value.shape[:-1] + (HEADS, HEAD))

def normalize(value, gain, shift):
    center = value - lax.optimization_barrier(jnp.mean(value, -1, keepdims=True))
    return center * lax.rsqrt(lax.optimization_barrier(jnp.mean(center * center, -1, keepdims=True)) + 1e-05) * gain + shift

def project(value, weight):
    return jnp.einsum('...d,de->...e', value, weight, precision=HIGHEST)

def softmax_last(scores):
    row_max = lax.optimization_barrier(jnp.max(scores, -1, keepdims=True))
    expon = jnp.exp(scores - row_max)
    return expon / lax.optimization_barrier(jnp.sum(expon, -1, keepdims=True))

def table_layer(inputs, usable, proj, outw, w_in, w_out, norms):
    score_scale = HEAD ** (-0.5)
    query_feat = rounded_both(project(inputs, proj[0]))
    key_feat = rounded_both(project(inputs, proj[1]))
    value_feat = rounded_both(project(inputs, proj[2]))
    scores = jnp.einsum('rfhe,rghe->rhfg', split_heads(query_feat), split_heads(key_feat), precision=HIGHEST) * score_scale
    probs = low(softmax_last(low_back(scores)))
    out_feat = jnp.einsum('rhfg,rghe->rfhe', probs, split_heads(value_feat), precision=HIGHEST).reshape(inputs.shape)
    out_feat = rounded_both(out_feat)
    hidden_one = normalize(inputs + low_back(project(out_feat, outw[0])), norms[0], norms[1])
    hidden_low = low(hidden_one)
    query_item = rounded_both(project(hidden_low, proj[3]))
    key_item = rounded_both(project(hidden_low, proj[4]))
    value_item = rounded_both(project(hidden_low, proj[5]))
    slot_keys = key_item.reshape(ROWS // ROW_DEV, ROW_DEV, F, D)[:, :KEY_DEV].reshape(KEYS, F, D)
    slot_values = value_item.reshape(ROWS // ROW_DEV, ROW_DEV, F, D)[:, :KEY_DEV].reshape(KEYS, F, D)
    item_scores = jnp.einsum('rfhe,kfhe->fhrk', split_heads(query_item), split_heads(slot_keys), precision=HIGHEST) * score_scale
    item_scores = jnp.where(usable[None, None, None, :], low_back(item_scores), -1e+30)
    item_probs = low(softmax_last(item_scores))
    out_item = jnp.einsum('fhrk,kfhe->rfhe', item_probs, split_heads(slot_values), precision=HIGHEST).reshape(inputs.shape)
    out_item = rounded_both(out_item)
    hidden_two = normalize(hidden_one + low_back(project(out_item, outw[1])), norms[2], norms[3])
    pre_act = low_back(project(low(hidden_two), w_in))
    activ = low(jax.nn.gelu(pre_act))
    branch = low_back(project(activ, w_out))
    return normalize(hidden_two + branch, norms[4], norms[5])

def factored_step(grad, rows_old, cols_old, weight):
    decay = 1.0 - STEP ** (-0.8)
    square = grad * grad + 1e-30
    rows_new = decay * rows_old + (1.0 - decay) * lax.optimization_barrier(jnp.mean(square, -1))
    cols_new = decay * cols_old + (1.0 - decay) * lax.optimization_barrier(jnp.mean(square, -2))
    estimate = rows_new[..., :, None] * cols_new[..., None, :] / lax.optimization_barrier(jnp.mean(rows_new, -1))[..., None, None]
    update = grad * lax.rsqrt(estimate)
    update_rms = jnp.sqrt(lax.optimization_barrier(jnp.mean(update * update, (-2, -1), keepdims=True)))
    update = update / jnp.maximum(1.0, update_rms / CLIP)
    weight_rms = jnp.sqrt(lax.optimization_barrier(jnp.mean(weight * weight, (-2, -1), keepdims=True)))
    return (weight - RATE * jnp.maximum(0.001, weight_rms) * update, rows_new, cols_new)

def vector_step(grad, second_old, param):
    decay = 1.0 - STEP ** (-0.8)
    second_new = decay * second_old + (1.0 - decay) * (grad * grad + 1e-30)
    update = grad * lax.rsqrt(second_new)
    update_rms = jnp.sqrt(lax.optimization_barrier(jnp.mean(update * update, -1, keepdims=True)))
    update = update / jnp.maximum(1.0, update_rms / CLIP)
    param_rms = jnp.sqrt(lax.optimization_barrier(jnp.mean(param * param, -1, keepdims=True)))
    return (param - RATE * jnp.maximum(0.001, param_rms) * update, second_new)

def reference(cells, cotangent, train_count, key_mask, train_order, proj_weights, out_weights, mlp_in, mlp_out, norm_params, square_rows, square_cols, mlp_model_stats, mlp_hidden_stats, norm_second):
    usable = (train_order < train_count[:, None]) & ((key_mask == 1) | (train_order == 0))

    def forward(inputs, proj, outw, w_in, w_out, norms):
        proj_low, outw_low, in_low, out_low = (low(proj), low(outw), low(w_in), low(w_out))

        def one_table(pair):
            return table_layer(pair[0], pair[1], proj_low, outw_low, in_low, out_low, norms)
        return lax.map(jax.checkpoint(one_table), (inputs, usable))
    result, pull = jax.vjp(forward, cells.astype(jnp.float32), proj_weights, out_weights, mlp_in, mlp_out, norm_params)
    grads = pull(cotangent.astype(jnp.float32))
    cells_grad, proj_grad, out_grad, in_grad, hid_grad, norm_grad = grads
    proj_new, proj_rows, proj_cols = factored_step(proj_grad, square_rows[:6], square_cols[:6], proj_weights)
    out_new, out_rows, out_cols = factored_step(out_grad, square_rows[6:], square_cols[6:], out_weights)
    in_new, in_rows, in_cols = factored_step(in_grad, mlp_model_stats[0], mlp_hidden_stats[0], mlp_in)
    hid_new, hid_rows, hid_cols = factored_step(hid_grad, mlp_hidden_stats[1], mlp_model_stats[1], mlp_out)
    norm_new, second_new = vector_step(norm_grad, norm_second, norm_params)
    rows_new = jnp.concatenate([proj_rows, out_rows], 0)
    cols_new = jnp.concatenate([proj_cols, out_cols], 0)
    model_new = jnp.stack([in_rows, hid_cols])
    hidden_new = jnp.stack([in_cols, hid_rows])
    return (result.astype(jnp.bfloat16), cells_grad, proj_grad, out_grad, in_grad, hid_grad, norm_grad, proj_new, out_new, in_new, hid_new, norm_new, rows_new, cols_new, model_new, hidden_new, second_new)
```

```python
import functools

import jax
import jax.numpy as jnp
import numpy as np
from jax import lax
from jax.experimental import pallas as pl
from jax.experimental.pallas import tpu as pltpu
from jax.sharding import PartitionSpec as P

BF, F32 = jnp.bfloat16, jnp.float32
D, DP = 192, 256
H, E = 6, 32
F, FP = 119, 128
FS = 120
FF = 768
STEP = 3
CLIP = 0.3
RATE = 0.5
SCALE = E**-0.5
SCALE2 = SCALE * 1.4426950408889634
C0 = 0.7978845608028654
C1 = 0.044715
NT = (((1,), (1,)), ((), ()))
TN = (((0,), (0,)), ((), ()))
PAIR = 576
TAIL = 3 * PAIR + 8
MID = 2 * 6 * D + PAIR + 8


def mm(a, b):
    return jnp.dot(a, b, preferred_element_type=F32)


def mm_nt(a, b):
    return lax.dot_general(a, b, NT, preferred_element_type=F32)


def mm_tn(a, b):
    return lax.dot_general(a, b, TN, preferred_element_type=F32)


def lanes():
    return lax.broadcasted_iota(jnp.int32, (1, DP), 1)


def head_masks():
    lane = lanes()
    return [
        jnp.where((lane >= E * h) & (lane < E * (h + 1)), 1.0, 0.0).astype(BF) for h in range(H)
    ]


def spread(w, masks):
    return jnp.concatenate([w * m for m in masks], 0)


def layer_norm(a, lane_ok):
    c = a - jnp.sum(a, -1, keepdims=True) * (1.0 / D) * lane_ok
    rc = lax.rsqrt(jnp.sum(c * c, -1, keepdims=True) * (1.0 / D) + 1e-5)
    return c * rc, rc


def norm_back(g, n, rc, gain, lane_ok):
    dn = g * gain
    m1 = jnp.sum(dn, -1, keepdims=True) * (1.0 / D)
    m2 = jnp.sum(dn * n, -1, keepdims=True) * (1.0 / D)
    return (dn - m1 * lane_ok - n * m2) * rc


def fold8(v):
    return jnp.sum(v.reshape(v.shape[0] // 8, 8, v.shape[1]), 0)


def diagonal(full, keys):
    lane = lax.broadcasted_iota(jnp.int32, (1, 128), 1)
    low = full[0:keys, 0:128]
    for h in range(1, 4):
        low = jnp.where(lane >= E * h, full[h * keys : (h + 1) * keys, 0:128], low)
    high = jnp.where(
        lane >= E, full[5 * keys : 6 * keys, 128:256], full[4 * keys : 5 * keys, 128:256]
    )
    return jnp.concatenate([low, high], 1)


def whole(a):
    nd = len(a.shape)
    return pl.BlockSpec(a.shape, lambda *i: (0,) * nd)


def shape(s, t=BF):
    return jax.ShapeDtypeStruct(s, t)


def params(mib=58):
    return pltpu.CompilerParams(vmem_limit_bytes=mib << 20)


def perm_matrix():
    place = np.zeros((256, 256), np.float32)
    for f in range(16):
        for r in range(16):
            place[f * 16 + r, r * 16 + f] = 1
    return jnp.asarray(place, BF)


def prep_kernel(
    proj, outw, w_in, w_out, norms, wqkv, wqkvT, wo, woT, wkv2, wk2T, wv2T, wq2, wq2T, wo2, wo2T, w1, w1T, w2, w2T, np8
):
    zc = jnp.zeros((D, DP - D), F32)
    zr = jnp.zeros((DP - D, DP), BF)

    def square(w):
        a = jnp.concatenate([w, zc], 1)
        a = jnp.concatenate([a.astype(BF), zr], 0)
        return a, a.T

    for i in range(3):
        a, t = square(proj[i])
        wqkv[:, i * DP : (i + 1) * DP] = a
        wqkvT[i * DP : (i + 1) * DP, :] = t
    for src, dst, dstT in ((outw[0], wo, woT), (proj[3], wq2, wq2T), (outw[1], wo2, wo2T)):
        a, t = square(src)
        dst[...] = a
        dstT[...] = t
    a, t = square(proj[4])
    wk2T[...] = t
    a, t = square(proj[5])
    wv2T[...] = t
    wkv2[0:D, :] = jnp.concatenate([proj[4], proj[5]], 1).astype(BF)
    wkv2[D:DP, :] = jnp.zeros((DP - D, 2 * D), BF)
    a = jnp.concatenate([w_in[...].astype(BF), jnp.zeros((DP - D, FF), BF)], 0)
    w1[...] = a
    w1T[...] = a.T
    a = jnp.concatenate([w_out[...], jnp.zeros((FF, DP - D), F32)], 1).astype(BF)
    w2[...] = a
    w2T[...] = a.T
    np8[...] = jnp.zeros((8, DP), F32)
    np8[0:6, 0:D] = norms[...]


def prepare(proj, outw, w_in, w_out, norms):
    sq = shape((DP, DP))
    outs = [
        shape((DP, 3 * DP)),
        shape((3 * DP, DP)),
        sq,
        sq,
        shape((DP, 2 * D)),
        sq,
        sq,
        sq,
        sq,
        sq,
        sq,
        shape((DP, FF)),
        shape((FF, DP)),
        shape((FF, DP)),
        shape((DP, FF)),
        shape((8, DP), F32),
    ]
    return pl.pallas_call(prep_kernel, out_shape=outs, compiler_params=params(), name="weights")(
        proj, outw, w_in, w_out, norms
    )


def feature_rows(x, wqkv, wo, masks, lane_ok, U, keep=None):
    qkv = mm(x, wqkv).astype(BF)
    outs = []
    for u in range(U):
        own = qkv[u * FP : (u + 1) * FP]
        q, k, v = own[:, 0:DP], own[:, DP : 2 * DP], own[:, 2 * DP : 3 * DP]
        st = mm_nt(k, spread(q, masks))
        row = lax.broadcasted_iota(jnp.int32, (8, 1), 0)
        st = jnp.concatenate([st[: FS - 8], jnp.where(row < F - FS + 8, st[FS - 8 : FS], -1e30)], 0)
        mx = jnp.max(st, 0, keepdims=True)
        e = jnp.exp2((st - mx) * SCALE2)
        total = jnp.sum(e, 0, keepdims=True)
        p = e * (1.0 / total)
        p = jnp.concatenate([p, jnp.zeros((FP - FS, H * FP), F32)], 0).astype(BF)
        vt = v.T
        ot = []
        for j in range(H // 2):
            t = mm(vt[64 * j : 64 * j + 64], p[:, 256 * j : 256 * j + 256])
            ot += [t[0:32, 0:128], t[32:64, 128:256]]
        ot = jnp.concatenate(ot + [jnp.zeros((DP - D, FP), F32)], 0).astype(BF)
        o = ot.T
        if keep is not None:
            keep(u, own, p, o)
        outs.append(o)
    o = jnp.concatenate(outs, 0)
    return layer_norm(x.astype(F32) + mm(o, wo), lane_ok)


def slots_kernel(SL, count_ref, mask_ref, order_ref, x_ref, wqkv_ref, wo_ref, wkv2_ref, np_ref, kv_ref, xs):
    xs[...] = jnp.zeros_like(xs)
    masks = head_masks()
    lane_ok = (lanes() < D).astype(F32)
    for u in range(SL):
        xs[u * FP : u * FP + F, 0:D] = x_ref[u]
    n, _ = feature_rows(xs[...], wqkv_ref[...], wo_ref[...], masks, lane_ok, SL)
    h = (n * np_ref[0:1, :] + np_ref[1:2, :]).astype(BF)
    kv = mm(h, wkv2_ref[...])
    row = lax.broadcasted_iota(jnp.int32, (FS, 1), 0)
    for u in range(SL):
        order = order_ref[0, u]
        usable = (order < count_ref[0]) & ((mask_ref[0, u] == 1) | (order == 0))
        flag = jnp.where(usable, 1.0, 0.0)
        kv_ref[u] = jnp.where(row < F, kv[u * FP : u * FP + FS], flag).astype(BF)


def slot_keys(count, mask, order, cells, wqkv, wo, wkv2, np8):
    SL = mask.shape[1]
    smem = pl.BlockSpec(memory_space=pltpu.SMEM)
    return pl.pallas_call(
        functools.partial(slots_kernel, SL),
        grid=(1,),
        in_specs=[smem, smem, smem, pl.BlockSpec((SL, F, D), lambda i: (0, 0, 0))]
        + [whole(a) for a in (wqkv, wo, wkv2, np8)],
        out_specs=pl.BlockSpec((SL, FS, 2 * D), lambda i: (0, 0, 0)),
        out_shape=shape((SL, FS, 2 * D)),
        scratch_shapes=[pltpu.VMEM((SL * FP, DP), BF)],
        compiler_params=params(),
        name="slot_keys",
    )(count, mask, order, cells, wqkv, wo, wkv2, np8)


def forward_kernel(R, U, x_ref, wqkv_ref, wo_ref, perm_ref, nt_ref, n_ref, qkv_ref, p_ref, of_ref, xs):
    @pl.when(pl.program_id(0) == 0)
    def _():
        xs[...] = jnp.zeros_like(xs)

    masks = head_masks()
    lane = lanes()
    lane_ok = (lane < D).astype(F32)

    def rows(i, carry):
        r0 = i * U
        for u in range(U):
            xs[u * FP : u * FP + F, 0:D] = x_ref[r0 + u]

        def keep(u, own, p, o):
            qkv_ref[r0 + u] = own
            p_ref[r0 + u] = p
            of_ref[r0 + u] = o

        n, rc = feature_rows(xs[...], wqkv_ref[...], wo_ref[...], masks, lane_ok, U, keep)
        n = jnp.where(lane >= D, rc, n).astype(BF)
        for u in range(U):
            n_ref[r0 + u] = n[u * FP : (u + 1) * FP]
        return carry

    lax.fori_loop(0, R // U, rows, 0)

    def turn(j, carry):
        f0 = pl.multiple_of(j * 16, 16)
        block = n_ref[:, pl.ds(f0, 16), :].reshape(R * 16, DP)
        nt_ref[pl.ds(f0, 16)] = mm(perm_ref[...], block).astype(BF).reshape(16, R, DP)
        return carry

    lax.fori_loop(0, FP // 16, turn, 0)


def feature_forward(cells, wqkv, wo, perm, R=16, U=4):
    rows = cells.shape[0]
    nat = lambda w: pl.BlockSpec((R, FP, w), lambda i: (i, 0, 0))
    return pl.pallas_call(
        functools.partial(forward_kernel, R, U),
        grid=(rows // R,),
        in_specs=[pl.BlockSpec((R, F, D), lambda i: (i, 0, 0)), whole(wqkv), whole(wo), whole(perm)],
        out_specs=[
            pl.BlockSpec((FP, R, DP), lambda i: (0, i, 0)),
            nat(DP),
            nat(3 * DP),
            nat(H * FP),
            nat(DP),
        ],
        out_shape=[
            shape((FP, rows, DP)),
            shape((rows, FP, DP)),
            shape((rows, FP, 3 * DP)),
            shape((rows, FP, H * FP)),
            shape((rows, FP, DP)),
        ],
        scratch_shapes=[pltpu.VMEM((U * FP, DP), BF)],
        compiler_params=params(),
        name="feature_forward",
    )(cells, wqkv, wo, perm)


def columns_kernel(x_ref, perm_ref, out_ref, xs):
    xs[...] = jnp.zeros_like(xs)
    xs[:, 0:F, 0:D] = x_ref[...]

    def turn(j, carry):
        f0 = pl.multiple_of(j * 16, 16)
        block = xs[:, pl.ds(f0, 16), :].reshape(256, DP)
        out_ref[pl.ds(f0, 16)] = mm(perm_ref[...], block).astype(BF).reshape(16, 16, DP)
        return carry

    lax.fori_loop(0, FP // 16, turn, 0)


def to_columns(x, perm):
    rows = x.shape[0]
    return pl.pallas_call(
        columns_kernel,
        grid=(rows // 16,),
        in_specs=[pl.BlockSpec((16, F, D), lambda i: (i, 0, 0)), whole(perm)],
        out_specs=pl.BlockSpec((FP, 16, DP), lambda i: (0, i, 0)),
        out_shape=shape((FP, rows, DP)),
        scratch_shapes=[pltpu.VMEM((16, FP, DP), BF)],
        compiler_params=params(),
        name="to_columns",
    )(x, perm)


def gathered_kernel(kv_ref, perm_ref, kt_ref, vt_ref, bias_ref, xs):
    xs[:, FS:FP, :] = jnp.zeros((16, FP - FS, 2 * D), BF)
    xs[:, 0:FS, :] = kv_ref[...]
    kt_ref[:, :, D:DP] = jnp.zeros((FP, 16, DP - D), BF)
    vt_ref[:, :, D:DP] = jnp.zeros((FP, 16, DP - D), BF)
    for j in range(FP // 16):
        f0 = 16 * j
        block = mm(perm_ref[...], xs[:, f0 : f0 + 16, :].reshape(256, 2 * D))
        if f0 < F <= f0 + 16:
            flag = block[(F - f0) * 16 : (F - f0 + 1) * 16, 0:128]
            bias_ref[...] = jnp.where(flag > 0.5, 0.0, -1e30)
        kt_ref[f0 : f0 + 16, :, 0:D] = block[:, 0:D].astype(BF).reshape(16, 16, D)
        vt_ref[f0 : f0 + 16, :, 0:D] = block[:, D : 2 * D].astype(BF).reshape(16, 16, D)


def gathered_columns(kv, perm):
    keys = kv.shape[0]
    col = pl.BlockSpec((FP, 16, DP), lambda i: (0, i, 0))
    return pl.pallas_call(
        gathered_kernel,
        grid=(keys // 16,),
        in_specs=[pl.BlockSpec((16, FS, 2 * D), lambda i: (i, 0, 0)), whole(perm)],
        out_specs=[col, col, pl.BlockSpec((16, 128), lambda i: (i, 0))],
        out_shape=[shape((FP, keys, DP)), shape((FP, keys, DP)), shape((keys, 128), F32)],
        scratch_shapes=[pltpu.VMEM((16, FP, 2 * D), BF)],
        compiler_params=params(),
        name="gathered_columns",
    )(kv, perm)


def parts_kernel(dk_ref, dv_ref, perm_ref, out_ref):
    col = lax.broadcasted_iota(jnp.int32, (16, 1, 1), 0)
    for j in range(FP // 16):
        f0 = 16 * j
        n = min(16, FS - f0)
        turned = []
        for ref in (dk_ref, dv_ref):
            block = ref[f0 : f0 + 16]
            if f0 + 16 > F:
                block = jnp.where(col < F - f0, block, 0).astype(BF)
            turned.append(mm(perm_ref[...], block.reshape(256, DP))[:, 0:D])
        both = jnp.concatenate(turned, 1).astype(BF).reshape(16, 16, 2 * D)
        out_ref[:, f0 : f0 + n, :] = both[:, 0:n, :]


def slot_parts(dk, dv, perm):
    keys = dk.shape[1]
    col = pl.BlockSpec((FP, 16, DP), lambda i: (0, i, 0))
    return pl.pallas_call(
        parts_kernel,
        grid=(keys // 16,),
        in_specs=[col, col, whole(perm)],
        out_specs=pl.BlockSpec((16, FS, 2 * D), lambda i: (i, 0, 0)),
        out_shape=shape((keys, FS, 2 * D)),
        compiler_params=params(),
        name="slot_parts",
    )(dk, dv, perm)


def pack_pair(ref, at, a, b):
    ref[at : at + D] = a[0:D, 0:128].astype(BF)
    ref[at + D : at + 2 * D] = b[0:D, 0:128].astype(BF)
    ref[at + 2 * D : at + 3 * D] = jnp.concatenate([a[0:D, 128:D], b[0:D, 128:D]], 1).astype(BF)


def pack_norms(ref, at, sums):
    rows = []
    for s in sums:
        v = jnp.sum(s, 0, keepdims=True)
        rows += [v[:, 0:128], v[:, 128:256]]
    rows.append(jnp.zeros((ref.shape[0] - at - len(rows), 128), F32))
    ref[at:] = jnp.concatenate(rows, 0).astype(BF)


def item_kernel(
    FB, RW, keys, CH, nt_ref, ct_ref, kt_ref, vt_ref, bias_ref, wq_ref, wqT_ref, wo_ref, woT_ref, w1_ref, w1T_ref,
    w2_ref, w2T_ref, np_ref, y_ref, g1_ref, dk_ref, dv_ref, pack_ref, dwq, dwo, dw1, dw2, dnp, h1b, qs, pbs, oi, da2s,
    dab, doi, dqs, h2b, dub, dbr, acts,
):
    M = FB * RW

    @pl.when(pl.program_id(0) == 0)
    def _():
        for ref in (dwq, dwo, dw1, dw2, dnp):
            ref[...] = jnp.zeros_like(ref)

    masks = head_masks()
    lane_ok = (lanes() < D).astype(F32)
    g0, b0, g1, b1, g2, b2 = [np_ref[i : i + 1, :] for i in range(6)]
    left = lax.broadcasted_iota(jnp.int32, (1, 2 * RW), 1) < RW
    HK = H * keys

    def attend(j, carry):
        s0 = pl.multiple_of(j * 2 * RW, 2 * RW)
        n = nt_ref[pl.ds(2 * j, 2)].reshape(2 * RW, DP).astype(F32)
        hb = (n * g0 + b0).astype(BF)
        h1b[pl.ds(s0, 2 * RW)] = hb
        q = mm(hb, wq_ref[...]).astype(BF)
        qs[pl.ds(s0, 2 * RW)] = q
        ka, kb = spread(kt_ref[2 * j], masks), spread(kt_ref[2 * j + 1], masks)
        st = jnp.where(left, mm_nt(ka, q), mm_nt(kb, q))
        st = st.reshape(H, keys, 2 * RW) + bias_ref[...][None]
        mx = jnp.max(st, 1, keepdims=True)
        e = jnp.exp2((st - mx) * SCALE2)
        total = jnp.sum(e, 1, keepdims=True)
        pb = (e * (1.0 / total)).reshape(HK, 2 * RW).astype(BF)
        pbs[j] = pb
        pt = pb.T
        va, vb = spread(vt_ref[2 * j], masks), spread(vt_ref[2 * j + 1], masks)
        oi[pl.ds(s0, RW)] = mm(pt[:RW], va).astype(BF)
        oi[pl.ds(s0 + RW, RW)] = mm(pt[RW:], vb).astype(BF)
        return carry

    lax.fori_loop(0, FB // 2, attend, 0)

    def dense(j, carry):
        gs2, bs2, gs1, bs1 = carry
        s0 = pl.multiple_of(j * CH, CH)
        cols = CH // RW
        h1 = nt_ref[pl.ds(j * cols, cols)].reshape(CH, DP).astype(F32) * g0 + b0
        n2, rc2 = layer_norm(h1 + mm(oi[pl.ds(s0, CH)], wo_ref[...]), lane_ok)
        h2 = n2 * g1 + b1
        hb = h2.astype(BF)
        h2b[pl.ds(s0, CH)] = hb
        u = mm(hb, w1_ref[...])
        uu = u * u
        th = jnp.tanh(u * (C0 + (C0 * C1) * uu))
        half = 0.5 + 0.5 * th
        act = (u * half).astype(BF)
        acts[pl.ds(s0, CH)] = act
        slope = half + (0.5 * u) * (1.0 - th * th) * (C0 + (3.0 * C0 * C1) * uu)
        n3, rc3 = layer_norm(h2 + mm(act, w2_ref[...]), lane_ok)
        y_ref[pl.ds(j * cols, cols)] = (n3 * g2 + b2).astype(BF).reshape(cols, RW, DP)
        g = ct_ref[pl.ds(j * cols, cols)].reshape(CH, DP).astype(F32)
        gs2 = gs2 + fold8(g * n3)
        bs2 = bs2 + fold8(g)
        d3 = norm_back(g, n3, rc3, g2, lane_ok)
        db = d3.astype(BF)
        dbr[pl.ds(s0, CH)] = db
        du = (mm(db, w2T_ref[...]) * slope).astype(BF)
        dub[pl.ds(s0, CH)] = du
        dh2 = d3 + mm(du, w1T_ref[...])
        gs1 = gs1 + fold8(dh2 * n2)
        bs1 = bs1 + fold8(dh2)
        d2 = norm_back(dh2, n2, rc2, g1, lane_ok)
        da2s[pl.ds(s0, CH)] = d2
        d2b = d2.astype(BF)
        dab[pl.ds(s0, CH)] = d2b
        doi[pl.ds(s0, CH)] = mm(d2b, woT_ref[...]).astype(BF)
        return gs2, bs2, gs1, bs1

    z = jnp.zeros((8, DP), F32)
    gs2, bs2, gs1, bs1 = lax.fori_loop(0, M // CH, dense, (z, z, z, z))
    dnp[0] += gs1
    dnp[1] += bs1
    dnp[2] += gs2
    dnp[3] += bs2
    zero = jnp.zeros((RW, DP), BF)

    def back(j, carry):
        s0 = pl.multiple_of(j * 2 * RW, 2 * RW)
        q, do = qs[pl.ds(s0, 2 * RW)], doi[pl.ds(s0, 2 * RW)]
        pb = pbs[j]
        ka, kb = spread(kt_ref[2 * j], masks), spread(kt_ref[2 * j + 1], masks)
        va, vb = spread(vt_ref[2 * j], masks), spread(vt_ref[2 * j + 1], masks)
        dp = jnp.where(left, mm_nt(va, do), mm_nt(vb, do)).reshape(H, keys, 2 * RW)
        p = pb.astype(F32).reshape(H, keys, 2 * RW)
        off = jnp.sum(p * dp, 1, keepdims=True)
        ds = (p * (dp - off)).reshape(HK, 2 * RW).astype(BF)
        dst = ds.T
        dq = jnp.concatenate([mm(dst[:RW], ka), mm(dst[RW:], kb)], 0) * SCALE
        dqs[pl.ds(s0, 2 * RW)] = dq.astype(BF)
        for c in range(2):
            part = slice(c * RW, (c + 1) * RW)
            qz = jnp.concatenate([q[part], zero] if c == 0 else [zero, q[part]], 0)
            dz = jnp.concatenate([do[part], zero] if c == 0 else [zero, do[part]], 0)
            dk_ref[2 * j + c] = (diagonal(mm(ds, qz), keys) * SCALE).astype(BF)
            dv_ref[2 * j + c] = diagonal(mm(pb, dz), keys).astype(BF)
        return carry

    lax.fori_loop(0, FB // 2, back, 0)

    def finish(j, carry):
        s0 = pl.multiple_of(j * CH, CH)
        cols = CH // RW
        g = da2s[pl.ds(s0, CH)] + mm(dqs[pl.ds(s0, CH)], wqT_ref[...])
        g1_ref[pl.ds(j * cols, cols)] = g.astype(BF).reshape(cols, RW, DP)
        return carry

    lax.fori_loop(0, M // CH, finish, 0)
    dwq[...] += mm_tn(h1b[...], dqs[...])
    dwo[...] += mm_tn(oi[...], dab[...])
    dw1[...] += mm_tn(h2b[...], dub[...])
    dw2[...] += mm_tn(dbr[...], acts[...])

    @pl.when(pl.program_id(0) == pl.num_programs(0) - 1)
    def _():
        at = 0
        for ref in (dw1, dw2):
            for j in range(FF // 128):
                pack_ref[at : at + D] = ref[0:D, 128 * j : 128 * j + 128].astype(BF)
                at += D
        pack_pair(pack_ref, at, dwq, dwo)
        pack_norms(pack_ref, at + PAIR, [dnp[i] for i in range(4)])


def item_and_dense(nt, ct, kt, vt, bias, ws, np8, packed, FB=8, CH=128):
    RW = nt.shape[1]
    keys = kt.shape[1]
    M = FB * RW
    cells = pl.BlockSpec((FB, RW, DP), lambda i: (i, 0, 0))
    slots = pl.BlockSpec((FB, keys, DP), lambda i: (i, 0, 0))
    own = pltpu.VMEM((M, DP), BF)
    wide = pltpu.VMEM((M, FF), BF)
    return pl.pallas_call(
        functools.partial(item_kernel, FB, RW, keys, CH),
        grid=(pl.cdiv(F, FB),),
        in_specs=[cells, cells, slots, slots, whole(bias)] + [whole(w) for w in ws] + [whole(np8)],
        out_specs=[cells, cells, slots, slots, pl.BlockSpec((packed, 128), lambda i: (0, 0))],
        out_shape=[shape((FP, RW, DP))] * 2 + [shape((FP, keys, DP))] * 2 + [shape((packed, 128))],
        scratch_shapes=[
            pltpu.VMEM((DP, DP), F32),
            pltpu.VMEM((DP, DP), F32),
            pltpu.VMEM((DP, FF), F32),
            pltpu.VMEM((DP, FF), F32),
            pltpu.VMEM((4, 8, DP), F32),
            own,
            own,
            pltpu.VMEM((FB // 2, H * keys, 2 * RW), BF),
            own,
            pltpu.VMEM((M, DP), F32),
            own,
            own,
            own,
            own,
            wide,
            own,
            wide,
        ],
        compiler_params=params(),
        name="item_and_dense",
    )(nt, ct, kt, vt, bias, *ws, np8)


def backward_kernel(R, U, SL, x_ref, qkv_ref, p_ref, of_ref, n_ref, g1t_ref, yt_ref, *rest):
    if SL:
        (dkv_ref, wk2T_ref, wv2T_ref, wqkvT_ref, woT_ref, np_ref, perm_ref, iqkv, iwo, inp, _, _,
         cg_ref, y_ref, pack_ref, gs, xs, dqkvs, dfbs, dqkv, dwo, dnp) = rest
    else:
        wqkvT_ref, woT_ref, np_ref, perm_ref, cg_ref, y_ref, dqkv, dwo, dnp, gs, xs, dqkvs, dfbs = rest
    masks = head_masks()
    lane_ok = (lanes() < D).astype(F32)

    @pl.when(pl.program_id(0) == 0)
    def _():
        xs[...] = jnp.zeros_like(xs)
        for i, ref in enumerate((dqkv, dwo, dnp)):
            ref[...] = (iqkv, iwo, inp)[i][...] if SL else jnp.zeros_like(ref)

    g0, b0 = np_ref[0:1, :], np_ref[1:2, :]
    col = lax.broadcasted_iota(jnp.int32, (16, 1, 1), 0)

    def turn(j, carry):
        f0 = pl.multiple_of(j * 16, 16)
        block = jnp.where(col < F - f0, g1t_ref[pl.ds(f0, 16)], 0).astype(BF).reshape(256, DP)
        gs[:, pl.ds(f0, 16)] = mm(perm_ref[...], block).reshape(R, 16, DP)
        return carry

    lax.fori_loop(0, FP // 16, turn, 0)

    def turn_y(j, carry):
        f0 = pl.multiple_of(j * 16, 16)
        block = yt_ref[pl.ds(f0, 16)].reshape(256, DP)
        y_ref[:, pl.ds(f0, 16), :] = mm(perm_ref[...], block).astype(BF).reshape(R, 16, DP)[:, :, 0:D]
        return carry

    lax.fori_loop(0, FP // 16 - 1, turn_y, 0)
    f0 = FP - 16
    block = jnp.where(col < F - f0, yt_ref[f0:FP], 0).astype(BF).reshape(256, DP)
    y_ref[:, f0:F, :] = mm(perm_ref[...], block).astype(BF).reshape(R, 16, DP)[:, 0 : F - f0, 0:D]

    if SL:
        both = dkv_ref[0].astype(F32)
        for i in range(1, dkv_ref.shape[0]):
            both = both + dkv_ref[i].astype(F32)
        both = both.astype(BF)
        z0 = jnp.zeros((SL, FP - FS, 2 * D), BF)
        zc = jnp.zeros((SL * FP, DP - D), BF)
        both = jnp.concatenate([both, z0], 1).reshape(SL * FP, 2 * D)
        dk2 = jnp.concatenate([both[:, 0:D], zc], 1)
        dv2 = jnp.concatenate([both[:, D : 2 * D], zc], 1)
        gs[0:SL] += (mm(dk2, wk2T_ref[...]) + mm(dv2, wv2T_ref[...])).reshape(SL, FP, DP)
        h1 = (n_ref[0:SL].astype(F32).reshape(SL * FP, DP) * g0 + b0).astype(BF)
        pack_pair(pack_ref, 2 * PAIR, mm_tn(h1, dk2), mm_tn(h1, dv2))

    def rows(i, carry):
        gsum, bsum = carry
        r0 = i * U
        g = gs[pl.ds(r0, U)].reshape(U * FP, DP)
        nf = n_ref[pl.ds(r0, U)].reshape(U * FP, DP).astype(F32)
        rc = nf[:, D : D + 1]
        n = nf * lane_ok
        gsum = gsum + fold8(g * n)
        bsum = bsum + fold8(g)
        da = norm_back(g, n, rc, g0, lane_ok)
        dfb = da.astype(BF)
        dfbs[pl.ds(pl.multiple_of(r0 * FP, FP), U * FP)] = dfb
        doa = mm(dfb, woT_ref[...]).astype(BF)
        outs = []
        for u in range(U):
            do = doa[u * FP : (u + 1) * FP]
            q = qkv_ref[r0 + u, :, 0:DP]
            k = qkv_ref[r0 + u, :, DP : 2 * DP]
            v = qkv_ref[r0 + u, :, 2 * DP : 3 * DP]
            p = p_ref[r0 + u]
            dom = spread(do, masks)
            dp = mm_nt(v, dom)
            pf = p.astype(F32)
            off = jnp.sum(pf * dp, 0, keepdims=True)
            ds = (pf * (dp - off)).astype(BF)
            dk = (mm(ds, spread(q, masks)) * SCALE).astype(BF)
            dv = mm(p, dom).astype(BF)
            kt = k.T
            dqt = []
            for j in range(H // 2):
                t = mm(kt[64 * j : 64 * j + 64], ds[:, 256 * j : 256 * j + 256])
                dqt += [t[0:32, 0:128], t[32:64, 128:256]]
            dqt = (jnp.concatenate(dqt + [jnp.zeros((DP - D, FP), F32)], 0) * SCALE).astype(BF)
            outs.append(jnp.concatenate([dqt.T, dk, dv], 1))
        all3 = jnp.concatenate(outs, 0)
        dqkvs[pl.ds(pl.multiple_of(r0 * FP, FP), U * FP)] = all3
        cg = da + mm(all3, wqkvT_ref[...])
        for u in range(U):
            cg_ref[r0 + u] = cg[u * FP : u * FP + F, 0:D]
            xs[r0 + u, 0:F, 0:D] = x_ref[r0 + u]
        return gsum, bsum

    z = jnp.zeros((8, DP), F32)
    gsum, bsum = lax.fori_loop(0, R // U, rows, (z, z))
    dnp[0] += gsum
    dnp[1] += bsum
    dqkv[...] += mm_tn(xs[...].reshape(R * FP, DP), dqkvs[...])
    dwo[...] += mm_tn(of_ref[...].reshape(R * FP, DP), dfbs[...])

    if SL:

        @pl.when(pl.program_id(0) == pl.num_programs(0) - 1)
        def _():
            a = dqkv[...]
            pack_pair(pack_ref, 0, a[:, 0:DP], a[:, DP : 2 * DP])
            pack_pair(pack_ref, PAIR, a[:, 2 * DP : 3 * DP], dwo)
            pack_norms(pack_ref, 3 * PAIR, [dnp[0], dnp[1]])


def feature_backward(x, qkv, p, of, n, g1t, yt, wqkvT, woT, np8, perm, row0, rows, R=16, U=2, slots=None, prev=None, packed=0):
    b0 = row0 // R
    nat = lambda w: pl.BlockSpec((R, FP, w), lambda i: (i + b0, 0, 0))
    turned = pl.BlockSpec((FP, R, DP), lambda i: (0, i + b0, 0))
    real = pl.BlockSpec((R, F, D), lambda i: (i + b0, 0, 0))
    accs = [shape((DP, 3 * DP), F32), shape((DP, DP), F32), shape((2, 8, DP), F32)]
    ins = [x, qkv, p, of, n, g1t, yt]
    specs = [real, nat(3 * DP), nat(H * FP), nat(DP), nat(DP), turned, turned]
    out_shape = [shape((x.shape[0], F, D), F32), shape((x.shape[0], F, D))]
    out_specs = [real, real]
    scratch = [
        pltpu.VMEM((R, FP, DP), F32),
        pltpu.VMEM((R, FP, DP), BF),
        pltpu.VMEM((R * FP, 3 * DP), BF),
        pltpu.VMEM((R * FP, DP), BF),
    ]
    SL = 0
    alias = {}
    shared = [wqkvT, woT, np8, perm]
    if slots is not None:
        SL = slots[0].shape[1]
        shared = list(slots) + shared
    ins += shared
    specs += [whole(a) for a in shared]
    if prev is not None:
        cg, y, *acc = prev
        ins += list(acc) + [cg, y]
        specs += [whole(a) for a in acc] + [pl.BlockSpec(memory_space=pl.ANY)] * 2
        alias = {len(ins) - 2: 0, len(ins) - 1: 1}
        out_shape.append(shape((packed, 128)))
        out_specs.append(pl.BlockSpec((packed, 128), lambda i: (0, 0)))
        scratch += [pltpu.VMEM(a.shape, F32) for a in accs]
    else:
        out_shape += accs
        out_specs += [whole(a) for a in accs]
    return pl.pallas_call(
        functools.partial(backward_kernel, R, U, SL),
        grid=(rows // R,),
        in_specs=specs,
        out_specs=out_specs,
        out_shape=out_shape,
        input_output_aliases=alias,
        scratch_shapes=scratch,
        compiler_params=params(),
        name="feature_backward",
    )(*ins)


def sum_kernel(parts_ref, out_ref):
    total = parts_ref[0].astype(F32)
    for i in range(1, parts_ref.shape[0]):
        total = total + parts_ref[i].astype(F32)
    out_ref[...] = total.astype(BF)


def sum_over_devices(packed, n):
    axes = ("table", "rows")
    rows = packed.shape[0] // n
    parts = lax.all_to_all(packed.reshape(n, rows, 128), axes, 0, 0)
    own = pl.pallas_call(
        sum_kernel, out_shape=shape((rows, 128)), compiler_params=params(), name="sum_parts"
    )(parts)
    copies = jnp.broadcast_to(own[None], (n, rows, 128))
    return lax.all_to_all(copies, axes, 0, 0).reshape(n * rows, 128)


def to_row(c):
    return jnp.broadcast_to(c, (c.shape[0], 128)).T[0:1]


def to_col(r):
    return jnp.broadcast_to(r, (128, r.shape[1])).T[:, 0:1]


def clipped(update, weight, count):
    def total(v):
        return jnp.sum(jnp.sum(v, 0, keepdims=True), 1, keepdims=True)

    rms = jnp.sqrt(total(update * update) * (1.0 / count))
    weight_rms = jnp.sqrt(total(weight * weight) * (1.0 / count))
    return update * (RATE * jnp.maximum(0.001, weight_rms) / jnp.maximum(1.0, rms / CLIP))


def optimizer_kernel(
    mid_ref, tail_ref, proj_ref, outw_ref, in_ref, hid_ref, norm_ref, sr_ref, sc_ref, mm_ref, mh_ref, ns_ref,
    proj_g, out_g, in_g, hid_g, norm_g, proj_n, out_n, in_n, hid_n, norm_n, sr_n, sc_n, mm_n, mh_n, ns_n,
):
    decay = 1.0 - STEP ** (-0.8)

    def stats(grad, col_old, row_old):
        square = grad * grad + 1e-30
        a, b = grad.shape
        over_sub = decay * row_old + (1.0 - decay) * (jnp.sum(square, 0, keepdims=True) * (1.0 / a))
        over_lane = decay * col_old + (1.0 - decay) * (jnp.sum(square, 1, keepdims=True) * (1.0 / b))
        return over_lane, over_sub

    def scaled(grad, col, row, mean):
        return grad * lax.rsqrt(col * (1.0 / mean)) * lax.rsqrt(row)

    def square_pair(ref, at):
        both = ref[at + 2 * D : at + 3 * D].astype(F32)
        a = jnp.concatenate([ref[at : at + D].astype(F32), both[:, 0:64]], 1)
        b = jnp.concatenate([ref[at + D : at + 2 * D].astype(F32), both[:, 64:128]], 1)
        return a, b

    wq, wk = square_pair(tail_ref, 0)
    wv, wo = square_pair(tail_ref, PAIR)
    wk2, wv2 = square_pair(tail_ref, 2 * PAIR)
    wq2, wo2 = square_pair(mid_ref, 12 * D)
    for i, grad in enumerate((wq, wk, wv, wq2, wk2, wv2, wo, wo2)):
        g_ref, n_ref, w_ref, j = (proj_g, proj_n, proj_ref, i) if i < 6 else (out_g, out_n, outw_ref, i - 6)
        g_ref[j] = grad
        col, row = stats(grad, to_col(sr_ref[i : i + 1, :]), sc_ref[i : i + 1, :])
        sr_n[i : i + 1, :] = to_row(col)
        sc_n[i : i + 1, :] = row
        mean = jnp.sum(col, 0, keepdims=True) * (1.0 / D)
        w = w_ref[j]
        n_ref[j] = w - clipped(scaled(grad, col, row, mean), w, D * D)

    def wide(at):
        return jnp.concatenate([mid_ref[at + D * j : at + D * j + D].astype(F32) for j in range(6)], 1)

    grad = wide(0)
    in_g[...] = grad
    col, row = stats(grad, to_col(mm_ref[0:1, :]), mh_ref[0:1, :])
    mm_n[0:1, :] = to_row(col)
    mh_n[0:1, :] = row
    mean = jnp.sum(col, 0, keepdims=True) * (1.0 / D)
    w = in_ref[...]
    in_n[...] = w - clipped(scaled(grad, col, row, mean), w, D * FF)
    grad = wide(6 * D)
    hid_g[...] = grad.T
    col, row = stats(grad, to_col(mm_ref[1:2, :]), mh_ref[1:2, :])
    mm_n[1:2, :] = to_row(col)
    mh_n[1:2, :] = row
    mean = jnp.sum(row, 1, keepdims=True) * (1.0 / FF)
    w = hid_ref[...]
    update = (grad * lax.rsqrt(col) * lax.rsqrt(row * (1.0 / mean))).T
    hid_n[...] = w - clipped(update, w, D * FF)

    pieces = []
    for ref, at, count in ((tail_ref, 3 * PAIR, 2), (mid_ref, 12 * D + PAIR, 4)):
        v = ref[at : at + 16].astype(F32)
        for i in range(count):
            pieces.append(jnp.concatenate([v[2 * i : 2 * i + 1], v[2 * i + 1 : 2 * i + 2, 0:64]], 1))
    grad = jnp.concatenate(pieces, 0)
    norm_g[...] = grad
    second = decay * ns_ref[...] + (1.0 - decay) * (grad * grad + 1e-30)
    ns_n[...] = second
    update = grad * lax.rsqrt(second)
    rms = jnp.sqrt(jnp.sum(update * update, 1, keepdims=True) * (1.0 / D))
    w = norm_ref[...]
    w_rms = jnp.sqrt(jnp.sum(w * w, 1, keepdims=True) * (1.0 / D))
    norm_n[...] = w - update * (RATE * jnp.maximum(0.001, w_rms) / jnp.maximum(1.0, rms / CLIP))


def optimizer(mid, tail, *state):
    proj, outw, w_in, w_out, norms, sr, sc, ms, hs, ns = state
    order = [proj, outw, w_in, w_out, norms, proj, outw, w_in, w_out, norms, sr, sc, ms, hs, ns]
    return pl.pallas_call(
        optimizer_kernel,
        out_shape=[shape(a.shape, F32) for a in order],
        compiler_params=params(),
        name="optimizer",
    )(mid, tail, *state)


def on_device(n, cells, cotangent, train_count, key_mask, train_order, *state):
    proj, outw, w_in, w_out, norms = state[:5]
    x = cells[0]
    rows_here = x.shape[0]
    unit = 8 * n
    tail_rows = -(-TAIL // unit) * unit
    mid_rows = -(-MID // unit) * unit
    perm = perm_matrix()
    (wqkv, wqkvT, wo, woT, wkv2, wk2T, wv2T, wq2, wq2T, wo2, wo2T, w1, w1T, w2, w2T, np8) = prepare(
        proj, outw, w_in, w_out, norms
    )
    own_kv = slot_keys(train_count, key_mask, train_order, x, wqkv, wo, wkv2, np8)
    shards = lax.axis_size("rows")
    copies = jnp.broadcast_to(own_kv[None], (shards,) + own_kv.shape)
    kv = lax.all_to_all(copies, "rows", 0, 0).reshape((-1,) + own_kv.shape[1:])
    nt, nn, qkv, p, of = feature_forward(x, wqkv, wo, perm)
    ct = to_columns(cotangent[0], perm)
    kt, vt, bias = gathered_columns(kv, perm)
    ws = (wq2, wq2T, wo2, wo2T, w1, w1T, w2, w2T)
    yt, g1t, dk, dv, mid = item_and_dense(nt, ct, kt, vt, bias, ws, np8, mid_rows)
    parts = slot_parts(dk, dv, perm).reshape((shards,) + own_kv.shape)
    parts = lax.all_to_all(parts, "rows", 0, 0)
    mid = sum_over_devices(mid, n)
    R = 16
    args = (x, qkv, p, of, nn, g1t, yt, wqkvT, woT, np8, perm)
    prev = feature_backward(*args, row0=R, rows=rows_here - R, R=R)
    cg, y, tail = feature_backward(
        *args, row0=0, rows=R, R=R, slots=(parts, wk2T, wv2T), prev=prev, packed=tail_rows
    )
    tail = sum_over_devices(tail, n)
    return (y[None], cg[None], *optimizer(mid, tail, *state))


def solution(mesh):
    n = int(mesh.shape["table"] * mesh.shape["rows"])
    cells = P("table", "rows", None, None)
    return jax.shard_map(
        functools.partial(on_device, n),
        mesh=mesh,
        in_specs=(cells, cells, P("table"), P("table", "rows"), P("table", "rows")) + (P(),) * 10,
        out_specs=(cells, cells) + (P(),) * 15,
        check_vma=False,
    )
```

```python
import functools

import jax
import jax.numpy as jnp
import numpy as np
from jax import lax
from jax.experimental import pallas as pl
from jax.experimental.pallas import tpu as pltpu
from jax.sharding import PartitionSpec as P

BF, F32 = jnp.bfloat16, jnp.float32
D, DP = 192, 256
H, E = 6, 32
F, FP = 119, 128
FS = 120
FF = 768
STEP = 3
CLIP = 0.3
RATE = 0.5
SCALE = E**-0.5
SCALE2 = SCALE * 1.4426950408889634
C0 = 0.7978845608028654
C1 = 0.044715
NT = (((1,), (1,)), ((), ()))
TN = (((0,), (0,)), ((), ()))
PAIR = 576
TAIL = 3 * PAIR + 8
MID = 2 * 6 * D + PAIR + 8


def mm(a, b):
    return jnp.dot(a, b, preferred_element_type=F32)


def mm_nt(a, b):
    return lax.dot_general(a, b, NT, preferred_element_type=F32)


def mm_tn(a, b):
    return lax.dot_general(a, b, TN, preferred_element_type=F32)


def lanes():
    return lax.broadcasted_iota(jnp.int32, (1, DP), 1)


def head_masks():
    lane = lanes()
    return [
        jnp.where((lane >= E * h) & (lane < E * (h + 1)), 1.0, 0.0).astype(BF) for h in range(H)
    ]


def spread(w, masks):
    return jnp.concatenate([w * m for m in masks], 0)


def layer_norm(a, lane_ok):
    c = a - jnp.sum(a, -1, keepdims=True) * (1.0 / D) * lane_ok
    rc = lax.rsqrt(jnp.sum(c * c, -1, keepdims=True) * (1.0 / D) + 1e-5)
    return c * rc, rc


def norm_back(g, n, rc, gain, lane_ok):
    dn = g * gain
    m1 = jnp.sum(dn, -1, keepdims=True) * (1.0 / D)
    m2 = jnp.sum(dn * n, -1, keepdims=True) * (1.0 / D)
    return (dn - m1 * lane_ok - n * m2) * rc


def fold8(v):
    return jnp.sum(v.reshape(v.shape[0] // 8, 8, v.shape[1]), 0)


def diagonal(full, keys):
    lane = lax.broadcasted_iota(jnp.int32, (1, 128), 1)
    low = full[0:keys, 0:128]
    for h in range(1, 4):
        low = jnp.where(lane >= E * h, full[h * keys : (h + 1) * keys, 0:128], low)
    high = jnp.where(
        lane >= E, full[5 * keys : 6 * keys, 128:256], full[4 * keys : 5 * keys, 128:256]
    )
    return jnp.concatenate([low, high], 1)


def whole(a):
    nd = len(a.shape)
    return pl.BlockSpec(a.shape, lambda *i: (0,) * nd)


def shape(s, t=BF):
    return jax.ShapeDtypeStruct(s, t)


def params(mib=58):
    return pltpu.CompilerParams(vmem_limit_bytes=mib << 20)


def cost(us):
    return pl.CostEstimate(flops=int(us * 1.1e9), bytes_accessed=int(us * 1e6), transcendentals=0)


def perm_matrix():
    place = np.zeros((256, 256), np.float32)
    for f in range(16):
        for r in range(16):
            place[f * 16 + r, r * 16 + f] = 1
    return jnp.asarray(place, BF)


def prep_kernel(
    proj, outw, w_in, w_out, norms, wqkv, wqkvT, wo, woT, wkv2, wk2T, wv2T, wq2, wq2T, wo2, wo2T, w1, w1T, w2, w2T, np8
):
    zc = jnp.zeros((D, DP - D), F32)
    zr = jnp.zeros((DP - D, DP), BF)

    def square(w):
        a = jnp.concatenate([w, zc], 1)
        a = jnp.concatenate([a.astype(BF), zr], 0)
        return a, a.T

    for i in range(3):
        a, t = square(proj[i])
        wqkv[:, i * DP : (i + 1) * DP] = a
        wqkvT[i * DP : (i + 1) * DP, :] = t
    for src, dst, dstT in ((outw[0], wo, woT), (proj[3], wq2, wq2T), (outw[1], wo2, wo2T)):
        a, t = square(src)
        dst[...] = a
        dstT[...] = t
    a, t = square(proj[4])
    wk2T[...] = t
    a, t = square(proj[5])
    wv2T[...] = t
    wkv2[0:D, :] = jnp.concatenate([proj[4], proj[5]], 1).astype(BF)
    wkv2[D:DP, :] = jnp.zeros((DP - D, 2 * D), BF)
    a = jnp.concatenate([w_in[...].astype(BF), jnp.zeros((DP - D, FF), BF)], 0)
    w1[...] = a
    w1T[...] = a.T
    a = jnp.concatenate([w_out[...], jnp.zeros((FF, DP - D), F32)], 1).astype(BF)
    w2[...] = a
    w2T[...] = a.T
    np8[...] = jnp.zeros((8, DP), F32)
    np8[0:6, 0:D] = norms[...]


def prepare(proj, outw, w_in, w_out, norms):
    sq = shape((DP, DP))
    outs = [
        shape((DP, 3 * DP)),
        shape((3 * DP, DP)),
        sq,
        sq,
        shape((DP, 2 * D)),
        sq,
        sq,
        sq,
        sq,
        sq,
        sq,
        shape((DP, FF)),
        shape((FF, DP)),
        shape((FF, DP)),
        shape((DP, FF)),
        shape((8, DP), F32),
    ]
    return pl.pallas_call(prep_kernel, out_shape=outs, compiler_params=params(), cost_estimate=cost(4), name="weights")(
        proj, outw, w_in, w_out, norms
    )


def feature_rows(x, wqkv, wo, masks, lane_ok, U, keep=None):
    qkv = mm(x, wqkv).astype(BF)
    outs = []
    for u in range(U):
        own = qkv[u * FP : (u + 1) * FP]
        q, k, v = own[:, 0:DP], own[:, DP : 2 * DP], own[:, 2 * DP : 3 * DP]
        st = mm_nt(k, spread(q, masks))
        row = lax.broadcasted_iota(jnp.int32, (8, 1), 0)
        st = jnp.concatenate([st[: FS - 8], jnp.where(row < F - FS + 8, st[FS - 8 : FS], -1e30)], 0)
        mx = jnp.max(st, 0, keepdims=True)
        e = jnp.exp2((st - mx) * SCALE2)
        total = jnp.sum(e, 0, keepdims=True)
        p = e * (1.0 / total)
        p = jnp.concatenate([p, jnp.zeros((FP - FS, H * FP), F32)], 0).astype(BF)
        vt = v.T
        ot = []
        for j in range(H // 2):
            t = mm(vt[64 * j : 64 * j + 64], p[:, 256 * j : 256 * j + 256])
            ot += [t[0:32, 0:128], t[32:64, 128:256]]
        ot = jnp.concatenate(ot + [jnp.zeros((DP - D, FP), F32)], 0).astype(BF)
        o = ot.T
        if keep is not None:
            keep(u, own, p, o)
        outs.append(o)
    o = jnp.concatenate(outs, 0)
    return layer_norm(x.astype(F32) + mm(o, wo), lane_ok)


def slots_kernel(SL, count_ref, mask_ref, order_ref, x_ref, wqkv_ref, wo_ref, wkv2_ref, np_ref, kv_ref, xs):
    xs[...] = jnp.zeros_like(xs)
    masks = head_masks()
    lane_ok = (lanes() < D).astype(F32)
    for u in range(SL):
        xs[u * FP : u * FP + F, 0:D] = x_ref[u]
    n, _ = feature_rows(xs[...], wqkv_ref[...], wo_ref[...], masks, lane_ok, SL)
    h = (n * np_ref[0:1, :] + np_ref[1:2, :]).astype(BF)
    kv = mm(h, wkv2_ref[...])
    row = lax.broadcasted_iota(jnp.int32, (FS, 1), 0)
    for u in range(SL):
        order = order_ref[0, u]
        usable = (order < count_ref[0]) & ((mask_ref[0, u] == 1) | (order == 0))
        flag = jnp.where(usable, 1.0, 0.0)
        kv_ref[u] = jnp.where(row < F, kv[u * FP : u * FP + FS], flag).astype(BF)


def slot_keys(count, mask, order, cells, wqkv, wo, wkv2, np8):
    SL = mask.shape[1]
    smem = pl.BlockSpec(memory_space=pltpu.SMEM)
    return pl.pallas_call(
        functools.partial(slots_kernel, SL),
        grid=(1,),
        in_specs=[smem, smem, smem, pl.BlockSpec((SL, F, D), lambda i: (0, 0, 0))]
        + [whole(a) for a in (wqkv, wo, wkv2, np8)],
        out_specs=pl.BlockSpec((SL, FS, 2 * D), lambda i: (0, 0, 0)),
        out_shape=shape((SL, FS, 2 * D)),
        scratch_shapes=[pltpu.VMEM((SL * FP, DP), BF)],
        compiler_params=params(),
        cost_estimate=cost(4), name="slot_keys",
    )(count, mask, order, cells, wqkv, wo, wkv2, np8)


def forward_kernel(R, U, x_ref, wqkv_ref, wo_ref, perm_ref, nt_ref, n_ref, qkv_ref, p_ref, of_ref, xs):
    @pl.when(pl.program_id(0) == 0)
    def _():
        xs[...] = jnp.zeros_like(xs)

    masks = head_masks()
    lane = lanes()
    lane_ok = (lane < D).astype(F32)

    def rows(i, carry):
        r0 = i * U
        for u in range(U):
            xs[u * FP : u * FP + F, 0:D] = x_ref[r0 + u]

        def keep(u, own, p, o):
            qkv_ref[r0 + u] = own
            p_ref[r0 + u] = p
            of_ref[r0 + u] = o

        n, rc = feature_rows(xs[...], wqkv_ref[...], wo_ref[...], masks, lane_ok, U, keep)
        n = jnp.where(lane >= D, rc, n).astype(BF)
        for u in range(U):
            n_ref[r0 + u] = n[u * FP : (u + 1) * FP]
        return carry

    lax.fori_loop(0, R // U, rows, 0)

    def turn(j, carry):
        f0 = pl.multiple_of(j * 16, 16)
        block = n_ref[:, pl.ds(f0, 16), :].reshape(R * 16, DP)
        nt_ref[pl.ds(f0, 16)] = mm(perm_ref[...], block).astype(BF).reshape(16, R, DP)
        return carry

    lax.fori_loop(0, FP // 16, turn, 0)


def feature_forward(cells, wqkv, wo, perm, R=16, U=4):
    rows = cells.shape[0]
    nat = lambda w: pl.BlockSpec((R, FP, w), lambda i: (i, 0, 0))
    return pl.pallas_call(
        functools.partial(forward_kernel, R, U),
        grid=(rows // R,),
        in_specs=[pl.BlockSpec((R, F, D), lambda i: (i, 0, 0)), whole(wqkv), whole(wo), whole(perm)],
        out_specs=[
            pl.BlockSpec((FP, R, DP), lambda i: (0, i, 0)),
            nat(DP),
            nat(3 * DP),
            nat(H * FP),
            nat(DP),
        ],
        out_shape=[
            shape((FP, rows, DP)),
            shape((rows, FP, DP)),
            shape((rows, FP, 3 * DP)),
            shape((rows, FP, H * FP)),
            shape((rows, FP, DP)),
        ],
        scratch_shapes=[pltpu.VMEM((U * FP, DP), BF)],
        compiler_params=params(),
        cost_estimate=cost(44), name="feature_forward",
    )(cells, wqkv, wo, perm)


def columns_kernel(x_ref, perm_ref, out_ref, xs):
    xs[...] = jnp.zeros_like(xs)
    xs[:, 0:F, 0:D] = x_ref[...]

    def turn(j, carry):
        f0 = pl.multiple_of(j * 16, 16)
        block = xs[:, pl.ds(f0, 16), :].reshape(256, DP)
        out_ref[pl.ds(f0, 16)] = mm(perm_ref[...], block).astype(BF).reshape(16, 16, DP)
        return carry

    lax.fori_loop(0, FP // 16, turn, 0)


def to_columns(x, perm):
    rows = x.shape[0]
    return pl.pallas_call(
        columns_kernel,
        grid=(rows // 16,),
        in_specs=[pl.BlockSpec((16, F, D), lambda i: (i, 0, 0)), whole(perm)],
        out_specs=pl.BlockSpec((FP, 16, DP), lambda i: (0, i, 0)),
        out_shape=shape((FP, rows, DP)),
        scratch_shapes=[pltpu.VMEM((16, FP, DP), BF)],
        compiler_params=params(),
        cost_estimate=cost(9), name="to_columns",
    )(x, perm)


def gathered_kernel(kv_ref, perm_ref, kt_ref, vt_ref, bias_ref, xs):
    xs[:, FS:FP, :] = jnp.zeros((16, FP - FS, 2 * D), BF)
    xs[:, 0:FS, :] = kv_ref[...]
    kt_ref[:, :, D:DP] = jnp.zeros((FP, 16, DP - D), BF)
    vt_ref[:, :, D:DP] = jnp.zeros((FP, 16, DP - D), BF)
    for j in range(FP // 16):
        f0 = 16 * j
        block = mm(perm_ref[...], xs[:, f0 : f0 + 16, :].reshape(256, 2 * D))
        if f0 < F <= f0 + 16:
            flag = block[(F - f0) * 16 : (F - f0 + 1) * 16, 0:128]
            bias_ref[...] = jnp.where(flag > 0.5, 0.0, -1e30)
        kt_ref[f0 : f0 + 16, :, 0:D] = block[:, 0:D].astype(BF).reshape(16, 16, D)
        vt_ref[f0 : f0 + 16, :, 0:D] = block[:, D : 2 * D].astype(BF).reshape(16, 16, D)


def gathered_columns(kv, perm):
    keys = kv.shape[0]
    col = pl.BlockSpec((FP, 16, DP), lambda i: (0, i, 0))
    return pl.pallas_call(
        gathered_kernel,
        grid=(keys // 16,),
        in_specs=[pl.BlockSpec((16, FS, 2 * D), lambda i: (i, 0, 0)), whole(perm)],
        out_specs=[col, col, pl.BlockSpec((16, 128), lambda i: (i, 0))],
        out_shape=[shape((FP, keys, DP)), shape((FP, keys, DP)), shape((keys, 128), F32)],
        scratch_shapes=[pltpu.VMEM((16, FP, 2 * D), BF)],
        compiler_params=params(),
        cost_estimate=cost(4), name="gathered_columns",
    )(kv, perm)


def parts_kernel(dk_ref, dv_ref, perm_ref, out_ref):
    col = lax.broadcasted_iota(jnp.int32, (16, 1, 1), 0)
    for j in range(FP // 16):
        f0 = 16 * j
        n = min(16, FS - f0)
        turned = []
        for ref in (dk_ref, dv_ref):
            block = ref[f0 : f0 + 16]
            if f0 + 16 > F:
                block = jnp.where(col < F - f0, block, 0).astype(BF)
            turned.append(mm(perm_ref[...], block.reshape(256, DP))[:, 0:D])
        both = jnp.concatenate(turned, 1).astype(BF).reshape(16, 16, 2 * D)
        out_ref[:, f0 : f0 + n, :] = both[:, 0:n, :]


def slot_parts(dk, dv, perm):
    keys = dk.shape[1]
    col = pl.BlockSpec((FP, 16, DP), lambda i: (0, i, 0))
    return pl.pallas_call(
        parts_kernel,
        grid=(keys // 16,),
        in_specs=[col, col, whole(perm)],
        out_specs=pl.BlockSpec((16, FS, 2 * D), lambda i: (i, 0, 0)),
        out_shape=shape((keys, FS, 2 * D)),
        compiler_params=params(),
        cost_estimate=cost(4), name="slot_parts",
    )(dk, dv, perm)


def pack_pair(ref, at, a, b):
    ref[at : at + D] = a[0:D, 0:128].astype(BF)
    ref[at + D : at + 2 * D] = b[0:D, 0:128].astype(BF)
    ref[at + 2 * D : at + 3 * D] = jnp.concatenate([a[0:D, 128:D], b[0:D, 128:D]], 1).astype(BF)


def pack_norms(ref, at, sums):
    rows = []
    for s in sums:
        v = jnp.sum(s, 0, keepdims=True)
        rows += [v[:, 0:128], v[:, 128:256]]
    rows.append(jnp.zeros((ref.shape[0] - at - len(rows), 128), F32))
    ref[at:] = jnp.concatenate(rows, 0).astype(BF)


def item_kernel(
    FB, RW, keys, CH, nt_ref, ct_ref, kt_ref, vt_ref, bias_ref, wq_ref, wqT_ref, wo_ref, woT_ref, w1_ref, w1T_ref,
    w2_ref, w2T_ref, np_ref, y_ref, g1_ref, dk_ref, dv_ref, pack_ref, dwq, dwo, dw1, dw2, dnp, h1b, qs, pbs, oi, da2s,
    dab, doi, dqs, h2b, dub, dbr, acts,
):
    M = FB * RW

    @pl.when(pl.program_id(0) == 0)
    def _():
        for ref in (dwq, dwo, dw1, dw2, dnp):
            ref[...] = jnp.zeros_like(ref)

    masks = head_masks()
    lane_ok = (lanes() < D).astype(F32)
    g0, b0, g1, b1, g2, b2 = [np_ref[i : i + 1, :] for i in range(6)]
    left = lax.broadcasted_iota(jnp.int32, (1, 2 * RW), 1) < RW
    HK = H * keys

    def attend(j, carry):
        s0 = pl.multiple_of(j * 2 * RW, 2 * RW)
        n = nt_ref[pl.ds(2 * j, 2)].reshape(2 * RW, DP).astype(F32)
        hb = (n * g0 + b0).astype(BF)
        h1b[pl.ds(s0, 2 * RW)] = hb
        q = mm(hb, wq_ref[...]).astype(BF)
        qs[pl.ds(s0, 2 * RW)] = q
        ka, kb = spread(kt_ref[2 * j], masks), spread(kt_ref[2 * j + 1], masks)
        st = jnp.where(left, mm_nt(ka, q), mm_nt(kb, q))
        st = st.reshape(H, keys, 2 * RW) + bias_ref[...][None]
        mx = jnp.max(st, 1, keepdims=True)
        e = jnp.exp2((st - mx) * SCALE2)
        total = jnp.sum(e, 1, keepdims=True)
        pb = (e * (1.0 / total)).reshape(HK, 2 * RW).astype(BF)
        pbs[j] = pb
        pt = pb.T
        va, vb = spread(vt_ref[2 * j], masks), spread(vt_ref[2 * j + 1], masks)
        oi[pl.ds(s0, RW)] = mm(pt[:RW], va).astype(BF)
        oi[pl.ds(s0 + RW, RW)] = mm(pt[RW:], vb).astype(BF)
        return carry

    lax.fori_loop(0, FB // 2, attend, 0)

    def dense(j, carry):
        gs2, bs2, gs1, bs1 = carry
        s0 = pl.multiple_of(j * CH, CH)
        cols = CH // RW
        h1 = nt_ref[pl.ds(j * cols, cols)].reshape(CH, DP).astype(F32) * g0 + b0
        n2, rc2 = layer_norm(h1 + mm(oi[pl.ds(s0, CH)], wo_ref[...]), lane_ok)
        h2 = n2 * g1 + b1
        hb = h2.astype(BF)
        h2b[pl.ds(s0, CH)] = hb
        u = mm(hb, w1_ref[...])
        uu = u * u
        th = jnp.tanh(u * (C0 + (C0 * C1) * uu))
        half = 0.5 + 0.5 * th
        act = (u * half).astype(BF)
        acts[pl.ds(s0, CH)] = act
        slope = half + (0.5 * u) * (1.0 - th * th) * (C0 + (3.0 * C0 * C1) * uu)
        n3, rc3 = layer_norm(h2 + mm(act, w2_ref[...]), lane_ok)
        y_ref[pl.ds(j * cols, cols)] = (n3 * g2 + b2).astype(BF).reshape(cols, RW, DP)
        g = ct_ref[pl.ds(j * cols, cols)].reshape(CH, DP).astype(F32)
        gs2 = gs2 + fold8(g * n3)
        bs2 = bs2 + fold8(g)
        d3 = norm_back(g, n3, rc3, g2, lane_ok)
        db = d3.astype(BF)
        dbr[pl.ds(s0, CH)] = db
        du = (mm(db, w2T_ref[...]) * slope).astype(BF)
        dub[pl.ds(s0, CH)] = du
        dh2 = d3 + mm(du, w1T_ref[...])
        gs1 = gs1 + fold8(dh2 * n2)
        bs1 = bs1 + fold8(dh2)
        d2 = norm_back(dh2, n2, rc2, g1, lane_ok)
        da2s[pl.ds(s0, CH)] = d2
        d2b = d2.astype(BF)
        dab[pl.ds(s0, CH)] = d2b
        doi[pl.ds(s0, CH)] = mm(d2b, woT_ref[...]).astype(BF)
        return gs2, bs2, gs1, bs1

    z = jnp.zeros((8, DP), F32)
    gs2, bs2, gs1, bs1 = lax.fori_loop(0, M // CH, dense, (z, z, z, z))
    dnp[0] += gs1
    dnp[1] += bs1
    dnp[2] += gs2
    dnp[3] += bs2
    zero = jnp.zeros((RW, DP), BF)

    def back(j, carry):
        s0 = pl.multiple_of(j * 2 * RW, 2 * RW)
        q, do = qs[pl.ds(s0, 2 * RW)], doi[pl.ds(s0, 2 * RW)]
        pb = pbs[j]
        ka, kb = spread(kt_ref[2 * j], masks), spread(kt_ref[2 * j + 1], masks)
        va, vb = spread(vt_ref[2 * j], masks), spread(vt_ref[2 * j + 1], masks)
        dp = jnp.where(left, mm_nt(va, do), mm_nt(vb, do)).reshape(H, keys, 2 * RW)
        p = pb.astype(F32).reshape(H, keys, 2 * RW)
        off = jnp.sum(p * dp, 1, keepdims=True)
        ds = (p * (dp - off)).reshape(HK, 2 * RW).astype(BF)
        dst = ds.T
        dq = jnp.concatenate([mm(dst[:RW], ka), mm(dst[RW:], kb)], 0) * SCALE
        dqs[pl.ds(s0, 2 * RW)] = dq.astype(BF)
        for c in range(2):
            part = slice(c * RW, (c + 1) * RW)
            qz = jnp.concatenate([q[part], zero] if c == 0 else [zero, q[part]], 0)
            dz = jnp.concatenate([do[part], zero] if c == 0 else [zero, do[part]], 0)
            dk_ref[2 * j + c] = (diagonal(mm(ds, qz), keys) * SCALE).astype(BF)
            dv_ref[2 * j + c] = diagonal(mm(pb, dz), keys).astype(BF)
        return carry

    lax.fori_loop(0, FB // 2, back, 0)

    def finish(j, carry):
        s0 = pl.multiple_of(j * CH, CH)
        cols = CH // RW
        g = da2s[pl.ds(s0, CH)] + mm(dqs[pl.ds(s0, CH)], wqT_ref[...])
        g1_ref[pl.ds(j * cols, cols)] = g.astype(BF).reshape(cols, RW, DP)
        return carry

    lax.fori_loop(0, M // CH, finish, 0)
    dwq[...] += mm_tn(h1b[...], dqs[...])
    dwo[...] += mm_tn(oi[...], dab[...])
    dw1[...] += mm_tn(h2b[...], dub[...])
    dw2[...] += mm_tn(dbr[...], acts[...])

    @pl.when(pl.program_id(0) == pl.num_programs(0) - 1)
    def _():
        at = 0
        for ref in (dw1, dw2):
            for j in range(FF // 128):
                pack_ref[at : at + D] = ref[0:D, 128 * j : 128 * j + 128].astype(BF)
                at += D
        pack_pair(pack_ref, at, dwq, dwo)
        pack_norms(pack_ref, at + PAIR, [dnp[i] for i in range(4)])


def item_and_dense(nt, ct, kt, vt, bias, ws, np8, packed, FB=8, CH=128):
    RW = nt.shape[1]
    keys = kt.shape[1]
    M = FB * RW
    cells = pl.BlockSpec((FB, RW, DP), lambda i: (i, 0, 0))
    slots = pl.BlockSpec((FB, keys, DP), lambda i: (i, 0, 0))
    own = pltpu.VMEM((M, DP), BF)
    wide = pltpu.VMEM((M, FF), BF)
    return pl.pallas_call(
        functools.partial(item_kernel, FB, RW, keys, CH),
        grid=(pl.cdiv(F, FB),),
        in_specs=[cells, cells, slots, slots, whole(bias)] + [whole(w) for w in ws] + [whole(np8)],
        out_specs=[cells, cells, slots, slots, pl.BlockSpec((packed, 128), lambda i: (0, 0))],
        out_shape=[shape((FP, RW, DP))] * 2 + [shape((FP, keys, DP))] * 2 + [shape((packed, 128))],
        scratch_shapes=[
            pltpu.VMEM((DP, DP), F32),
            pltpu.VMEM((DP, DP), F32),
            pltpu.VMEM((DP, FF), F32),
            pltpu.VMEM((DP, FF), F32),
            pltpu.VMEM((4, 8, DP), F32),
            own,
            own,
            pltpu.VMEM((FB // 2, H * keys, 2 * RW), BF),
            own,
            pltpu.VMEM((M, DP), F32),
            own,
            own,
            own,
            own,
            wide,
            own,
            wide,
        ],
        compiler_params=params(),
        cost_estimate=cost(180), name="item_and_dense",
    )(nt, ct, kt, vt, bias, *ws, np8)


def backward_kernel(R, U, SL, x_ref, qkv_ref, p_ref, of_ref, n_ref, g1t_ref, yt_ref, *rest):
    if SL:
        (dkv_ref, wk2T_ref, wv2T_ref, wqkvT_ref, woT_ref, np_ref, perm_ref, iqkv, iwo, inp, _, _,
         cg_ref, y_ref, pack_ref, gs, xs, dqkvs, dfbs, dqkv, dwo, dnp) = rest
    else:
        wqkvT_ref, woT_ref, np_ref, perm_ref, cg_ref, y_ref, dqkv, dwo, dnp, gs, xs, dqkvs, dfbs = rest
    masks = head_masks()
    lane_ok = (lanes() < D).astype(F32)

    @pl.when(pl.program_id(0) == 0)
    def _():
        xs[...] = jnp.zeros_like(xs)
        for i, ref in enumerate((dqkv, dwo, dnp)):
            ref[...] = (iqkv, iwo, inp)[i][...] if SL else jnp.zeros_like(ref)

    g0, b0 = np_ref[0:1, :], np_ref[1:2, :]
    col = lax.broadcasted_iota(jnp.int32, (16, 1, 1), 0)

    def turn(j, carry):
        f0 = pl.multiple_of(j * 16, 16)
        block = jnp.where(col < F - f0, g1t_ref[pl.ds(f0, 16)], 0).astype(BF).reshape(256, DP)
        gs[:, pl.ds(f0, 16)] = mm(perm_ref[...], block).reshape(R, 16, DP)
        return carry

    lax.fori_loop(0, FP // 16, turn, 0)

    def turn_y(j, carry):
        f0 = pl.multiple_of(j * 16, 16)
        block = yt_ref[pl.ds(f0, 16)].reshape(256, DP)
        y_ref[:, pl.ds(f0, 16), :] = mm(perm_ref[...], block).astype(BF).reshape(R, 16, DP)[:, :, 0:D]
        return carry

    lax.fori_loop(0, FP // 16 - 1, turn_y, 0)
    f0 = FP - 16
    block = jnp.where(col < F - f0, yt_ref[f0:FP], 0).astype(BF).reshape(256, DP)
    y_ref[:, f0:F, :] = mm(perm_ref[...], block).astype(BF).reshape(R, 16, DP)[:, 0 : F - f0, 0:D]

    if SL:
        both = dkv_ref[0].astype(F32)
        for i in range(1, dkv_ref.shape[0]):
            both = both + dkv_ref[i].astype(F32)
        both = both.astype(BF)
        z0 = jnp.zeros((SL, FP - FS, 2 * D), BF)
        zc = jnp.zeros((SL * FP, DP - D), BF)
        both = jnp.concatenate([both, z0], 1).reshape(SL * FP, 2 * D)
        dk2 = jnp.concatenate([both[:, 0:D], zc], 1)
        dv2 = jnp.concatenate([both[:, D : 2 * D], zc], 1)
        gs[0:SL] += (mm(dk2, wk2T_ref[...]) + mm(dv2, wv2T_ref[...])).reshape(SL, FP, DP)
        h1 = (n_ref[0:SL].astype(F32).reshape(SL * FP, DP) * g0 + b0).astype(BF)
        pack_pair(pack_ref, 2 * PAIR, mm_tn(h1, dk2), mm_tn(h1, dv2))

    def rows(i, carry):
        gsum, bsum = carry
        r0 = i * U
        g = gs[pl.ds(r0, U)].reshape(U * FP, DP)
        nf = n_ref[pl.ds(r0, U)].reshape(U * FP, DP).astype(F32)
        rc = nf[:, D : D + 1]
        n = nf * lane_ok
        gsum = gsum + fold8(g * n)
        bsum = bsum + fold8(g)
        da = norm_back(g, n, rc, g0, lane_ok)
        dfb = da.astype(BF)
        dfbs[pl.ds(pl.multiple_of(r0 * FP, FP), U * FP)] = dfb
        doa = mm(dfb, woT_ref[...]).astype(BF)
        outs = []
        for u in range(U):
            do = doa[u * FP : (u + 1) * FP]
            q = qkv_ref[r0 + u, :, 0:DP]
            k = qkv_ref[r0 + u, :, DP : 2 * DP]
            v = qkv_ref[r0 + u, :, 2 * DP : 3 * DP]
            p = p_ref[r0 + u]
            dom = spread(do, masks)
            dp = mm_nt(v, dom)
            pf = p.astype(F32)
            off = jnp.sum(pf * dp, 0, keepdims=True)
            ds = (pf * (dp - off)).astype(BF)
            dk = (mm(ds, spread(q, masks)) * SCALE).astype(BF)
            dv = mm(p, dom).astype(BF)
            kt = k.T
            dqt = []
            for j in range(H // 2):
                t = mm(kt[64 * j : 64 * j + 64], ds[:, 256 * j : 256 * j + 256])
                dqt += [t[0:32, 0:128], t[32:64, 128:256]]
            dqt = (jnp.concatenate(dqt + [jnp.zeros((DP - D, FP), F32)], 0) * SCALE).astype(BF)
            outs.append(jnp.concatenate([dqt.T, dk, dv], 1))
        all3 = jnp.concatenate(outs, 0)
        dqkvs[pl.ds(pl.multiple_of(r0 * FP, FP), U * FP)] = all3
        cg = da + mm(all3, wqkvT_ref[...])
        for u in range(U):
            cg_ref[r0 + u] = cg[u * FP : u * FP + F, 0:D]
            xs[r0 + u, 0:F, 0:D] = x_ref[r0 + u]
        return gsum, bsum

    z = jnp.zeros((8, DP), F32)
    gsum, bsum = lax.fori_loop(0, R // U, rows, (z, z))
    dnp[0] += gsum
    dnp[1] += bsum
    dqkv[...] += mm_tn(xs[...].reshape(R * FP, DP), dqkvs[...])
    dwo[...] += mm_tn(of_ref[...].reshape(R * FP, DP), dfbs[...])

    if SL:

        @pl.when(pl.program_id(0) == pl.num_programs(0) - 1)
        def _():
            a = dqkv[...]
            pack_pair(pack_ref, 0, a[:, 0:DP], a[:, DP : 2 * DP])
            pack_pair(pack_ref, PAIR, a[:, 2 * DP : 3 * DP], dwo)
            pack_norms(pack_ref, 3 * PAIR, [dnp[0], dnp[1]])


def feature_backward(x, qkv, p, of, n, g1t, yt, wqkvT, woT, np8, perm, row0, rows, R=16, U=2, slots=None, prev=None, packed=0):
    b0 = row0 // R
    nat = lambda w: pl.BlockSpec((R, FP, w), lambda i: (i + b0, 0, 0))
    turned = pl.BlockSpec((FP, R, DP), lambda i: (0, i + b0, 0))
    real = pl.BlockSpec((R, F, D), lambda i: (i + b0, 0, 0))
    accs = [shape((DP, 3 * DP), F32), shape((DP, DP), F32), shape((2, 8, DP), F32)]
    ins = [x, qkv, p, of, n, g1t, yt]
    specs = [real, nat(3 * DP), nat(H * FP), nat(DP), nat(DP), turned, turned]
    out_shape = [shape((x.shape[0], F, D), F32), shape((x.shape[0], F, D))]
    out_specs = [real, real]
    scratch = [
        pltpu.VMEM((R, FP, DP), F32),
        pltpu.VMEM((R, FP, DP), BF),
        pltpu.VMEM((R * FP, 3 * DP), BF),
        pltpu.VMEM((R * FP, DP), BF),
    ]
    SL = 0
    alias = {}
    shared = [wqkvT, woT, np8, perm]
    if slots is not None:
        SL = slots[0].shape[1]
        shared = list(slots) + shared
    ins += shared
    specs += [whole(a) for a in shared]
    if prev is not None:
        cg, y, *acc = prev
        ins += list(acc) + [cg, y]
        specs += [whole(a) for a in acc] + [pl.BlockSpec(memory_space=pl.ANY)] * 2
        alias = {len(ins) - 2: 0, len(ins) - 1: 1}
        out_shape.append(shape((packed, 128)))
        out_specs.append(pl.BlockSpec((packed, 128), lambda i: (0, 0)))
        scratch += [pltpu.VMEM(a.shape, F32) for a in accs]
    else:
        out_shape += accs
        out_specs += [whole(a) for a in accs]
    return pl.pallas_call(
        functools.partial(backward_kernel, R, U, SL),
        grid=(rows // R,),
        in_specs=specs,
        out_specs=out_specs,
        out_shape=out_shape,
        input_output_aliases=alias,
        scratch_shapes=scratch,
        compiler_params=params(),
        cost_estimate=cost(60), name="feature_backward",
    )(*ins)


def sum_kernel(parts_ref, out_ref):
    total = parts_ref[0].astype(F32)
    for i in range(1, parts_ref.shape[0]):
        total = total + parts_ref[i].astype(F32)
    total = total.astype(BF)
    for i in range(parts_ref.shape[0]):
        out_ref[i] = total


def sum_over_devices(packed, n):
    axes = ("table", "rows")
    rows = packed.shape[0] // n
    parts = lax.all_to_all(packed.reshape(n, rows, 128), axes, 0, 0)
    copies = pl.pallas_call(
        sum_kernel, out_shape=shape((n, rows, 128)), compiler_params=params(), cost_estimate=cost(2), name="sum_parts"
    )(parts)
    return lax.all_to_all(copies, axes, 0, 0).reshape(n * rows, 128)


def to_row(c):
    return jnp.broadcast_to(c, (c.shape[0], 128)).T[0:1]


def to_col(r):
    return jnp.broadcast_to(r, (128, r.shape[1])).T[:, 0:1]


def clipped(update, weight, count):
    def total(v):
        return jnp.sum(jnp.sum(v, 0, keepdims=True), 1, keepdims=True)

    rms = jnp.sqrt(total(update * update) * (1.0 / count))
    weight_rms = jnp.sqrt(total(weight * weight) * (1.0 / count))
    return update * (RATE * jnp.maximum(0.001, weight_rms) / jnp.maximum(1.0, rms / CLIP))


def optimizer_kernel(
    mid_ref, tail_ref, proj_ref, outw_ref, in_ref, hid_ref, norm_ref, sr_ref, sc_ref, mm_ref, mh_ref, ns_ref,
    proj_g, out_g, in_g, hid_g, norm_g, proj_n, out_n, in_n, hid_n, norm_n, sr_n, sc_n, mm_n, mh_n, ns_n,
):
    decay = 1.0 - STEP ** (-0.8)

    def stats(grad, col_old, row_old):
        square = grad * grad + 1e-30
        a, b = grad.shape
        over_sub = decay * row_old + (1.0 - decay) * (jnp.sum(square, 0, keepdims=True) * (1.0 / a))
        over_lane = decay * col_old + (1.0 - decay) * (jnp.sum(square, 1, keepdims=True) * (1.0 / b))
        return over_lane, over_sub

    def scaled(grad, col, row, mean):
        return grad * lax.rsqrt(col * (1.0 / mean)) * lax.rsqrt(row)

    def square_pair(ref, at):
        both = ref[at + 2 * D : at + 3 * D].astype(F32)
        a = jnp.concatenate([ref[at : at + D].astype(F32), both[:, 0:64]], 1)
        b = jnp.concatenate([ref[at + D : at + 2 * D].astype(F32), both[:, 64:128]], 1)
        return a, b

    wq, wk = square_pair(tail_ref, 0)
    wv, wo = square_pair(tail_ref, PAIR)
    wk2, wv2 = square_pair(tail_ref, 2 * PAIR)
    wq2, wo2 = square_pair(mid_ref, 12 * D)
    for i, grad in enumerate((wq, wk, wv, wq2, wk2, wv2, wo, wo2)):
        g_ref, n_ref, w_ref, j = (proj_g, proj_n, proj_ref, i) if i < 6 else (out_g, out_n, outw_ref, i - 6)
        g_ref[j] = grad
        col, row = stats(grad, to_col(sr_ref[i : i + 1, :]), sc_ref[i : i + 1, :])
        sr_n[i : i + 1, :] = to_row(col)
        sc_n[i : i + 1, :] = row
        mean = jnp.sum(col, 0, keepdims=True) * (1.0 / D)
        w = w_ref[j]
        n_ref[j] = w - clipped(scaled(grad, col, row, mean), w, D * D)

    def wide(at):
        return jnp.concatenate([mid_ref[at + D * j : at + D * j + D].astype(F32) for j in range(6)], 1)

    grad = wide(0)
    in_g[...] = grad
    col, row = stats(grad, to_col(mm_ref[0:1, :]), mh_ref[0:1, :])
    mm_n[0:1, :] = to_row(col)
    mh_n[0:1, :] = row
    mean = jnp.sum(col, 0, keepdims=True) * (1.0 / D)
    w = in_ref[...]
    in_n[...] = w - clipped(scaled(grad, col, row, mean), w, D * FF)
    grad = wide(6 * D)
    hid_g[...] = grad.T
    col, row = stats(grad, to_col(mm_ref[1:2, :]), mh_ref[1:2, :])
    mm_n[1:2, :] = to_row(col)
    mh_n[1:2, :] = row
    mean = jnp.sum(row, 1, keepdims=True) * (1.0 / FF)
    w = hid_ref[...]
    update = (grad * lax.rsqrt(col) * lax.rsqrt(row * (1.0 / mean))).T
    hid_n[...] = w - clipped(update, w, D * FF)

    pieces = []
    for ref, at, count in ((tail_ref, 3 * PAIR, 2), (mid_ref, 12 * D + PAIR, 4)):
        v = ref[at : at + 16].astype(F32)
        for i in range(count):
            pieces.append(jnp.concatenate([v[2 * i : 2 * i + 1], v[2 * i + 1 : 2 * i + 2, 0:64]], 1))
    grad = jnp.concatenate(pieces, 0)
    norm_g[...] = grad
    second = decay * ns_ref[...] + (1.0 - decay) * (grad * grad + 1e-30)
    ns_n[...] = second
    update = grad * lax.rsqrt(second)
    rms = jnp.sqrt(jnp.sum(update * update, 1, keepdims=True) * (1.0 / D))
    w = norm_ref[...]
    w_rms = jnp.sqrt(jnp.sum(w * w, 1, keepdims=True) * (1.0 / D))
    norm_n[...] = w - update * (RATE * jnp.maximum(0.001, w_rms) / jnp.maximum(1.0, rms / CLIP))


def optimizer(mid, tail, *state):
    proj, outw, w_in, w_out, norms, sr, sc, ms, hs, ns = state
    order = [proj, outw, w_in, w_out, norms, proj, outw, w_in, w_out, norms, sr, sc, ms, hs, ns]
    return pl.pallas_call(
        optimizer_kernel,
        out_shape=[shape(a.shape, F32) for a in order],
        compiler_params=params(),
        cost_estimate=cost(8), name="optimizer",
    )(mid, tail, *state)


def on_device(n, cells, cotangent, train_count, key_mask, train_order, *state):
    proj, outw, w_in, w_out, norms = state[:5]
    x = cells[0]
    rows_here = x.shape[0]
    unit = 8 * n
    tail_rows = -(-TAIL // unit) * unit
    mid_rows = -(-MID // unit) * unit
    perm = perm_matrix()
    (wqkv, wqkvT, wo, woT, wkv2, wk2T, wv2T, wq2, wq2T, wo2, wo2T, w1, w1T, w2, w2T, np8) = prepare(
        proj, outw, w_in, w_out, norms
    )
    own_kv = slot_keys(train_count, key_mask, train_order, x, wqkv, wo, wkv2, np8)
    shards = lax.axis_size("rows")
    kv = lax.all_gather(own_kv, "rows", axis=0, tiled=True)
    nt, nn, qkv, p, of = feature_forward(x, wqkv, wo, perm)
    ct = to_columns(cotangent[0], perm)
    kt, vt, bias = gathered_columns(kv, perm)
    ws = (wq2, wq2T, wo2, wo2T, w1, w1T, w2, w2T)
    yt, g1t, dk, dv, mid = item_and_dense(nt, ct, kt, vt, bias, ws, np8, mid_rows)
    parts = slot_parts(dk, dv, perm).reshape((shards,) + own_kv.shape)
    parts = lax.all_to_all(parts, "rows", 0, 0)
    mid = sum_over_devices(mid, n)
    R = 16
    args = (x, qkv, p, of, nn, g1t, yt, wqkvT, woT, np8, perm)
    prev = feature_backward(*args, row0=R, rows=rows_here - R, R=R)
    cg, y, tail = feature_backward(
        *args, row0=0, rows=R, R=R, slots=(parts, wk2T, wv2T), prev=prev, packed=tail_rows
    )
    tail = sum_over_devices(tail, n)
    return (y[None], cg[None], *optimizer(mid, tail, *state))


def solution(mesh):
    n = int(mesh.shape["table"] * mesh.shape["rows"])
    cells = P("table", "rows", None, None)
    return jax.shard_map(
        functools.partial(on_device, n),
        mesh=mesh,
        in_specs=(cells, cells, P("table"), P("table", "rows"), P("table", "rows")) + (P(),) * 10,
        out_specs=(cells, cells) + (P(),) * 15,
        check_vma=False,
    )
```

```python
import functools

import jax
import jax.numpy as jnp
import numpy as np
from jax import lax
from jax.experimental import pallas as pl
from jax.experimental.pallas import tpu as pltpu
from jax.sharding import PartitionSpec as P

BF, F32 = jnp.bfloat16, jnp.float32
D, DP = 192, 256
H, E = 6, 32
F, FP = 119, 128
FS = 120
FF = 768
STEP = 3
CLIP = 0.3
RATE = 0.5
SCALE = E**-0.5
SCALE2 = SCALE * 1.4426950408889634
C0 = 0.7978845608028654
C1 = 0.044715
NT = (((1,), (1,)), ((), ()))
TN = (((0,), (0,)), ((), ()))
PAIR = 576
TAIL = 3 * PAIR + 8
MID = 2 * 6 * D + PAIR + 8


def mm(a, b):
    return jnp.dot(a, b, preferred_element_type=F32)


def mm_nt(a, b):
    return lax.dot_general(a, b, NT, preferred_element_type=F32)


def mm_tn(a, b):
    return lax.dot_general(a, b, TN, preferred_element_type=F32)


def lanes():
    return lax.broadcasted_iota(jnp.int32, (1, DP), 1)


def head_masks():
    lane = lanes()
    return [
        jnp.where((lane >= E * h) & (lane < E * (h + 1)), 1.0, 0.0).astype(BF) for h in range(H)
    ]


def spread(w, masks):
    return jnp.concatenate([w * m for m in masks], 0)


def layer_norm(a, lane_ok):
    c = a - jnp.sum(a, -1, keepdims=True) * (1.0 / D) * lane_ok
    rc = lax.rsqrt(jnp.sum(c * c, -1, keepdims=True) * (1.0 / D) + 1e-5)
    return c * rc, rc


def norm_back(g, n, rc, gain, lane_ok):
    dn = g * gain
    m1 = jnp.sum(dn, -1, keepdims=True) * (1.0 / D)
    m2 = jnp.sum(dn * n, -1, keepdims=True) * (1.0 / D)
    return (dn - m1 * lane_ok - n * m2) * rc


def fold8(v):
    return jnp.sum(v.reshape(v.shape[0] // 8, 8, v.shape[1]), 0)


def diagonal(full, keys):
    lane = lax.broadcasted_iota(jnp.int32, (1, 128), 1)
    low = full[0:keys, 0:128]
    for h in range(1, 4):
        low = jnp.where(lane >= E * h, full[h * keys : (h + 1) * keys, 0:128], low)
    high = jnp.where(
        lane >= E, full[5 * keys : 6 * keys, 128:256], full[4 * keys : 5 * keys, 128:256]
    )
    return jnp.concatenate([low, high], 1)


def whole(a):
    nd = len(a.shape)
    return pl.BlockSpec(a.shape, lambda *i: (0,) * nd)


def shape(s, t=BF):
    return jax.ShapeDtypeStruct(s, t)


def params(mib=58):
    return pltpu.CompilerParams(vmem_limit_bytes=mib << 20)


def cost(us):
    return pl.CostEstimate(flops=int(us * 1.1e9), bytes_accessed=int(us * 1e6), transcendentals=0)


def perm_matrix():
    place = np.zeros((256, 256), np.float32)
    for f in range(16):
        for r in range(16):
            place[f * 16 + r, r * 16 + f] = 1
    return jnp.asarray(place, BF)


def prep_kernel(
    proj, outw, w_in, w_outT, norms, wqkv, wqkvT, wo, woT, wkv2, wk2T, wv2T, wq2, wq2T, wo2I, wo2, w1T, w1, w2T, w2, np8, vec
):
    zc = jnp.zeros((D, DP - D), F32)
    zr = jnp.zeros((DP - D, DP), BF)

    def square(w):
        a = jnp.concatenate([w, zc], 1)
        a = jnp.concatenate([a.astype(BF), zr], 0)
        return a, a.T

    for i in range(3):
        a, t = square(proj[i])
        wqkv[:, i * DP : (i + 1) * DP] = a
        wqkvT[i * DP : (i + 1) * DP, :] = t
    for src, dst, dstT in ((outw[0], wo, woT), (proj[3], wq2, wq2T)):
        a, t = square(src)
        dst[...] = a
        dstT[...] = t
    a, t = square(outw[1])
    wo2[...] = a[0:D]
    wo2I[:, 0:DP] = t[0:D]
    row = lax.broadcasted_iota(jnp.int32, (D, DP), 0)
    wo2I[:, DP : 2 * DP] = jnp.where(row == lax.broadcasted_iota(jnp.int32, (D, DP), 1), 1.0, 0.0).astype(BF)
    a, t = square(proj[4])
    wk2T[...] = t
    a, t = square(proj[5])
    wv2T[...] = t
    wkv2[0:D, :] = jnp.concatenate([proj[4], proj[5]], 1).astype(BF)
    wkv2[D:DP, :] = jnp.zeros((DP - D, 2 * D), BF)
    zw = jnp.zeros((DP - D, FF), BF)
    a = w_in[...].astype(BF)
    w1[...] = a
    w1T[...] = jnp.concatenate([a, zw], 0).T
    a = w_outT[...].astype(BF)
    w2T[...] = a
    w2[...] = jnp.concatenate([a, zw], 0).T
    np8[...] = jnp.zeros((8, DP), F32)
    np8[0:6, 0:D] = norms[...]
    for i in range(6):
        vec[i] = jnp.broadcast_to(np8[i : i + 1, :], (128, DP)).T[0:D]


def prepare(proj, outw, w_in, w_outT, norms):
    sq = shape((DP, DP))
    outs = [
        shape((DP, 3 * DP)),
        shape((3 * DP, DP)),
        sq,
        sq,
        shape((DP, 2 * D)),
        sq,
        sq,
        sq,
        sq,
        shape((D, 2 * DP)),
        shape((D, DP)),
        shape((FF, DP)),
        shape((D, FF)),
        shape((D, FF)),
        shape((FF, DP)),
        shape((8, DP), F32),
        shape((6, D, 128), F32),
    ]
    return pl.pallas_call(
        prep_kernel, out_shape=outs, compiler_params=params(), cost_estimate=cost(4), name="weights"
    )(proj, outw, w_in, w_outT, norms)


def feature_rows(x, wqkv, wo, masks, lane_ok, U, keep=None):
    qkv = mm(x, wqkv).astype(BF)
    outs = []
    for u in range(U):
        own = qkv[u * FP : (u + 1) * FP]
        q, k, v = own[:, 0:DP], own[:, DP : 2 * DP], own[:, 2 * DP : 3 * DP]
        st = mm_nt(k, spread(q, masks))
        row = lax.broadcasted_iota(jnp.int32, (8, 1), 0)
        st = jnp.concatenate([st[: FS - 8], jnp.where(row < F - FS + 8, st[FS - 8 : FS], -1e30)], 0)
        mx = jnp.max(st, 0, keepdims=True)
        e = jnp.exp2((st - mx) * SCALE2)
        total = jnp.sum(e, 0, keepdims=True)
        p = e * (1.0 / total)
        p = jnp.concatenate([p, jnp.zeros((FP - FS, H * FP), F32)], 0).astype(BF)
        vt = v.T
        ot = []
        for j in range(H // 2):
            t = mm(vt[64 * j : 64 * j + 64], p[:, 256 * j : 256 * j + 256])
            ot += [t[0:32, 0:128], t[32:64, 128:256]]
        ot = jnp.concatenate(ot + [jnp.zeros((DP - D, FP), F32)], 0).astype(BF)
        o = ot.T
        if keep is not None:
            keep(u, own, p, o)
        outs.append(o)
    o = jnp.concatenate(outs, 0)
    return layer_norm(x.astype(F32) + mm(o, wo), lane_ok)


def slots_kernel(SL, count_ref, mask_ref, order_ref, x_ref, wqkv_ref, wo_ref, wkv2_ref, np_ref, kv_ref, xs):
    xs[...] = jnp.zeros_like(xs)
    masks = head_masks()
    lane_ok = (lanes() < D).astype(F32)
    for u in range(SL):
        xs[u * FP : u * FP + F, 0:D] = x_ref[u]
    n, _ = feature_rows(xs[...], wqkv_ref[...], wo_ref[...], masks, lane_ok, SL)
    h = (n * np_ref[0:1, :] + np_ref[1:2, :]).astype(BF)
    kv = mm(h, wkv2_ref[...])
    row = lax.broadcasted_iota(jnp.int32, (FS, 1), 0)
    for u in range(SL):
        order = order_ref[0, u]
        usable = (order < count_ref[0]) & ((mask_ref[0, u] == 1) | (order == 0))
        flag = jnp.where(usable, 1.0, 0.0)
        kv_ref[u] = jnp.where(row < F, kv[u * FP : u * FP + FS], flag).astype(BF)


def slot_keys(count, mask, order, cells, wqkv, wo, wkv2, np8):
    SL = mask.shape[1]
    smem = pl.BlockSpec(memory_space=pltpu.SMEM)
    return pl.pallas_call(
        functools.partial(slots_kernel, SL),
        grid=(1,),
        in_specs=[smem, smem, smem, pl.BlockSpec((SL, F, D), lambda i: (0, 0, 0))]
        + [whole(a) for a in (wqkv, wo, wkv2, np8)],
        out_specs=pl.BlockSpec((SL, FS, 2 * D), lambda i: (0, 0, 0)),
        out_shape=shape((SL, FS, 2 * D)),
        scratch_shapes=[pltpu.VMEM((SL * FP, DP), BF)],
        compiler_params=params(),
        cost_estimate=cost(4), name="slot_keys",
    )(count, mask, order, cells, wqkv, wo, wkv2, np8)


def forward_kernel(R, U, x_ref, wqkv_ref, wo_ref, np_ref, perm_ref, nt_ref, n_ref, qkv_ref, p_ref, of_ref, xs, hs):
    @pl.when(pl.program_id(0) == 0)
    def _():
        xs[...] = jnp.zeros_like(xs)

    masks = head_masks()
    lane = lanes()
    lane_ok = (lane < D).astype(F32)

    def rows(i, carry):
        r0 = i * U
        for u in range(U):
            xs[u * FP : u * FP + F, 0:D] = x_ref[r0 + u]

        def keep(u, own, p, o):
            qkv_ref[r0 + u] = own
            p_ref[r0 + u] = p
            of_ref[r0 + u] = o

        n, rc = feature_rows(xs[...], wqkv_ref[...], wo_ref[...], masks, lane_ok, U, keep)
        h = (n * np_ref[0:1, :] + np_ref[1:2, :]).astype(BF)
        n = jnp.where(lane >= D, rc, n).astype(BF)
        for u in range(U):
            n_ref[r0 + u] = n[u * FP : (u + 1) * FP]
            hs[r0 + u] = h[u * FP : (u + 1) * FP]
        return carry

    lax.fori_loop(0, R // U, rows, 0)

    def turn(j, carry):
        f0 = pl.multiple_of(j * 16, 16)
        block = hs[:, pl.ds(f0, 16), :].reshape(R * 16, DP)
        nt_ref[pl.ds(f0, 16)] = mm(perm_ref[...], block).astype(BF).reshape(16, R, DP)
        return carry

    lax.fori_loop(0, FP // 16, turn, 0)


def feature_forward(cells, wqkv, wo, np8, perm, R=16, U=4):
    rows = cells.shape[0]
    nat = lambda w: pl.BlockSpec((R, FP, w), lambda i: (i, 0, 0))
    return pl.pallas_call(
        functools.partial(forward_kernel, R, U),
        grid=(rows // R,),
        in_specs=[pl.BlockSpec((R, F, D), lambda i: (i, 0, 0)), whole(wqkv), whole(wo), whole(np8), whole(perm)],
        out_specs=[
            pl.BlockSpec((FP, R, DP), lambda i: (0, i, 0)),
            nat(DP),
            nat(3 * DP),
            nat(H * FP),
            nat(DP),
        ],
        out_shape=[
            shape((FP, rows, DP)),
            shape((rows, FP, DP)),
            shape((rows, FP, 3 * DP)),
            shape((rows, FP, H * FP)),
            shape((rows, FP, DP)),
        ],
        scratch_shapes=[pltpu.VMEM((U * FP, DP), BF), pltpu.VMEM((R, FP, DP), BF)],
        compiler_params=params(),
        cost_estimate=cost(44), name="feature_forward",
    )(cells, wqkv, wo, np8, perm)


def columns_kernel(x_ref, perm_ref, out_ref, xs):
    xs[...] = jnp.zeros_like(xs)
    xs[:, 0:F, 0:D] = x_ref[...]

    def turn(j, carry):
        f0 = pl.multiple_of(j * 16, 16)
        block = xs[:, pl.ds(f0, 16), :].reshape(256, DP)
        out_ref[pl.ds(f0, 16)] = mm(perm_ref[...], block).astype(BF).reshape(16, 16, DP)
        return carry

    lax.fori_loop(0, FP // 16, turn, 0)


def to_columns(x, perm):
    rows = x.shape[0]
    return pl.pallas_call(
        columns_kernel,
        grid=(rows // 16,),
        in_specs=[pl.BlockSpec((16, F, D), lambda i: (i, 0, 0)), whole(perm)],
        out_specs=pl.BlockSpec((FP, 16, DP), lambda i: (0, i, 0)),
        out_shape=shape((FP, rows, DP)),
        scratch_shapes=[pltpu.VMEM((16, FP, DP), BF)],
        compiler_params=params(),
        cost_estimate=cost(9), name="to_columns",
    )(x, perm)


def gathered_kernel(kv_ref, perm_ref, kt_ref, vt_ref, bias_ref, xs):
    xs[:, FS:FP, :] = jnp.zeros((16, FP - FS, 2 * D), BF)
    xs[:, 0:FS, :] = kv_ref[...]
    kt_ref[:, :, D:DP] = jnp.zeros((FP, 16, DP - D), BF)
    vt_ref[:, :, D:DP] = jnp.zeros((FP, 16, DP - D), BF)
    for j in range(FP // 16):
        f0 = 16 * j
        block = mm(perm_ref[...], xs[:, f0 : f0 + 16, :].reshape(256, 2 * D))
        if f0 < F <= f0 + 16:
            flag = block[(F - f0) * 16 : (F - f0 + 1) * 16, 0:128]
            bias_ref[...] = jnp.where(flag > 0.5, 0.0, -1e30)
        kt_ref[f0 : f0 + 16, :, 0:D] = block[:, 0:D].astype(BF).reshape(16, 16, D)
        vt_ref[f0 : f0 + 16, :, 0:D] = block[:, D : 2 * D].astype(BF).reshape(16, 16, D)


def gathered_columns(kv, perm):
    keys = kv.shape[0]
    col = pl.BlockSpec((FP, 16, DP), lambda i: (0, i, 0))
    return pl.pallas_call(
        gathered_kernel,
        grid=(keys // 16,),
        in_specs=[pl.BlockSpec((16, FS, 2 * D), lambda i: (i, 0, 0)), whole(perm)],
        out_specs=[col, col, pl.BlockSpec((16, 128), lambda i: (i, 0))],
        out_shape=[shape((FP, keys, DP)), shape((FP, keys, DP)), shape((keys, 128), F32)],
        scratch_shapes=[pltpu.VMEM((16, FP, 2 * D), BF)],
        compiler_params=params(),
        cost_estimate=cost(4), name="gathered_columns",
    )(kv, perm)


def parts_kernel(dk_ref, dv_ref, perm_ref, out_ref):
    col = lax.broadcasted_iota(jnp.int32, (16, 1, 1), 0)
    for j in range(FP // 16):
        f0 = 16 * j
        n = min(16, FS - f0)
        turned = []
        for ref in (dk_ref, dv_ref):
            block = ref[f0 : f0 + 16]
            if f0 + 16 > F:
                block = jnp.where(col < F - f0, block, 0).astype(BF)
            turned.append(mm(perm_ref[...], block.reshape(256, DP))[:, 0:D])
        both = jnp.concatenate(turned, 1).astype(BF).reshape(16, 16, 2 * D)
        out_ref[:, f0 : f0 + n, :] = both[:, 0:n, :]


def slot_parts(dk, dv, perm):
    keys = dk.shape[1]
    col = pl.BlockSpec((FP, 16, DP), lambda i: (0, i, 0))
    return pl.pallas_call(
        parts_kernel,
        grid=(keys // 16,),
        in_specs=[col, col, whole(perm)],
        out_specs=pl.BlockSpec((16, FS, 2 * D), lambda i: (i, 0, 0)),
        out_shape=shape((keys, FS, 2 * D)),
        compiler_params=params(),
        cost_estimate=cost(4), name="slot_parts",
    )(dk, dv, perm)


def pack_pair(ref, at, a, b):
    ref[at : at + D] = a[0:D, 0:128].astype(BF)
    ref[at + D : at + 2 * D] = b[0:D, 0:128].astype(BF)
    ref[at + 2 * D : at + 3 * D] = jnp.concatenate([a[0:D, 128:D], b[0:D, 128:D]], 1).astype(BF)


def pack_norms(ref, at, sums):
    rows = []
    for s in sums:
        if s.shape[0] == D:
            s = jnp.concatenate([s, jnp.zeros((DP - D, 128), F32)], 0).T
        v = jnp.sum(s, 0, keepdims=True)
        rows += [v[:, 0:128], v[:, 128:256]]
    rows.append(jnp.zeros((ref.shape[0] - at - len(rows), 128), F32))
    ref[at:] = jnp.concatenate(rows, 0).astype(BF)


def half_masks():
    lane = lax.broadcasted_iota(jnp.int32, (1, 128), 1)
    return [jnp.where((lane >= E * h) & (lane < E * (h + 1)), 1.0, 0.0).astype(BF) for h in range(4)]

def spread_halves(w, masks):
    z = jnp.zeros((w.shape[0], 128), BF)
    lo, hi = w[:, 0:128], w[:, 128:256]
    return jnp.concatenate(
        [jnp.concatenate([lo * masks[h], z], 1) for h in range(4)]
        + [jnp.concatenate([z, hi * masks[h]], 1) for h in range(2)], 0)

def mean0(a): return jnp.sum(a, 0, keepdims=True) * (1.0 / D)

def norm_t(a):
    c = a - mean0(a)
    rc = lax.rsqrt(mean0(c * c) + 1e-5)
    return c * rc, rc

def norm_back_t(g, n, rc, gain):
    dn = g * gain
    return (dn - mean0(dn) - n * mean0(dn * n)) * rc

def tall(a):
    return jnp.concatenate([a, jnp.zeros((DP - D, a.shape[1]), a.dtype)], 0)

def gelu_parts(u):
    uu = u * u
    th = jnp.tanh(u * (BF(C0) + BF(C0 * C1) * uu))
    half = BF(0.5) + BF(0.5) * th
    act = u * half
    slope = half + act * (BF(1.0) - th) * (BF(C0) + BF(3.0 * C0 * C1) * uu)
    return act, slope


def weave(streams):
    live=[[g,s,p] for g,s,p in streams]
    turn=0
    while live:
        for it in list(live):
            if turn>=it[1]:
                for _ in range(it[2]):
                    try: next(it[0])
                    except StopIteration:
                        live.remove(it); break
        turn+=1

def item_kernel(FB, RW, keys, OFF, WP, CC, WC,
    ht_ref, ct_ref, kt_ref, vt_ref, bias_ref, wq_ref, wqT_ref, woI_ref, wo_ref, w1T_ref, w1_ref, w2T_ref, w2_ref, vec_ref,
    y_ref, g1_ref, dk_ref, dv_ref, pack_ref, dwq, dwo, dw1, dw2, dnp,
    hbTs, ois, hb2Ts, actss, dbTs, duss, dabTs, dqss, slp):
    step = pl.program_id(0)
    @pl.when(step == 0)
    def _():
        for ref in (dwq, dwo, dw1, dw2, dnp):
            ref[...] = jnp.zeros_like(ref)
        for ref in (hbTs, ois, hb2Ts, actss, dbTs, duss, dabTs, dqss):
            ref[1] = jnp.zeros_like(ref[1])
    cur = step % 2
    masks = half_masks()
    LW = 2 * RW
    left = lax.broadcasted_iota(jnp.int32, (1, LW), 1) < RW
    HK = H * keys
    hbT, oi, hb2T, acts, dbT, dus, dabT, dqs = [r.at[cur] for r in (hbTs, ois, hb2Ts, actss, dbTs, duss, dabTs, dqss)]
    def attend(j, out):
        h = ht_ref[2 * j:2 * j + 2].reshape(LW, DP)
        q = (mm(h, wq_ref[...]) * SCALE2).astype(BF)
        yield
        ks = [spread_halves(kt_ref[2 * j + c], masks) for c in range(2)]
        hbT[:, j * LW:(j + 1) * LW] = h.T[0:D]
        yield
        st = jnp.where(left, mm_nt(ks[0], q), mm_nt(ks[1], q))
        yield
        vs = [spread_halves(vt_ref[2 * j + c], masks) for c in range(2)]
        pbs = []
        for hh in range(H):
            s = st[hh * keys:(hh + 1) * keys] + bias_ref[...]
            e = jnp.exp2(s - jnp.max(s, 0, keepdims=True))
            pbs.append((e * (1.0 / jnp.sum(e, 0, keepdims=True))).astype(BF))
            if hh % 2: yield
        pb = jnp.concatenate(pbs, 0)
        pt = pb.T
        yield
        o = jnp.concatenate([mm(pt[:RW], vs[0]), mm(pt[RW:], vs[1])], 0).astype(BF)
        oi[j * LW:(j + 1) * LW] = o
        out.extend([q, pb, ks, vs, o])
        yield
    def dense(i, os, out):
        c0 = i * 2 * LW
        g1v, b1v, g2v, b2v = [vec_ref[i] for i in range(2, 6)]
        h = ht_ref[4 * i:4 * i + 4].reshape(2 * LW, DP)
        o = jnp.concatenate(os, 0)
        aT = mm_nt(woI_ref[...], jnp.concatenate([o, h], 1))
        yield
        n2, rc2, h2, hb2 = [], [], [], []
        for t in range(2):
            n, rc = norm_t(aT[:, t * LW:(t + 1) * LW])
            hh = n * g1v + b1v
            n2.append(n.astype(BF)); rc2.append(rc); hb2.append(hh.astype(BF))
            yield
        hb2 = jnp.concatenate(hb2, 1)
        hb2T[:, c0:c0 + 2 * LW] = hb2
        hb2 = tall(hb2)
        C = CC
        u = mm(w1T_ref[0:C], hb2)
        for c in range(FF // C):
            un = mm(w1T_ref[C * c + C:C * c + 2 * C], hb2) if c + 1 < FF // C else None
            act, slope = gelu_parts(u.astype(BF))
            acts[C * c:C * c + C, c0:c0 + 2 * LW] = act
            slp[C * c:C * c + C, c0:c0 + 2 * LW] = slope
            u = un
            yield
        gT = ct_ref[4 * i:4 * i + 4].reshape(2 * LW, DP).T[0:D].astype(F32)
        z = mm(w2T_ref[...], acts[:, c0:c0 + 2 * LW])
        yield
        dbs, d3s = [], []
        ys = []
        for t in range(2):
            sl = slice(t * LW, (t + 1) * LW)
            n3, rc3 = norm_t(hb2[0:D, sl].astype(F32) + z[:, sl])
            ys.append((n3 * g2v + b2v).astype(BF))
            yield
            g = gT[:, sl]
            dnp[2] += g * n3
            dnp[3] += g
            d3 = norm_back_t(g, n3, rc3, g2v)
            dbs.append(d3.astype(BF))
            yield
        db = jnp.concatenate(dbs, 1)
        dbT[:, c0:c0 + 2 * LW] = db
        db = tall(db)
        w = mm(w2_ref[0:C], db)
        for c in range(FF // C):
            wn = mm(w2_ref[C * c + C:C * c + 2 * C], db) if c + 1 < FF // C else None
            dus[C * c:C * c + C, c0:c0 + 2 * LW] = w.astype(BF) * slp[C * c:C * c + C, c0:c0 + 2 * LW]
            w = wn
            yield
        dh = mm(w1_ref[...], dus[:, c0:c0 + 2 * LW])
        yT = tall(jnp.concatenate(ys, 1))
        y_ref[4 * i:4 * i + 4] = yT.T.reshape(4, RW, DP)
        yield
        dabs = []
        for t in range(2):
            dh2 = dbs[t].astype(F32) + dh[:, t * LW:(t + 1) * LW]
            n2f = n2[t].astype(F32)
            dnp[0] += dh2 * n2f
            dnp[1] += dh2
            dabs.append(norm_back_t(dh2, n2f, rc2[t], g1v).astype(BF))
            yield
        dab = jnp.concatenate(dabs, 1)
        dabT[:, c0:c0 + 2 * LW] = dab
        doT = mm(wo_ref[...], tall(dab)).astype(BF)
        out.extend([dab, doT])
        yield
    def back(j, at, doT, out):
        q, pb, ks, vs, _ = at
        do = tall(doT)
        don = do.T
        dp = jnp.where(left, mm(vs[0], do), mm(vs[1], do))
        yield
        slot_sums(dv_ref, j, pb, don, None)
        yield
        dss = []
        for hh in range(H):
            sl = slice(hh * keys, (hh + 1) * keys)
            p, d = pb[sl].astype(F32), dp[sl]
            dss.append((p * (d - jnp.sum(p * d, 0, keepdims=True))).astype(BF))
            if hh % 2: yield
        ds = jnp.concatenate(dss, 0)
        dst = ds.T
        yield
        slot_sums(dk_ref, j, ds, q, 0.6931471805599453)
        yield
        dq = jnp.concatenate([mm(dst[:RW], ks[0]), mm(dst[RW:], ks[1])], 0) * SCALE
        dq = dq.astype(BF)
        dqs[j * LW:(j + 1) * LW] = dq
        out.append(dq)
        yield
    lane = lax.broadcasted_iota(jnp.int32, (1, 128), 1)
    zq = jnp.zeros((RW, 128), BF)
    def slot_sums(ref, j, w, rows, scale):
        out = [[], []]
        for t, heads in ((0, 4), (1, 2)):
            r = rows[:, 128 * t:128 * t + 128]
            both = jnp.concatenate([jnp.concatenate([r[:RW], zq], 0), jnp.concatenate([zq, r[RW:]], 0)], 1)
            full = mm(w[4 * t * keys:(4 * t + heads) * keys], both)
            for c in range(2):
                col = full[:, 128 * c:128 * c + 128]
                v = col[0:keys]
                for hh in range(1, heads):
                    v = jnp.where(lane >= E * hh, col[hh * keys:(hh + 1) * keys], v)
                out[c].append(v)
        for c in range(2):
            v = jnp.concatenate(out[c], 1)
            ref[2 * j + c] = (v if scale is None else v * scale).astype(BF)
    def finish(i, dqv, dab):
        dq = jnp.concatenate(dqv, 0)
        g1 = mm(dq, wqT_ref[...]) + tall(dab).T.astype(F32)
        g1_ref[4 * i:4 * i + 4] = g1.astype(BF).reshape(4, RW, DP)
        yield
    def chunk(i):
        at = [[], []]
        ga, gb = attend(2 * i, at[0]), attend(2 * i + 1, at[1])
        for _ in zip(ga, gb): yield
        for _ in ga: yield
        for _ in gb: yield
        out = []
        yield from dense(i, [at[0][4], at[1][4]], out)
        dab, doT = out
        dq = []
        for t in range(2):
            yield from back(2 * i + t, at[t], doT[:, t * LW:(t + 1) * LW], dq)
        yield from finish(i, dq, dab)
    def wgrad(b):
        dwq[...] += mm(hbTs[b], dqss[b])
        yield
        dwo[...] += mm(dabTs[b], ois[b])
        yield
        for c in range(0, FF, WC):
            dw1[c:c + WC] += mm_nt(duss[b, c:c + WC], hb2Ts[b])
            yield
        for c in range(0, FF, WC):
            dw2[c:c + WC] += mm_nt(actss[b, c:c + WC], dbTs[b])
            yield
    NC = FB // 4
    if True:
        weave([(chunk(i), i * OFF, 1) for i in range(NC)] + [(wgrad(1 - cur), WP, 1)])
        @pl.when(step == pl.num_programs(0) - 1)
        def _():
            for _ in wgrad(cur): pass
            at = 0
            for ref in (dw1, dw2):
                t = ref[...].T
                for j in range(FF // 128):
                    pack_ref[at:at + D] = t[:, 128 * j:128 * j + 128].astype(BF)
                    at += D
            pack_pair(pack_ref, at, dwq, tall(dwo[...]).T)
            pack_norms(pack_ref, at + PAIR, [dnp[i] for i in range(4)])


def item_and_dense(ht, ct, kt, vt, bias, ws, vec, packed, FB=8, OFF=0, WP=20, CC=384, WC=384):
    RW = ht.shape[1]
    keys = kt.shape[1]
    M = FB * RW
    cells = pl.BlockSpec((FB, RW, DP), lambda i: (i, 0, 0))
    slots = pl.BlockSpec((FB, keys, DP), lambda i: (i, 0, 0))
    accs = [(D, DP), (D, DP), (FF, D), (FF, D), (4, D, 128)]
    kept = [(D, M), (M, DP), (D, M), (FF, M), (D, M), (FF, M), (D, M), (M, DP)]
    return pl.pallas_call(
        functools.partial(item_kernel, FB, RW, keys, OFF, WP, CC, WC),
        grid=(pl.cdiv(F, FB),),
        in_specs=[cells, cells, slots, slots, whole(bias)] + [whole(w) for w in ws] + [whole(vec)],
        out_specs=[cells, cells, slots, slots, pl.BlockSpec((packed, 128), lambda i: (0, 0))],
        out_shape=[shape((FP, RW, DP))] * 2 + [shape((FP, keys, DP))] * 2 + [shape((packed, 128))],
        scratch_shapes=[pltpu.VMEM(a, F32) for a in accs]
        + [pltpu.VMEM((2,) + a, BF) for a in kept]
        + [pltpu.VMEM((FF, M), BF)],
        compiler_params=params(),
        cost_estimate=cost(110),
        name="item_and_dense",
    )(ht, ct, kt, vt, bias, *ws, vec)


def backward_kernel(R, U, SL, x_ref, qkv_ref, p_ref, of_ref, n_ref, g1t_ref, yt_ref, *rest):
    if SL:
        (dkv_ref, wk2T_ref, wv2T_ref, wqkvT_ref, woT_ref, np_ref, perm_ref, iqkv, iwo, inp, _, _,
         cg_ref, y_ref, pack_ref, gs, xs, dqkvs, dfbs, dqkv, dwo, dnp) = rest
    else:
        wqkvT_ref, woT_ref, np_ref, perm_ref, cg_ref, y_ref, dqkv, dwo, dnp, gs, xs, dqkvs, dfbs = rest
    masks = head_masks()
    lane_ok = (lanes() < D).astype(F32)

    @pl.when(pl.program_id(0) == 0)
    def _():
        xs[...] = jnp.zeros_like(xs)
        for i, ref in enumerate((dqkv, dwo, dnp)):
            ref[...] = (iqkv, iwo, inp)[i][...] if SL else jnp.zeros_like(ref)

    g0, b0 = np_ref[0:1, :], np_ref[1:2, :]
    col = lax.broadcasted_iota(jnp.int32, (16, 1, 1), 0)

    def turn(j, carry):
        f0 = pl.multiple_of(j * 16, 16)
        block = jnp.where(col < F - f0, g1t_ref[pl.ds(f0, 16)], 0).astype(BF).reshape(256, DP)
        gs[:, pl.ds(f0, 16)] = mm(perm_ref[...], block).reshape(R, 16, DP)
        return carry

    lax.fori_loop(0, FP // 16, turn, 0)

    def turn_y(j, carry):
        f0 = pl.multiple_of(j * 16, 16)
        block = yt_ref[pl.ds(f0, 16)].reshape(256, DP)
        y_ref[:, pl.ds(f0, 16), :] = mm(perm_ref[...], block).astype(BF).reshape(R, 16, DP)[:, :, 0:D]
        return carry

    lax.fori_loop(0, FP // 16 - 1, turn_y, 0)
    f0 = FP - 16
    block = jnp.where(col < F - f0, yt_ref[f0:FP], 0).astype(BF).reshape(256, DP)
    y_ref[:, f0:F, :] = mm(perm_ref[...], block).astype(BF).reshape(R, 16, DP)[:, 0 : F - f0, 0:D]

    if SL:
        both = dkv_ref[0].astype(F32)
        for i in range(1, dkv_ref.shape[0]):
            both = both + dkv_ref[i].astype(F32)
        both = both.astype(BF)
        z0 = jnp.zeros((SL, FP - FS, 2 * D), BF)
        zc = jnp.zeros((SL * FP, DP - D), BF)
        both = jnp.concatenate([both, z0], 1).reshape(SL * FP, 2 * D)
        dk2 = jnp.concatenate([both[:, 0:D], zc], 1)
        dv2 = jnp.concatenate([both[:, D : 2 * D], zc], 1)
        gs[0:SL] += (mm(dk2, wk2T_ref[...]) + mm(dv2, wv2T_ref[...])).reshape(SL, FP, DP)
        h1 = (n_ref[0:SL].astype(F32).reshape(SL * FP, DP) * g0 + b0).astype(BF)
        pack_pair(pack_ref, 2 * PAIR, mm_tn(h1, dk2), mm_tn(h1, dv2))

    def rows(i, carry):
        gsum, bsum = carry
        r0 = i * U
        g = gs[pl.ds(r0, U)].reshape(U * FP, DP)
        nf = n_ref[pl.ds(r0, U)].reshape(U * FP, DP).astype(F32)
        rc = nf[:, D : D + 1]
        n = nf * lane_ok
        gsum = gsum + fold8(g * n)
        bsum = bsum + fold8(g)
        da = norm_back(g, n, rc, g0, lane_ok)
        dfb = da.astype(BF)
        dfbs[pl.ds(pl.multiple_of(r0 * FP, FP), U * FP)] = dfb
        doa = mm(dfb, woT_ref[...]).astype(BF)
        outs = []
        for u in range(U):
            do = doa[u * FP : (u + 1) * FP]
            q = qkv_ref[r0 + u, :, 0:DP]
            k = qkv_ref[r0 + u, :, DP : 2 * DP]
            v = qkv_ref[r0 + u, :, 2 * DP : 3 * DP]
            p = p_ref[r0 + u]
            dom = spread(do, masks)
            dp = mm_nt(v, dom)
            pf = p.astype(F32)
            off = jnp.sum(pf * dp, 0, keepdims=True)
            ds = (pf * (dp - off)).astype(BF)
            dk = (mm(ds, spread(q, masks)) * SCALE).astype(BF)
            dv = mm(p, dom).astype(BF)
            kt = k.T
            dqt = []
            for j in range(H // 2):
                t = mm(kt[64 * j : 64 * j + 64], ds[:, 256 * j : 256 * j + 256])
                dqt += [t[0:32, 0:128], t[32:64, 128:256]]
            dqt = (jnp.concatenate(dqt + [jnp.zeros((DP - D, FP), F32)], 0) * SCALE).astype(BF)
            outs.append(jnp.concatenate([dqt.T, dk, dv], 1))
        all3 = jnp.concatenate(outs, 0)
        dqkvs[pl.ds(pl.multiple_of(r0 * FP, FP), U * FP)] = all3
        cg = da + mm(all3, wqkvT_ref[...])
        for u in range(U):
            cg_ref[r0 + u] = cg[u * FP : u * FP + F, 0:D]
            xs[r0 + u, 0:F, 0:D] = x_ref[r0 + u]
        return gsum, bsum

    z = jnp.zeros((8, DP), F32)
    gsum, bsum = lax.fori_loop(0, R // U, rows, (z, z))
    dnp[0] += gsum
    dnp[1] += bsum
    dqkv[...] += mm_tn(xs[...].reshape(R * FP, DP), dqkvs[...])
    dwo[...] += mm_tn(of_ref[...].reshape(R * FP, DP), dfbs[...])

    if SL:

        @pl.when(pl.program_id(0) == pl.num_programs(0) - 1)
        def _():
            a = dqkv[...]
            pack_pair(pack_ref, 0, a[:, 0:DP], a[:, DP : 2 * DP])
            pack_pair(pack_ref, PAIR, a[:, 2 * DP : 3 * DP], dwo)
            pack_norms(pack_ref, 3 * PAIR, [dnp[0], dnp[1]])


def feature_backward(x, qkv, p, of, n, g1t, yt, wqkvT, woT, np8, perm, row0, rows, R=16, U=2, slots=None, prev=None, packed=0):
    b0 = row0 // R
    nat = lambda w: pl.BlockSpec((R, FP, w), lambda i: (i + b0, 0, 0))
    turned = pl.BlockSpec((FP, R, DP), lambda i: (0, i + b0, 0))
    real = pl.BlockSpec((R, F, D), lambda i: (i + b0, 0, 0))
    accs = [shape((DP, 3 * DP), F32), shape((DP, DP), F32), shape((2, 8, DP), F32)]
    ins = [x, qkv, p, of, n, g1t, yt]
    specs = [real, nat(3 * DP), nat(H * FP), nat(DP), nat(DP), turned, turned]
    out_shape = [shape((x.shape[0], F, D), F32), shape((x.shape[0], F, D))]
    out_specs = [real, real]
    scratch = [
        pltpu.VMEM((R, FP, DP), F32),
        pltpu.VMEM((R, FP, DP), BF),
        pltpu.VMEM((R * FP, 3 * DP), BF),
        pltpu.VMEM((R * FP, DP), BF),
    ]
    SL = 0
    alias = {}
    shared = [wqkvT, woT, np8, perm]
    if slots is not None:
        SL = slots[0].shape[1]
        shared = list(slots) + shared
    ins += shared
    specs += [whole(a) for a in shared]
    if prev is not None:
        cg, y, *acc = prev
        ins += list(acc) + [cg, y]
        specs += [whole(a) for a in acc] + [pl.BlockSpec(memory_space=pl.ANY)] * 2
        alias = {len(ins) - 2: 0, len(ins) - 1: 1}
        out_shape.append(shape((packed, 128)))
        out_specs.append(pl.BlockSpec((packed, 128), lambda i: (0, 0)))
        scratch += [pltpu.VMEM(a.shape, F32) for a in accs]
    else:
        out_shape += accs
        out_specs += [whole(a) for a in accs]
    return pl.pallas_call(
        functools.partial(backward_kernel, R, U, SL),
        grid=(rows // R,),
        in_specs=specs,
        out_specs=out_specs,
        out_shape=out_shape,
        input_output_aliases=alias,
        scratch_shapes=scratch,
        compiler_params=params(),
        cost_estimate=cost(60), name="feature_backward",
    )(*ins)


def sum_kernel(parts_ref, out_ref):
    total = parts_ref[0].astype(F32)
    for i in range(1, parts_ref.shape[0]):
        total = total + parts_ref[i].astype(F32)
    total = total.astype(BF)
    for i in range(parts_ref.shape[0]):
        out_ref[i] = total


def sum_over_devices(packed, n):
    axes = ("table", "rows")
    rows = packed.shape[0] // n
    parts = lax.all_to_all(packed.reshape(n, rows, 128), axes, 0, 0)
    copies = pl.pallas_call(
        sum_kernel, out_shape=shape((n, rows, 128)), compiler_params=params(), cost_estimate=cost(2), name="sum_parts"
    )(parts)
    return lax.all_to_all(copies, axes, 0, 0).reshape(n * rows, 128)


def to_row(c):
    return jnp.broadcast_to(c, (c.shape[0], 128)).T[0:1]


def to_col(r):
    return jnp.broadcast_to(r, (128, r.shape[1])).T[:, 0:1]


def clipped(update, weight, count):
    def total(v):
        return jnp.sum(jnp.sum(v, 0, keepdims=True), 1, keepdims=True)

    rms = jnp.sqrt(total(update * update) * (1.0 / count))
    weight_rms = jnp.sqrt(total(weight * weight) * (1.0 / count))
    return update * (RATE * jnp.maximum(0.001, weight_rms) / jnp.maximum(1.0, rms / CLIP))


def optimizer_kernel(
    mid_ref, tail_ref, proj_ref, outw_ref, in_ref, hid_ref, norm_ref, sr_ref, sc_ref, mm_ref, mh_ref, ns_ref,
    proj_g, out_g, in_g, hid_g, norm_g, proj_n, out_n, in_n, hid_n, norm_n, sr_n, sc_n, mm_n, mh_n, ns_n,
):
    decay = 1.0 - STEP ** (-0.8)

    def stats(grad, col_old, row_old):
        square = grad * grad + 1e-30
        a, b = grad.shape
        over_sub = decay * row_old + (1.0 - decay) * (jnp.sum(square, 0, keepdims=True) * (1.0 / a))
        over_lane = decay * col_old + (1.0 - decay) * (jnp.sum(square, 1, keepdims=True) * (1.0 / b))
        return over_lane, over_sub

    def scaled(grad, col, row, mean):
        return grad * lax.rsqrt(col * (1.0 / mean)) * lax.rsqrt(row)

    def square_pair(ref, at):
        both = ref[at + 2 * D : at + 3 * D].astype(F32)
        a = jnp.concatenate([ref[at : at + D].astype(F32), both[:, 0:64]], 1)
        b = jnp.concatenate([ref[at + D : at + 2 * D].astype(F32), both[:, 64:128]], 1)
        return a, b

    wq, wk = square_pair(tail_ref, 0)
    wv, wo = square_pair(tail_ref, PAIR)
    wk2, wv2 = square_pair(tail_ref, 2 * PAIR)
    wq2, wo2 = square_pair(mid_ref, 12 * D)
    for i, grad in enumerate((wq, wk, wv, wq2, wk2, wv2, wo, wo2)):
        g_ref, n_ref, w_ref, j = (proj_g, proj_n, proj_ref, i) if i < 6 else (out_g, out_n, outw_ref, i - 6)
        g_ref[j] = grad
        col, row = stats(grad, to_col(sr_ref[i : i + 1, :]), sc_ref[i : i + 1, :])
        sr_n[i : i + 1, :] = to_row(col)
        sc_n[i : i + 1, :] = row
        mean = jnp.sum(col, 0, keepdims=True) * (1.0 / D)
        w = w_ref[j]
        n_ref[j] = w - clipped(scaled(grad, col, row, mean), w, D * D)

    def wide(at):
        return jnp.concatenate([mid_ref[at + D * j : at + D * j + D].astype(F32) for j in range(6)], 1)

    grad = wide(0)
    in_g[...] = grad
    col, row = stats(grad, to_col(mm_ref[0:1, :]), mh_ref[0:1, :])
    mm_n[0:1, :] = to_row(col)
    mh_n[0:1, :] = row
    mean = jnp.sum(col, 0, keepdims=True) * (1.0 / D)
    w = in_ref[...]
    in_n[...] = w - clipped(scaled(grad, col, row, mean), w, D * FF)
    grad = wide(6 * D)
    hid_g[...] = grad
    col, row = stats(grad, to_col(mm_ref[1:2, :]), mh_ref[1:2, :])
    mm_n[1:2, :] = to_row(col)
    mh_n[1:2, :] = row
    mean = jnp.sum(row, 1, keepdims=True) * (1.0 / FF)
    w = hid_ref[...]
    update = grad * lax.rsqrt(col) * lax.rsqrt(row * (1.0 / mean))
    hid_n[...] = w - clipped(update, w, D * FF)

    pieces = []
    for ref, at, count in ((tail_ref, 3 * PAIR, 2), (mid_ref, 12 * D + PAIR, 4)):
        v = ref[at : at + 16].astype(F32)
        for i in range(count):
            pieces.append(jnp.concatenate([v[2 * i : 2 * i + 1], v[2 * i + 1 : 2 * i + 2, 0:64]], 1))
    grad = jnp.concatenate(pieces, 0)
    norm_g[...] = grad
    second = decay * ns_ref[...] + (1.0 - decay) * (grad * grad + 1e-30)
    ns_n[...] = second
    update = grad * lax.rsqrt(second)
    rms = jnp.sqrt(jnp.sum(update * update, 1, keepdims=True) * (1.0 / D))
    w = norm_ref[...]
    w_rms = jnp.sqrt(jnp.sum(w * w, 1, keepdims=True) * (1.0 / D))
    norm_n[...] = w - update * (RATE * jnp.maximum(0.001, w_rms) / jnp.maximum(1.0, rms / CLIP))


def optimizer(mid, tail, *state):
    proj, outw, w_in, w_outT, norms, sr, sc, ms, hs, ns = state
    order = [proj, outw, w_in, w_outT, norms, proj, outw, w_in, w_outT, norms, sr, sc, ms, hs, ns]
    outs = pl.pallas_call(
        optimizer_kernel,
        out_shape=[shape(a.shape, F32) for a in order],
        compiler_params=params(),
        cost_estimate=cost(8), name="optimizer",
    )(mid, tail, *state)
    outs = list(outs)
    for i in (3, 8):
        outs[i] = outs[i].T
    return outs


def on_device(n, cells, cotangent, train_count, key_mask, train_order, *state):
    state = list(state)
    state[3] = state[3].T
    proj, outw, w_in, w_outT, norms = state[:5]
    x = cells[0]
    rows_here = x.shape[0]
    unit = 8 * n
    tail_rows = -(-TAIL // unit) * unit
    mid_rows = -(-MID // unit) * unit
    perm = perm_matrix()
    (wqkv, wqkvT, wo, woT, wkv2, wk2T, wv2T, wq2, wq2T, wo2I, wo2, w1T, w1, w2T, w2, np8, vec) = prepare(
        proj, outw, w_in, w_outT, norms
    )
    own_kv = slot_keys(train_count, key_mask, train_order, x, wqkv, wo, wkv2, np8)
    shards = lax.axis_size("rows")
    kv = lax.all_gather(own_kv, "rows", axis=0, tiled=True)
    ht, nn, qkv, p, of = feature_forward(x, wqkv, wo, np8, perm)
    ct = to_columns(cotangent[0], perm)
    kt, vt, bias = gathered_columns(kv, perm)
    ws = (wq2, wq2T, wo2I, wo2, w1T, w1, w2T, w2)
    yt, g1t, dk, dv, mid = item_and_dense(ht, ct, kt, vt, bias, ws, vec, mid_rows)
    parts = slot_parts(dk, dv, perm).reshape((shards,) + own_kv.shape)
    parts = lax.all_to_all(parts, "rows", 0, 0)
    mid = sum_over_devices(mid, n)
    R = 16
    args = (x, qkv, p, of, nn, g1t, yt, wqkvT, woT, np8, perm)
    prev = feature_backward(*args, row0=R, rows=rows_here - R, R=R)
    cg, y, tail = feature_backward(
        *args, row0=0, rows=R, R=R, slots=(parts, wk2T, wv2T), prev=prev, packed=tail_rows
    )
    tail = sum_over_devices(tail, n)
    return (y[None], cg[None], *optimizer(mid, tail, *state))


def solution(mesh):
    n = int(mesh.shape["table"] * mesh.shape["rows"])
    cells = P("table", "rows", None, None)
    return jax.shard_map(
        functools.partial(on_device, n),
        mesh=mesh,
        in_specs=(cells, cells, P("table"), P("table", "rows"), P("table", "rows")) + (P(),) * 10,
        out_specs=(cells, cells) + (P(),) * 15,
        check_vma=False,
    )
```

```python
import functools

import jax
import jax.numpy as jnp
import numpy as np
from jax import lax
from jax.experimental import pallas as pl
from jax.experimental.pallas import tpu as pltpu
from jax.sharding import PartitionSpec as P

BF, F32 = jnp.bfloat16, jnp.float32
D, DP = 192, 256
H, E = 6, 32
F, FP = 119, 128
FS = 120
FF = 768
STEP = 3
CLIP = 0.3
RATE = 0.5
FB = 8
PARTS = (8, 7)
SCALE = E**-0.5
SCALE2 = SCALE * 1.4426950408889634
C0 = 0.7978845608028654
C1 = 0.044715
NT = (((1,), (1,)), ((), ()))
TN = (((0,), (0,)), ((), ()))
PAIR = 576
TAIL = 3 * PAIR + 8
MID = 2 * 6 * D + PAIR + 8


def mm(a, b):
    return jnp.dot(a, b, preferred_element_type=F32)


def mm_nt(a, b):
    return lax.dot_general(a, b, NT, preferred_element_type=F32)


def mm_tn(a, b):
    return lax.dot_general(a, b, TN, preferred_element_type=F32)


def lanes():
    return lax.broadcasted_iota(jnp.int32, (1, DP), 1)


def whole(a):
    nd = len(a.shape)
    return pl.BlockSpec(a.shape, lambda *i: (0,) * nd)


def half_masks():
    lane = lax.broadcasted_iota(jnp.int32, (1, 128), 1)
    return [jnp.where((lane >= E * h) & (lane < E * (h + 1)), 1.0, 0.0).astype(BF) for h in range(4)]


def spread_halves(w, masks):
    z = jnp.zeros((w.shape[0], 128), BF)
    lo, hi = w[:, 0:128], w[:, 128:256]
    return jnp.concatenate(
        [jnp.concatenate([lo * masks[h], z], 1) for h in range(4)]
        + [jnp.concatenate([z, hi * masks[h]], 1) for h in range(2)], 0)


def mean0(a): return jnp.sum(a, 0, keepdims=True) * (1.0 / D)


def norm_t(a):
    c = a - mean0(a)
    rc = lax.rsqrt(mean0(c * c) + 1e-5)
    return c * rc, rc


def norm_back_t(g, n, rc, gain):
    dn = g * gain
    return (dn - mean0(dn) - n * mean0(dn * n)) * rc


def tall(a):
    return jnp.concatenate([a, jnp.zeros((DP - D, a.shape[1]), a.dtype)], 0)


def gelu_parts(u):
    uu = u * u
    th = jnp.tanh(u * (BF(C0) + BF(C0 * C1) * uu))
    half = BF(0.5) + BF(0.5) * th
    act = u * half
    slope = half + act * (BF(1.0) - th) * (BF(C0) + BF(3.0 * C0 * C1) * uu)
    return act, slope


def weave(streams):
    live=[[g,s,p] for g,s,p in streams]
    turn=0
    while live:
        for it in list(live):
            if turn>=it[1]:
                for _ in range(it[2]):
                    try: next(it[0])
                    except StopIteration:
                        live.remove(it); break
        turn+=1

def shape(s, t=BF):
    return jax.ShapeDtypeStruct(s, t)


def params(mib=58):
    return pltpu.CompilerParams(vmem_limit_bytes=mib << 20)


def cost(us):
    return pl.CostEstimate(flops=int(us * 1.1e9), bytes_accessed=int(us * 1e6), transcendentals=0)


def perm_matrix():
    place = np.zeros((256, 256), np.float32)
    for f in range(16):
        for r in range(16):
            place[f * 16 + r, r * 16 + f] = 1
    return jnp.asarray(place, BF)


def prep_kernel(
    proj, outw, w_in, w_outT, norms, wqkvT, wqkvI, wo, woT, wkv2T, wk2, wv2, wq2, wq2T, wo2I, wo2, w1T, w1, w2T, w2, vec, nrow
):
    zc = jnp.zeros((D, DP - D), F32)
    zr = jnp.zeros((DP - D, DP), BF)
    row = lax.broadcasted_iota(jnp.int32, (D, DP), 0)
    eye = jnp.where(row == lax.broadcasted_iota(jnp.int32, (D, DP), 1), 1.0, 0.0).astype(BF)

    def square(w):
        a = jnp.concatenate([w, zc], 1)
        a = jnp.concatenate([a.astype(BF), zr], 0)
        return a, a.T

    for i in range(3):
        a, t = square(proj[i])
        wqkvT[i * D : (i + 1) * D, :] = t[0:D]
    wqkvI[...] = jnp.concatenate([proj[0], proj[1], proj[2], eye[:, 0:D].astype(F32)], 1).astype(BF)
    a, t = square(outw[0])
    wo[...] = a[0:D]
    woT[...] = t[0:D]
    a, t = square(proj[3])
    wq2[...] = a
    wq2T[...] = t
    a, t = square(outw[1])
    wo2[...] = a[0:D]
    wo2I[:, 0:DP] = t[0:D]
    wo2I[:, DP : 2 * DP] = eye
    a, t = square(proj[4])
    wk2[...] = a[0:D]
    wkv2T[0:D, :] = t[0:D]
    a, t = square(proj[5])
    wv2[...] = a[0:D]
    wkv2T[D : 2 * D, :] = t[0:D]
    zw = jnp.zeros((DP - D, FF), BF)
    a = w_in[...].astype(BF)
    w1[...] = a
    w1T[...] = jnp.concatenate([a, zw], 0).T
    a = w_outT[...].astype(BF)
    w2T[...] = a
    w2[...] = jnp.concatenate([a, zw], 0).T
    nrow[...] = jnp.zeros((8, DP), F32)
    nrow[0:6, 0:D] = norms[...]
    for i in range(6):
        vec[i] = jnp.broadcast_to(nrow[i : i + 1, :], (128, DP)).T[0:D]


def prepare(proj, outw, w_in, w_outT, norms):
    sq, half = shape((DP, DP)), shape((D, DP))
    outs = [shape((3 * D, DP)), shape((D, 4 * D)), half, half, shape((2 * D, DP)), half, half, sq, sq]
    outs += [shape((D, 2 * DP)), half, shape((FF, DP)), shape((D, FF)), shape((D, FF)), shape((FF, DP))]
    outs += [shape((6, D, 128), F32)]
    return pl.pallas_call(
        prep_kernel,
        out_shape=outs,
        scratch_shapes=[pltpu.VMEM((8, DP), F32)],
        compiler_params=params(),
        cost_estimate=cost(4),
        name="weights",
    )(proj, outw, w_in, w_outT, norms)


def two_heads(a, b):
    z = jnp.zeros(a.shape, a.dtype)
    return jnp.concatenate([jnp.concatenate([a, z], 1), jnp.concatenate([z, b], 1)], 0)


def feature_pair(x, wqkvT_ref, woT_ref, keep, out):
    qkv = mm(wqkvT_ref[...], x)
    q = (qkv[0:D] * SCALE2).astype(BF)
    k = qkv[D : 2 * D].astype(BF)
    v = qkv[2 * D : 3 * D].astype(BF)
    yield
    row = lax.broadcasted_iota(jnp.int32, (8, 1), 0)
    outs = []
    for u in range(2):
        own = slice(u * FP, (u + 1) * FP)
        keep("qkv", u, (q[:, own], k[:, own], v[:, own]))
        ot = []
        for j in range(H // 2):
            hs = slice(64 * j, 64 * j + 64)
            qm = two_heads(q[64 * j : 64 * j + 32, own], q[64 * j + 32 : 64 * j + 64, own])
            st = mm(k[hs, own].T, qm)
            yield
            last = jnp.where(row < F - FS + 8, st[FS - 8 : FS], -1e30)
            mx = jnp.maximum(jnp.max(st[0 : FS - 8], 0, keepdims=True), jnp.max(last, 0, keepdims=True))
            e = jnp.exp2(st[0 : FS - 8] - mx)
            last = jnp.exp2(last - mx)
            inv = 1.0 / (jnp.sum(e, 0, keepdims=True) + jnp.sum(last, 0, keepdims=True))
            e = jnp.concatenate([e, last, jnp.zeros((FP - FS, 2 * FP), F32)], 0).astype(BF)
            keep("p", (u, j), (e, inv))
            yield
            t = mm(v[hs, own], e)
            ot.append(t[0:32, 0:128] * inv[:, 0:128])
            ot.append(t[32:64, 128:256] * inv[:, 128:256])
            yield
        ot = jnp.concatenate(ot, 0).astype(BF)
        keep("o", u, ot)
        outs.append(ot)
    a = mm(woT_ref[...], tall(jnp.concatenate(outs, 1)))
    yield
    for u in range(2):
        own = slice(u * FP, (u + 1) * FP)
        out.append(norm_t(x[0:D, own].astype(F32) + a[:, own]))
        yield


def slots_kernel(
    SL, count_ref, mask_ref, order_ref, x_ref, wqkvT_ref, woT_ref, wkv2T_ref, vec_ref, *refs
):
    *kv_refs, xs = refs
    xs[...] = jnp.zeros_like(xs)

    def pair(c):
        for u in range(2):
            xs[c, 0:D, u * FP : u * FP + F] = x_ref[2 * c + u]
        out = []
        yield from feature_pair(xs[c], wqkvT_ref, woT_ref, lambda *a: None, out)
        for u in range(2):
            r = 2 * c + u
            n, _ = out[u]
            h = tall((n * vec_ref[0] + vec_ref[1]).astype(BF))
            kv = mm(wkv2T_ref[...], h).astype(BF).T
            order = order_ref[0, r]
            usable = (order < count_ref[0]) & ((mask_ref[0, r] == 1) | (order == 0))
            flag = jnp.full((8, 2 * D), jnp.where(usable, 1.0, 0.0), F32).astype(BF)
            at = 0
            for part, ref in enumerate(kv_refs):
                cols = FB * PARTS[part]
                for i in range(ref.shape[0]):
                    ref[i, r, 0:cols, :] = kv[at : at + cols]
                    if part == 0:
                        ref[i, r, cols:, :] = flag
                at += cols
            yield

    weave([(pair(c), 0, 1) for c in range(SL // 2)])


def slot_keys(shards, count, mask, order, cells, wqkvT, woT, wkv2T, vec):
    SL = mask.shape[1]
    smem = pl.BlockSpec(memory_space=pltpu.SMEM)
    sent = [shape((shards, SL, FB * p + (0 if i else 8), 2 * D)) for i, p in enumerate(PARTS)]
    return pl.pallas_call(
        functools.partial(slots_kernel, SL),
        grid=(1,),
        in_specs=[smem, smem, smem, pl.BlockSpec((SL, D, F), lambda i: (0, 0, 0))]
        + [whole(a) for a in (wqkvT, woT, wkv2T, vec)],
        out_specs=[whole(a) for a in sent],
        out_shape=sent,
        scratch_shapes=[pltpu.VMEM((SL // 2, DP, 2 * FP), BF)],
        compiler_params=params(),
        cost_estimate=cost(5),
        name="slot_keys",
    )(count, mask, order, cells, wqkvT, woT, wkv2T, vec)


def turn_block(perm_ref, block, R):
    return mm(perm_ref[...], block.reshape(256, block.shape[-1])).astype(BF).reshape(16, R, block.shape[-1])


def forward_kernel(
    R, OFF, x_ref, c_ref, wqkvT_ref, woT_ref, vec_ref, perm_ref, ht_ref, ct_ref, n_ref, qkv_ref, p_ref, l_ref, of_ref, xs, hs, cp, cs
):
    @pl.when(pl.program_id(0) == 0)
    def _():
        xs[...] = jnp.zeros_like(xs)
        cp[...] = jnp.zeros_like(cp)

    def pair(c):
        for u in range(2):
            xs[c, 0:D, u * FP : u * FP + F] = x_ref[2 * c + u]

        def keep(what, at, val):
            if what == "qkv":
                for i in range(3):
                    qkv_ref[2 * c + at, i * D : (i + 1) * D, :] = val[i]
            elif what == "p":
                u, j = at
                p_ref[2 * c + u, :, 256 * j : 256 * j + 256] = val[0]
                l_ref[2 * c + u, j : j + 1, :] = val[1]
            else:
                of_ref[2 * c + at] = val

        out = []
        yield from feature_pair(xs[c], wqkvT_ref, woT_ref, keep, out)
        for u in range(2):
            r = 2 * c + u
            n, rc = out[u]
            n_ref[r, 0:D, :] = n.astype(BF)
            n_ref[r, D : D + 16, :] = jnp.broadcast_to(rc, (16, FP)).astype(BF)
            h = tall((n * vec_ref[0] + vec_ref[1]).astype(BF))
            hs[r] = h.T
            yield

    def cotangents():
        for r in range(R):
            cp[r % 4, 0:D, 0:F] = c_ref[r]
            cs[r] = cp[r % 4].T
            yield
        for j in range(FP // 16):
            ct_ref[16 * j : 16 * j + 16] = turn_block(perm_ref, cs[:, 16 * j : 16 * j + 16, :], R)
            yield

    weave([(pair(c), c * OFF, 1) for c in range(R // 2)] + [(cotangents(), 4, 1)])
    for j in range(FP // 16):
        ht_ref[16 * j : 16 * j + 16] = turn_block(perm_ref, hs[:, 16 * j : 16 * j + 16, :], R)


def feature_forward(cells, cot, ws, R=16, OFF=6):
    rows = cells.shape[0]
    nat = lambda a, b: pl.BlockSpec((R, a, b), lambda i: (i, 0, 0))
    turned = pl.BlockSpec((FP, R, DP), lambda i: (0, i, 0))
    sizes = [(D + 16, FP), (3 * D, FP), (FP, H * FP), (8, 2 * FP), (D, FP)]
    kinds = [BF, BF, BF, F32, BF]
    return pl.pallas_call(
        functools.partial(forward_kernel, R, OFF),
        grid=(rows // R,),
        in_specs=[nat(D, F), nat(D, F)] + [whole(a) for a in ws],
        out_specs=[turned, turned] + [nat(*a) for a in sizes],
        out_shape=[shape((FP, rows, DP))] * 2 + [shape((rows,) + a, t) for a, t in zip(sizes, kinds)],
        scratch_shapes=[
            pltpu.VMEM((R // 2, DP, 2 * FP), BF),
            pltpu.VMEM((R, FP, DP), BF),
            pltpu.VMEM((4, DP, FP), BF),
            pltpu.VMEM((R, FP, DP), BF),
        ],
        compiler_params=params(),
        cost_estimate=cost(9 * rows // R),
        name="feature_forward",
    )(cells, cot, *ws)


def pack_pair(ref, at, a, b):
    ref[at : at + D] = a[0:D, 0:128].astype(BF)
    ref[at + D : at + 2 * D] = b[0:D, 0:128].astype(BF)
    ref[at + 2 * D : at + 3 * D] = jnp.concatenate([a[0:D, 128:D], b[0:D, 128:D]], 1).astype(BF)


def pack_norms(ref, at, sums):
    rows = []
    for s in sums:
        if s.shape[0] == D:
            s = jnp.concatenate([s, jnp.zeros((DP - D, 128), F32)], 0).T
        v = jnp.sum(s, 0, keepdims=True)
        rows += [v[:, 0:128], v[:, 128:256]]
    rows.append(jnp.zeros((ref.shape[0] - at - len(rows), 128), F32))
    ref[at:] = jnp.concatenate(rows, 0).astype(BF)


def item_kernel(part, RW, keys, OFF, WP, CC, WC, ht_ref, ct_ref, kv_ref, perm_ref, *refs):
    first, final = part == 0, part == len(PARTS) - 1
    wq_ref, wqT_ref, woI_ref, wo_ref, w1T_ref, w1_ref, w2T_ref, w2_ref, vec_ref, *refs = refs
    if not first:
        bias_ref, *refs = refs
        before, refs = refs[:5], refs[5:]
    y_ref, g1_ref, dkv_ref, *refs = refs
    if first:
        bias_ref, *refs = refs
    if final:
        pack_ref, *refs = refs
    accs, refs = refs[:5], refs[5:]
    dwq, dwo, dw1, dw2, dnp = accs
    kt_ref, vt_ref, dk_ref, dv_ref, hbTs, ois, hb2Ts, actss, dbTs, duss, dabTs, dqss, slp = refs
    step = pl.program_id(0)
    cols = FB * PARTS[part]
    blocks = [(s, b, min(16, cols - b)) for s in range(0, keys, 16) for b in range(0, cols, 16)]

    @pl.when(step == 0)
    def _():
        for i, ref in enumerate(accs):
            ref[...] = jnp.zeros_like(ref) if first else before[i][...]
        for ref in (hbTs, ois, hb2Ts, actss, dbTs, duss, dabTs, dqss):
            ref[1] = jnp.zeros_like(ref[1])
        for ref in (kt_ref, vt_ref):
            ref[:, :, D:DP] = jnp.zeros(ref.shape[:2] + (DP - D,), BF)
        for s, b, n in blocks:
            own = kv_ref[s : s + 16, b : b + n, :]
            if n < 16:
                own = jnp.concatenate([own, jnp.zeros((16, 16 - n, 2 * D), BF)], 1)
            both = turn_block(perm_ref, own, 16)[0:n]
            kt_ref[b : b + n, s : s + 16, 0:D] = both[:, :, 0:D]
            vt_ref[b : b + n, s : s + 16, 0:D] = both[:, :, D : 2 * D]
        if first:
            flag = kv_ref[:, cols, 0:128].astype(F32)
            bias_ref[...] = jnp.where(flag > 0.5, 0.0, -1e30)

    cur = step % 2
    masks = half_masks()
    LW = 2 * RW
    left = lax.broadcasted_iota(jnp.int32, (1, LW), 1) < RW
    HK = H * keys
    hbT, oi, hb2T, acts, dbT, dus, dabT, dqs = [r.at[cur] for r in (hbTs, ois, hb2Ts, actss, dbTs, duss, dabTs, dqss)]
    def attend(j, out):
        h = ht_ref[2 * j:2 * j + 2].reshape(LW, DP)
        q = (mm(h, wq_ref[...]) * SCALE2).astype(BF)
        yield
        ks = [spread_halves(kt_ref[step * FB + 2 * j + c], masks) for c in range(2)]
        hbT[:, j * LW:(j + 1) * LW] = h.T[0:D]
        yield
        st = jnp.where(left, mm_nt(ks[0], q), mm_nt(ks[1], q))
        yield
        vs = [spread_halves(vt_ref[step * FB + 2 * j + c], masks) for c in range(2)]
        pbs = []
        for hh in range(H):
            s = st[hh * keys:(hh + 1) * keys] + bias_ref[...]
            e = jnp.exp2(s - jnp.max(s, 0, keepdims=True))
            pbs.append((e * (1.0 / jnp.sum(e, 0, keepdims=True))).astype(BF))
            if hh % 2: yield
        pb = jnp.concatenate(pbs, 0)
        pt = pb.T
        yield
        o = jnp.concatenate([mm(pt[:RW], vs[0]), mm(pt[RW:], vs[1])], 0).astype(BF)
        oi[j * LW:(j + 1) * LW] = o
        out.extend([q, pb, ks, vs, o])
        yield
    def dense(i, os, out):
        c0 = i * 2 * LW
        g1v, b1v, g2v, b2v = [vec_ref[i] for i in range(2, 6)]
        h = ht_ref[4 * i:4 * i + 4].reshape(2 * LW, DP)
        o = jnp.concatenate(os, 0)
        aT = mm_nt(woI_ref[...], jnp.concatenate([o, h], 1))
        yield
        n2, rc2, h2, hb2 = [], [], [], []
        for t in range(2):
            n, rc = norm_t(aT[:, t * LW:(t + 1) * LW])
            hh = n * g1v + b1v
            n2.append(n.astype(BF)); rc2.append(rc); hb2.append(hh.astype(BF))
            yield
        hb2 = jnp.concatenate(hb2, 1)
        hb2T[:, c0:c0 + 2 * LW] = hb2
        hb2 = tall(hb2)
        C = CC
        u = mm(w1T_ref[0:C], hb2)
        for c in range(FF // C):
            un = mm(w1T_ref[C * c + C:C * c + 2 * C], hb2) if c + 1 < FF // C else None
            act, slope = gelu_parts(u.astype(BF))
            acts[C * c:C * c + C, c0:c0 + 2 * LW] = act
            slp[C * c:C * c + C, c0:c0 + 2 * LW] = slope
            u = un
            yield
        gT = ct_ref[4 * i:4 * i + 4].reshape(2 * LW, DP).T[0:D].astype(F32)
        z = mm(w2T_ref[...], acts[:, c0:c0 + 2 * LW])
        yield
        dbs, d3s = [], []
        ys = []
        for t in range(2):
            sl = slice(t * LW, (t + 1) * LW)
            n3, rc3 = norm_t(hb2[0:D, sl].astype(F32) + z[:, sl])
            ys.append((n3 * g2v + b2v).astype(BF))
            yield
            g = gT[:, sl]
            dnp[2] += g * n3
            dnp[3] += g
            d3 = norm_back_t(g, n3, rc3, g2v)
            dbs.append(d3.astype(BF))
            yield
        db = jnp.concatenate(dbs, 1)
        dbT[:, c0:c0 + 2 * LW] = db
        db = tall(db)
        w = mm(w2_ref[0:C], db)
        for c in range(FF // C):
            wn = mm(w2_ref[C * c + C:C * c + 2 * C], db) if c + 1 < FF // C else None
            dus[C * c:C * c + C, c0:c0 + 2 * LW] = w.astype(BF) * slp[C * c:C * c + C, c0:c0 + 2 * LW]
            w = wn
            yield
        dh = mm(w1_ref[...], dus[:, c0:c0 + 2 * LW])
        yT = tall(jnp.concatenate(ys, 1))
        y_ref[4 * i:4 * i + 4] = yT.T.reshape(4, RW, DP)
        yield
        dabs = []
        for t in range(2):
            dh2 = dbs[t].astype(F32) + dh[:, t * LW:(t + 1) * LW]
            n2f = n2[t].astype(F32)
            dnp[0] += dh2 * n2f
            dnp[1] += dh2
            dabs.append(norm_back_t(dh2, n2f, rc2[t], g1v).astype(BF))
            yield
        dab = jnp.concatenate(dabs, 1)
        dabT[:, c0:c0 + 2 * LW] = dab
        doT = mm(wo_ref[...], tall(dab)).astype(BF)
        out.extend([dab, doT])
        yield
    def back(j, at, doT, out):
        q, pb, ks, vs, _ = at
        do = tall(doT)
        don = do.T
        dp = jnp.where(left, mm(vs[0], do), mm(vs[1], do))
        yield
        slot_sums(dv_ref, j, pb, don, None)
        yield
        dss = []
        for hh in range(H):
            sl = slice(hh * keys, (hh + 1) * keys)
            p, d = pb[sl].astype(F32), dp[sl]
            dss.append((p * (d - jnp.sum(p * d, 0, keepdims=True))).astype(BF))
            if hh % 2: yield
        ds = jnp.concatenate(dss, 0)
        dst = ds.T
        yield
        slot_sums(dk_ref, j, ds, q, 0.6931471805599453)
        yield
        dq = jnp.concatenate([mm(dst[:RW], ks[0]), mm(dst[RW:], ks[1])], 0) * SCALE
        dq = dq.astype(BF)
        dqs[j * LW:(j + 1) * LW] = dq
        out.append(dq)
        yield
    lane = lax.broadcasted_iota(jnp.int32, (1, 128), 1)
    zq = jnp.zeros((RW, 128), BF)
    def slot_sums(ref, j, w, rows, scale):
        out = [[], []]
        for t, heads in ((0, 4), (1, 2)):
            r = rows[:, 128 * t:128 * t + 128]
            both = jnp.concatenate([jnp.concatenate([r[:RW], zq], 0), jnp.concatenate([zq, r[RW:]], 0)], 1)
            full = mm(w[4 * t * keys:(4 * t + heads) * keys], both)
            for c in range(2):
                col = full[:, 128 * c:128 * c + 128]
                v = col[0:keys]
                for hh in range(1, heads):
                    v = jnp.where(lane >= E * hh, col[hh * keys:(hh + 1) * keys], v)
                out[c].append(v)
        for c in range(2):
            v = jnp.concatenate(out[c], 1)
            ref[step * FB + 2 * j + c] = (v if scale is None else v * scale).astype(BF)
    def finish(i, dqv, dab):
        dq = jnp.concatenate(dqv, 0)
        g1 = mm(dq, wqT_ref[...]) + tall(dab).T.astype(F32)
        g1_ref[4 * i:4 * i + 4] = g1.astype(BF).reshape(4, RW, DP)
        yield
    def chunk(i):
        at = [[], []]
        ga, gb = attend(2 * i, at[0]), attend(2 * i + 1, at[1])
        for _ in zip(ga, gb): yield
        for _ in ga: yield
        for _ in gb: yield
        out = []
        yield from dense(i, [at[0][4], at[1][4]], out)
        dab, doT = out
        dq = []
        for t in range(2):
            yield from back(2 * i + t, at[t], doT[:, t * LW:(t + 1) * LW], dq)
        yield from finish(i, dq, dab)
    def wgrad(b):
        dwq[...] += mm(hbTs[b], dqss[b])
        yield
        dwo[...] += mm(dabTs[b], ois[b])
        yield
        for c in range(0, FF, WC):
            dw1[c:c + WC] += mm_nt(duss[b, c:c + WC], hb2Ts[b])
            yield
        for c in range(0, FF, WC):
            dw2[c:c + WC] += mm_nt(actss[b, c:c + WC], dbTs[b])
            yield
    NC = FB // 4
    weave([(chunk(i), i * OFF, 1) for i in range(NC)] + [(wgrad(1 - cur), WP, 1)])

    @pl.when(step == pl.num_programs(0) - 1)
    def _():
        for _ in wgrad(cur):
            pass
        for s, b, n in blocks:
            turned = []
            for ref in (dk_ref, dv_ref):
                own = ref[b : b + n, s : s + 16, :]
                if n < 16:
                    own = jnp.concatenate([own, jnp.zeros((16 - n, 16, DP), BF)], 0)
                turned.append(turn_block(perm_ref, own, 16)[:, 0:n, 0:D])
            dkv_ref[s : s + 16, b : b + n, :] = jnp.concatenate(turned, 2)
        if final:
            at = 0
            for ref in (dw1, dw2):
                t = ref[...].T
                for j in range(FF // 128):
                    pack_ref[at : at + D] = t[:, 128 * j : 128 * j + 128].astype(BF)
                    at += D
            pack_pair(pack_ref, at, dwq, tall(dwo[...]).T)
            pack_norms(pack_ref, at + PAIR, [dnp[i] for i in range(4)])


def item_and_dense(part, ht, ct, kv, perm, ws, vec, packed, bias=None, before=None, OFF=0, WP=20, CC=384, WC=384):
    RW = ht.shape[1]
    keys = kv.shape[0]
    M = FB * RW
    cols = FB * PARTS[part]
    b0 = sum(PARTS[:part])
    cells = pl.BlockSpec((FB, RW, DP), lambda i: (i + b0, 0, 0))
    own = pl.BlockSpec((FB, RW, DP), lambda i: (i, 0, 0))
    accs = [shape(a, F32) for a in ((D, DP), (D, DP), (FF, D), (FF, D), (4, D, 128))]
    kept = [(D, M), (M, DP), (D, M), (FF, M), (D, M), (FF, M), (D, M), (M, DP)]
    flat = [kv, perm, *ws, vec]
    if part:
        flat += [bias, *before]
    outs = [shape((cols, RW, DP))] * 2 + [shape((keys, cols, 2 * D))]
    if part == 0:
        outs += [shape((keys, 128), F32)]
    scratch = []
    if part == len(PARTS) - 1:
        outs += [shape((packed, 128))]
        scratch = [pltpu.VMEM(a.shape, F32) for a in accs]
    else:
        outs += accs
    slots = [pltpu.VMEM((cols, keys, DP), BF)] * 4
    return pl.pallas_call(
        functools.partial(item_kernel, part, RW, keys, OFF, WP, CC, WC),
        grid=(PARTS[part],),
        in_specs=[cells, cells] + [whole(a) for a in flat],
        out_specs=[own, own] + [whole(a) for a in outs[2:]],
        out_shape=outs,
        scratch_shapes=scratch + slots + [pltpu.VMEM((2,) + a, BF) for a in kept] + [pltpu.VMEM((FF, M), BF)],
        compiler_params=params(),
        cost_estimate=cost(60),
        name="item_and_dense",
    )(ht, ct, *flat)


def backward_kernel(R, OFF, SL, x_ref, n_ref, qkv_ref, p_ref, l_ref, of_ref, *rest):
    NP = len(PARTS)
    g1t_refs, yt_refs, rest = rest[:NP], rest[NP : 2 * NP], rest[2 * NP :]
    if SL:
        dkv_refs, rest = rest[:NP], rest[NP:]
        (wk2_ref, wv2_ref, wqkvI_ref, wo_ref, vec_ref, perm_ref, iqkv, iwo, inp, _, _,
         cg_ref, y_ref, pack_ref, gs, ys, xs, os, dqs, das, dqkv, dwo, dnp) = rest
    else:
        (wqkvI_ref, wo_ref, vec_ref, perm_ref, cg_ref, y_ref, dqkv, dwo, dnp, gs, ys, xs, os, dqs, das) = rest

    @pl.when(pl.program_id(0) == 0)
    def _():
        xs[...] = jnp.zeros_like(xs)
        for i, ref in enumerate((dqkv, dwo, dnp)):
            ref[...] = (iqkv, iwo, inp)[i][...] if SL else jnp.zeros_like(ref)

    col = lax.broadcasted_iota(jnp.int32, (16, 1, 1), 0)

    def turn(refs, out, j):
        part, at = 0, 16 * j
        while at >= FB * PARTS[part]:
            at -= FB * PARTS[part]
            part += 1
        n = min(16, FB * PARTS[part] - at)
        block = refs[part][at : at + n]
        if n < 16:
            block = jnp.concatenate([block, jnp.zeros((16 - n,) + block.shape[1:], BF)], 0)
        if 16 * j + 16 > F:
            block = jnp.where(col < F - 16 * j, block, 0).astype(BF)
        out[:, 16 * j : 16 * j + 16, :] = turn_block(perm_ref, block, 16)

    for j in range(FP // 16):
        turn(g1t_refs, gs, j)
    back = []
    if SL:
        pieces = []
        for ref in dkv_refs:
            both = ref[0].astype(F32)
            for i in range(1, ref.shape[0]):
                both = both + ref[i].astype(F32)
            pieces.append(both.astype(BF))
        z0 = jnp.zeros((FP - FS, 2 * D), BF)
        dk2, dv2, h1 = [], [], []
        for r in range(SL):
            t = jnp.concatenate([both[r] for both in pieces] + [z0], 0).T
            dk2.append(t[0:D])
            dv2.append(t[D : 2 * D])
            back.append(mm(wk2_ref[...], tall(dk2[r])) + mm(wv2_ref[...], tall(dv2[r])))
            h1.append((n_ref[r, 0:D, :].astype(F32) * vec_ref[0] + vec_ref[1]).astype(BF))
        h1 = jnp.concatenate(h1, 1)
        pair2 = [mm_nt(h1, tall(jnp.concatenate(a, 1))) for a in (dk2, dv2)]
        pack_pair(pack_ref, 2 * PAIR, *pair2)

    def pair(c):
        at = slice(2 * c * FP, (2 * c + 2) * FP)
        dabs, das32 = [], []
        for u in range(2):
            r = 2 * c + u
            xs[:, r * FP : r * FP + F] = x_ref[r]
            os[:, r * FP : (r + 1) * FP] = of_ref[r]
            g = gs[r].T[0:D].astype(F32)
            if r < SL:
                g = g + back[r]
            n = n_ref[r, 0:D, :].astype(F32)
            rc = n_ref[r, D : D + 16, :].astype(F32)[0:1]
            dnp[0] += g * n
            dnp[1] += g
            dabs.append(norm_back_t(g, n, rc, vec_ref[0]).astype(BF))
            yield
        dab = jnp.concatenate(dabs, 1)
        das[:, at] = dab
        do = mm(wo_ref[...], tall(dab))
        yield
        for u in range(2):
            r = 2 * c + u
            own = slice(u * FP, (u + 1) * FP)
            lanes_r = slice(r * FP, (r + 1) * FP)
            for j in range(H // 2):
                inv = l_ref[r, j : j + 1, :]
                parts, offs = [], []
                for t in range(2):
                    hs = slice(64 * j + 32 * t, 64 * j + 32 * t + 32)
                    d = do[hs, own] * inv[:, t * FP : (t + 1) * FP]
                    offs.append(jnp.sum(d * of_ref[r, hs, :].astype(F32), 0, keepdims=True))
                    parts.append(d.astype(BF))
                dom = two_heads(*parts)
                off = jnp.concatenate(offs, 1).astype(BF)
                dp = mm(qkv_ref[r, 2 * D + 64 * j : 2 * D + 64 * j + 64, :].T, dom)
                yield
                e = p_ref[r, :, 256 * j : 256 * j + 256]
                ds = e * (dp.astype(BF) - off)
                dv = mm_nt(dom, e)
                yield
                qm = two_heads(
                    qkv_ref[r, 64 * j : 64 * j + 32, :], qkv_ref[r, 64 * j + 32 : 64 * j + 64, :]
                )
                dk = mm_nt(qm, ds) * 0.6931471805599453
                dq = mm(qkv_ref[r, D + 64 * j : D + 64 * j + 64, :], ds)
                dq = jnp.concatenate([dq[0:32, 0:128], dq[32:64, 128:256]], 0) * SCALE
                yield
                for i, d in enumerate((dq, dk, dv)):
                    dqs[i * D + 64 * j : i * D + 64 * j + 64, lanes_r] = d.astype(BF)
        yield
        cg = mm(wqkvI_ref[...], jnp.concatenate([dqs[:, at], dab], 0))
        for u in range(2):
            cg_ref[2 * c + u] = cg[:, u * FP : u * FP + F]
        yield

    def outputs():
        for j in range(FP // 16):
            turn(yt_refs, ys, j)
            yield
        for r in range(R):
            y_ref[r] = ys[r].T[0:D, 0:F]
            yield

    def sums(part):
        at = slice(part * R * FP // 2, (part + 1) * R * FP // 2)
        for i in range(3):
            dqkv[i * D : (i + 1) * D] += mm_nt(dqs[i * D : (i + 1) * D, at], xs[:, at])
            yield
        dwo[...] += mm_nt(os[:, at], das[:, at])
        yield

    Q = R // 4
    for half in range(2):
        streams = [(pair(c), (c - half * Q) * OFF, 1) for c in range(half * Q, (half + 1) * Q)]
        streams.append((sums(0) if half else outputs(), 3, 1))
        weave(streams)
    for _ in sums(1):
        pass

    if SL:

        @pl.when(pl.program_id(0) == pl.num_programs(0) - 1)
        def _():
            zc = jnp.zeros((D, DP - D), F32)
            three = [jnp.concatenate([dqkv[i * D : (i + 1) * D], zc], 1).T for i in range(3)]
            pack_pair(pack_ref, 0, three[0], three[1])
            pack_pair(pack_ref, PAIR, three[2], dwo)
            pack_norms(pack_ref, 3 * PAIR, [dnp[0], dnp[1]])


def feature_backward(x, saved, g1t, yt, wqkvI, wo, vec, perm, row0, rows, R=16, OFF=6, slots=None, prev=None, packed=0):
    b0 = row0 // R
    nat = lambda a: pl.BlockSpec((R,) + a.shape[1:], lambda i: (i + b0, 0, 0))
    turned = [pl.BlockSpec((FB * p, R, DP), lambda i: (0, i + b0, 0)) for p in PARTS]
    real = pl.BlockSpec((R, D, F), lambda i: (i + b0, 0, 0))
    accs = [shape((3 * D, D), F32), shape((D, D), F32), shape((2, D, FP), F32)]
    ins = [x, *saved, *g1t, *yt]
    specs = [real] + [nat(a) for a in saved] + turned * 2
    out_shape = [shape((x.shape[0], D, F), F32), shape((x.shape[0], D, F))]
    out_specs = [real, real]
    M = R * FP
    scratch = [pltpu.VMEM(a, BF) for a in ((R, FP, DP), (R, FP, DP), (D, M), (D, M), (3 * D, M), (D, M))]
    SL = 0
    alias = {}
    shared = [wqkvI, wo, vec, perm]
    if slots is not None:
        SL = slots[0][0].shape[1]
        shared = [*slots[0], *slots[1:]] + shared
    ins += shared
    specs += [whole(a) for a in shared]
    if prev is not None:
        cg, y, *acc = prev
        ins += list(acc) + [cg, y]
        specs += [whole(a) for a in acc] + [pl.BlockSpec(memory_space=pl.ANY)] * 2
        alias = {len(ins) - 2: 0, len(ins) - 1: 1}
        out_shape.append(shape((packed, 128)))
        out_specs.append(pl.BlockSpec((packed, 128), lambda i: (0, 0)))
        scratch += [pltpu.VMEM(a.shape, F32) for a in accs]
    else:
        out_shape += accs
        out_specs += [whole(a) for a in accs]
    return pl.pallas_call(
        functools.partial(backward_kernel, R, OFF, SL),
        grid=(rows // R,),
        in_specs=specs,
        out_specs=out_specs,
        out_shape=out_shape,
        input_output_aliases=alias,
        scratch_shapes=scratch,
        compiler_params=params(),
        cost_estimate=cost(60 * rows // R),
        name="feature_backward",
    )(*ins)


def sum_kernel(n, *refs):
    *ready_refs, parts_ref, out_ref = refs
    total = parts_ref[0].astype(F32)
    for i in range(1, n):
        total = total + parts_ref[i].astype(F32)
    total = total.astype(BF)
    if not ready_refs:
        out_ref[...] = total
        return
    rows = ready_refs[0].shape[0]
    for i in range(out_ref.shape[0]):
        out_ref[i, 0:rows] = ready_refs[0][...]
        out_ref[i, rows:] = total


def sum_parts(packed, n, ready=None):
    rows = packed.shape[0] // n
    parts = lax.all_to_all(packed.reshape(n, rows, 128), ("table", "rows"), 0, 0)
    ins = [parts] if ready is None else [ready, parts]
    out = (rows, 128) if ready is None else (lax.axis_size("rows"), ready.shape[0] + rows, 128)
    return pl.pallas_call(
        functools.partial(sum_kernel, n),
        out_shape=shape(out),
        compiler_params=params(),
        cost_estimate=cost(2),
        name="sum_parts",
    )(*ins)


def gather_all(copies):
    tables = lax.axis_size("table")
    ny = tables // 2
    own = lax.all_to_all(copies, "rows", 0, 0)
    pieces = [own]
    for s in range(1, ny):
        pieces.append(lax.ppermute(own, "table", [(t, (t // 2 + s) % ny * 2 + t % 2) for t in range(tables)]))
    other = [lax.ppermute(a, "table", [(t, t ^ 1) for t in range(tables)]) for a in pieces]
    return [a for pair in zip(pieces, other) for a in pair]


def to_row(c):
    return jnp.broadcast_to(c, (c.shape[0], 128)).T[0:1]


def to_col(r):
    return jnp.broadcast_to(r, (128, r.shape[1])).T[:, 0:1]


def clipped(update, weight, count):
    def total(v):
        return jnp.sum(jnp.sum(v, 0, keepdims=True), 1, keepdims=True)

    rms = jnp.sqrt(total(update * update) * (1.0 / count))
    weight_rms = jnp.sqrt(total(weight * weight) * (1.0 / count))
    return update * (RATE * jnp.maximum(0.001, weight_rms) / jnp.maximum(1.0, rms / CLIP))


def optimizer_kernel(
    tables, mid_rows, *refs):
    table_ref, *refs = refs
    piece_refs, refs = refs[:tables], refs[tables:]
    mid_ref, tail_ref = refs[-2:]
    table = table_ref[0]
    ny = tables // 2
    for i, ref in enumerate(piece_refs):
        place = lax.rem(table // 2 - i // 2 + ny, ny) * 2 + lax.rem(table + i % 2, 2)
        for out, at, end in ((mid_ref, 0, mid_rows), (tail_ref, mid_rows, ref.shape[1])):
            rows = ref.shape[0] * (end - at)
            start = pl.multiple_of(place * rows, 8)
            out[pl.ds(start, rows)] = ref[:, at:end, :].astype(F32).reshape(rows, 128)
    optimizer_steps(*refs)


def optimizer_steps(
    proj_ref, outw_ref, in_ref, hid_ref, norm_ref, sr_ref, sc_ref, mm_ref, mh_ref, ns_ref,
    proj_g, out_g, in_g, hid_g, norm_g, proj_n, out_n, in_n, hid_n, norm_n, sr_n, sc_n, mm_n, mh_n, ns_n, mid_ref, tail_ref,
):
    decay = 1.0 - STEP ** (-0.8)

    def stats(grad, col_old, row_old):
        square = grad * grad + 1e-30
        a, b = grad.shape
        over_sub = decay * row_old + (1.0 - decay) * (jnp.sum(square, 0, keepdims=True) * (1.0 / a))
        over_lane = decay * col_old + (1.0 - decay) * (jnp.sum(square, 1, keepdims=True) * (1.0 / b))
        return over_lane, over_sub

    def scaled(grad, col, row, mean):
        return grad * lax.rsqrt(col * (1.0 / mean)) * lax.rsqrt(row)

    def square_pair(ref, at):
        both = ref[at + 2 * D : at + 3 * D].astype(F32)
        a = jnp.concatenate([ref[at : at + D].astype(F32), both[:, 0:64]], 1)
        b = jnp.concatenate([ref[at + D : at + 2 * D].astype(F32), both[:, 64:128]], 1)
        return a, b

    wq, wk = square_pair(tail_ref, 0)
    wv, wo = square_pair(tail_ref, PAIR)
    wk2, wv2 = square_pair(tail_ref, 2 * PAIR)
    wq2, wo2 = square_pair(mid_ref, 12 * D)
    for i, grad in enumerate((wq, wk, wv, wq2, wk2, wv2, wo, wo2)):
        g_ref, n_ref, w_ref, j = (proj_g, proj_n, proj_ref, i) if i < 6 else (out_g, out_n, outw_ref, i - 6)
        g_ref[j] = grad
        col, row = stats(grad, to_col(sr_ref[i : i + 1, :]), sc_ref[i : i + 1, :])
        sr_n[i : i + 1, :] = to_row(col)
        sc_n[i : i + 1, :] = row
        mean = jnp.sum(col, 0, keepdims=True) * (1.0 / D)
        w = w_ref[j]
        n_ref[j] = w - clipped(scaled(grad, col, row, mean), w, D * D)

    def wide(at):
        return jnp.concatenate([mid_ref[at + D * j : at + D * j + D].astype(F32) for j in range(6)], 1)

    grad = wide(0)
    in_g[...] = grad
    col, row = stats(grad, to_col(mm_ref[0:1, :]), mh_ref[0:1, :])
    mm_n[0:1, :] = to_row(col)
    mh_n[0:1, :] = row
    mean = jnp.sum(col, 0, keepdims=True) * (1.0 / D)
    w = in_ref[...]
    in_n[...] = w - clipped(scaled(grad, col, row, mean), w, D * FF)
    grad = wide(6 * D)
    hid_g[...] = grad
    col, row = stats(grad, to_col(mm_ref[1:2, :]), mh_ref[1:2, :])
    mm_n[1:2, :] = to_row(col)
    mh_n[1:2, :] = row
    mean = jnp.sum(row, 1, keepdims=True) * (1.0 / FF)
    w = hid_ref[...]
    update = grad * lax.rsqrt(col) * lax.rsqrt(row * (1.0 / mean))
    hid_n[...] = w - clipped(update, w, D * FF)

    pieces = []
    for ref, at, count in ((tail_ref, 3 * PAIR, 2), (mid_ref, 12 * D + PAIR, 4)):
        v = ref[at : at + 16].astype(F32)
        for i in range(count):
            pieces.append(jnp.concatenate([v[2 * i : 2 * i + 1], v[2 * i + 1 : 2 * i + 2, 0:64]], 1))
    grad = jnp.concatenate(pieces, 0)
    norm_g[...] = grad
    second = decay * ns_ref[...] + (1.0 - decay) * (grad * grad + 1e-30)
    ns_n[...] = second
    update = grad * lax.rsqrt(second)
    rms = jnp.sqrt(jnp.sum(update * update, 1, keepdims=True) * (1.0 / D))
    w = norm_ref[...]
    w_rms = jnp.sqrt(jnp.sum(w * w, 1, keepdims=True) * (1.0 / D))
    norm_n[...] = w - update * (RATE * jnp.maximum(0.001, w_rms) / jnp.maximum(1.0, rms / CLIP))


def optimizer(pieces, mid_rows, *state):
    proj, outw, w_in, w_outT, norms, sr, sc, ms, hs, ns = state
    shards, rows, _ = pieces[0].shape
    table = lax.axis_index("table").astype(jnp.int32).reshape(1)
    order = [proj, outw, w_in, w_outT, norms, proj, outw, w_in, w_outT, norms, sr, sc, ms, hs, ns]
    outs = pl.pallas_call(
        functools.partial(optimizer_kernel, len(pieces), mid_rows),
        in_specs=[pl.BlockSpec(memory_space=pltpu.SMEM)] + [whole(a) for a in (*pieces, *state)],
        out_shape=[shape(a.shape, F32) for a in order],
        scratch_shapes=[
            pltpu.VMEM((len(pieces) * shards * mid_rows, 128), F32),
            pltpu.VMEM((len(pieces) * shards * (rows - mid_rows), 128), F32),
        ],
        compiler_params=params(),
        cost_estimate=cost(8), name="optimizer",
    )(table, *pieces, *state)
    outs = list(outs)
    for i in (3, 8):
        outs[i] = outs[i].T
    return outs


def on_device(n, cells, cotangent, train_count, key_mask, train_order, *state):
    state = list(state)
    state[3] = state[3].T
    proj, outw, w_in, w_outT, norms = state[:5]
    x = jnp.swapaxes(cells[0], 1, 2)
    cot = jnp.swapaxes(cotangent[0], 1, 2)
    rows_here = x.shape[0]
    unit = 8 * n
    tail_rows = -(-TAIL // unit) * unit
    mid_rows = -(-MID // unit) * unit
    perm = perm_matrix()
    (wqkvT, wqkvI, wo, woT, wkv2T, wk2, wv2, wq2, wq2T, wo2I, wo2, w1T, w1, w2T, w2, vec) = prepare(
        proj, outw, w_in, w_outT, norms
    )
    R = 16
    shards = lax.axis_size("rows")
    kvs = [
        lax.all_to_all(a, "rows", 0, 0).reshape((-1,) + a.shape[2:])
        for a in slot_keys(shards, train_count, key_mask, train_order, x, wqkvT, woT, wkv2T, vec)
    ]
    ht, ct, *saved = feature_forward(x, cot, (wqkvT, woT, vec, perm))
    ws = (wq2, wq2T, wo2I, wo2, w1T, w1, w2T, w2)
    bias = before = None
    yt, g1t, sent = [], [], []
    for part, kv in enumerate(kvs):
        y, g, dkv, *rest = item_and_dense(part, ht, ct, kv, perm, ws, vec, mid_rows, bias, before)
        yt.append(y)
        g1t.append(g)
        if part == 0:
            bias, *rest = rest
        before = rest
        dkv = dkv.reshape((shards, -1) + dkv.shape[1:])
        sent.append(lax.all_to_all(dkv, "rows", 0, 0))
    g1t[0], sent[0] = lax.optimization_barrier((g1t[0], sent[0]))
    args = (x, saved, g1t, yt, wqkvI, wo, vec, perm)
    prev = list(feature_backward(*args, row0=R, rows=rows_here - R, R=R))
    packed, prev[4] = lax.optimization_barrier((before[0], prev[4]))
    mid = sum_parts(packed, n)
    cg, y, tail = feature_backward(*args, row0=0, rows=R, R=R, slots=(sent, wk2, wv2), prev=prev, packed=tail_rows)
    tail, mid = lax.optimization_barrier((tail, mid))
    pieces = gather_all(sum_parts(tail, n, mid))
    return (jnp.swapaxes(y, 1, 2)[None], jnp.swapaxes(cg, 1, 2)[None], *optimizer(pieces, mid.shape[0], *state))


def solution(mesh):
    n = int(mesh.shape["table"] * mesh.shape["rows"])
    cells = P("table", "rows", None, None)
    return jax.shard_map(
        functools.partial(on_device, n),
        mesh=mesh,
        in_specs=(cells, cells, P("table"), P("table", "rows"), P("table", "rows")) + (P(),) * 10,
        out_specs=(cells, cells) + (P(),) * 15,
        check_vma=False,
    )
```

```python
import functools

import jax
import jax.numpy as jnp
import numpy as np
from jax import lax
from jax.experimental import pallas as pl
from jax.experimental.pallas import tpu as pltpu
from jax.sharding import PartitionSpec as P

BF, F32 = jnp.bfloat16, jnp.float32
D, DP = 192, 256
H, E = 6, 32
F, FP = 119, 128
FS = 120
FF = 768
STEP = 3
CLIP = 0.3
RATE = 0.5
FB = 8
SCALE = E**-0.5
SCALE2 = SCALE * 1.4426950408889634
C0 = 0.7978845608028654
C1 = 0.044715
NT = (((1,), (1,)), ((), ()))
TN = (((0,), (0,)), ((), ()))
PAIR = 576
TAIL = 2 * PAIR + 8
MID = 2 * 6 * D + 2 * PAIR + 8


def mm(a, b):
    return jnp.dot(a, b, preferred_element_type=F32)


def mm_nt(a, b):
    return lax.dot_general(a, b, NT, preferred_element_type=F32)


def mm_tn(a, b):
    return lax.dot_general(a, b, TN, preferred_element_type=F32)


def lanes():
    return lax.broadcasted_iota(jnp.int32, (1, DP), 1)


def whole(a):
    nd = len(a.shape)
    return pl.BlockSpec(a.shape, lambda *i: (0,) * nd)


def half_masks():
    lane = lax.broadcasted_iota(jnp.int32, (1, 128), 1)
    return [jnp.where((lane >= E * h) & (lane < E * (h + 1)), 1.0, 0.0).astype(BF) for h in range(4)]


def spread_halves(w, masks):
    z = jnp.zeros((w.shape[0], 128), BF)
    lo, hi = w[:, 0:128], w[:, 128:256]
    return jnp.concatenate(
        [jnp.concatenate([lo * masks[h], z], 1) for h in range(4)]
        + [jnp.concatenate([z, hi * masks[h]], 1) for h in range(2)], 0)


def mean0(a): return jnp.sum(a, 0, keepdims=True) * (1.0 / D)


def norm_t(a):
    c = a - mean0(a)
    rc = lax.rsqrt(mean0(c * c) + 1e-5)
    return c * rc, rc


def norm_back_t(g, n, rc, gain):
    dn = g * gain
    return (dn - mean0(dn) - n * mean0(dn * n)) * rc


def tall(a):
    return jnp.concatenate([a, jnp.zeros((DP - D, a.shape[1]), a.dtype)], 0)


def gelu_parts(u):
    uu = u * u
    th = jnp.tanh(u * (BF(C0) + BF(C0 * C1) * uu))
    half = BF(0.5) + BF(0.5) * th
    act = u * half
    slope = half + act * (BF(1.0) - th) * (BF(C0) + BF(3.0 * C0 * C1) * uu)
    return act, slope


def weave(streams):
    live=[[g,s,p] for g,s,p in streams]
    turn=0
    while live:
        for it in list(live):
            if turn>=it[1]:
                for _ in range(it[2]):
                    try: next(it[0])
                    except StopIteration:
                        live.remove(it); break
        turn+=1

def shape(s, t=BF):
    return jax.ShapeDtypeStruct(s, t)


def params(mib=58):
    return pltpu.CompilerParams(vmem_limit_bytes=mib << 20)


def cost(us):
    return pl.CostEstimate(flops=int(us * 1.1e9), bytes_accessed=int(us * 1e6), transcendentals=0)


def perm_matrix():
    place = np.zeros((256, 256), np.float32)
    for f in range(16):
        for r in range(16):
            place[f * 16 + r, r * 16 + f] = 1
    return jnp.asarray(place, BF)


def prep_kernel(
    proj, outw, w_in, w_outT, norms, wqkvT, wqkvI, wo, woT, wkv2, wkv2T, wq2, wq2T, wo2I, wo2, w1T, w1, w2T, w2, vec, nrow
):
    zc = jnp.zeros((D, DP - D), F32)
    zr = jnp.zeros((DP - D, DP), BF)
    row = lax.broadcasted_iota(jnp.int32, (D, DP), 0)
    eye = jnp.where(row == lax.broadcasted_iota(jnp.int32, (D, DP), 1), 1.0, 0.0).astype(BF)

    def square(w):
        a = jnp.concatenate([w, zc], 1)
        a = jnp.concatenate([a.astype(BF), zr], 0)
        return a, a.T

    for i in range(3):
        a, t = square(proj[i])
        wqkvT[i * D : (i + 1) * D, :] = t[0:D]
    wqkvI[...] = jnp.concatenate([proj[0], proj[1], proj[2], eye[:, 0:D].astype(F32)], 1).astype(BF)
    a, t = square(outw[0])
    wo[...] = a[0:D]
    woT[...] = t[0:D]
    a, t = square(proj[3])
    wq2[...] = a
    wq2T[...] = t
    a, t = square(outw[1])
    wo2[...] = a[0:D]
    wo2I[:, 0:DP] = t[0:D]
    wo2I[:, DP : 2 * DP] = eye
    for i in range(2):
        a, t = square(proj[4 + i])
        wkv2[:, i * DP : (i + 1) * DP] = a
        wkv2T[i * DP : (i + 1) * DP, :] = t
    zw = jnp.zeros((DP - D, FF), BF)
    a = w_in[...].astype(BF)
    w1[...] = a
    w1T[...] = jnp.concatenate([a, zw], 0).T
    a = w_outT[...].astype(BF)
    w2T[...] = a
    w2[...] = jnp.concatenate([a, zw], 0).T
    nrow[...] = jnp.zeros((8, DP), F32)
    nrow[0:6, 0:D] = norms[...]
    for i in range(6):
        vec[i] = jnp.broadcast_to(nrow[i : i + 1, :], (128, DP)).T[0:D]


def prepare(proj, outw, w_in, w_outT, norms):
    sq, half = shape((DP, DP)), shape((D, DP))
    outs = [shape((3 * D, DP)), shape((D, 4 * D)), half, half, shape((DP, 2 * DP)), shape((2 * DP, DP)), sq, sq]
    outs += [shape((D, 2 * DP)), half, shape((FF, DP)), shape((D, FF)), shape((D, FF)), shape((FF, DP))]
    outs += [shape((6, D, 128), F32)]
    return pl.pallas_call(
        prep_kernel,
        out_shape=outs,
        scratch_shapes=[pltpu.VMEM((8, DP), F32)],
        compiler_params=params(),
        cost_estimate=cost(4),
        name="weights",
    )(proj, outw, w_in, w_outT, norms)


def two_heads(a, b):
    z = jnp.zeros(a.shape, a.dtype)
    return jnp.concatenate([jnp.concatenate([a, z], 1), jnp.concatenate([z, b], 1)], 0)


def feature_pair(x, wqkvT_ref, woT_ref, keep, out):
    qkv = mm(wqkvT_ref[...], x)
    q = (qkv[0:D] * SCALE2).astype(BF)
    k = qkv[D : 2 * D].astype(BF)
    v = qkv[2 * D : 3 * D].astype(BF)
    yield
    row = lax.broadcasted_iota(jnp.int32, (8, 1), 0)
    outs = []
    for u in range(2):
        own = slice(u * FP, (u + 1) * FP)
        keep("qkv", u, (q[:, own], k[:, own], v[:, own]))
        ot = []
        for j in range(H // 2):
            hs = slice(64 * j, 64 * j + 64)
            qm = two_heads(q[64 * j : 64 * j + 32, own], q[64 * j + 32 : 64 * j + 64, own])
            st = mm(k[hs, own].T, qm)
            yield
            last = jnp.where(row < F - FS + 8, st[FS - 8 : FS], -1e30)
            mx = jnp.maximum(jnp.max(st[0 : FS - 8], 0, keepdims=True), jnp.max(last, 0, keepdims=True))
            e = jnp.exp2(st[0 : FS - 8] - mx)
            last = jnp.exp2(last - mx)
            inv = 1.0 / (jnp.sum(e, 0, keepdims=True) + jnp.sum(last, 0, keepdims=True))
            e = jnp.concatenate([e, last, jnp.zeros((FP - FS, 2 * FP), F32)], 0).astype(BF)
            keep("p", (u, j), (e, inv))
            yield
            t = mm(v[hs, own], e)
            ot.append(t[0:32, 0:128] * inv[:, 0:128])
            ot.append(t[32:64, 128:256] * inv[:, 128:256])
            yield
        ot = jnp.concatenate(ot, 0).astype(BF)
        keep("o", u, ot)
        outs.append(ot)
    a = mm(woT_ref[...], tall(jnp.concatenate(outs, 1)))
    yield
    for u in range(2):
        own = slice(u * FP, (u + 1) * FP)
        out.append(norm_t(x[0:D, own].astype(F32) + a[:, own]))
        yield


def slots_kernel(SL, count_ref, mask_ref, order_ref, x_ref, wqkvT_ref, woT_ref, vec_ref, out_ref, xs):
    xs[...] = jnp.zeros_like(xs)
    row = lax.broadcasted_iota(jnp.int32, (FS, 1), 0)
    lane = lax.broadcasted_iota(jnp.int32, (1, 2 * D), 1)

    def flag(r):
        order = order_ref[0, r]
        usable = (order < count_ref[0]) & ((mask_ref[0, r] == 1) | (order == 0))
        return jnp.where(usable, 1.0, 0.0)

    def pair(c):
        for u in range(2):
            xs[c, 0:D, u * FP : u * FP + F] = x_ref[2 * c + u]
        out = []
        yield from feature_pair(xs[c], wqkvT_ref, woT_ref, lambda *a: None, out)
        both = jnp.concatenate([(n * vec_ref[0] + vec_ref[1]).astype(BF) for n, _ in out], 0)
        flags = jnp.where(lane < D, flag(2 * c), flag(2 * c + 1))
        both = jnp.where(row < F, both.T[0:FS].astype(F32), flags).astype(BF)
        for i in range(out_ref.shape[0]):
            out_ref[i, c] = both
        yield

    weave([(pair(c), 0, 1) for c in range(SL // 2)])


def slot_rows(shards, count, mask, order, cells, wqkvT, woT, vec):
    SL = mask.shape[1]
    smem = pl.BlockSpec(memory_space=pltpu.SMEM)
    sent = shape((shards, SL // 2, FS, 2 * D))
    return pl.pallas_call(
        functools.partial(slots_kernel, SL),
        grid=(1,),
        in_specs=[smem, smem, smem, pl.BlockSpec((SL, D, F), lambda i: (0, 0, 0))]
        + [whole(a) for a in (wqkvT, woT, vec)],
        out_specs=whole(sent),
        out_shape=sent,
        scratch_shapes=[pltpu.VMEM((SL // 2, DP, 2 * FP), BF)],
        compiler_params=params(),
        cost_estimate=cost(5),
        name="slot_rows",
    )(count, mask, order, cells, wqkvT, woT, vec)


def turn_block(perm_ref, block, R):
    return mm(perm_ref[...], block.reshape(256, block.shape[-1])).astype(BF).reshape(16, R, block.shape[-1])


def forward_kernel(
    R, OFF, x_ref, c_ref, wqkvT_ref, woT_ref, vec_ref, perm_ref, ht_ref, ct_ref, n_ref, qkv_ref, p_ref, l_ref, of_ref, xs, hs, cp, cs
):
    @pl.when(pl.program_id(0) == 0)
    def _():
        xs[...] = jnp.zeros_like(xs)
        cp[...] = jnp.zeros_like(cp)

    def pair(c):
        for u in range(2):
            xs[c, 0:D, u * FP : u * FP + F] = x_ref[2 * c + u]

        def keep(what, at, val):
            if what == "qkv":
                for i in range(3):
                    qkv_ref[2 * c + at, i * D : (i + 1) * D, :] = val[i]
            elif what == "p":
                u, j = at
                p_ref[2 * c + u, :, 256 * j : 256 * j + 256] = val[0]
                l_ref[2 * c + u, j : j + 1, :] = val[1]
            else:
                of_ref[2 * c + at] = val

        out = []
        yield from feature_pair(xs[c], wqkvT_ref, woT_ref, keep, out)
        for u in range(2):
            r = 2 * c + u
            n, rc = out[u]
            n_ref[r, 0:D, :] = n.astype(BF)
            n_ref[r, D : D + 16, :] = jnp.broadcast_to(rc, (16, FP)).astype(BF)
            h = tall((n * vec_ref[0] + vec_ref[1]).astype(BF))
            hs[r] = h.T
            yield

    def cotangents():
        for r in range(R):
            cp[r % 4, 0:D, 0:F] = c_ref[r]
            cs[r] = cp[r % 4].T
            yield
        for j in range(FP // 16):
            ct_ref[16 * j : 16 * j + 16] = turn_block(perm_ref, cs[:, 16 * j : 16 * j + 16, :], R)
            yield

    weave([(pair(c), c * OFF, 1) for c in range(R // 2)] + [(cotangents(), 4, 1)])
    for j in range(FP // 16):
        ht_ref[16 * j : 16 * j + 16] = turn_block(perm_ref, hs[:, 16 * j : 16 * j + 16, :], R)


def feature_forward(cells, cot, ws, R=16, OFF=6):
    rows = cells.shape[0]
    nat = lambda a, b: pl.BlockSpec((R, a, b), lambda i: (i, 0, 0))
    turned = pl.BlockSpec((FP, R, DP), lambda i: (0, i, 0))
    sizes = [(D + 16, FP), (3 * D, FP), (FP, H * FP), (8, 2 * FP), (D, FP)]
    kinds = [BF, BF, BF, F32, BF]
    return pl.pallas_call(
        functools.partial(forward_kernel, R, OFF),
        grid=(rows // R,),
        in_specs=[nat(D, F), nat(D, F)] + [whole(a) for a in ws],
        out_specs=[turned, turned] + [nat(*a) for a in sizes],
        out_shape=[shape((FP, rows, DP))] * 2 + [shape((rows,) + a, t) for a, t in zip(sizes, kinds)],
        scratch_shapes=[
            pltpu.VMEM((R // 2, DP, 2 * FP), BF),
            pltpu.VMEM((R, FP, DP), BF),
            pltpu.VMEM((4, DP, FP), BF),
            pltpu.VMEM((R, FP, DP), BF),
        ],
        compiler_params=params(),
        cost_estimate=cost(9 * rows // R),
        name="feature_forward",
    )(cells, cot, *ws)


def pack_pair(ref, at, a, b):
    ref[at : at + D] = a[0:D, 0:128].astype(BF)
    ref[at + D : at + 2 * D] = b[0:D, 0:128].astype(BF)
    ref[at + 2 * D : at + 3 * D] = jnp.concatenate([a[0:D, 128:D], b[0:D, 128:D]], 1).astype(BF)


def pack_norms(ref, at, sums):
    rows = []
    for s in sums:
        if s.shape[0] == D:
            s = jnp.concatenate([s, jnp.zeros((DP - D, 128), F32)], 0).T
        v = jnp.sum(s, 0, keepdims=True)
        rows += [v[:, 0:128], v[:, 128:256]]
    rows.append(jnp.zeros((ref.shape[0] - at - len(rows), 128), F32))
    ref[at:] = jnp.concatenate(rows, 0).astype(BF)


def item_kernel(
    RW, keys, OFF, WP, CC, WC, ht_ref, ct_ref, slot_ref, perm_ref, wq_ref, wqT_ref, woI_ref, wo_ref, w1T_ref, w1_ref, w2T_ref, w2_ref,
    wkv_ref, wkvT_ref, vec_ref, y_ref, g1_ref, back_ref, pack_ref, dwq, dwo, dw1, dw2, dnp, dwkv, bias_ref, hk_ref, bk_ref,
    dk_ref, dv_ref, hbTs, ois, hb2Ts, actss, dbTs, duss, dabTs, dqss, slp,
):
    step = pl.program_id(0)
    blocks = [(s, b, min(16, FS - b)) for s in range(0, keys, 16) for b in range(0, FS, 16)]

    @pl.when(step == 0)
    def _():
        for ref in (dwq, dwo, dw1, dw2, dnp, dwkv):
            ref[...] = jnp.zeros_like(ref)
        for ref in (hbTs, ois, hb2Ts, actss, dbTs, duss, dabTs, dqss):
            ref[1] = jnp.zeros_like(ref[1])
        hk_ref[:, :, D:DP] = jnp.zeros((FS, keys, DP - D), BF)
        for s, b, n in blocks:
            own = slot_ref[s // 2 : s // 2 + 8, b : b + n, :]
            own = jnp.concatenate([own[:, :, 0:D], own[:, :, D : 2 * D]], 0)
            if n < 16:
                own = jnp.concatenate([own, jnp.zeros((16, 16 - n, D), BF)], 1)
            hk_ref[b : b + n, s : s + 16, 0:D] = turn_block(perm_ref, own, 16)[0:n]
        for s in range(0, keys, 16):
            flag = slot_ref[s // 2 : s // 2 + 8, F, :].astype(F32)
            for i, at in enumerate((0, DP)):
                bias_ref[s + 8 * i : s + 8 * i + 8] = jnp.where(flag[:, at : at + 128] > 0.5, 0.0, -1e30)

    cur = step % 2
    masks = half_masks()
    LW = 2 * RW
    left = lax.broadcasted_iota(jnp.int32, (1, LW), 1) < RW
    HK = H * keys
    hbT, oi, hb2T, acts, dbT, dus, dabT, dqs = [r.at[cur] for r in (hbTs, ois, hb2Ts, actss, dbTs, duss, dabTs, dqss)]
    hk = hk_ref[pl.ds(pl.multiple_of(step * FB, FB), FB)].reshape(FB * keys, DP)
    kvs = [mm(hk, wkv_ref[...]).astype(BF)]

    def attend(j, out):
        h = ht_ref[2 * j:2 * j + 2].reshape(LW, DP)
        q = (mm(h, wq_ref[...]) * SCALE2).astype(BF)
        yield
        ks = [spread_halves(kvs[0][(2 * j + c) * keys : (2 * j + c + 1) * keys, 0:DP], masks) for c in range(2)]
        hbT[:, j * LW:(j + 1) * LW] = h.T[0:D]
        yield
        st = jnp.where(left, mm_nt(ks[0], q), mm_nt(ks[1], q))
        yield
        vs = [spread_halves(kvs[0][(2 * j + c) * keys : (2 * j + c + 1) * keys, DP:], masks) for c in range(2)]
        pbs = []
        for hh in range(H):
            s = st[hh * keys:(hh + 1) * keys] + bias_ref[...]
            e = jnp.exp2(s - jnp.max(s, 0, keepdims=True))
            pbs.append((e * (1.0 / jnp.sum(e, 0, keepdims=True))).astype(BF))
            if hh % 2: yield
        pb = jnp.concatenate(pbs, 0)
        pt = pb.T
        yield
        o = jnp.concatenate([mm(pt[:RW], vs[0]), mm(pt[RW:], vs[1])], 0).astype(BF)
        oi[j * LW:(j + 1) * LW] = o
        out.extend([q, pb, ks, vs, o])
        yield
    def dense(i, os, out):
        c0 = i * 2 * LW
        g1v, b1v, g2v, b2v = [vec_ref[i] for i in range(2, 6)]
        h = ht_ref[4 * i:4 * i + 4].reshape(2 * LW, DP)
        o = jnp.concatenate(os, 0)
        aT = mm_nt(woI_ref[...], jnp.concatenate([o, h], 1))
        yield
        n2, rc2, h2, hb2 = [], [], [], []
        for t in range(2):
            n, rc = norm_t(aT[:, t * LW:(t + 1) * LW])
            hh = n * g1v + b1v
            n2.append(n.astype(BF)); rc2.append(rc); hb2.append(hh.astype(BF))
            yield
        hb2 = jnp.concatenate(hb2, 1)
        hb2T[:, c0:c0 + 2 * LW] = hb2
        hb2 = tall(hb2)
        C = CC
        u = mm(w1T_ref[0:C], hb2)
        for c in range(FF // C):
            un = mm(w1T_ref[C * c + C:C * c + 2 * C], hb2) if c + 1 < FF // C else None
            act, slope = gelu_parts(u.astype(BF))
            acts[C * c:C * c + C, c0:c0 + 2 * LW] = act
            slp[C * c:C * c + C, c0:c0 + 2 * LW] = slope
            u = un
            yield
        gT = ct_ref[4 * i:4 * i + 4].reshape(2 * LW, DP).T[0:D].astype(F32)
        z = mm(w2T_ref[...], acts[:, c0:c0 + 2 * LW])
        yield
        dbs, d3s = [], []
        ys = []
        for t in range(2):
            sl = slice(t * LW, (t + 1) * LW)
            n3, rc3 = norm_t(hb2[0:D, sl].astype(F32) + z[:, sl])
            ys.append((n3 * g2v + b2v).astype(BF))
            yield
            g = gT[:, sl]
            dnp[2] += g * n3
            dnp[3] += g
            d3 = norm_back_t(g, n3, rc3, g2v)
            dbs.append(d3.astype(BF))
            yield
        db = jnp.concatenate(dbs, 1)
        dbT[:, c0:c0 + 2 * LW] = db
        db = tall(db)
        w = mm(w2_ref[0:C], db)
        for c in range(FF // C):
            wn = mm(w2_ref[C * c + C:C * c + 2 * C], db) if c + 1 < FF // C else None
            dus[C * c:C * c + C, c0:c0 + 2 * LW] = w.astype(BF) * slp[C * c:C * c + C, c0:c0 + 2 * LW]
            w = wn
            yield
        dh = mm(w1_ref[...], dus[:, c0:c0 + 2 * LW])
        yT = tall(jnp.concatenate(ys, 1))
        y_ref[4 * i:4 * i + 4] = yT.T.reshape(4, RW, DP)
        yield
        dabs = []
        for t in range(2):
            dh2 = dbs[t].astype(F32) + dh[:, t * LW:(t + 1) * LW]
            n2f = n2[t].astype(F32)
            dnp[0] += dh2 * n2f
            dnp[1] += dh2
            dabs.append(norm_back_t(dh2, n2f, rc2[t], g1v).astype(BF))
            yield
        dab = jnp.concatenate(dabs, 1)
        dabT[:, c0:c0 + 2 * LW] = dab
        doT = mm(wo_ref[...], tall(dab)).astype(BF)
        out.extend([dab, doT])
        yield
    def back(j, at, doT, out):
        q, pb, ks, vs, _ = at
        do = tall(doT)
        don = do.T
        dp = jnp.where(left, mm(vs[0], do), mm(vs[1], do))
        yield
        slot_sums(dv_ref, j, pb, don, None)
        yield
        dss = []
        for hh in range(H):
            sl = slice(hh * keys, (hh + 1) * keys)
            p, d = pb[sl].astype(F32), dp[sl]
            dss.append((p * (d - jnp.sum(p * d, 0, keepdims=True))).astype(BF))
            if hh % 2: yield
        ds = jnp.concatenate(dss, 0)
        dst = ds.T
        yield
        slot_sums(dk_ref, j, ds, q, 0.6931471805599453)
        yield
        dq = jnp.concatenate([mm(dst[:RW], ks[0]), mm(dst[RW:], ks[1])], 0) * SCALE
        dq = dq.astype(BF)
        dqs[j * LW:(j + 1) * LW] = dq
        out.append(dq)
        yield
    lane = lax.broadcasted_iota(jnp.int32, (1, 128), 1)
    zq = jnp.zeros((RW, 128), BF)
    def slot_sums(ref, j, w, rows, scale):
        out = [[], []]
        for t, heads in ((0, 4), (1, 2)):
            r = rows[:, 128 * t:128 * t + 128]
            both = jnp.concatenate([jnp.concatenate([r[:RW], zq], 0), jnp.concatenate([zq, r[RW:]], 0)], 1)
            full = mm(w[4 * t * keys:(4 * t + heads) * keys], both)
            for c in range(2):
                col = full[:, 128 * c:128 * c + 128]
                v = col[0:keys]
                for hh in range(1, heads):
                    v = jnp.where(lane >= E * hh, col[hh * keys:(hh + 1) * keys], v)
                out[c].append(v)
        for c in range(2):
            v = jnp.concatenate(out[c], 1)
            ref[2 * j + c] = (v if scale is None else v * scale).astype(BF)
    def finish(i, dqv, dab):
        dq = jnp.concatenate(dqv, 0)
        g1 = mm(dq, wqT_ref[...]) + tall(dab).T.astype(F32)
        g1_ref[4 * i:4 * i + 4] = g1.astype(BF).reshape(4, RW, DP)
        yield
    def chunk(i):
        at = [[], []]
        ga, gb = attend(2 * i, at[0]), attend(2 * i + 1, at[1])
        for _ in zip(ga, gb): yield
        for _ in ga: yield
        for _ in gb: yield
        out = []
        yield from dense(i, [at[0][4], at[1][4]], out)
        dab, doT = out
        dq = []
        for t in range(2):
            yield from back(2 * i + t, at[t], doT[:, t * LW:(t + 1) * LW], dq)
        yield from finish(i, dq, dab)
    def wgrad(b):
        dwq[...] += mm(hbTs[b], dqss[b])
        yield
        dwo[...] += mm(dabTs[b], ois[b])
        yield
        for c in range(0, FF, WC):
            dw1[c:c + WC] += mm_nt(duss[b, c:c + WC], hb2Ts[b])
            yield
        for c in range(0, FF, WC):
            dw2[c:c + WC] += mm_nt(actss[b, c:c + WC], dbTs[b])
            yield
    NC = FB // 4
    weave([(chunk(i), i * OFF, 1) for i in range(NC)] + [(wgrad(1 - cur), WP, 1)])
    dkv = jnp.concatenate([r[...].reshape(FB * keys, DP) for r in (dk_ref, dv_ref)], 1)
    dwkv[...] += mm_tn(hk, dkv)
    bk_ref[pl.ds(pl.multiple_of(step * FB, FB), FB)] = mm(dkv, wkvT_ref[...]).astype(BF).reshape(FB, keys, DP)

    @pl.when(step == pl.num_programs(0) - 1)
    def _():
        for _ in wgrad(cur):
            pass
        for s, b, n in blocks:
            own = bk_ref[b : b + n, s : s + 16, :]
            if n < 16:
                own = jnp.concatenate([own, jnp.zeros((16 - n, 16, DP), BF)], 0)
            own = turn_block(perm_ref, own, 16)[:, 0:n, 0:D]
            back_ref[s // 2 : s // 2 + 8, b : b + n, :] = jnp.concatenate([own[0:8], own[8:16]], 2)
        at = 0
        for ref in (dw1, dw2):
            t = ref[...].T
            for j in range(FF // 128):
                pack_ref[at : at + D] = t[:, 128 * j : 128 * j + 128].astype(BF)
                at += D
        pack_pair(pack_ref, at, dwq, tall(dwo[...]).T)
        pack_pair(pack_ref, at + PAIR, dwkv[:, 0:DP], dwkv[:, DP:])
        pack_norms(pack_ref, at + 2 * PAIR, [dnp[i] for i in range(4)])


def item_and_dense(ht, ct, slots, perm, ws, vec, packed, OFF=0, WP=20, CC=384, WC=384):
    RW = ht.shape[1]
    keys = 2 * slots.shape[0]
    M = FB * RW
    cells = pl.BlockSpec((FB, RW, DP), lambda i: (i, 0, 0))
    accs = [(D, DP), (D, DP), (FF, D), (FF, D), (4, D, 128), (DP, 2 * DP), (keys, 128)]
    kept = [(D, M), (M, DP), (D, M), (FF, M), (D, M), (FF, M), (D, M), (M, DP)]
    flat = [slots, perm, *ws, vec]
    outs = [shape((FS, RW, DP))] * 2 + [shape(slots.shape), shape((packed, 128))]
    return pl.pallas_call(
        functools.partial(item_kernel, RW, keys, OFF, WP, CC, WC),
        grid=(FS // FB,),
        in_specs=[cells, cells] + [whole(a) for a in flat],
        out_specs=[cells, cells] + [whole(a) for a in outs[2:]],
        out_shape=outs,
        scratch_shapes=[pltpu.VMEM(a, F32) for a in accs]
        + [pltpu.VMEM((FS, keys, DP), BF)] * 2
        + [pltpu.VMEM((FB, keys, DP), BF)] * 2
        + [pltpu.VMEM((2,) + a, BF) for a in kept]
        + [pltpu.VMEM((FF, M), BF)],
        compiler_params=params(),
        cost_estimate=cost(66),
        name="item_and_dense",
    )(ht, ct, *flat)


def backward_kernel(R, OFF, SL, x_ref, n_ref, qkv_ref, p_ref, l_ref, of_ref, g1t_ref, yt_ref, *rest):
    if SL:
        (dsl_ref, wqkvI_ref, wo_ref, vec_ref, perm_ref, iqkv, iwo, inp, _, _,
         cg_ref, y_ref, pack_ref, gs, ys, xs, os, dqs, das, dqkv, dwo, dnp) = rest
    else:
        (wqkvI_ref, wo_ref, vec_ref, perm_ref, cg_ref, y_ref, dqkv, dwo, dnp, gs, ys, xs, os, dqs, das) = rest

    @pl.when(pl.program_id(0) == 0)
    def _():
        xs[...] = jnp.zeros_like(xs)
        for i, ref in enumerate((dqkv, dwo, dnp)):
            ref[...] = (iqkv, iwo, inp)[i][...] if SL else jnp.zeros_like(ref)

    col = lax.broadcasted_iota(jnp.int32, (16, 1, 1), 0)

    def turn(ref, out, j):
        block = ref[16 * j : min(16 * j + 16, FS)]
        if block.shape[0] < 16:
            block = jnp.concatenate([block, jnp.zeros((16 - block.shape[0],) + block.shape[1:], BF)], 0)
        if 16 * j + 16 > F:
            block = jnp.where(col < F - 16 * j, block, 0).astype(BF)
        out[:, 16 * j : 16 * j + 16, :] = turn_block(perm_ref, block, 16)

    for j in range(FP // 16):
        turn(g1t_ref, gs, j)
    back = []
    if SL:
        both = dsl_ref[0].astype(F32)
        for i in range(1, dsl_ref.shape[0]):
            both = both + dsl_ref[i].astype(F32)
        z0 = jnp.zeros((FP - FS, 2 * D), F32)
        for c in range(SL // 2):
            t = jnp.concatenate([both[c], z0], 0).T
            back += [t[0:D], t[D : 2 * D]]

    def pair(c):
        at = slice(2 * c * FP, (2 * c + 2) * FP)
        dabs, das32 = [], []
        for u in range(2):
            r = 2 * c + u
            xs[:, r * FP : r * FP + F] = x_ref[r]
            os[:, r * FP : (r + 1) * FP] = of_ref[r]
            g = gs[r].T[0:D].astype(F32)
            if r < SL:
                g = g + back[r]
            n = n_ref[r, 0:D, :].astype(F32)
            rc = n_ref[r, D : D + 16, :].astype(F32)[0:1]
            dnp[0] += g * n
            dnp[1] += g
            dabs.append(norm_back_t(g, n, rc, vec_ref[0]).astype(BF))
            yield
        dab = jnp.concatenate(dabs, 1)
        das[:, at] = dab
        do = mm(wo_ref[...], tall(dab))
        yield
        for u in range(2):
            r = 2 * c + u
            own = slice(u * FP, (u + 1) * FP)
            lanes_r = slice(r * FP, (r + 1) * FP)
            for j in range(H // 2):
                inv = l_ref[r, j : j + 1, :]
                parts, offs = [], []
                for t in range(2):
                    hs = slice(64 * j + 32 * t, 64 * j + 32 * t + 32)
                    d = do[hs, own] * inv[:, t * FP : (t + 1) * FP]
                    offs.append(jnp.sum(d * of_ref[r, hs, :].astype(F32), 0, keepdims=True))
                    parts.append(d.astype(BF))
                dom = two_heads(*parts)
                off = jnp.concatenate(offs, 1).astype(BF)
                dp = mm(qkv_ref[r, 2 * D + 64 * j : 2 * D + 64 * j + 64, :].T, dom)
                yield
                e = p_ref[r, :, 256 * j : 256 * j + 256]
                ds = e * (dp.astype(BF) - off)
                dv = mm_nt(dom, e)
                yield
                qm = two_heads(
                    qkv_ref[r, 64 * j : 64 * j + 32, :], qkv_ref[r, 64 * j + 32 : 64 * j + 64, :]
                )
                dk = mm_nt(qm, ds) * 0.6931471805599453
                dq = mm(qkv_ref[r, D + 64 * j : D + 64 * j + 64, :], ds)
                dq = jnp.concatenate([dq[0:32, 0:128], dq[32:64, 128:256]], 0) * SCALE
                yield
                for i, d in enumerate((dq, dk, dv)):
                    dqs[i * D + 64 * j : i * D + 64 * j + 64, lanes_r] = d.astype(BF)
        yield
        cg = mm(wqkvI_ref[...], jnp.concatenate([dqs[:, at], dab], 0))
        for u in range(2):
            cg_ref[2 * c + u] = cg[:, u * FP : u * FP + F]
        yield

    def outputs():
        for j in range(FP // 16):
            turn(yt_ref, ys, j)
            yield
        for r in range(R):
            y_ref[r] = ys[r].T[0:D, 0:F]
            yield

    def sums(part):
        at = slice(part * R * FP // 2, (part + 1) * R * FP // 2)
        for i in range(3):
            dqkv[i * D : (i + 1) * D] += mm_nt(dqs[i * D : (i + 1) * D, at], xs[:, at])
            yield
        dwo[...] += mm_nt(os[:, at], das[:, at])
        yield

    Q = R // 4
    for half in range(2):
        streams = [(pair(c), (c - half * Q) * OFF, 1) for c in range(half * Q, (half + 1) * Q)]
        streams.append((sums(0) if half else outputs(), 3, 1))
        weave(streams)
    for _ in sums(1):
        pass

    if SL:

        @pl.when(pl.program_id(0) == pl.num_programs(0) - 1)
        def _():
            zc = jnp.zeros((D, DP - D), F32)
            three = [jnp.concatenate([dqkv[i * D : (i + 1) * D], zc], 1).T for i in range(3)]
            pack_pair(pack_ref, 0, three[0], three[1])
            pack_pair(pack_ref, PAIR, three[2], dwo)
            pack_norms(pack_ref, 2 * PAIR, [dnp[0], dnp[1]])


def feature_backward(x, saved, g1t, yt, wqkvI, wo, vec, perm, row0, rows, R=16, OFF=6, slots=None, prev=None, packed=0):
    b0 = row0 // R
    nat = lambda a: pl.BlockSpec((R,) + a.shape[1:], lambda i: (i + b0, 0, 0))
    turned = pl.BlockSpec((FS, R, DP), lambda i: (0, i + b0, 0))
    real = pl.BlockSpec((R, D, F), lambda i: (i + b0, 0, 0))
    accs = [shape((3 * D, D), F32), shape((D, D), F32), shape((2, D, FP), F32)]
    ins = [x, *saved, g1t, yt]
    specs = [real] + [nat(a) for a in saved] + [turned] * 2
    out_shape = [shape((x.shape[0], D, F), F32), shape((x.shape[0], D, F))]
    out_specs = [real, real]
    M = R * FP
    scratch = [pltpu.VMEM(a, BF) for a in ((R, FP, DP), (R, FP, DP), (D, M), (D, M), (3 * D, M), (D, M))]
    SL = 0
    alias = {}
    shared = [wqkvI, wo, vec, perm]
    if slots is not None:
        SL = 2 * slots.shape[1]
        shared = [slots] + shared
    ins += shared
    specs += [whole(a) for a in shared]
    if prev is not None:
        cg, y, *acc = prev
        ins += list(acc) + [cg, y]
        specs += [whole(a) for a in acc] + [pl.BlockSpec(memory_space=pl.ANY)] * 2
        alias = {len(ins) - 2: 0, len(ins) - 1: 1}
        out_shape.append(shape((packed, 128)))
        out_specs.append(pl.BlockSpec((packed, 128), lambda i: (0, 0)))
        scratch += [pltpu.VMEM(a.shape, F32) for a in accs]
    else:
        out_shape += accs
        out_specs += [whole(a) for a in accs]
    return pl.pallas_call(
        functools.partial(backward_kernel, R, OFF, SL),
        grid=(rows // R,),
        in_specs=specs,
        out_specs=out_specs,
        out_shape=out_shape,
        input_output_aliases=alias,
        scratch_shapes=scratch,
        compiler_params=params(),
        cost_estimate=cost(60 * rows // R),
        name="feature_backward",
    )(*ins)


def sum_kernel(n, *refs):
    *ready_refs, parts_ref, out_ref = refs
    total = parts_ref[0].astype(F32)
    for i in range(1, n):
        total = total + parts_ref[i].astype(F32)
    total = total.astype(BF)
    if not ready_refs:
        out_ref[...] = total
        return
    rows = ready_refs[0].shape[0]
    for i in range(out_ref.shape[0]):
        out_ref[i, 0:rows] = ready_refs[0][...]
        out_ref[i, rows:] = total


def sum_parts(packed, n, ready=None):
    rows = packed.shape[0] // n
    parts = lax.all_to_all(packed.reshape(n, rows, 128), ("table", "rows"), 0, 0)
    ins = [parts] if ready is None else [ready, parts]
    out = (rows, 128) if ready is None else (lax.axis_size("rows"), ready.shape[0] + rows, 128)
    return pl.pallas_call(
        functools.partial(sum_kernel, n),
        out_shape=shape(out),
        compiler_params=params(),
        cost_estimate=cost(2),
        name="sum_parts",
    )(*ins)


def gather_all(copies):
    tables = lax.axis_size("table")
    ny = tables // 2
    own = lax.all_to_all(copies, "rows", 0, 0)
    pieces = [own]
    for s in range(1, ny):
        pieces.append(lax.ppermute(own, "table", [(t, (t // 2 + s) % ny * 2 + t % 2) for t in range(tables)]))
    other = [lax.ppermute(a, "table", [(t, t ^ 1) for t in range(tables)]) for a in pieces]
    return [a for pair in zip(pieces, other) for a in pair]


def to_row(c):
    return jnp.broadcast_to(c, (c.shape[0], 128)).T[0:1]


def to_col(r):
    return jnp.broadcast_to(r, (128, r.shape[1])).T[:, 0:1]


def clipped(update, weight, count):
    def total(v):
        return jnp.sum(jnp.sum(v, 0, keepdims=True), 1, keepdims=True)

    rms = jnp.sqrt(total(update * update) * (1.0 / count))
    weight_rms = jnp.sqrt(total(weight * weight) * (1.0 / count))
    return update * (RATE * jnp.maximum(0.001, weight_rms) / jnp.maximum(1.0, rms / CLIP))


def optimizer_kernel(
    tables, mid_rows, *refs):
    table_ref, *refs = refs
    piece_refs, refs = refs[:tables], refs[tables:]
    mid_ref, tail_ref = refs[-2:]
    table = table_ref[0]
    ny = tables // 2
    for i, ref in enumerate(piece_refs):
        place = lax.rem(table // 2 - i // 2 + ny, ny) * 2 + lax.rem(table + i % 2, 2)
        for out, at, end in ((mid_ref, 0, mid_rows), (tail_ref, mid_rows, ref.shape[1])):
            rows = ref.shape[0] * (end - at)
            start = pl.multiple_of(place * rows, 8)
            out[pl.ds(start, rows)] = ref[:, at:end, :].astype(F32).reshape(rows, 128)
    optimizer_steps(*refs)


def optimizer_steps(
    proj_ref, outw_ref, in_ref, hid_ref, norm_ref, sr_ref, sc_ref, mm_ref, mh_ref, ns_ref,
    proj_g, out_g, in_g, hid_g, norm_g, proj_n, out_n, in_n, hid_n, norm_n, sr_n, sc_n, mm_n, mh_n, ns_n, mid_ref, tail_ref,
):
    decay = 1.0 - STEP ** (-0.8)

    def stats(grad, col_old, row_old):
        square = grad * grad + 1e-30
        a, b = grad.shape
        over_sub = decay * row_old + (1.0 - decay) * (jnp.sum(square, 0, keepdims=True) * (1.0 / a))
        over_lane = decay * col_old + (1.0 - decay) * (jnp.sum(square, 1, keepdims=True) * (1.0 / b))
        return over_lane, over_sub

    def scaled(grad, col, row, mean):
        return grad * lax.rsqrt(col * (1.0 / mean)) * lax.rsqrt(row)

    def square_pair(ref, at):
        both = ref[at + 2 * D : at + 3 * D].astype(F32)
        a = jnp.concatenate([ref[at : at + D].astype(F32), both[:, 0:64]], 1)
        b = jnp.concatenate([ref[at + D : at + 2 * D].astype(F32), both[:, 64:128]], 1)
        return a, b

    wq, wk = square_pair(tail_ref, 0)
    wv, wo = square_pair(tail_ref, PAIR)
    wq2, wo2 = square_pair(mid_ref, 12 * D)
    wk2, wv2 = square_pair(mid_ref, 12 * D + PAIR)
    for i, grad in enumerate((wq, wk, wv, wq2, wk2, wv2, wo, wo2)):
        g_ref, n_ref, w_ref, j = (proj_g, proj_n, proj_ref, i) if i < 6 else (out_g, out_n, outw_ref, i - 6)
        g_ref[j] = grad
        col, row = stats(grad, to_col(sr_ref[i : i + 1, :]), sc_ref[i : i + 1, :])
        sr_n[i : i + 1, :] = to_row(col)
        sc_n[i : i + 1, :] = row
        mean = jnp.sum(col, 0, keepdims=True) * (1.0 / D)
        w = w_ref[j]
        n_ref[j] = w - clipped(scaled(grad, col, row, mean), w, D * D)

    def wide(at):
        return jnp.concatenate([mid_ref[at + D * j : at + D * j + D].astype(F32) for j in range(6)], 1)

    grad = wide(0)
    in_g[...] = grad
    col, row = stats(grad, to_col(mm_ref[0:1, :]), mh_ref[0:1, :])
    mm_n[0:1, :] = to_row(col)
    mh_n[0:1, :] = row
    mean = jnp.sum(col, 0, keepdims=True) * (1.0 / D)
    w = in_ref[...]
    in_n[...] = w - clipped(scaled(grad, col, row, mean), w, D * FF)
    grad = wide(6 * D)
    hid_g[...] = grad
    col, row = stats(grad, to_col(mm_ref[1:2, :]), mh_ref[1:2, :])
    mm_n[1:2, :] = to_row(col)
    mh_n[1:2, :] = row
    mean = jnp.sum(row, 1, keepdims=True) * (1.0 / FF)
    w = hid_ref[...]
    update = grad * lax.rsqrt(col) * lax.rsqrt(row * (1.0 / mean))
    hid_n[...] = w - clipped(update, w, D * FF)

    pieces = []
    for ref, at, count in ((tail_ref, 2 * PAIR, 2), (mid_ref, 12 * D + 2 * PAIR, 4)):
        v = ref[at : at + 16].astype(F32)
        for i in range(count):
            pieces.append(jnp.concatenate([v[2 * i : 2 * i + 1], v[2 * i + 1 : 2 * i + 2, 0:64]], 1))
    grad = jnp.concatenate(pieces, 0)
    norm_g[...] = grad
    second = decay * ns_ref[...] + (1.0 - decay) * (grad * grad + 1e-30)
    ns_n[...] = second
    update = grad * lax.rsqrt(second)
    rms = jnp.sqrt(jnp.sum(update * update, 1, keepdims=True) * (1.0 / D))
    w = norm_ref[...]
    w_rms = jnp.sqrt(jnp.sum(w * w, 1, keepdims=True) * (1.0 / D))
    norm_n[...] = w - update * (RATE * jnp.maximum(0.001, w_rms) / jnp.maximum(1.0, rms / CLIP))


def optimizer(pieces, mid_rows, *state):
    proj, outw, w_in, w_outT, norms, sr, sc, ms, hs, ns = state
    shards, rows, _ = pieces[0].shape
    table = lax.axis_index("table").astype(jnp.int32).reshape(1)
    order = [proj, outw, w_in, w_outT, norms, proj, outw, w_in, w_outT, norms, sr, sc, ms, hs, ns]
    outs = pl.pallas_call(
        functools.partial(optimizer_kernel, len(pieces), mid_rows),
        in_specs=[pl.BlockSpec(memory_space=pltpu.SMEM)] + [whole(a) for a in (*pieces, *state)],
        out_shape=[shape(a.shape, F32) for a in order],
        scratch_shapes=[
            pltpu.VMEM((len(pieces) * shards * mid_rows, 128), F32),
            pltpu.VMEM((len(pieces) * shards * (rows - mid_rows), 128), F32),
        ],
        compiler_params=params(),
        cost_estimate=cost(8), name="optimizer",
    )(table, *pieces, *state)
    outs = list(outs)
    for i in (3, 8):
        outs[i] = outs[i].T
    return outs


def on_device(n, cells, cotangent, train_count, key_mask, train_order, *state):
    state = list(state)
    state[3] = state[3].T
    proj, outw, w_in, w_outT, norms = state[:5]
    x = jnp.swapaxes(cells[0], 1, 2)
    cot = jnp.swapaxes(cotangent[0], 1, 2)
    rows_here = x.shape[0]
    unit = 8 * n
    tail_rows = -(-TAIL // unit) * unit
    mid_rows = -(-MID // unit) * unit
    perm = perm_matrix()
    (wqkvT, wqkvI, wo, woT, wkv2, wkv2T, wq2, wq2T, wo2I, wo2, w1T, w1, w2T, w2, vec) = prepare(
        proj, outw, w_in, w_outT, norms
    )
    R = 16
    shards = lax.axis_size("rows")
    own = slot_rows(shards, train_count, key_mask, train_order, x, wqkvT, woT, vec)
    slots = lax.all_to_all(own, "rows", 0, 0).reshape((-1,) + own.shape[2:])
    ht, ct, *saved = feature_forward(x, cot, (wqkvT, woT, vec, perm))
    ws = (wq2, wq2T, wo2I, wo2, w1T, w1, w2T, w2, wkv2, wkv2T)
    yt, g1t, back, mid = item_and_dense(ht, ct, slots, perm, ws, vec, mid_rows)
    back = lax.all_to_all(back.reshape(own.shape), "rows", 0, 0)
    args = (x, saved, g1t, yt, wqkvI, wo, vec, perm)
    prev = list(feature_backward(*args, row0=R, rows=rows_here - R, R=R))
    mid, back, prev[4] = lax.optimization_barrier((mid, back, prev[4]))
    mid = sum_parts(mid, n)
    cg, y, tail = feature_backward(*args, row0=0, rows=R, R=R, slots=back, prev=prev, packed=tail_rows)
    tail, mid = lax.optimization_barrier((tail, mid))
    pieces = gather_all(sum_parts(tail, n, mid))
    return (jnp.swapaxes(y, 1, 2)[None], jnp.swapaxes(cg, 1, 2)[None], *optimizer(pieces, mid.shape[0], *state))


def solution(mesh):
    n = int(mesh.shape["table"] * mesh.shape["rows"])
    cells = P("table", "rows", None, None)
    return jax.shard_map(
        functools.partial(on_device, n),
        mesh=mesh,
        in_specs=(cells, cells, P("table"), P("table", "rows"), P("table", "rows")) + (P(),) * 10,
        out_specs=(cells, cells) + (P(),) * 15,
        check_vma=False,
    )
```

```python
import functools

import jax
import jax.numpy as jnp
import numpy as np
from jax import lax
from jax.experimental import pallas as pl
from jax.experimental.pallas import tpu as pltpu
from jax.sharding import PartitionSpec as P

BF, F32 = jnp.bfloat16, jnp.float32
D, DP = 192, 256
H, E = 6, 32
F, FP = 119, 128
FS = 120
FF = 768
STEP = 3
CLIP = 0.3
RATE = 0.5
FB = 8
SCALE = E**-0.5
SCALE2 = SCALE * 1.4426950408889634
C0 = 0.7978845608028654
C1 = 0.044715
NT = (((1,), (1,)), ((), ()))
TN = (((0,), (0,)), ((), ()))
PAIR = 576
TAIL = 2 * PAIR + 8
MID = 2 * 6 * D + 2 * PAIR + 8


def mm(a, b):
    return jnp.dot(a, b, preferred_element_type=F32)


def mm_nt(a, b):
    return lax.dot_general(a, b, NT, preferred_element_type=F32)


def mm_tn(a, b):
    return lax.dot_general(a, b, TN, preferred_element_type=F32)


def lanes():
    return lax.broadcasted_iota(jnp.int32, (1, DP), 1)


def whole(a):
    nd = len(a.shape)
    return pl.BlockSpec(a.shape, lambda *i: (0,) * nd)


def half_masks():
    lane = lax.broadcasted_iota(jnp.int32, (1, 128), 1)
    return [jnp.where((lane >= E * h) & (lane < E * (h + 1)), 1.0, 0.0).astype(BF) for h in range(4)]


def spread_halves(w, masks):
    z = jnp.zeros((w.shape[0], 128), BF)
    lo, hi = w[:, 0:128], w[:, 128:256]
    return jnp.concatenate(
        [jnp.concatenate([lo * masks[h], z], 1) for h in range(4)]
        + [jnp.concatenate([z, hi * masks[h]], 1) for h in range(2)], 0)


def mean0(a): return jnp.sum(a, 0, keepdims=True) * (1.0 / D)


def norm_t(a):
    c = a - mean0(a)
    rc = lax.rsqrt(mean0(c * c) + 1e-5)
    return c * rc, rc


def norm_back_t(g, n, rc, gain):
    dn = g * gain
    return (dn - mean0(dn) - n * mean0(dn * n)) * rc


def tall(a):
    return jnp.concatenate([a, jnp.zeros((DP - D, a.shape[1]), a.dtype)], 0)


def gelu_parts(u):
    uu = u * u
    th = jnp.tanh(u * (BF(C0) + BF(C0 * C1) * uu))
    half = BF(0.5) + BF(0.5) * th
    act = u * half
    slope = half + act * (BF(1.0) - th) * (BF(C0) + BF(3.0 * C0 * C1) * uu)
    return act, slope


def weave(streams):
    live=[[g,s,p] for g,s,p in streams]
    turn=0
    while live:
        for it in list(live):
            if turn>=it[1]:
                for _ in range(it[2]):
                    try: next(it[0])
                    except StopIteration:
                        live.remove(it); break
        turn+=1

def shape(s, t=BF):
    return jax.ShapeDtypeStruct(s, t)


def params(mib=58):
    return pltpu.CompilerParams(vmem_limit_bytes=mib << 20)


def cost(us):
    return pl.CostEstimate(flops=int(us * 1.1e9), bytes_accessed=int(us * 1e6), transcendentals=0)


def perm_matrix():
    place = np.zeros((256, 256), np.float32)
    for f in range(16):
        for r in range(16):
            place[f * 16 + r, r * 16 + f] = 1
    return jnp.asarray(place, BF)


def padded_square(w):
    a = jnp.concatenate([w, jnp.zeros((D, DP - D), F32)], 1).astype(BF)
    a = jnp.concatenate([a, jnp.zeros((DP - D, DP), BF)], 0)
    return a, a.T


def first_weights_kernel(proj, outw, norms, wqkvT, woT, vec, nrow):
    for i in range(3):
        wqkvT[i * D : (i + 1) * D, :] = padded_square(proj[i])[1][0:D]
    woT[...] = padded_square(outw[0])[1][0:D]
    nrow[...] = jnp.zeros((8, DP), F32)
    nrow[0:6, 0:D] = norms[...]
    for i in range(6):
        vec[i] = jnp.broadcast_to(nrow[i : i + 1, :], (128, DP)).T[0:D]


def first_weights(proj, outw, norms):
    return pl.pallas_call(
        first_weights_kernel,
        grid=(1,),
        in_specs=[
            pl.BlockSpec((3, D, D), lambda i: (0, 0, 0)),
            pl.BlockSpec((1, D, D), lambda i: (0, 0, 0)),
            whole(norms),
        ],
        out_specs=[whole(shape(a)) for a in ((3 * D, DP), (D, DP), (6, D, 128))],
        out_shape=[shape((3 * D, DP)), shape((D, DP)), shape((6, D, 128), F32)],
        scratch_shapes=[pltpu.VMEM((8, DP), F32)],
        compiler_params=params(),
        cost_estimate=cost(2),
        name="first_weights",
    )(proj, outw, norms)


def weights_kernel(proj, outw, w_in, w_outT, wqkvI, wo, wkv2, wkv2T, wq2, wq2T, wo2I, wo2, w1T, w1, w2T, w2):
    row = lax.broadcasted_iota(jnp.int32, (D, DP), 0)
    eye = jnp.where(row == lax.broadcasted_iota(jnp.int32, (D, DP), 1), 1.0, 0.0).astype(BF)
    wqkvI[...] = jnp.concatenate([proj[0], proj[1], proj[2], eye[:, 0:D].astype(F32)], 1).astype(BF)
    wo[...] = jnp.concatenate([outw[0], jnp.zeros((D, DP - D), F32)], 1).astype(BF)
    a, t = padded_square(proj[3])
    wq2[...] = a
    wq2T[...] = t
    a, t = padded_square(outw[1])
    wo2[...] = a[0:D]
    wo2I[:, 0:DP] = t[0:D]
    wo2I[:, DP : 2 * DP] = eye
    for i in range(2):
        a, t = padded_square(proj[4 + i])
        wkv2[:, i * DP : (i + 1) * DP] = a
        wkv2T[i * DP : (i + 1) * DP, :] = t
    zw = jnp.zeros((DP - D, FF), BF)
    a = w_in[...].astype(BF)
    w1[...] = a
    w1T[...] = jnp.concatenate([a, zw], 0).T
    a = w_outT[...].astype(BF)
    w2T[...] = a
    w2[...] = jnp.concatenate([a, zw], 0).T


def other_weights(proj, outw, w_in, w_outT):
    sq, half = shape((DP, DP)), shape((D, DP))
    outs = [shape((D, 4 * D)), half, shape((DP, 2 * DP)), shape((2 * DP, DP)), sq, sq]
    outs += [shape((D, 2 * DP)), half, shape((FF, DP)), shape((D, FF)), shape((D, FF)), shape((FF, DP))]
    return pl.pallas_call(
        weights_kernel,
        out_shape=outs,
        compiler_params=params(),
        cost_estimate=cost(4),
        name="other_weights",
    )(proj, outw, w_in, w_outT)


def two_heads(a, b):
    z = jnp.zeros(a.shape, a.dtype)
    return jnp.concatenate([jnp.concatenate([a, z], 1), jnp.concatenate([z, b], 1)], 0)


def feature_pair(x, wqkvT_ref, woT_ref, keep, out):
    qkv = mm(wqkvT_ref[...], x)
    q = (qkv[0:D] * SCALE2).astype(BF)
    k = qkv[D : 2 * D].astype(BF)
    v = qkv[2 * D : 3 * D].astype(BF)
    yield
    row = lax.broadcasted_iota(jnp.int32, (8, 1), 0)
    outs = []
    for u in range(2):
        own = slice(u * FP, (u + 1) * FP)
        keep("qkv", u, (q[:, own], k[:, own], v[:, own]))
        ot = []
        for j in range(H // 2):
            hs = slice(64 * j, 64 * j + 64)
            qm = two_heads(q[64 * j : 64 * j + 32, own], q[64 * j + 32 : 64 * j + 64, own])
            st = mm(k[hs, own].T, qm)
            yield
            last = jnp.where(row < F - FS + 8, st[FS - 8 : FS], -1e30)
            mx = jnp.maximum(jnp.max(st[0 : FS - 8], 0, keepdims=True), jnp.max(last, 0, keepdims=True))
            e = jnp.exp2(st[0 : FS - 8] - mx)
            last = jnp.exp2(last - mx)
            inv = 1.0 / (jnp.sum(e, 0, keepdims=True) + jnp.sum(last, 0, keepdims=True))
            e = jnp.concatenate([e, last, jnp.zeros((FP - FS, 2 * FP), F32)], 0).astype(BF)
            keep("p", (u, j), (e, inv))
            yield
            t = mm(v[hs, own], e)
            ot.append(t[0:32, 0:128] * inv[:, 0:128])
            ot.append(t[32:64, 128:256] * inv[:, 128:256])
            yield
        ot = jnp.concatenate(ot, 0).astype(BF)
        keep("o", u, ot)
        outs.append(ot)
    a = mm(woT_ref[...], tall(jnp.concatenate(outs, 1)))
    yield
    for u in range(2):
        own = slice(u * FP, (u + 1) * FP)
        out.append(norm_t(x[0:D, own].astype(F32) + a[:, own]))
        yield


def slots_kernel(SL, count_ref, mask_ref, order_ref, x_ref, wqkvT_ref, woT_ref, vec_ref, out_ref, xs):
    xs[...] = jnp.zeros_like(xs)
    row = lax.broadcasted_iota(jnp.int32, (FS, 1), 0)
    lane = lax.broadcasted_iota(jnp.int32, (1, 2 * D), 1)

    def flag(r):
        order = order_ref[0, r]
        usable = (order < count_ref[0]) & ((mask_ref[0, r] == 1) | (order == 0))
        return jnp.where(usable, 1.0, 0.0)

    def pair(c):
        for u in range(2):
            xs[c, 0:D, u * FP : u * FP + F] = x_ref[2 * c + u]
        out = []
        yield from feature_pair(xs[c], wqkvT_ref, woT_ref, lambda *a: None, out)
        both = jnp.concatenate([(n * vec_ref[0] + vec_ref[1]).astype(BF) for n, _ in out], 0)
        flags = jnp.where(lane < D, flag(2 * c), flag(2 * c + 1))
        both = jnp.where(row < F, both.T[0:FS].astype(F32), flags).astype(BF)
        for i in range(out_ref.shape[0]):
            out_ref[i, c] = both
        yield

    weave([(pair(c), 0, 1) for c in range(SL // 2)])


def slot_rows(shards, count, mask, order, cells, wqkvT, woT, vec):
    SL = mask.shape[1]
    smem = pl.BlockSpec(memory_space=pltpu.SMEM)
    sent = shape((shards, SL // 2, FS, 2 * D))
    return pl.pallas_call(
        functools.partial(slots_kernel, SL),
        grid=(1,),
        in_specs=[smem, smem, smem, pl.BlockSpec((SL, D, F), lambda i: (0, 0, 0))]
        + [whole(a) for a in (wqkvT, woT, vec)],
        out_specs=whole(sent),
        out_shape=sent,
        scratch_shapes=[pltpu.VMEM((SL // 2, DP, 2 * FP), BF)],
        compiler_params=params(),
        cost_estimate=cost(5),
        name="slot_rows",
    )(count, mask, order, cells, wqkvT, woT, vec)


def turn_block(perm_ref, block, R):
    return mm(perm_ref[...], block.reshape(256, block.shape[-1])).astype(BF).reshape(16, R, block.shape[-1])


def forward_kernel(
    R, OFF, x_ref, c_ref, wqkvT_ref, woT_ref, vec_ref, perm_ref, ht_ref, ct_ref, n_ref, qkv_ref, p_ref, l_ref, of_ref, xs, hs, cp, cs
):
    @pl.when(pl.program_id(0) == 0)
    def _():
        xs[...] = jnp.zeros_like(xs)
        cp[...] = jnp.zeros_like(cp)

    def pair(c):
        for u in range(2):
            xs[c, 0:D, u * FP : u * FP + F] = x_ref[2 * c + u]

        def keep(what, at, val):
            if what == "qkv":
                for i in range(3):
                    qkv_ref[2 * c + at, i * D : (i + 1) * D, :] = val[i]
            elif what == "p":
                u, j = at
                p_ref[2 * c + u, :, 256 * j : 256 * j + 256] = val[0]
                l_ref[2 * c + u, j : j + 1, :] = val[1]
            else:
                of_ref[2 * c + at] = val

        out = []
        yield from feature_pair(xs[c], wqkvT_ref, woT_ref, keep, out)
        for u in range(2):
            r = 2 * c + u
            n, rc = out[u]
            n_ref[r, 0:D, :] = n.astype(BF)
            n_ref[r, D : D + 16, :] = jnp.broadcast_to(rc, (16, FP)).astype(BF)
            h = tall((n * vec_ref[0] + vec_ref[1]).astype(BF))
            hs[r] = h.T
            yield

    def cotangents():
        for r in range(R):
            cp[r % 4, 0:D, 0:F] = c_ref[r]
            cs[r] = cp[r % 4].T
            yield
        for j in range(FP // 16):
            ct_ref[16 * j : 16 * j + 16] = turn_block(perm_ref, cs[:, 16 * j : 16 * j + 16, :], R)
            yield

    weave([(pair(c), c * OFF, 1) for c in range(R // 2)] + [(cotangents(), 4, 1)])
    for j in range(FP // 16):
        ht_ref[16 * j : 16 * j + 16] = turn_block(perm_ref, hs[:, 16 * j : 16 * j + 16, :], R)


def feature_forward(cells, cot, ws, R=16, OFF=2):
    rows = cells.shape[0]
    nat = lambda a, b: pl.BlockSpec((R, a, b), lambda i: (i, 0, 0))
    turned = pl.BlockSpec((FP, R, DP), lambda i: (0, i, 0))
    sizes = [(D + 16, FP), (3 * D, FP), (FP, H * FP), (8, 2 * FP), (D, FP)]
    kinds = [BF, BF, BF, F32, BF]
    return pl.pallas_call(
        functools.partial(forward_kernel, R, OFF),
        grid=(rows // R,),
        in_specs=[nat(D, F), nat(D, F)] + [whole(a) for a in ws],
        out_specs=[turned, turned] + [nat(*a) for a in sizes],
        out_shape=[shape((FP, rows, DP))] * 2 + [shape((rows,) + a, t) for a, t in zip(sizes, kinds)],
        scratch_shapes=[
            pltpu.VMEM((R // 2, DP, 2 * FP), BF),
            pltpu.VMEM((R, FP, DP), BF),
            pltpu.VMEM((4, DP, FP), BF),
            pltpu.VMEM((R, FP, DP), BF),
        ],
        compiler_params=params(),
        cost_estimate=cost(9 * rows // R),
        name="feature_forward",
    )(cells, cot, *ws)


def pair_up(table, i, ny, back=False):
    shift = ny - i // 2 if back else i // 2
    return lax.rem(table // 2 + shift, ny) * 2 + lax.rem(table + i % 2, 2)


def hand_out(table_ref, pack, piece_refs):
    tables = len(piece_refs)
    rows = pack.shape[0] // tables
    for i, ref in enumerate(piece_refs):
        place = pair_up(table_ref[0], i, tables // 2)
        ref[...] = pack[pl.ds(pl.multiple_of(place * rows, 8), rows)].astype(BF)


def pack_pair(ref, at, a, b):
    ref[at : at + D] = a[0:D, 0:128]
    ref[at + D : at + 2 * D] = b[0:D, 0:128]
    ref[at + 2 * D : at + 3 * D] = jnp.concatenate([a[0:D, 128:D], b[0:D, 128:D]], 1)


def pack_norms(ref, at, sums):
    rows = []
    for s in sums:
        if s.shape[0] == D:
            s = jnp.concatenate([s, jnp.zeros((DP - D, 128), F32)], 0).T
        v = jnp.sum(s, 0, keepdims=True)
        rows += [v[:, 0:128], v[:, 128:256]]
    rows.append(jnp.zeros((ref.shape[0] - at - len(rows), 128), F32))
    ref[at:] = jnp.concatenate(rows, 0)


def item_kernel(
    RW, keys, tables, OFF, WP, CC, WC, table_ref, ht_ref, ct_ref, slot_ref, perm_ref, wq_ref, wqT_ref, woI_ref, wo_ref, w1T_ref, w1_ref, w2T_ref, w2_ref,
    wkv_ref, wkvT_ref, vec_ref, y_ref, g1_ref, back_ref, *rest
):
    piece_refs, rest = rest[:tables], rest[tables:]
    (dwq, dwo, dw1, dw2, dnp, dwkv, bias_ref, pack_ref, hk_ref, bk_ref,
     dk_ref, dv_ref, hbTs, ois, hb2Ts, actss, dbTs, duss, dabTs, dqss, slp) = rest
    step = pl.program_id(0)
    blocks = [(s, b, min(16, FS - b)) for s in range(0, keys, 16) for b in range(0, FS, 16)]

    @pl.when(step == 0)
    def _():
        for ref in (dwq, dwo, dw1, dw2, dnp, dwkv):
            ref[...] = jnp.zeros_like(ref)
        for ref in (hbTs, ois, hb2Ts, actss, dbTs, duss, dabTs, dqss):
            ref[1] = jnp.zeros_like(ref[1])
        hk_ref[:, :, D:DP] = jnp.zeros((FS, keys, DP - D), BF)
        for s, b, n in blocks:
            own = slot_ref[s // 2 : s // 2 + 8, b : b + n, :]
            own = jnp.concatenate([own[:, :, 0:D], own[:, :, D : 2 * D]], 0)
            if n < 16:
                own = jnp.concatenate([own, jnp.zeros((16, 16 - n, D), BF)], 1)
            hk_ref[b : b + n, s : s + 16, 0:D] = turn_block(perm_ref, own, 16)[0:n]
        for s in range(0, keys, 16):
            flag = slot_ref[s // 2 : s // 2 + 8, F, :].astype(F32)
            for i, at in enumerate((0, DP)):
                bias_ref[s + 8 * i : s + 8 * i + 8] = jnp.where(flag[:, at : at + 128] > 0.5, 0.0, -1e30)

    cur = step % 2
    masks = half_masks()
    LW = 2 * RW
    left = lax.broadcasted_iota(jnp.int32, (1, LW), 1) < RW
    HK = H * keys
    hbT, oi, hb2T, acts, dbT, dus, dabT, dqs = [r.at[cur] for r in (hbTs, ois, hb2Ts, actss, dbTs, duss, dabTs, dqss)]
    hk = hk_ref[pl.ds(pl.multiple_of(step * FB, FB), FB)].reshape(FB * keys, DP)
    kvs = [mm(hk, wkv_ref[...]).astype(BF)]

    def attend(j, out):
        h = ht_ref[2 * j:2 * j + 2].reshape(LW, DP)
        q = (mm(h, wq_ref[...]) * SCALE2).astype(BF)
        yield
        ks = [spread_halves(kvs[0][(2 * j + c) * keys : (2 * j + c + 1) * keys, 0:DP], masks) for c in range(2)]
        hbT[:, j * LW:(j + 1) * LW] = h.T[0:D]
        yield
        st = jnp.where(left, mm_nt(ks[0], q), mm_nt(ks[1], q))
        yield
        vs = [spread_halves(kvs[0][(2 * j + c) * keys : (2 * j + c + 1) * keys, DP:], masks) for c in range(2)]
        pbs = []
        for hh in range(H):
            s = st[hh * keys:(hh + 1) * keys] + bias_ref[...]
            e = jnp.exp2(s - jnp.max(s, 0, keepdims=True))
            pbs.append((e * (1.0 / jnp.sum(e, 0, keepdims=True))).astype(BF))
            if hh % 2: yield
        pb = jnp.concatenate(pbs, 0)
        pt = pb.T
        yield
        o = jnp.concatenate([mm(pt[:RW], vs[0]), mm(pt[RW:], vs[1])], 0).astype(BF)
        oi[j * LW:(j + 1) * LW] = o
        out.extend([q, pb, ks, vs, o])
        yield
    def dense(i, os, out):
        c0 = i * 2 * LW
        g1v, b1v, g2v, b2v = [vec_ref[i] for i in range(2, 6)]
        h = ht_ref[4 * i:4 * i + 4].reshape(2 * LW, DP)
        o = jnp.concatenate(os, 0)
        aT = mm_nt(woI_ref[...], jnp.concatenate([o, h], 1))
        yield
        n2, rc2, h2, hb2 = [], [], [], []
        for t in range(2):
            n, rc = norm_t(aT[:, t * LW:(t + 1) * LW])
            hh = n * g1v + b1v
            n2.append(n.astype(BF)); rc2.append(rc); hb2.append(hh.astype(BF))
            yield
        hb2 = jnp.concatenate(hb2, 1)
        hb2T[:, c0:c0 + 2 * LW] = hb2
        hb2 = tall(hb2)
        C = CC
        u = mm(w1T_ref[0:C], hb2)
        for c in range(FF // C):
            un = mm(w1T_ref[C * c + C:C * c + 2 * C], hb2) if c + 1 < FF // C else None
            act, slope = gelu_parts(u.astype(BF))
            acts[C * c:C * c + C, c0:c0 + 2 * LW] = act
            slp[C * c:C * c + C, c0:c0 + 2 * LW] = slope
            u = un
            yield
        gT = ct_ref[4 * i:4 * i + 4].reshape(2 * LW, DP).T[0:D].astype(F32)
        z = mm(w2T_ref[...], acts[:, c0:c0 + 2 * LW])
        yield
        dbs, d3s = [], []
        ys = []
        for t in range(2):
            sl = slice(t * LW, (t + 1) * LW)
            n3, rc3 = norm_t(hb2[0:D, sl].astype(F32) + z[:, sl])
            ys.append((n3 * g2v + b2v).astype(BF))
            yield
            g = gT[:, sl]
            dnp[2] += g * n3
            dnp[3] += g
            d3 = norm_back_t(g, n3, rc3, g2v)
            dbs.append(d3.astype(BF))
            yield
        db = jnp.concatenate(dbs, 1)
        dbT[:, c0:c0 + 2 * LW] = db
        db = tall(db)
        w = mm(w2_ref[0:C], db)
        for c in range(FF // C):
            wn = mm(w2_ref[C * c + C:C * c + 2 * C], db) if c + 1 < FF // C else None
            dus[C * c:C * c + C, c0:c0 + 2 * LW] = w.astype(BF) * slp[C * c:C * c + C, c0:c0 + 2 * LW]
            w = wn
            yield
        dh = mm(w1_ref[...], dus[:, c0:c0 + 2 * LW])
        yT = tall(jnp.concatenate(ys, 1))
        y_ref[4 * i:4 * i + 4] = yT.T.reshape(4, RW, DP)
        yield
        dabs = []
        for t in range(2):
            dh2 = dbs[t].astype(F32) + dh[:, t * LW:(t + 1) * LW]
            n2f = n2[t].astype(F32)
            dnp[0] += dh2 * n2f
            dnp[1] += dh2
            dabs.append(norm_back_t(dh2, n2f, rc2[t], g1v).astype(BF))
            yield
        dab = jnp.concatenate(dabs, 1)
        dabT[:, c0:c0 + 2 * LW] = dab
        doT = mm(wo_ref[...], tall(dab)).astype(BF)
        out.extend([dab, doT])
        yield
    def back(j, at, doT, out):
        q, pb, ks, vs, _ = at
        do = tall(doT)
        don = do.T
        dp = jnp.where(left, mm(vs[0], do), mm(vs[1], do))
        yield
        slot_sums(dv_ref, j, pb, don, None)
        yield
        dss = []
        for hh in range(H):
            sl = slice(hh * keys, (hh + 1) * keys)
            p, d = pb[sl].astype(F32), dp[sl]
            dss.append((p * (d - jnp.sum(p * d, 0, keepdims=True))).astype(BF))
            if hh % 2: yield
        ds = jnp.concatenate(dss, 0)
        dst = ds.T
        yield
        slot_sums(dk_ref, j, ds, q, 0.6931471805599453)
        yield
        dq = jnp.concatenate([mm(dst[:RW], ks[0]), mm(dst[RW:], ks[1])], 0) * SCALE
        dq = dq.astype(BF)
        dqs[j * LW:(j + 1) * LW] = dq
        out.append(dq)
        yield
    lane = lax.broadcasted_iota(jnp.int32, (1, 128), 1)
    zq = jnp.zeros((RW, 128), BF)
    def slot_sums(ref, j, w, rows, scale):
        out = [[], []]
        for t, heads in ((0, 4), (1, 2)):
            r = rows[:, 128 * t:128 * t + 128]
            both = jnp.concatenate([jnp.concatenate([r[:RW], zq], 0), jnp.concatenate([zq, r[RW:]], 0)], 1)
            full = mm(w[4 * t * keys:(4 * t + heads) * keys], both)
            for c in range(2):
                col = full[:, 128 * c:128 * c + 128]
                v = col[0:keys]
                for hh in range(1, heads):
                    v = jnp.where(lane >= E * hh, col[hh * keys:(hh + 1) * keys], v)
                out[c].append(v)
        for c in range(2):
            v = jnp.concatenate(out[c], 1)
            ref[2 * j + c] = (v if scale is None else v * scale).astype(BF)
    def finish(i, dqv, dab):
        dq = jnp.concatenate(dqv, 0)
        g1 = mm(dq, wqT_ref[...]) + tall(dab).T.astype(F32)
        g1_ref[4 * i:4 * i + 4] = g1.astype(BF).reshape(4, RW, DP)
        yield
    def chunk(i):
        at = [[], []]
        ga, gb = attend(2 * i, at[0]), attend(2 * i + 1, at[1])
        for _ in zip(ga, gb): yield
        for _ in ga: yield
        for _ in gb: yield
        out = []
        yield from dense(i, [at[0][4], at[1][4]], out)
        dab, doT = out
        dq = []
        for t in range(2):
            yield from back(2 * i + t, at[t], doT[:, t * LW:(t + 1) * LW], dq)
        yield from finish(i, dq, dab)
    def wgrad(b):
        dwq[...] += mm(hbTs[b], dqss[b])
        yield
        dwo[...] += mm(dabTs[b], ois[b])
        yield
        for c in range(0, FF, WC):
            dw1[c:c + WC] += mm_nt(duss[b, c:c + WC], hb2Ts[b])
            yield
        for c in range(0, FF, WC):
            dw2[c:c + WC] += mm_nt(actss[b, c:c + WC], dbTs[b])
            yield
    NC = FB // 4
    weave([(chunk(i), i * OFF, 1) for i in range(NC)] + [(wgrad(1 - cur), WP, 1)])
    dkv = jnp.concatenate([r[...].reshape(FB * keys, DP) for r in (dk_ref, dv_ref)], 1)
    dwkv[...] += mm_tn(hk, dkv)
    bk_ref[pl.ds(pl.multiple_of(step * FB, FB), FB)] = mm(dkv, wkvT_ref[...]).astype(BF).reshape(FB, keys, DP)

    @pl.when(step == pl.num_programs(0) - 1)
    def _():
        for _ in wgrad(cur):
            pass
        for s, b, n in blocks:
            own = bk_ref[b : b + n, s : s + 16, :]
            if n < 16:
                own = jnp.concatenate([own, jnp.zeros((16 - n, 16, DP), BF)], 0)
            own = turn_block(perm_ref, own, 16)[:, 0:n, 0:D]
            back_ref[s // 2 : s // 2 + 8, b : b + n, :] = jnp.concatenate([own[0:8], own[8:16]], 2)
        at = 0
        for ref in (dw1, dw2):
            t = ref[...].T
            for j in range(FF // 128):
                pack_ref[at : at + D] = t[:, 128 * j : 128 * j + 128]
                at += D
        pack_pair(pack_ref, at, dwq, tall(dwo[...]).T)
        pack_pair(pack_ref, at + PAIR, dwkv[:, 0:DP], dwkv[:, DP:])
        pack_norms(pack_ref, at + 2 * PAIR, [dnp[i] for i in range(4)])
        hand_out(table_ref, pack_ref, piece_refs)


def item_and_dense(table, ht, ct, slots, perm, ws, vec, packed, tables, OFF=0, WP=20, CC=384, WC=384):
    RW = ht.shape[1]
    keys = 2 * slots.shape[0]
    M = FB * RW
    cells = pl.BlockSpec((FB, RW, DP), lambda i: (i, 0, 0))
    accs = [(D, DP), (D, DP), (FF, D), (FF, D), (4, D, 128), (DP, 2 * DP), (keys, 128), (packed, 128)]
    kept = [(D, M), (M, DP), (D, M), (FF, M), (D, M), (FF, M), (D, M), (M, DP)]
    flat = [slots, perm, *ws, vec]
    outs = [shape((FS, RW, DP))] * 2 + [shape(slots.shape)] + [shape((packed // tables, 128))] * tables
    return pl.pallas_call(
        functools.partial(item_kernel, RW, keys, tables, OFF, WP, CC, WC),
        grid=(FS // FB,),
        in_specs=[pl.BlockSpec(memory_space=pltpu.SMEM), cells, cells] + [whole(a) for a in flat],
        out_specs=[cells, cells] + [whole(a) for a in outs[2:]],
        out_shape=outs,
        scratch_shapes=[pltpu.VMEM(a, F32) for a in accs]
        + [pltpu.VMEM((FS, keys, DP), BF)] * 2
        + [pltpu.VMEM((FB, keys, DP), BF)] * 2
        + [pltpu.VMEM((2,) + a, BF) for a in kept]
        + [pltpu.VMEM((FF, M), BF)],
        compiler_params=params(),
        cost_estimate=cost(66),
        name="item_and_dense",
    )(table, ht, ct, *flat)


def backward_rows(
    x_ref, n_ref, qkv_ref, p_ref, l_ref, of_ref, wqkvI_ref, wo_ref, vec_ref, cg_ref, xs, os, dqs, das, dqkv, dwo, dnp, grad_of, base_ref=None
):
    def pair(c):
        at = slice(2 * c * FP, (2 * c + 2) * FP)
        dabs = []
        for u in range(2):
            r = 2 * c + u
            xs[:, r * FP : r * FP + F] = x_ref[r]
            os[:, r * FP : (r + 1) * FP] = of_ref[r]
            g = grad_of(r)
            n = n_ref[r, 0:D, :].astype(F32)
            rc = n_ref[r, D : D + 16, :].astype(F32)[0:1]
            dnp[0] += g * n
            dnp[1] += g
            dabs.append(norm_back_t(g, n, rc, vec_ref[0]).astype(BF))
            yield
        dab = jnp.concatenate(dabs, 1)
        das[:, at] = dab
        do = mm(wo_ref[...], tall(dab))
        yield
        for u in range(2):
            r = 2 * c + u
            own = slice(u * FP, (u + 1) * FP)
            lanes_r = slice(r * FP, (r + 1) * FP)
            for j in range(H // 2):
                inv = l_ref[r, j : j + 1, :]
                parts, offs = [], []
                for t in range(2):
                    hs = slice(64 * j + 32 * t, 64 * j + 32 * t + 32)
                    d = do[hs, own] * inv[:, t * FP : (t + 1) * FP]
                    offs.append(jnp.sum(d * of_ref[r, hs, :].astype(F32), 0, keepdims=True))
                    parts.append(d.astype(BF))
                dom = two_heads(*parts)
                off = jnp.concatenate(offs, 1).astype(BF)
                dp = mm(qkv_ref[r, 2 * D + 64 * j : 2 * D + 64 * j + 64, :].T, dom)
                yield
                e = p_ref[r, :, 256 * j : 256 * j + 256]
                ds = e * (dp.astype(BF) - off)
                dv = mm_nt(dom, e)
                yield
                qm = two_heads(
                    qkv_ref[r, 64 * j : 64 * j + 32, :], qkv_ref[r, 64 * j + 32 : 64 * j + 64, :]
                )
                dk = mm_nt(qm, ds) * 0.6931471805599453
                dq = mm(qkv_ref[r, D + 64 * j : D + 64 * j + 64, :], ds)
                dq = jnp.concatenate([dq[0:32, 0:128], dq[32:64, 128:256]], 0) * SCALE
                yield
                for i, d in enumerate((dq, dk, dv)):
                    dqs[i * D + 64 * j : i * D + 64 * j + 64, lanes_r] = d.astype(BF)
        yield
        cg = mm(wqkvI_ref[...], jnp.concatenate([dqs[:, at], dab], 0))
        for u in range(2):
            own = cg[:, u * FP : u * FP + F]
            cg_ref[2 * c + u] = own if base_ref is None else own + base_ref[2 * c + u]
        yield

    def sums(at):
        dqkv[...] += mm_nt(dqs[:, at], xs[:, at])
        yield
        dwo[...] += mm_nt(os[:, at], das[:, at])
        yield

    return pair, sums


def backward_kernel(
    R, OFF, x_ref, n_ref, qkv_ref, p_ref, l_ref, of_ref, g1t_ref, yt_ref, wqkvI_ref, wo_ref, vec_ref, perm_ref,
    cg_ref, y_ref, dqkv, dwo, dnp, gs, ys, xs, os, dqs, das,
):
    @pl.when(pl.program_id(0) == 0)
    def _():
        for ref in (xs, dqkv, dwo, dnp):
            ref[...] = jnp.zeros_like(ref)

    col = lax.broadcasted_iota(jnp.int32, (16, 1, 1), 0)

    def turn(ref, out, j):
        block = ref[16 * j : min(16 * j + 16, FS)]
        if block.shape[0] < 16:
            block = jnp.concatenate([block, jnp.zeros((16 - block.shape[0],) + block.shape[1:], BF)], 0)
        if 16 * j + 16 > F:
            block = jnp.where(col < F - 16 * j, block, 0).astype(BF)
        out[:, 16 * j : 16 * j + 16, :] = turn_block(perm_ref, block, 16)

    for j in range(FP // 16):
        turn(g1t_ref, gs, j)

    def outputs():
        for j in range(FP // 16):
            turn(yt_ref, ys, j)
            yield
        for r in range(R):
            y_ref[r] = ys[r].T[0:D, 0:F]
            yield

    pair, sums = backward_rows(
        x_ref, n_ref, qkv_ref, p_ref, l_ref, of_ref, wqkvI_ref, wo_ref, vec_ref, cg_ref, xs, os, dqs, das, dqkv, dwo, dnp,
        lambda r: gs[r].T[0:D].astype(F32),
    )
    Q = R // 4
    M = R * FP // 2
    for half in range(2):
        streams = [(pair(c), (c - half * Q) * OFF, 1) for c in range(half * Q, (half + 1) * Q)]
        streams.append((sums(slice(0, M)) if half else outputs(), 3, 1))
        weave(streams)
    for _ in sums(slice(M, 2 * M)):
        pass


def feature_backward(x, saved, g1t, yt, wqkvI, wo, vec, perm, R=16, OFF=1):
    rows = x.shape[0]
    nat = lambda a: pl.BlockSpec((R,) + a.shape[1:], lambda i: (i, 0, 0))
    turned = pl.BlockSpec((FS, R, DP), lambda i: (0, i, 0))
    accs = [shape((3 * D, D), F32), shape((D, D), F32), shape((2, D, FP), F32)]
    shared = [wqkvI, wo, vec, perm]
    M = R * FP
    return pl.pallas_call(
        functools.partial(backward_kernel, R, OFF),
        grid=(rows // R,),
        in_specs=[nat(x)] + [nat(a) for a in saved] + [turned] * 2 + [whole(a) for a in shared],
        out_specs=[nat(x), nat(x)] + [whole(a) for a in accs],
        out_shape=[shape(x.shape, F32), shape(x.shape)] + accs,
        scratch_shapes=[pltpu.VMEM(a, BF) for a in ((R, FP, DP), (R, FP, DP), (D, M), (D, M), (3 * D, M), (D, M))],
        compiler_params=params(),
        cost_estimate=cost(60 * rows // R),
        name="feature_backward",
    )(x, *saved, g1t, yt, *shared)


def slots_back_kernel(
    SL, tables, table_ref, x_ref, n_ref, qkv_ref, p_ref, l_ref, of_ref, slot_ref, base_ref, iqkv, iwo, inp, wqkvI_ref, wo_ref, vec_ref,
    cg_ref, *rest,
):
    piece_refs, rest = rest[:tables], rest[tables:]
    pack_ref, xs, os, dqs, das, dqkv, dwo, dnp = rest
    xs[...] = jnp.zeros_like(xs)
    for ref, init in ((dqkv, iqkv), (dwo, iwo), (dnp, inp)):
        ref[...] = init[...]
    both = slot_ref[0].astype(F32)
    for i in range(1, slot_ref.shape[0]):
        both = both + slot_ref[i].astype(F32)
    z0 = jnp.zeros((FP - FS, 2 * D), F32)
    live = lax.broadcasted_iota(jnp.int32, (1, FP), 1) < F
    back = []
    for c in range(SL // 2):
        t = jnp.where(live, jnp.concatenate([both[c], z0], 0).T, 0.0)
        back += [t[0:D], t[D : 2 * D]]
    pair, sums = backward_rows(
        x_ref, n_ref, qkv_ref, p_ref, l_ref, of_ref, wqkvI_ref, wo_ref, vec_ref, cg_ref, xs, os, dqs, das, dqkv, dwo, dnp,
        lambda r: back[r], base_ref,
    )
    weave([(pair(c), 0, 1) for c in range(SL // 2)])
    for _ in sums(slice(0, SL * FP)):
        pass
    zc = jnp.zeros((D, DP - D), F32)
    three = [jnp.concatenate([dqkv[i * D : (i + 1) * D], zc], 1).T for i in range(3)]
    pack_pair(pack_ref, 0, three[0], three[1])
    pack_pair(pack_ref, PAIR, three[2], dwo)
    pack_norms(pack_ref, 2 * PAIR, [dnp[0], dnp[1]])
    hand_out(table_ref, pack_ref, piece_refs)


def slots_backward(table, x, saved, slots, prev, wqkvI, wo, vec, packed, tables):
    SL = 2 * slots.shape[1]
    nat = lambda a: pl.BlockSpec((SL,) + a.shape[1:], lambda i: (i, 0, 0))
    cg, *accs = prev
    flat = list(accs) + [wqkvI, wo, vec]
    pieces = [shape((packed // tables, 128))] * tables
    M = SL * FP
    ins = [table, x, *saved, slots, cg, *flat]
    return pl.pallas_call(
        functools.partial(slots_back_kernel, SL, tables),
        grid=(1,),
        in_specs=[pl.BlockSpec(memory_space=pltpu.SMEM), nat(x)]
        + [nat(a) for a in saved]
        + [whole(slots), nat(cg)]
        + [whole(a) for a in flat],
        out_specs=[nat(cg)] + [whole(a) for a in pieces],
        out_shape=[shape(cg.shape, F32)] + pieces,
        input_output_aliases={len(saved) + 3: 0},
        scratch_shapes=[pltpu.VMEM((packed, 128), F32)]
        + [pltpu.VMEM(a, BF) for a in ((D, M), (D, M), (3 * D, M), (D, M))]
        + [pltpu.VMEM(a.shape, F32) for a in accs],
        compiler_params=params(),
        cost_estimate=cost(8),
        name="slots_backward",
    )(*ins)


def table_sums(tables, pieces):
    sent = []
    for i, a in enumerate(pieces):
        to = [(t, (t // 2 + i // 2) % (tables // 2) * 2 + (t + i) % 2) for t in range(tables)]
        sent.append(lax.ppermute(a, "table", to) if i else a)
    return sent


def join_kernel(tables, *refs):
    out_ref = refs[-1]
    at = 0
    for group in (refs[:tables], refs[tables : 2 * tables]):
        total = group[0][...].astype(F32)
        for ref in group[1:]:
            total = total + ref[...].astype(F32)
        rows = total.shape[0] // out_ref.shape[0]
        for i in range(out_ref.shape[0]):
            out_ref[i, at : at + rows] = total[i * rows : (i + 1) * rows].astype(BF)
        at += rows


def join_tables(shards, mids, tails):
    rows = (mids[0].shape[0] + tails[0].shape[0]) // shards
    return pl.pallas_call(
        functools.partial(join_kernel, len(mids)),
        out_shape=shape((shards, rows, 128)),
        compiler_params=params(),
        cost_estimate=cost(2),
        name="join_tables",
    )(*mids, *tails)


def sum_kernel(parts_ref, out_ref):
    total = parts_ref[0].astype(F32)
    for i in range(1, parts_ref.shape[0]):
        total = total + parts_ref[i].astype(F32)
    total = total.astype(BF)
    for i in range(out_ref.shape[0]):
        out_ref[i] = total


def sum_rows(parts):
    parts = lax.all_to_all(parts, "rows", 0, 0)
    return pl.pallas_call(
        sum_kernel,
        out_shape=shape(parts.shape),
        compiler_params=params(),
        cost_estimate=cost(2),
        name="sum_rows",
    )(parts)


def gather_all(copies):
    tables = lax.axis_size("table")
    ny = tables // 2
    own = lax.all_to_all(copies, "rows", 0, 0)
    pieces = [own]
    for s in range(1, ny):
        pieces.append(lax.ppermute(own, "table", [(t, (t // 2 + s) % ny * 2 + t % 2) for t in range(tables)]))
    other = [lax.ppermute(a, "table", [(t, t ^ 1) for t in range(tables)]) for a in pieces]
    return [a for pair in zip(pieces, other) for a in pair]


def to_row(c):
    return jnp.broadcast_to(c, (c.shape[0], 128)).T[0:1]


def to_col(r):
    return jnp.broadcast_to(r, (128, r.shape[1])).T[:, 0:1]


def clipped(update, weight, count):
    def total(v):
        return jnp.sum(jnp.sum(v, 0, keepdims=True), 1, keepdims=True)

    rms = jnp.sqrt(total(update * update) * (1.0 / count))
    weight_rms = jnp.sqrt(total(weight * weight) * (1.0 / count))
    return update * (RATE * jnp.maximum(0.001, weight_rms) / jnp.maximum(1.0, rms / CLIP))


def optimizer_kernel(
    tables, mid_rows, *refs):
    table_ref, *refs = refs
    piece_refs, refs = refs[:tables], refs[tables:]
    mid_ref, tail_ref = refs[-2:]
    table = table_ref[0]
    ny = tables // 2
    for i, ref in enumerate(piece_refs):
        place = pair_up(table, i, ny, True)
        for out, at, end in ((mid_ref, 0, mid_rows), (tail_ref, mid_rows, ref.shape[1])):
            rows = ref.shape[0] * (end - at)
            start = pl.multiple_of(place * rows, 8)
            out[pl.ds(start, rows)] = ref[:, at:end, :].astype(F32).reshape(rows, 128)
    optimizer_steps(*refs)


def optimizer_steps(
    proj_ref, outw_ref, in_ref, hid_ref, norm_ref, sr_ref, sc_ref, mm_ref, mh_ref, ns_ref,
    proj_g, out_g, in_g, hid_g, norm_g, proj_n, out_n, in_n, hid_n, norm_n, sr_n, sc_n, mm_n, mh_n, ns_n, mid_ref, tail_ref,
):
    decay = 1.0 - STEP ** (-0.8)

    def stats(grad, col_old, row_old):
        square = grad * grad + 1e-30
        a, b = grad.shape
        over_sub = decay * row_old + (1.0 - decay) * (jnp.sum(square, 0, keepdims=True) * (1.0 / a))
        over_lane = decay * col_old + (1.0 - decay) * (jnp.sum(square, 1, keepdims=True) * (1.0 / b))
        return over_lane, over_sub

    def scaled(grad, col, row, mean):
        return grad * lax.rsqrt(col * (1.0 / mean)) * lax.rsqrt(row)

    def square_pair(ref, at):
        both = ref[at + 2 * D : at + 3 * D].astype(F32)
        a = jnp.concatenate([ref[at : at + D].astype(F32), both[:, 0:64]], 1)
        b = jnp.concatenate([ref[at + D : at + 2 * D].astype(F32), both[:, 64:128]], 1)
        return a, b

    wq, wk = square_pair(tail_ref, 0)
    wv, wo = square_pair(tail_ref, PAIR)
    wq2, wo2 = square_pair(mid_ref, 12 * D)
    wk2, wv2 = square_pair(mid_ref, 12 * D + PAIR)
    for i, grad in enumerate((wq, wk, wv, wq2, wk2, wv2, wo, wo2)):
        g_ref, n_ref, w_ref, j = (proj_g, proj_n, proj_ref, i) if i < 6 else (out_g, out_n, outw_ref, i - 6)
        g_ref[j] = grad
        col, row = stats(grad, to_col(sr_ref[i : i + 1, :]), sc_ref[i : i + 1, :])
        sr_n[i : i + 1, :] = to_row(col)
        sc_n[i : i + 1, :] = row
        mean = jnp.sum(col, 0, keepdims=True) * (1.0 / D)
        w = w_ref[j]
        n_ref[j] = w - clipped(scaled(grad, col, row, mean), w, D * D)

    def wide(at):
        return jnp.concatenate([mid_ref[at + D * j : at + D * j + D].astype(F32) for j in range(6)], 1)

    grad = wide(0)
    in_g[...] = grad
    col, row = stats(grad, to_col(mm_ref[0:1, :]), mh_ref[0:1, :])
    mm_n[0:1, :] = to_row(col)
    mh_n[0:1, :] = row
    mean = jnp.sum(col, 0, keepdims=True) * (1.0 / D)
    w = in_ref[...]
    in_n[...] = w - clipped(scaled(grad, col, row, mean), w, D * FF)
    grad = wide(6 * D)
    hid_g[...] = grad
    col, row = stats(grad, to_col(mm_ref[1:2, :]), mh_ref[1:2, :])
    mm_n[1:2, :] = to_row(col)
    mh_n[1:2, :] = row
    mean = jnp.sum(row, 1, keepdims=True) * (1.0 / FF)
    w = hid_ref[...]
    update = grad * lax.rsqrt(col) * lax.rsqrt(row * (1.0 / mean))
    hid_n[...] = w - clipped(update, w, D * FF)

    pieces = []
    for ref, at, count in ((tail_ref, 2 * PAIR, 2), (mid_ref, 12 * D + 2 * PAIR, 4)):
        v = ref[at : at + 16].astype(F32)
        for i in range(count):
            pieces.append(jnp.concatenate([v[2 * i : 2 * i + 1], v[2 * i + 1 : 2 * i + 2, 0:64]], 1))
    grad = jnp.concatenate(pieces, 0)
    norm_g[...] = grad
    second = decay * ns_ref[...] + (1.0 - decay) * (grad * grad + 1e-30)
    ns_n[...] = second
    update = grad * lax.rsqrt(second)
    rms = jnp.sqrt(jnp.sum(update * update, 1, keepdims=True) * (1.0 / D))
    w = norm_ref[...]
    w_rms = jnp.sqrt(jnp.sum(w * w, 1, keepdims=True) * (1.0 / D))
    norm_n[...] = w - update * (RATE * jnp.maximum(0.001, w_rms) / jnp.maximum(1.0, rms / CLIP))


def optimizer(table, pieces, mid_rows, *state):
    proj, outw, w_in, w_outT, norms, sr, sc, ms, hs, ns = state
    shards, rows, _ = pieces[0].shape
    order = [proj, outw, w_in, w_outT, norms, proj, outw, w_in, w_outT, norms, sr, sc, ms, hs, ns]
    outs = pl.pallas_call(
        functools.partial(optimizer_kernel, len(pieces), mid_rows),
        in_specs=[pl.BlockSpec(memory_space=pltpu.SMEM)] + [whole(a) for a in (*pieces, *state)],
        out_shape=[shape(a.shape, F32) for a in order],
        scratch_shapes=[
            pltpu.VMEM((len(pieces) * shards * mid_rows, 128), F32),
            pltpu.VMEM((len(pieces) * shards * (rows - mid_rows), 128), F32),
        ],
        compiler_params=params(),
        cost_estimate=cost(8), name="optimizer",
    )(table, *pieces, *state)
    outs = list(outs)
    for i in (3, 8):
        outs[i] = outs[i].T
    return outs


def on_device(n, cells, cotangent, train_count, key_mask, train_order, *state):
    state = list(state)
    state[3] = state[3].T
    proj, outw, w_in, w_outT, norms = state[:5]
    x = jnp.swapaxes(cells[0], 1, 2)
    cot = jnp.swapaxes(cotangent[0], 1, 2)
    rows_here = x.shape[0]
    unit = 8 * n
    tail_rows = -(-TAIL // unit) * unit
    mid_rows = -(-MID // unit) * unit
    perm = perm_matrix()
    shards, tables = lax.axis_size("rows"), lax.axis_size("table")
    table = lax.axis_index("table").astype(jnp.int32).reshape(1)
    wqkvT, woT, vec = first_weights(proj, outw, norms)
    own = slot_rows(shards, train_count, key_mask, train_order, x, wqkvT, woT, vec)
    slots = lax.all_to_all(own, "rows", 0, 0).reshape((-1,) + own.shape[2:])
    w_in, _ = lax.optimization_barrier((w_in, own))
    wqkvI, wo, *ws = other_weights(proj, outw, w_in, w_outT)
    ht, ct, *saved = feature_forward(x, cot, (wqkvT, woT, vec, perm))
    wkv2, wkv2T, *ws = ws
    yt, g1t, back, *mids = item_and_dense(table, ht, ct, slots, perm, (*ws, wkv2, wkv2T), vec, mid_rows, tables)
    back = lax.all_to_all(back.reshape(own.shape), "rows", 0, 0)
    mids = table_sums(tables, mids)
    cg, y, *accs = feature_backward(x, saved, g1t, yt, wqkvI, wo, vec, perm)
    mids, accs = lax.optimization_barrier((mids, accs))
    cg, *tails = slots_backward(table, x, saved, back, (cg, *accs), wqkvI, wo, vec, tail_rows, tables)
    tails = table_sums(tables, tails)
    pieces = gather_all(sum_rows(join_tables(shards, mids, tails)))
    return (jnp.swapaxes(y, 1, 2)[None], jnp.swapaxes(cg, 1, 2)[None], *optimizer(table, pieces, mid_rows // n, *state))


def solution(mesh):
    n = int(mesh.shape["table"] * mesh.shape["rows"])
    cells = P("table", "rows", None, None)
    return jax.shard_map(
        functools.partial(on_device, n),
        mesh=mesh,
        in_specs=(cells, cells, P("table"), P("table", "rows"), P("table", "rows")) + (P(),) * 10,
        out_specs=(cells, cells) + (P(),) * 15,
        check_vma=False,
    )
```

```python
import functools

import jax
import jax.numpy as jnp
import numpy as np
from jax import lax
from jax.experimental import pallas as pl
from jax.experimental.pallas import tpu as pltpu
from jax.sharding import PartitionSpec as P

BF, F32 = jnp.bfloat16, jnp.float32
D, DP = 192, 256
H, E = 6, 32
F, FP = 119, 128
FS = 120
FF = 768
STEP = 3
CLIP = 0.3
RATE = 0.5
FB = 8
SCALE = E**-0.5
SCALE2 = SCALE * 1.4426950408889634
C0 = 0.7978845608028654
C1 = 0.044715
NT = (((1,), (1,)), ((), ()))
TN = (((0,), (0,)), ((), ()))
PAIR = 576
TAIL = 2 * PAIR + 8
MID = 2 * 6 * D + 2 * PAIR + 8


def mm(a, b):
    return jnp.dot(a, b, preferred_element_type=F32)


def mm_nt(a, b):
    return lax.dot_general(a, b, NT, preferred_element_type=F32)


def mm_tn(a, b):
    return lax.dot_general(a, b, TN, preferred_element_type=F32)


def lanes():
    return lax.broadcasted_iota(jnp.int32, (1, DP), 1)


def whole(a):
    nd = len(a.shape)
    return pl.BlockSpec(a.shape, lambda *i: (0,) * nd)


def half_masks():
    lane = lax.broadcasted_iota(jnp.int32, (1, 128), 1)
    return [jnp.where((lane >= E * h) & (lane < E * (h + 1)), 1.0, 0.0).astype(BF) for h in range(4)]


def spread_halves(w, masks):
    z = jnp.zeros((w.shape[0], 128), BF)
    lo, hi = w[:, 0:128], w[:, 128:256]
    return jnp.concatenate(
        [jnp.concatenate([lo * masks[h], z], 1) for h in range(4)]
        + [jnp.concatenate([z, hi * masks[h]], 1) for h in range(2)], 0)


def mean0(a): return jnp.sum(a, 0, keepdims=True) * (1.0 / D)


def norm_t(a):
    c = a - mean0(a)
    rc = lax.rsqrt(mean0(c * c) + 1e-5)
    return c * rc, rc


def norm_back_t(g, n, rc, gain):
    dn = g * gain
    return (dn - mean0(dn) - n * mean0(dn * n)) * rc


def tall(a):
    return jnp.concatenate([a, jnp.zeros((DP - D, a.shape[1]), a.dtype)], 0)


def gelu_parts(u):
    uu = u * u
    th = jnp.tanh(u * (BF(C0) + BF(C0 * C1) * uu))
    half = BF(0.5) + BF(0.5) * th
    act = u * half
    slope = half + act * (BF(1.0) - th) * (BF(C0) + BF(3.0 * C0 * C1) * uu)
    return act, slope


def weave(streams):
    live=[[g,s,p] for g,s,p in streams]
    turn=0
    while live:
        for it in list(live):
            if turn>=it[1]:
                for _ in range(it[2]):
                    try: next(it[0])
                    except StopIteration:
                        live.remove(it); break
        turn+=1

def shape(s, t=BF):
    return jax.ShapeDtypeStruct(s, t)


def params(mib=58):
    return pltpu.CompilerParams(vmem_limit_bytes=mib << 20)


def cost(us):
    return pl.CostEstimate(flops=int(us * 1.1e9), bytes_accessed=int(us * 1e6), transcendentals=0)


def perm_matrix():
    place = np.zeros((256, 256), np.float32)
    for f in range(16):
        for r in range(16):
            place[f * 16 + r, r * 16 + f] = 1
    return jnp.asarray(place, BF)


def padded_square(w):
    a = jnp.concatenate([w, jnp.zeros((D, DP - D), F32)], 1).astype(BF)
    a = jnp.concatenate([a, jnp.zeros((DP - D, DP), BF)], 0)
    return a, a.T


def first_weights(proj, outw, norms, wqkvT, woT, vec, nrow):
    for i in range(3):
        wqkvT[i * D : (i + 1) * D, :] = padded_square(proj[i])[1][0:D]
    woT[...] = padded_square(outw[0])[1][0:D]
    nrow[...] = jnp.zeros((8, DP), F32)
    nrow[0:6, 0:D] = norms[...]
    for i in range(6):
        vec[i] = jnp.broadcast_to(nrow[i : i + 1, :], (128, DP)).T[0:D]


def weights_kernel(proj, outw, w_in, w_outT, wqkvI, wo, wkv2, wkv2T, wq2, wq2T, wo2I, wo2, w1T, w1, w2T, w2):
    row = lax.broadcasted_iota(jnp.int32, (D, DP), 0)
    eye = jnp.where(row == lax.broadcasted_iota(jnp.int32, (D, DP), 1), 1.0, 0.0).astype(BF)
    wqkvI[...] = jnp.concatenate([proj[0], proj[1], proj[2], eye[:, 0:D].astype(F32)], 1).astype(BF)
    wo[...] = jnp.concatenate([outw[0], jnp.zeros((D, DP - D), F32)], 1).astype(BF)
    a, t = padded_square(proj[3])
    wq2[...] = a
    wq2T[...] = t
    a, t = padded_square(outw[1])
    wo2[...] = a[0:D]
    wo2I[:, 0:DP] = t[0:D]
    wo2I[:, DP : 2 * DP] = eye
    for i in range(2):
        a, t = padded_square(proj[4 + i])
        wkv2[:, i * DP : (i + 1) * DP] = a
        wkv2T[i * DP : (i + 1) * DP, :] = t
    zw = jnp.zeros((DP - D, FF), BF)
    a = w_in[...].astype(BF)
    w1[...] = a
    w1T[...] = jnp.concatenate([a, zw], 0).T
    a = w_outT[...].astype(BF)
    w2T[...] = a
    w2[...] = jnp.concatenate([a, zw], 0).T


def other_weights(proj, outw, w_in, w_outT):
    sq, half = shape((DP, DP)), shape((D, DP))
    outs = [shape((D, 4 * D)), half, shape((DP, 2 * DP)), shape((2 * DP, DP)), sq, sq]
    outs += [shape((D, 2 * DP)), half, shape((FF, DP)), shape((D, FF)), shape((D, FF)), shape((FF, DP))]
    return pl.pallas_call(
        weights_kernel,
        out_shape=outs,
        compiler_params=params(),
        cost_estimate=cost(4),
        name="other_weights",
    )(proj, outw, w_in, w_outT)


def two_heads(a, b):
    z = jnp.zeros(a.shape, a.dtype)
    return jnp.concatenate([jnp.concatenate([a, z], 1), jnp.concatenate([z, b], 1)], 0)


def feature_pair(x, wqkvT_ref, woT_ref, keep, out):
    qkv = mm(wqkvT_ref[...], x)
    q = (qkv[0:D] * SCALE2).astype(BF)
    k = qkv[D : 2 * D].astype(BF)
    v = qkv[2 * D : 3 * D].astype(BF)
    yield
    row = lax.broadcasted_iota(jnp.int32, (8, 1), 0)
    outs = []
    for u in range(2):
        own = slice(u * FP, (u + 1) * FP)
        keep("qkv", u, (q[:, own], k[:, own], v[:, own]))
        ot = []
        for j in range(H // 2):
            hs = slice(64 * j, 64 * j + 64)
            qm = two_heads(q[64 * j : 64 * j + 32, own], q[64 * j + 32 : 64 * j + 64, own])
            st = mm(k[hs, own].T, qm)
            yield
            last = jnp.where(row < F - FS + 8, st[FS - 8 : FS], -1e30)
            mx = jnp.maximum(jnp.max(st[0 : FS - 8], 0, keepdims=True), jnp.max(last, 0, keepdims=True))
            e = jnp.exp2(st[0 : FS - 8] - mx)
            last = jnp.exp2(last - mx)
            inv = 1.0 / (jnp.sum(e, 0, keepdims=True) + jnp.sum(last, 0, keepdims=True))
            e = jnp.concatenate([e, last, jnp.zeros((FP - FS, 2 * FP), F32)], 0).astype(BF)
            keep("p", (u, j), (e, inv))
            yield
            t = mm(v[hs, own], e)
            ot.append(t[0:32, 0:128] * inv[:, 0:128])
            ot.append(t[32:64, 128:256] * inv[:, 128:256])
            yield
        ot = jnp.concatenate(ot, 0).astype(BF)
        keep("o", u, ot)
        outs.append(ot)
    a = mm(woT_ref[...], tall(jnp.concatenate(outs, 1)))
    yield
    for u in range(2):
        own = slice(u * FP, (u + 1) * FP)
        out.append(norm_t(x[0:D, own].astype(F32) + a[:, own]))
        yield


def slots_kernel(
    SL, count_ref, mask_ref, order_ref, x_ref, proj_ref, outw_ref, norm_ref, out_ref, wqkvT_ref, woT_ref, vec_ref, xs, nrow
):
    xs[...] = jnp.zeros_like(xs)
    first_weights(proj_ref, outw_ref, norm_ref, wqkvT_ref, woT_ref, vec_ref, nrow)
    row = lax.broadcasted_iota(jnp.int32, (FS, 1), 0)
    lane = lax.broadcasted_iota(jnp.int32, (1, 2 * D), 1)

    def flag(r):
        order = order_ref[0, r]
        usable = (order < count_ref[0]) & ((mask_ref[0, r] == 1) | (order == 0))
        return jnp.where(usable, 1.0, 0.0)

    def pair(c):
        for u in range(2):
            xs[c, 0:D, u * FP : u * FP + F] = x_ref[2 * c + u]
        out = []
        yield from feature_pair(xs[c], wqkvT_ref, woT_ref, lambda *a: None, out)
        both = jnp.concatenate([(n * vec_ref[0] + vec_ref[1]).astype(BF) for n, _ in out], 0)
        flags = jnp.where(lane < D, flag(2 * c), flag(2 * c + 1))
        both = jnp.where(row < F, both.T[0:FS].astype(F32), flags).astype(BF)
        for i in range(out_ref.shape[0]):
            out_ref[i, c] = both
        yield

    weave([(pair(c), 0, 1) for c in range(SL // 2)])


def slot_rows(shards, count, mask, order, cells, proj, outw, norms):
    SL = mask.shape[1]
    smem = pl.BlockSpec(memory_space=pltpu.SMEM)
    part = lambda a, k: pl.BlockSpec((k,) + a.shape[1:], lambda i: (0, 0, 0))
    outs = [shape((shards, SL // 2, FS, 2 * D)), shape((3 * D, DP)), shape((D, DP)), shape((6, D, 128), F32)]
    return pl.pallas_call(
        functools.partial(slots_kernel, SL),
        grid=(1,),
        in_specs=[smem, smem, smem, part(cells, SL), part(proj, 3), part(outw, 1), whole(norms)],
        out_specs=[whole(a) for a in outs],
        out_shape=outs,
        scratch_shapes=[pltpu.VMEM((SL // 2, DP, 2 * FP), BF), pltpu.VMEM((8, DP), F32)],
        compiler_params=params(),
        cost_estimate=cost(6),
        name="slot_rows",
    )(count, mask, order, cells, proj, outw, norms)


def turn_block(perm_ref, block, R):
    return mm(perm_ref[...], block.reshape(256, block.shape[-1])).astype(BF).reshape(16, R, block.shape[-1])


def forward_kernel(
    R, OFF, x_ref, c_ref, wqkvT_ref, woT_ref, vec_ref, perm_ref, wq_ref, ht_ref, ct_ref, qt_ref, n_ref, qkv_ref, p_ref, l_ref, of_ref, xs, hs, cp, cs
):
    @pl.when(pl.program_id(0) == 0)
    def _():
        xs[...] = jnp.zeros_like(xs)
        cp[...] = jnp.zeros_like(cp)

    def pair(c):
        for u in range(2):
            xs[c, 0:D, u * FP : u * FP + F] = x_ref[2 * c + u]

        def keep(what, at, val):
            if what == "qkv":
                for i in range(3):
                    qkv_ref[2 * c + at, i * D : (i + 1) * D, :] = val[i]
            elif what == "p":
                u, j = at
                p_ref[2 * c + u, :, 256 * j : 256 * j + 256] = val[0]
                l_ref[2 * c + u, j : j + 1, :] = val[1]
            else:
                of_ref[2 * c + at] = val

        out = []
        yield from feature_pair(xs[c], wqkvT_ref, woT_ref, keep, out)
        for u in range(2):
            r = 2 * c + u
            n, rc = out[u]
            n_ref[r, 0:D, :] = n.astype(BF)
            n_ref[r, D : D + 16, :] = jnp.broadcast_to(rc, (16, FP)).astype(BF)
            h = tall((n * vec_ref[0] + vec_ref[1]).astype(BF))
            hs[r] = h.T
            yield

    def cotangents():
        for r in range(R):
            cp[r % 4, 0:D, 0:F] = c_ref[r]
            cs[r] = cp[r % 4].T
            yield
        for j in range(FP // 16):
            ct_ref[16 * j : 16 * j + 16] = turn_block(perm_ref, cs[:, 16 * j : 16 * j + 16, :], R)
            yield

    weave([(pair(c), c * OFF, 1) for c in range(R // 2)] + [(cotangents(), 4, 1)])
    for j in range(FP // 16):
        block = turn_block(perm_ref, hs[:, 16 * j : 16 * j + 16, :], R)
        ht_ref[16 * j : 16 * j + 16] = block
        q = (mm(block.reshape(16 * R, DP), wq_ref[...]) * SCALE2).astype(BF)
        qt_ref[16 * j : 16 * j + 16] = q.reshape(16, R, DP)


def feature_forward(cells, cot, ws, R=16, OFF=2):
    rows = cells.shape[0]
    nat = lambda a, b: pl.BlockSpec((R, a, b), lambda i: (i, 0, 0))
    turned = pl.BlockSpec((FP, R, DP), lambda i: (0, i, 0))
    sizes = [(D + 16, FP), (3 * D, FP), (FP, H * FP), (8, 2 * FP), (D, FP)]
    kinds = [BF, BF, BF, F32, BF]
    return pl.pallas_call(
        functools.partial(forward_kernel, R, OFF),
        grid=(rows // R,),
        in_specs=[nat(D, F), nat(D, F)] + [whole(a) for a in ws],
        out_specs=[turned] * 3 + [nat(*a) for a in sizes],
        out_shape=[shape((FP, rows, DP))] * 3 + [shape((rows,) + a, t) for a, t in zip(sizes, kinds)],
        scratch_shapes=[
            pltpu.VMEM((R // 2, DP, 2 * FP), BF),
            pltpu.VMEM((R, FP, DP), BF),
            pltpu.VMEM((4, DP, FP), BF),
            pltpu.VMEM((R, FP, DP), BF),
        ],
        compiler_params=params(),
        cost_estimate=cost(9 * rows // R),
        name="feature_forward",
    )(cells, cot, *ws)


def pair_up(table, i, ny, back=False):
    shift = ny - i // 2 if back else i // 2
    return lax.rem(table // 2 + shift, ny) * 2 + lax.rem(table + i % 2, 2)


def hand_out(table_ref, pack, piece_refs):
    tables = len(piece_refs)
    rows = pack.shape[0] // tables
    for i, ref in enumerate(piece_refs):
        place = pair_up(table_ref[0], i, tables // 2)
        ref[...] = pack[pl.ds(pl.multiple_of(place * rows, 8), rows)].astype(BF)


def pack_pair(ref, at, a, b):
    ref[at : at + D] = a[0:D, 0:128]
    ref[at + D : at + 2 * D] = b[0:D, 0:128]
    ref[at + 2 * D : at + 3 * D] = jnp.concatenate([a[0:D, 128:D], b[0:D, 128:D]], 1)


def pack_norms(ref, at, sums):
    rows = []
    for s in sums:
        if s.shape[0] == D:
            s = jnp.concatenate([s, jnp.zeros((DP - D, 128), F32)], 0).T
        v = jnp.sum(s, 0, keepdims=True)
        rows += [v[:, 0:128], v[:, 128:256]]
    rows.append(jnp.zeros((ref.shape[0] - at - len(rows), 128), F32))
    ref[at:] = jnp.concatenate(rows, 0)


def item_kernel(
    RW, keys, tables, OFF, AO, AS, WP, CC, WC, table_ref, ht_ref, next_ref, q_ref, qnext_ref, ct_ref, slot_ref, perm_ref, wqT_ref, woI_ref, wo_ref, w1T_ref, w1_ref, w2T_ref, w2_ref,
    wkv_ref, wkvT_ref, vec_ref, y_ref, g1_ref, back_ref, *rest
):
    piece_refs, rest = rest[:tables], rest[tables:]
    (dwq, dwo, dw1, dw2, dnp, dwkv, bias_ref, pack_ref, hk_ref, bk_ref,
     dks, dvs, hbTs, ois, hb2Ts, actss, dbTs, duss, dabTs, dqss, pbss, kvss, slp) = rest
    step = pl.program_id(0)
    blocks = [(s, b, min(16, FS - b)) for s in range(0, keys, 16) for b in range(0, FS, 16)]

    @pl.when(step == 0)
    def _():
        for ref in (dwq, dwo, dw1, dw2, dnp, dwkv):
            ref[...] = jnp.zeros_like(ref)
        for ref in (hb2Ts, actss, dbTs, duss, dabTs, dqss, dks, dvs):
            ref[1] = jnp.zeros_like(ref[1])
        for ref in (hbTs, ois):
            ref[2] = jnp.zeros_like(ref[2])
        hk_ref[:, :, D:DP] = jnp.zeros((FS, keys, DP - D), BF)
        for s, b, n in blocks:
            own = slot_ref[s // 2 : s // 2 + 8, b : b + n, :]
            own = jnp.concatenate([own[:, :, 0:D], own[:, :, D : 2 * D]], 0)
            if n < 16:
                own = jnp.concatenate([own, jnp.zeros((16, 16 - n, D), BF)], 1)
            hk_ref[b : b + n, s : s + 16, 0:D] = turn_block(perm_ref, own, 16)[0:n]
        for s in range(0, keys, 16):
            flag = slot_ref[s // 2 : s // 2 + 8, F, :].astype(F32)
            for i, at in enumerate((0, DP)):
                bias_ref[s + 8 * i : s + 8 * i + 8] = jnp.where(flag[:, at : at + 128] > 0.5, 0.0, -1e30)

    masks = half_masks()
    LW = 2 * RW
    left = lax.broadcasted_iota(jnp.int32, (1, LW), 1) < RW
    HK = H * keys
    cur, prev = lax.rem(step, 2), lax.rem(step + 1, 2)
    cur3, next3, prev3 = [lax.rem(step + i, 3) for i in range(3)]
    hb2T, acts, dbT, dus, dabT, dqs = [r.at[cur] for r in (hb2Ts, actss, dbTs, duss, dabTs, dqss)]

    def step_rows(at):
        return hk_ref[pl.ds(pl.multiple_of(at * FB, FB), FB)].reshape(FB * keys, DP)

    def keys_values(at, to):
        kvss[to] = mm(step_rows(at), wkv_ref[...]).astype(BF)

    def spreads(to, j, first):
        return [
            spread_halves(kvss[to, (2 * j + c) * keys : (2 * j + c + 1) * keys, first : first + DP], masks)
            for c in range(2)
        ]

    def attend(j, ref, qref, to, to3):
        h = ref[2 * j : 2 * j + 2].reshape(LW, DP)
        q = qref[2 * j : 2 * j + 2].reshape(LW, DP)
        ks = spreads(to, j, 0)
        hbTs[to3, :, j * LW : (j + 1) * LW] = h.T[0:D]
        yield
        st = jnp.where(left, mm_nt(ks[0], q), mm_nt(ks[1], q))
        yield
        vs = spreads(to, j, DP)
        pbs = []
        for hh in range(H):
            s = st[hh * keys : (hh + 1) * keys] + bias_ref[...]
            e = jnp.exp2(s - jnp.max(s, 0, keepdims=True))
            pbs.append((e * (1.0 / jnp.sum(e, 0, keepdims=True))).astype(BF))
            if hh % 2:
                yield
        pb = jnp.concatenate(pbs, 0)
        pbss[to, j] = pb
        pt = pb.T
        yield
        o = jnp.concatenate([mm(pt[:RW], vs[0]), mm(pt[RW:], vs[1])], 0).astype(BF)
        ois[to3, j * LW : (j + 1) * LW] = o
        yield

    @pl.when(step == 0)
    def _():
        keys_values(0, 0)
        weave([(attend(j, ht_ref, q_ref, 0, 0), 0, 1) for j in range(FB // 2)])

    def dense(i, out):
        c0 = i * 2 * LW
        g1v, b1v, g2v, b2v = [vec_ref[i] for i in range(2, 6)]
        h = ht_ref[4 * i:4 * i + 4].reshape(2 * LW, DP)
        o = ois[cur3, c0 : c0 + 2 * LW]
        aT = mm_nt(woI_ref[...], jnp.concatenate([o, h], 1))
        yield
        n2, rc2, h2, hb2 = [], [], [], []
        for t in range(2):
            n, rc = norm_t(aT[:, t * LW:(t + 1) * LW])
            hh = n * g1v + b1v
            n2.append(n.astype(BF)); rc2.append(rc); hb2.append(hh.astype(BF))
            yield
        hb2 = jnp.concatenate(hb2, 1)
        hb2T[:, c0:c0 + 2 * LW] = hb2
        hb2 = tall(hb2)
        C = CC
        u = mm(w1T_ref[0:C], hb2)
        for c in range(FF // C):
            un = mm(w1T_ref[C * c + C:C * c + 2 * C], hb2) if c + 1 < FF // C else None
            act, slope = gelu_parts(u.astype(BF))
            acts[C * c:C * c + C, c0:c0 + 2 * LW] = act
            slp[C * c:C * c + C, c0:c0 + 2 * LW] = slope
            u = un
            yield
        gT = ct_ref[4 * i:4 * i + 4].reshape(2 * LW, DP).T[0:D].astype(F32)
        z = mm(w2T_ref[...], acts[:, c0:c0 + 2 * LW])
        yield
        dbs, d3s = [], []
        ys = []
        for t in range(2):
            sl = slice(t * LW, (t + 1) * LW)
            n3, rc3 = norm_t(hb2[0:D, sl].astype(F32) + z[:, sl])
            ys.append((n3 * g2v + b2v).astype(BF))
            yield
            g = gT[:, sl]
            dnp[2] += g * n3
            dnp[3] += g
            d3 = norm_back_t(g, n3, rc3, g2v)
            dbs.append(d3.astype(BF))
            yield
        db = jnp.concatenate(dbs, 1)
        dbT[:, c0:c0 + 2 * LW] = db
        db = tall(db)
        w = mm(w2_ref[0:C], db)
        for c in range(FF // C):
            wn = mm(w2_ref[C * c + C:C * c + 2 * C], db) if c + 1 < FF // C else None
            dus[C * c:C * c + C, c0:c0 + 2 * LW] = w.astype(BF) * slp[C * c:C * c + C, c0:c0 + 2 * LW]
            w = wn
            yield
        dh = mm(w1_ref[...], dus[:, c0:c0 + 2 * LW])
        yT = tall(jnp.concatenate(ys, 1))
        y_ref[4 * i:4 * i + 4] = yT.T.reshape(4, RW, DP)
        yield
        dabs = []
        for t in range(2):
            dh2 = dbs[t].astype(F32) + dh[:, t * LW:(t + 1) * LW]
            n2f = n2[t].astype(F32)
            dnp[0] += dh2 * n2f
            dnp[1] += dh2
            dabs.append(norm_back_t(dh2, n2f, rc2[t], g1v).astype(BF))
            yield
        dab = jnp.concatenate(dabs, 1)
        dabT[:, c0:c0 + 2 * LW] = dab
        doT = mm(wo_ref[...], tall(dab)).astype(BF)
        out.extend([dab, doT])
        yield
    def back(j, doT, out):
        q, pb = q_ref[2 * j : 2 * j + 2].reshape(LW, DP), pbss[cur, j]
        ks, vs = spreads(cur, j, 0), spreads(cur, j, DP)
        do = tall(doT)
        don = do.T
        dp = jnp.where(left, mm(vs[0], do), mm(vs[1], do))
        yield
        slot_sums(dvs, j, pb, don, None)
        yield
        dss = []
        for hh in range(H):
            sl = slice(hh * keys, (hh + 1) * keys)
            p, d = pb[sl].astype(F32), dp[sl]
            dss.append((p * (d - jnp.sum(p * d, 0, keepdims=True))).astype(BF))
            if hh % 2: yield
        ds = jnp.concatenate(dss, 0)
        dst = ds.T
        yield
        slot_sums(dks, j, ds, q, 0.6931471805599453)
        yield
        dq = jnp.concatenate([mm(dst[:RW], ks[0]), mm(dst[RW:], ks[1])], 0) * SCALE
        dq = dq.astype(BF)
        dqs[j * LW:(j + 1) * LW] = dq
        out.append(dq)
        yield
    lane = lax.broadcasted_iota(jnp.int32, (1, 128), 1)
    zq = jnp.zeros((RW, 128), BF)
    def slot_sums(ref, j, w, rows, scale):
        out = [[], []]
        for t, heads in ((0, 4), (1, 2)):
            r = rows[:, 128 * t:128 * t + 128]
            both = jnp.concatenate([jnp.concatenate([r[:RW], zq], 0), jnp.concatenate([zq, r[RW:]], 0)], 1)
            full = mm(w[4 * t * keys:(4 * t + heads) * keys], both)
            for c in range(2):
                col = full[:, 128 * c:128 * c + 128]
                v = col[0:keys]
                for hh in range(1, heads):
                    v = jnp.where(lane >= E * hh, col[hh * keys:(hh + 1) * keys], v)
                out[c].append(v)
        for c in range(2):
            v = jnp.concatenate(out[c], 1)
            ref[cur, 2 * j + c] = (v if scale is None else v * scale).astype(BF)
    def finish(i, dqv, dab):
        dq = jnp.concatenate(dqv, 0)
        g1 = mm(dq, wqT_ref[...]) + tall(dab).T.astype(F32)
        g1_ref[4 * i:4 * i + 4] = g1.astype(BF).reshape(4, RW, DP)
        yield
    def chunk(i):
        out = []
        yield from dense(i, out)
        dab, doT = out
        dq = []
        for t in range(2):
            yield from back(2 * i + t, doT[:, t * LW : (t + 1) * LW], dq)
        yield from finish(i, dq, dab)

    def wgrad(at, b, b3):
        dwq[...] += mm(hbTs[b3], dqss[b])
        yield
        dwo[...] += mm(dabTs[b], ois[b3])
        yield
        for c in range(0, FF, WC):
            dw1[c : c + WC] += mm_nt(duss[b, c : c + WC], hb2Ts[b])
            yield
        for c in range(0, FF, WC):
            dw2[c : c + WC] += mm_nt(actss[b, c : c + WC], dbTs[b])
            yield
        dkv = jnp.concatenate([r[b].reshape(FB * keys, DP) for r in (dks, dvs)], 1)
        dwkv[...] += mm_tn(step_rows(at), dkv)
        yield
        back_rows = mm(dkv, wkvT_ref[...]).astype(BF).reshape(FB, keys, DP)
        bk_ref[pl.ds(pl.multiple_of(at * FB, FB), FB)] = back_rows
        yield

    def ahead():
        keys_values(jnp.minimum(step + 1, pl.num_programs(0) - 1), prev)
        yield

    NC = FB // 4
    streams = [(ahead(), 0, 1)] + [(chunk(i), i * OFF, 1) for i in range(NC)]
    streams += [(attend(j, next_ref, qnext_ref, prev, next3), AO + j * AS, 1) for j in range(FB // 2)]
    streams += [(wgrad(jnp.maximum(step - 1, 0), prev, prev3), WP, 1)]
    weave(streams)

    @pl.when(step == pl.num_programs(0) - 1)
    def _():
        for _ in wgrad(step, cur, cur3):
            pass
        for s, b, n in blocks:
            own = bk_ref[b : b + n, s : s + 16, :]
            if n < 16:
                own = jnp.concatenate([own, jnp.zeros((16 - n, 16, DP), BF)], 0)
            own = turn_block(perm_ref, own, 16)[:, 0:n, 0:D]
            back_ref[s // 2 : s // 2 + 8, b : b + n, :] = jnp.concatenate([own[0:8], own[8:16]], 2)
        at = 0
        for ref in (dw1, dw2):
            t = ref[...].astype(BF).T.astype(F32)
            for j in range(FF // 128):
                pack_ref[at : at + D] = t[:, 128 * j : 128 * j + 128]
                at += D
        pack_pair(pack_ref, at, dwq, tall(dwo[...]).T)
        pack_pair(pack_ref, at + PAIR, dwkv[:, 0:DP], dwkv[:, DP:])
        pack_norms(pack_ref, at + 2 * PAIR, [dnp[i] for i in range(4)])
        hand_out(table_ref, pack_ref, piece_refs)


def item_and_dense(table, ht, qt, ct, slots, perm, ws, vec, packed, tables, OFF=0, AO=2, AS=6, WP=4, CC=384, WC=192):
    RW = ht.shape[1]
    keys = 2 * slots.shape[0]
    M = FB * RW
    cells = pl.BlockSpec((FB, RW, DP), lambda i: (i, 0, 0))
    accs = [(D, DP), (D, DP), (FF, D), (FF, D), (4, D, 128), (DP, 2 * DP), (keys, 128), (packed, 128)]
    kept = [(3, D, M), (3, M, DP)] + [(2,) + a for a in ((D, M), (FF, M), (D, M), (FF, M), (D, M), (M, DP))]
    kept += [(2, FB // 2, H * keys, 2 * RW), (2, FB * keys, 2 * DP), (FF, M)]
    ahead = pl.BlockSpec((FB, RW, DP), lambda i: (jnp.minimum(i + 1, FS // FB - 1), 0, 0))
    flat = [slots, perm, *ws, vec]
    outs = [shape((FS, RW, DP))] * 2 + [shape(slots.shape)] + [shape((packed // tables, 128))] * tables
    return pl.pallas_call(
        functools.partial(item_kernel, RW, keys, tables, OFF, AO, AS, WP, CC, WC),
        grid=(FS // FB,),
        in_specs=[pl.BlockSpec(memory_space=pltpu.SMEM), cells, ahead, cells, ahead, cells] + [whole(a) for a in flat],
        out_specs=[cells, cells] + [whole(a) for a in outs[2:]],
        out_shape=outs,
        scratch_shapes=[pltpu.VMEM(a, F32) for a in accs]
        + [pltpu.VMEM((FS, keys, DP), BF)] * 2
        + [pltpu.VMEM((2, FB, keys, DP), BF)] * 2
        + [pltpu.VMEM(a, BF) for a in kept],
        compiler_params=params(),
        cost_estimate=cost(66),
        name="item_and_dense",
    )(table, ht, ht, qt, qt, ct, *flat)


def backward_rows(
    x_ref, n_ref, qkv_ref, p_ref, l_ref, of_ref, wqkvI_ref, wo_ref, vec_ref, cg_ref, xs, os, dqs, das, dqkv, dwo, dnp, grad_of, base_ref=None
):
    def pair(c):
        at = slice(2 * c * FP, (2 * c + 2) * FP)
        dabs = []
        for u in range(2):
            r = 2 * c + u
            xs[:, r * FP : r * FP + F] = x_ref[r]
            os[:, r * FP : (r + 1) * FP] = of_ref[r]
            g = grad_of(r)
            n = n_ref[r, 0:D, :].astype(F32)
            rc = n_ref[r, D : D + 16, :].astype(F32)[0:1]
            dnp[0] += g * n
            dnp[1] += g
            dabs.append(norm_back_t(g, n, rc, vec_ref[0]).astype(BF))
            yield
        dab = jnp.concatenate(dabs, 1)
        das[:, at] = dab
        do = mm(wo_ref[...], tall(dab))
        yield
        for u in range(2):
            r = 2 * c + u
            own = slice(u * FP, (u + 1) * FP)
            lanes_r = slice(r * FP, (r + 1) * FP)
            for j in range(H // 2):
                inv = l_ref[r, j : j + 1, :]
                parts, offs = [], []
                for t in range(2):
                    hs = slice(64 * j + 32 * t, 64 * j + 32 * t + 32)
                    d = do[hs, own] * inv[:, t * FP : (t + 1) * FP]
                    offs.append(jnp.sum(d * of_ref[r, hs, :].astype(F32), 0, keepdims=True))
                    parts.append(d.astype(BF))
                dom = two_heads(*parts)
                off = jnp.concatenate(offs, 1).astype(BF)
                dp = mm(qkv_ref[r, 2 * D + 64 * j : 2 * D + 64 * j + 64, :].T, dom)
                yield
                e = p_ref[r, :, 256 * j : 256 * j + 256]
                ds = e * (dp.astype(BF) - off)
                dv = mm_nt(dom, e)
                yield
                qm = two_heads(
                    qkv_ref[r, 64 * j : 64 * j + 32, :], qkv_ref[r, 64 * j + 32 : 64 * j + 64, :]
                )
                dk = mm_nt(qm, ds) * 0.6931471805599453
                dq = mm(qkv_ref[r, D + 64 * j : D + 64 * j + 64, :], ds)
                dq = jnp.concatenate([dq[0:32, 0:128], dq[32:64, 128:256]], 0) * SCALE
                yield
                for i, d in enumerate((dq, dk, dv)):
                    dqs[i * D + 64 * j : i * D + 64 * j + 64, lanes_r] = d.astype(BF)
        yield
        cg = mm(wqkvI_ref[...], jnp.concatenate([dqs[:, at], dab], 0))
        for u in range(2):
            own = cg[:, u * FP : u * FP + F]
            cg_ref[2 * c + u] = own if base_ref is None else own + base_ref[2 * c + u]
        yield

    def sums(at):
        dqkv[...] += mm_nt(dqs[:, at], xs[:, at])
        yield
        dwo[...] += mm_nt(os[:, at], das[:, at])
        yield

    return pair, sums


def backward_kernel(
    R, OFF, YO, x_ref, n_ref, qkv_ref, p_ref, l_ref, of_ref, g1t_ref, yt_ref, wqkvI_ref, wo_ref, vec_ref, perm_ref,
    cg_ref, y_ref, dqkv, dwo, dnp, gs, ys, xs, os, dqs, das,
):
    @pl.when(pl.program_id(0) == 0)
    def _():
        for ref in (xs, dqkv, dwo, dnp):
            ref[...] = jnp.zeros_like(ref)

    col = lax.broadcasted_iota(jnp.int32, (16, 1, 1), 0)

    def turn(ref, out, j):
        block = ref[16 * j : min(16 * j + 16, FS)]
        if block.shape[0] < 16:
            block = jnp.concatenate([block, jnp.zeros((16 - block.shape[0],) + block.shape[1:], BF)], 0)
        if 16 * j + 16 > F:
            block = jnp.where(col < F - 16 * j, block, 0).astype(BF)
        out[:, 16 * j : 16 * j + 16, :] = turn_block(perm_ref, block, 16)

    for j in range(FP // 16):
        turn(g1t_ref, gs, j)

    def outputs():
        for j in range(FP // 16):
            turn(yt_ref, ys, j)
            yield
        for r in range(R):
            y_ref[r] = ys[r].T[0:D, 0:F]
            yield

    pair, sums = backward_rows(
        x_ref, n_ref, qkv_ref, p_ref, l_ref, of_ref, wqkvI_ref, wo_ref, vec_ref, cg_ref, xs, os, dqs, das, dqkv, dwo, dnp,
        lambda r: gs[r].T[0:D].astype(F32),
    )
    streams = [(pair(c), c * OFF, 1) for c in range(R // 2)]
    streams.append((outputs(), YO, 1))
    weave(streams)
    for _ in sums(slice(0, R * FP)):
        pass


def feature_backward(x, saved, g1t, yt, wqkvI, wo, vec, perm, R=16, OFF=2, YO=3):
    rows = x.shape[0]
    nat = lambda a: pl.BlockSpec((R,) + a.shape[1:], lambda i: (i, 0, 0))
    turned = pl.BlockSpec((FS, R, DP), lambda i: (0, i, 0))
    accs = [shape((3 * D, D), F32), shape((D, D), F32), shape((2, D, FP), F32)]
    shared = [wqkvI, wo, vec, perm]
    M = R * FP
    return pl.pallas_call(
        functools.partial(backward_kernel, R, OFF, YO),
        grid=(rows // R,),
        in_specs=[nat(x)] + [nat(a) for a in saved] + [turned] * 2 + [whole(a) for a in shared],
        out_specs=[nat(x), nat(x)] + [whole(a) for a in accs],
        out_shape=[shape(x.shape, F32), shape(x.shape)] + accs,
        scratch_shapes=[pltpu.VMEM(a, BF) for a in ((R, FP, DP), (R, FP, DP), (D, M), (D, M), (3 * D, M), (D, M))],
        compiler_params=params(),
        cost_estimate=cost(60 * rows // R),
        name="feature_backward",
    )(x, *saved, g1t, yt, *shared)


def slots_back_kernel(
    SL, tables, table_ref, x_ref, n_ref, qkv_ref, p_ref, l_ref, of_ref, slot_ref, base_ref, iqkv, iwo, inp, wqkvI_ref, wo_ref, vec_ref,
    cg_ref, *rest,
):
    piece_refs, rest = rest[:tables], rest[tables:]
    pack_ref, xs, os, dqs, das, dqkv, dwo, dnp = rest
    xs[...] = jnp.zeros_like(xs)
    for ref, init in ((dqkv, iqkv), (dwo, iwo), (dnp, inp)):
        ref[...] = init[...]
    both = slot_ref[0].astype(F32)
    for i in range(1, slot_ref.shape[0]):
        both = both + slot_ref[i].astype(F32)
    z0 = jnp.zeros((FP - FS, 2 * D), F32)
    live = lax.broadcasted_iota(jnp.int32, (1, FP), 1) < F
    back = []
    for c in range(SL // 2):
        t = jnp.where(live, jnp.concatenate([both[c], z0], 0).T, 0.0)
        back += [t[0:D], t[D : 2 * D]]
    pair, sums = backward_rows(
        x_ref, n_ref, qkv_ref, p_ref, l_ref, of_ref, wqkvI_ref, wo_ref, vec_ref, cg_ref, xs, os, dqs, das, dqkv, dwo, dnp,
        lambda r: back[r], base_ref,
    )
    weave([(pair(c), 0, 1) for c in range(SL // 2)])
    for _ in sums(slice(0, SL * FP)):
        pass
    zc = jnp.zeros((D, DP - D), F32)
    three = [jnp.concatenate([dqkv[i * D : (i + 1) * D], zc], 1).T for i in range(3)]
    pack_pair(pack_ref, 0, three[0], three[1])
    pack_pair(pack_ref, PAIR, three[2], dwo)
    pack_norms(pack_ref, 2 * PAIR, [dnp[0], dnp[1]])
    hand_out(table_ref, pack_ref, piece_refs)


def slots_backward(table, x, saved, slots, prev, wqkvI, wo, vec, packed, tables):
    SL = 2 * slots.shape[1]
    nat = lambda a: pl.BlockSpec((SL,) + a.shape[1:], lambda i: (i, 0, 0))
    cg, *accs = prev
    flat = list(accs) + [wqkvI, wo, vec]
    pieces = [shape((packed // tables, 128))] * tables
    M = SL * FP
    ins = [table, x, *saved, slots, cg, *flat]
    return pl.pallas_call(
        functools.partial(slots_back_kernel, SL, tables),
        grid=(1,),
        in_specs=[pl.BlockSpec(memory_space=pltpu.SMEM), nat(x)]
        + [nat(a) for a in saved]
        + [whole(slots), nat(cg)]
        + [whole(a) for a in flat],
        out_specs=[nat(cg)] + [whole(a) for a in pieces],
        out_shape=[shape(cg.shape, F32)] + pieces,
        input_output_aliases={len(saved) + 3: 0},
        scratch_shapes=[pltpu.VMEM((packed, 128), F32)]
        + [pltpu.VMEM(a, BF) for a in ((D, M), (D, M), (3 * D, M), (D, M))]
        + [pltpu.VMEM(a.shape, F32) for a in accs],
        compiler_params=params(),
        cost_estimate=cost(8),
        name="slots_backward",
    )(*ins)


def table_sums(tables, pieces):
    sent = []
    for i, a in enumerate(pieces):
        to = [(t, (t // 2 + i // 2) % (tables // 2) * 2 + (t + i) % 2) for t in range(tables)]
        sent.append(lax.ppermute(a, "table", to) if i else a)
    return sent


def join_kernel(tables, *refs):
    out_ref = refs[-1]
    at = 0
    for group in (refs[:tables], refs[tables : 2 * tables]):
        total = group[0][...].astype(F32)
        for ref in group[1:]:
            total = total + ref[...].astype(F32)
        rows = total.shape[0] // out_ref.shape[0]
        for i in range(out_ref.shape[0]):
            out_ref[i, at : at + rows] = total[i * rows : (i + 1) * rows].astype(BF)
        at += rows


def join_tables(shards, mids, tails):
    rows = (mids[0].shape[0] + tails[0].shape[0]) // shards
    return pl.pallas_call(
        functools.partial(join_kernel, len(mids)),
        out_shape=shape((shards, rows, 128)),
        compiler_params=params(),
        cost_estimate=cost(2),
        name="join_tables",
    )(*mids, *tails)


def sum_kernel(parts_ref, out_ref):
    total = parts_ref[0].astype(F32)
    for i in range(1, parts_ref.shape[0]):
        total = total + parts_ref[i].astype(F32)
    total = total.astype(BF)
    for i in range(out_ref.shape[0]):
        out_ref[i] = total


def sum_rows(parts):
    parts = lax.all_to_all(parts, "rows", 0, 0)
    return pl.pallas_call(
        sum_kernel,
        out_shape=shape(parts.shape),
        compiler_params=params(),
        cost_estimate=cost(2),
        name="sum_rows",
    )(parts)


def gather_all(copies):
    tables = lax.axis_size("table")
    ny = tables // 2
    own = lax.all_to_all(copies, "rows", 0, 0)
    pieces = [own]
    for s in range(1, ny):
        pieces.append(lax.ppermute(own, "table", [(t, (t // 2 + s) % ny * 2 + t % 2) for t in range(tables)]))
    other = [lax.ppermute(a, "table", [(t, t ^ 1) for t in range(tables)]) for a in pieces]
    return [a for pair in zip(pieces, other) for a in pair]


def to_row(c):
    return jnp.broadcast_to(c, (c.shape[0], 128)).T[0:1]


def to_col(r):
    return jnp.broadcast_to(r, (128, r.shape[1])).T[:, 0:1]


def clipped(update, weight, count):
    def total(v):
        return jnp.sum(jnp.sum(v, 0, keepdims=True), 1, keepdims=True)

    rms = jnp.sqrt(total(update * update) * (1.0 / count))
    weight_rms = jnp.sqrt(total(weight * weight) * (1.0 / count))
    return update * (RATE * jnp.maximum(0.001, weight_rms) / jnp.maximum(1.0, rms / CLIP))


def optimizer_kernel(
    tables, mid_rows, *refs):
    table_ref, *refs = refs
    piece_refs, refs = refs[:tables], refs[tables:]
    mid_ref, tail_ref = refs[-2:]
    table = table_ref[0]
    ny = tables // 2
    for i, ref in enumerate(piece_refs):
        place = pair_up(table, i, ny, True)
        for out, at, end in ((mid_ref, 0, mid_rows), (tail_ref, mid_rows, ref.shape[1])):
            rows = ref.shape[0] * (end - at)
            start = pl.multiple_of(place * rows, 8)
            out[pl.ds(start, rows)] = ref[:, at:end, :].astype(F32).reshape(rows, 128)
    optimizer_steps(*refs)


def optimizer_steps(
    proj_ref, outw_ref, in_ref, hid_ref, norm_ref, sr_ref, sc_ref, mm_ref, mh_ref, ns_ref,
    proj_gx, out_gx, in_gx, hid_gx, norm_g, proj_nx, out_nx, in_nx, hid_nx, norm_n, sr_n, sc_n, mm_n, mh_n, ns_n,
    proj_g, out_g, in_g, hid_g, proj_n, out_n, in_n, hid_n, sems, mid_ref, tail_ref,
):
    copies = []

    def send(a, b):
        copies.append(pltpu.make_async_copy(a, b, sems.at[len(copies)]))
        copies[-1].start()

    decay = 1.0 - STEP ** (-0.8)

    def stats(grad, col_old, row_old):
        square = grad * grad + 1e-30
        a, b = grad.shape
        over_sub = decay * row_old + (1.0 - decay) * (jnp.sum(square, 0, keepdims=True) * (1.0 / a))
        over_lane = decay * col_old + (1.0 - decay) * (jnp.sum(square, 1, keepdims=True) * (1.0 / b))
        return over_lane, over_sub

    def scaled(grad, col, row, mean):
        return grad * lax.rsqrt(col * (1.0 / mean)) * lax.rsqrt(row)

    def square_pair(ref, at):
        both = ref[at + 2 * D : at + 3 * D].astype(F32)
        a = jnp.concatenate([ref[at : at + D].astype(F32), both[:, 0:64]], 1)
        b = jnp.concatenate([ref[at + D : at + 2 * D].astype(F32), both[:, 64:128]], 1)
        return a, b

    wq, wk = square_pair(tail_ref, 0)
    wv, wo = square_pair(tail_ref, PAIR)
    wq2, wo2 = square_pair(mid_ref, 12 * D)
    wk2, wv2 = square_pair(mid_ref, 12 * D + PAIR)
    for i, grad in enumerate((wq, wk, wv, wq2, wk2, wv2, wo, wo2)):
        g_ref, n_ref, w_ref, j = (proj_g, proj_n, proj_ref, i) if i < 6 else (out_g, out_n, outw_ref, i - 6)
        gx, nx = (proj_gx, proj_nx) if i < 6 else (out_gx, out_nx)
        g_ref[j] = grad
        send(g_ref.at[j], gx.at[j])
        col, row = stats(grad, to_col(sr_ref[i : i + 1, :]), sc_ref[i : i + 1, :])
        sr_n[i : i + 1, :] = to_row(col)
        sc_n[i : i + 1, :] = row
        mean = jnp.sum(col, 0, keepdims=True) * (1.0 / D)
        w = w_ref[j]
        n_ref[j] = w - clipped(scaled(grad, col, row, mean), w, D * D)
        send(n_ref.at[j], nx.at[j])

    def wide(at):
        return jnp.concatenate([mid_ref[at + D * j : at + D * j + D].astype(F32) for j in range(6)], 1)

    grad = wide(0)
    in_g[...] = grad
    send(in_g, in_gx)
    col, row = stats(grad, to_col(mm_ref[0:1, :]), mh_ref[0:1, :])
    mm_n[0:1, :] = to_row(col)
    mh_n[0:1, :] = row
    mean = jnp.sum(col, 0, keepdims=True) * (1.0 / D)
    w = in_ref[...]
    in_n[...] = w - clipped(scaled(grad, col, row, mean), w, D * FF)
    send(in_n, in_nx)
    grad = wide(6 * D)
    hid_g[...] = grad
    send(hid_g, hid_gx)
    col, row = stats(grad, to_col(mm_ref[1:2, :]), mh_ref[1:2, :])
    mm_n[1:2, :] = to_row(col)
    mh_n[1:2, :] = row
    mean = jnp.sum(row, 1, keepdims=True) * (1.0 / FF)
    w = hid_ref[...]
    update = grad * lax.rsqrt(col) * lax.rsqrt(row * (1.0 / mean))
    hid_n[...] = w - clipped(update, w, D * FF)
    send(hid_n, hid_nx)

    pieces = []
    for ref, at, count in ((tail_ref, 2 * PAIR, 2), (mid_ref, 12 * D + 2 * PAIR, 4)):
        v = ref[at : at + 16].astype(F32)
        for i in range(count):
            pieces.append(jnp.concatenate([v[2 * i : 2 * i + 1], v[2 * i + 1 : 2 * i + 2, 0:64]], 1))
    grad = jnp.concatenate(pieces, 0)
    norm_g[...] = grad
    second = decay * ns_ref[...] + (1.0 - decay) * (grad * grad + 1e-30)
    ns_n[...] = second
    update = grad * lax.rsqrt(second)
    rms = jnp.sqrt(jnp.sum(update * update, 1, keepdims=True) * (1.0 / D))
    w = norm_ref[...]
    w_rms = jnp.sqrt(jnp.sum(w * w, 1, keepdims=True) * (1.0 / D))
    norm_n[...] = w - update * (RATE * jnp.maximum(0.001, w_rms) / jnp.maximum(1.0, rms / CLIP))
    for copy in copies:
        copy.wait()


def optimizer(table, pieces, mid_rows, *state):
    proj, outw, w_in, w_outT, norms, sr, sc, ms, hs, ns = state
    shards, rows, _ = pieces[0].shape
    order = [proj, outw, w_in, w_outT, norms, proj, outw, w_in, w_outT, norms, sr, sc, ms, hs, ns]
    big = (0, 1, 2, 3, 5, 6, 7, 8)
    outs = pl.pallas_call(
        functools.partial(optimizer_kernel, len(pieces), mid_rows),
        in_specs=[pl.BlockSpec(memory_space=pltpu.SMEM)] + [whole(a) for a in (*pieces, *state)],
        out_specs=[pl.BlockSpec(memory_space=pl.ANY) if i in big else whole(a) for i, a in enumerate(order)],
        out_shape=[shape(a.shape, F32) for a in order],
        scratch_shapes=[pltpu.VMEM(order[i].shape, F32) for i in big]
        + [
            pltpu.SemaphoreType.DMA((20,)),
            pltpu.VMEM((len(pieces) * shards * mid_rows, 128), F32),
            pltpu.VMEM((len(pieces) * shards * (rows - mid_rows), 128), F32),
        ],
        compiler_params=params(),
        cost_estimate=cost(8),
        name="optimizer",
    )(table, *pieces, *state)
    outs = list(outs)
    for i in (3, 8):
        outs[i] = outs[i].T
    return outs


def on_device(n, cells, cotangent, train_count, key_mask, train_order, *state):
    state = list(state)
    state[3] = state[3].T
    proj, outw, w_in, w_outT, norms = state[:5]
    x = jnp.swapaxes(cells[0], 1, 2)
    cot = jnp.swapaxes(cotangent[0], 1, 2)
    rows_here = x.shape[0]
    unit = 8 * n
    tail_rows = -(-TAIL // unit) * unit
    mid_rows = -(-MID // unit) * unit
    perm = perm_matrix()
    shards, tables = lax.axis_size("rows"), lax.axis_size("table")
    table = lax.axis_index("table").astype(jnp.int32).reshape(1)
    own, wqkvT, woT, vec = slot_rows(shards, train_count, key_mask, train_order, x, proj, outw, norms)
    slots = lax.all_to_all(own, "rows", 0, 0).reshape((-1,) + own.shape[2:])
    w_in, _ = lax.optimization_barrier((w_in, own))
    wqkvI, wo, *ws = other_weights(proj, outw, w_in, w_outT)
    wkv2, wkv2T, wq2, *ws = ws
    ht, ct, qt, *saved = feature_forward(x, cot, (wqkvT, woT, vec, perm, wq2))
    yt, g1t, back, *mids = item_and_dense(table, ht, qt, ct, slots, perm, (*ws, wkv2, wkv2T), vec, mid_rows, tables)
    back = lax.all_to_all(back.reshape(own.shape), "rows", 0, 0)
    mids = table_sums(tables, mids)
    cg, y, *accs = feature_backward(x, saved, g1t, yt, wqkvI, wo, vec, perm)
    mids, accs = lax.optimization_barrier((mids, accs))
    cg, *tails = slots_backward(table, x, saved, back, (cg, *accs), wqkvI, wo, vec, tail_rows, tables)
    tails = table_sums(tables, tails)
    pieces = gather_all(sum_rows(join_tables(shards, mids, tails)))
    return (jnp.swapaxes(y, 1, 2)[None], jnp.swapaxes(cg, 1, 2)[None], *optimizer(table, pieces, mid_rows // n, *state))


def solution(mesh):
    n = int(mesh.shape["table"] * mesh.shape["rows"])
    cells = P("table", "rows", None, None)
    return jax.shard_map(
        functools.partial(on_device, n),
        mesh=mesh,
        in_specs=(cells, cells, P("table"), P("table", "rows"), P("table", "rows")) + (P(),) * 10,
        out_specs=(cells, cells) + (P(),) * 15,
        check_vma=False,
    )
```

```python
import functools

import jax
import jax.numpy as jnp
import numpy as np
from jax import lax
from jax.experimental import pallas as pl
from jax.experimental.pallas import tpu as pltpu
from jax.sharding import PartitionSpec as P

BF, F32 = jnp.bfloat16, jnp.float32
D, DP = 192, 256
H, E = 6, 32
F, FP = 119, 128
FS = 120
FF = 768
STEP = 3
CLIP = 0.3
RATE = 0.5
WV = 0
FB = 8
SCALE = E**-0.5
SCALE2 = SCALE * 1.4426950408889634
C0 = 0.7978845608028654
C1 = 0.044715
NT = (((1,), (1,)), ((), ()))
TN = (((0,), (0,)), ((), ()))
PAIR = 576
TAIL = 2 * PAIR + 8
MID = 2 * 6 * D + 2 * PAIR + 8


def mm(a, b):
    return jnp.dot(a, b, preferred_element_type=F32)


def mm_nt(a, b):
    return lax.dot_general(a, b, NT, preferred_element_type=F32)


def mm_tn(a, b):
    return lax.dot_general(a, b, TN, preferred_element_type=F32)


def lanes():
    return lax.broadcasted_iota(jnp.int32, (1, DP), 1)


def whole(a):
    nd = len(a.shape)
    return pl.BlockSpec(a.shape, lambda *i: (0,) * nd)


def half_masks():
    lane = lax.broadcasted_iota(jnp.int32, (1, 128), 1)
    return [jnp.where((lane >= E * h) & (lane < E * (h + 1)), 1.0, 0.0).astype(BF) for h in range(4)]


def spread_halves(w, masks):
    z = jnp.zeros((w.shape[0], 128), BF)
    lo, hi = w[:, 0:128], w[:, 128:256]
    return jnp.concatenate(
        [jnp.concatenate([lo * masks[h], z], 1) for h in range(4)]
        + [jnp.concatenate([z, hi * masks[h]], 1) for h in range(2)], 0)


def mean0(a): return jnp.sum(a, 0, keepdims=True) * (1.0 / D)


def norm_t(a):
    c = a - mean0(a)
    rc = lax.rsqrt(mean0(c * c) + 1e-5)
    return c * rc, rc


def norm_back_t(g, n, rc, gain):
    dn = g * gain
    return (dn - mean0(dn) - n * mean0(dn * n)) * rc


def tall(a):
    return jnp.concatenate([a, jnp.zeros((DP - D, a.shape[1]), a.dtype)], 0)


def gelu_parts(u):
    uu = u * u
    th = jnp.tanh(u * (BF(C0) + BF(C0 * C1) * uu))
    half = BF(0.5) + BF(0.5) * th
    act = u * half
    slope = half + act * (BF(1.0) - th) * (BF(C0) + BF(3.0 * C0 * C1) * uu)
    return act, slope


def weave(streams):
    live=[[g,s,p] for g,s,p in streams]
    turn=0
    while live:
        for it in list(live):
            if turn>=it[1]:
                for _ in range(it[2]):
                    try: next(it[0])
                    except StopIteration:
                        live.remove(it); break
        turn+=1

def shape(s, t=BF):
    return jax.ShapeDtypeStruct(s, t)


def params(mib=58):
    return pltpu.CompilerParams(vmem_limit_bytes=mib << 20)


def cost(us):
    return pl.CostEstimate(flops=int(us * 1.1e9), bytes_accessed=int(us * 1e6), transcendentals=0)


def perm_matrix():
    place = np.zeros((256, 256), np.float32)
    for f in range(16):
        for r in range(16):
            place[f * 16 + r, r * 16 + f] = 1
    return jnp.asarray(place, BF)


def padded_square(w):
    a = jnp.concatenate([w, jnp.zeros((D, DP - D), F32)], 1).astype(BF)
    a = jnp.concatenate([a, jnp.zeros((DP - D, DP), BF)], 0)
    return a, a.T


def first_weights(proj, outw, norms, wqkvT, woT, vec, nrow):
    for i in range(3):
        wqkvT[i * D : (i + 1) * D, :] = padded_square(proj[i])[1][0:D]
    woT[...] = padded_square(outw[0])[1][0:D]
    nrow[...] = jnp.zeros((8, DP), F32)
    nrow[0:6, 0:D] = norms[...]
    for i in range(6):
        vec[i] = jnp.broadcast_to(nrow[i : i + 1, :], (128, DP)).T[0:D]


def weights_kernel(proj, outw, w_in, w_outT, wqkvI, wo, wkv2, wkv2T, wq2, wq2T, wo2I, wo2, w1T, w1, w2T, w2):
    row = lax.broadcasted_iota(jnp.int32, (D, DP), 0)
    eye = jnp.where(row == lax.broadcasted_iota(jnp.int32, (D, DP), 1), 1.0, 0.0).astype(BF)
    wqkvI[...] = jnp.concatenate([proj[0], proj[1], proj[2], eye[:, 0:D].astype(F32)], 1).astype(BF)
    wo[...] = jnp.concatenate([outw[0], jnp.zeros((D, DP - D), F32)], 1).astype(BF)
    a, t = padded_square(proj[3])
    wq2[...] = a
    wq2T[...] = t
    a, t = padded_square(outw[1])
    wo2[...] = a[0:D]
    wo2I[:, 0:DP] = t[0:D]
    wo2I[:, DP : 2 * DP] = eye
    for i in range(2):
        a, t = padded_square(proj[4 + i])
        wkv2[:, i * DP : (i + 1) * DP] = a
        wkv2T[i * DP : (i + 1) * DP, :] = t
    zw = jnp.zeros((DP - D, FF), BF)
    a = w_in[...].astype(BF)
    w1[...] = a
    w1T[...] = jnp.concatenate([a, zw], 0).T
    a = w_outT[...].astype(BF)
    w2T[...] = a
    w2[...] = jnp.concatenate([a, zw], 0).T


def other_weights(proj, outw, w_in, w_outT):
    sq, half = shape((DP, DP)), shape((D, DP))
    outs = [shape((D, 4 * D)), half, shape((DP, 2 * DP)), shape((2 * DP, DP)), sq, sq]
    outs += [shape((D, 2 * DP)), half, shape((FF, DP)), shape((D, FF)), shape((D, FF)), shape((FF, DP))]
    return pl.pallas_call(
        weights_kernel,
        out_shape=outs,
        compiler_params=params(),
        cost_estimate=cost(4),
        name="other_weights",
    )(proj, outw, w_in, w_outT)


def two_heads(a, b):
    z = jnp.zeros(a.shape, a.dtype)
    return jnp.concatenate([jnp.concatenate([a, z], 1), jnp.concatenate([z, b], 1)], 0)


def feature_pair(x, wqkvT_ref, woT_ref, keep, out):
    qkv = mm(wqkvT_ref[...], x)
    q = (qkv[0:D] * SCALE2).astype(BF)
    k = qkv[D : 2 * D].astype(BF)
    v = qkv[2 * D : 3 * D].astype(BF)
    yield
    row = lax.broadcasted_iota(jnp.int32, (8, 1), 0)
    outs = []
    for u in range(2):
        own = slice(u * FP, (u + 1) * FP)
        keep("qkv", u, (q[:, own], k[:, own], v[:, own]))
        ot = []
        for j in range(H // 2):
            hs = slice(64 * j, 64 * j + 64)
            qm = two_heads(q[64 * j : 64 * j + 32, own], q[64 * j + 32 : 64 * j + 64, own])
            st = mm(k[hs, own].T, qm)
            yield
            last = jnp.where(row < F - FS + 8, st[FS - 8 : FS], -1e30)
            mx = jnp.maximum(jnp.max(st[0 : FS - 8], 0, keepdims=True), jnp.max(last, 0, keepdims=True))
            e = jnp.exp2(st[0 : FS - 8] - mx)
            last = jnp.exp2(last - mx)
            inv = 1.0 / (jnp.sum(e, 0, keepdims=True) + jnp.sum(last, 0, keepdims=True))
            e = jnp.concatenate([e, last, jnp.zeros((FP - FS, 2 * FP), F32)], 0).astype(BF)
            keep("p", (u, j), (e, inv))
            yield
            t = mm(v[hs, own], e)
            ot.append(t[0:32, 0:128] * inv[:, 0:128])
            ot.append(t[32:64, 128:256] * inv[:, 128:256])
            yield
        ot = jnp.concatenate(ot, 0).astype(BF)
        keep("o", u, ot)
        outs.append(ot)
    a = mm(woT_ref[...], tall(jnp.concatenate(outs, 1)))
    yield
    for u in range(2):
        own = slice(u * FP, (u + 1) * FP)
        out.append(norm_t(x[0:D, own].astype(F32) + a[:, own]))
        yield


def slots_kernel(
    SL, count_ref, mask_ref, order_ref, x_ref, proj_ref, outw_ref, norm_ref, out_ref, wqkvT_ref, woT_ref, vec_ref, xs, nrow
):
    xs[...] = jnp.zeros_like(xs)
    first_weights(proj_ref, outw_ref, norm_ref, wqkvT_ref, woT_ref, vec_ref, nrow)
    row = lax.broadcasted_iota(jnp.int32, (FS, 1), 0)
    lane = lax.broadcasted_iota(jnp.int32, (1, 2 * D), 1)

    def flag(r):
        order = order_ref[0, r]
        usable = (order < count_ref[0]) & ((mask_ref[0, r] == 1) | (order == 0))
        return jnp.where(usable, 1.0, 0.0)

    def pair(c):
        for u in range(2):
            xs[c, 0:D, u * FP : u * FP + F] = x_ref[2 * c + u]
        out = []
        yield from feature_pair(xs[c], wqkvT_ref, woT_ref, lambda *a: None, out)
        both = jnp.concatenate([(n * vec_ref[0] + vec_ref[1]).astype(BF) for n, _ in out], 0)
        flags = jnp.where(lane < D, flag(2 * c), flag(2 * c + 1))
        both = jnp.where(row < F, both.T[0:FS].astype(F32), flags).astype(BF)
        for i in range(out_ref.shape[0]):
            out_ref[i, c] = both
        yield

    weave([(pair(c), 0, 1) for c in range(SL // 2)])


def slot_rows(shards, count, mask, order, cells, proj, outw, norms):
    SL = mask.shape[1]
    smem = pl.BlockSpec(memory_space=pltpu.SMEM)
    part = lambda a, k: pl.BlockSpec((k,) + a.shape[1:], lambda i: (0, 0, 0))
    outs = [shape((shards, SL // 2, FS, 2 * D)), shape((3 * D, DP)), shape((D, DP)), shape((6, D, 128), F32)]
    return pl.pallas_call(
        functools.partial(slots_kernel, SL),
        grid=(1,),
        in_specs=[smem, smem, smem, part(cells, SL), part(proj, 3), part(outw, 1), whole(norms)],
        out_specs=[whole(a) for a in outs],
        out_shape=outs,
        scratch_shapes=[pltpu.VMEM((SL // 2, DP, 2 * FP), BF), pltpu.VMEM((8, DP), F32)],
        compiler_params=params(),
        cost_estimate=cost(6),
        name="slot_rows",
    )(count, mask, order, cells, proj, outw, norms)


def turn_block(perm_ref, block, R):
    return mm(perm_ref[...], block.reshape(256, block.shape[-1])).astype(BF).reshape(16, R, block.shape[-1])


def forward_kernel(
    R, OFF, x_ref, c_ref, wqkvT_ref, woT_ref, vec_ref, perm_ref, wq_ref, ht_ref, ct_ref, qt_ref, n_ref, qkv_ref, p_ref, l_ref, of_ref, xs, hs, cp, cs
):
    @pl.when(pl.program_id(0) == 0)
    def _():
        xs[...] = jnp.zeros_like(xs)
        cp[...] = jnp.zeros_like(cp)

    def pair(c):
        for u in range(2):
            xs[c, 0:D, u * FP : u * FP + F] = x_ref[2 * c + u]

        def keep(what, at, val):
            if what == "qkv":
                for i in range(3):
                    qkv_ref[2 * c + at, i * D : (i + 1) * D, :] = val[i]
            elif what == "p":
                u, j = at
                p_ref[2 * c + u, :, 256 * j : 256 * j + 256] = val[0]
                l_ref[2 * c + u, j : j + 1, :] = val[1]
            else:
                of_ref[2 * c + at] = val

        out = []
        yield from feature_pair(xs[c], wqkvT_ref, woT_ref, keep, out)
        for u in range(2):
            r = 2 * c + u
            n, rc = out[u]
            n_ref[r, 0:D, :] = n.astype(BF)
            n_ref[r, D : D + 16, :] = jnp.broadcast_to(rc, (16, FP)).astype(BF)
            h = tall((n * vec_ref[0] + vec_ref[1]).astype(BF))
            hs[r] = h.T
            yield

    def cotangents():
        for r in range(R):
            cp[r % 4, 0:D, 0:F] = c_ref[r]
            cs[r] = cp[r % 4].T
            yield
        for j in range(FP // 16):
            ct_ref[16 * j : 16 * j + 16] = turn_block(perm_ref, cs[:, 16 * j : 16 * j + 16, :], R)
            yield

    weave([(pair(c), c * OFF, 1) for c in range(R // 2)] + [(cotangents(), 4, 1)])
    for j in range(FP // 16):
        block = turn_block(perm_ref, hs[:, 16 * j : 16 * j + 16, :], R)
        ht_ref[16 * j : 16 * j + 16] = block
        q = (mm(block.reshape(16 * R, DP), wq_ref[...]) * SCALE2).astype(BF)
        qt_ref[16 * j : 16 * j + 16] = q.reshape(16, R, DP)


def feature_forward(cells, cot, ws, R=16, OFF=2):
    rows = cells.shape[0]
    nat = lambda a, b: pl.BlockSpec((R, a, b), lambda i: (i, 0, 0))
    turned = pl.BlockSpec((FP, R, DP), lambda i: (0, i, 0))
    sizes = [(D + 16, FP), (3 * D, FP), (FP, H * FP), (8, 2 * FP), (D, FP)]
    kinds = [BF, BF, BF, F32, BF]
    return pl.pallas_call(
        functools.partial(forward_kernel, R, OFF),
        grid=(rows // R,),
        in_specs=[nat(D, F), nat(D, F)] + [whole(a) for a in ws],
        out_specs=[turned] * 3 + [nat(*a) for a in sizes],
        out_shape=[shape((FP, rows, DP))] * 3 + [shape((rows,) + a, t) for a, t in zip(sizes, kinds)],
        scratch_shapes=[
            pltpu.VMEM((R // 2, DP, 2 * FP), BF),
            pltpu.VMEM((R, FP, DP), BF),
            pltpu.VMEM((4, DP, FP), BF),
            pltpu.VMEM((R, FP, DP), BF),
        ],
        compiler_params=params(),
        cost_estimate=cost(9 * rows // R),
        name="feature_forward",
    )(cells, cot, *ws)


def pair_up(table, i, ny, back=False):
    shift = ny - i // 2 if back else i // 2
    return lax.rem(table // 2 + shift, ny) * 2 + lax.rem(table + i % 2, 2)


def hand_out(table_ref, pack, piece_refs):
    tables = len(piece_refs)
    rows = pack.shape[0] // tables
    for i, ref in enumerate(piece_refs):
        place = pair_up(table_ref[0], i, tables // 2)
        ref[...] = pack[pl.ds(pl.multiple_of(place * rows, 8), rows)].astype(BF)


def pack_pair(ref, at, a, b):
    ref[at : at + D] = a[0:D, 0:128]
    ref[at + D : at + 2 * D] = b[0:D, 0:128]
    ref[at + 2 * D : at + 3 * D] = jnp.concatenate([a[0:D, 128:D], b[0:D, 128:D]], 1)


def pack_norms(ref, at, sums):
    rows = []
    for s in sums:
        if s.shape[0] == D:
            s = jnp.concatenate([s, jnp.zeros((DP - D, 128), F32)], 0).T
        v = jnp.sum(s, 0, keepdims=True)
        rows += [v[:, 0:128], v[:, 128:256]]
    rows.append(jnp.zeros((ref.shape[0] - at - len(rows), 128), F32))
    ref[at:] = jnp.concatenate(rows, 0)


def item_kernel(
    RW, keys, tables, OFF, AO, AS, WP, CC, WC, table_ref, ht_ref, next_ref, q_ref, qnext_ref, ct_ref, slot_ref, perm_ref, wqT_ref, woI_ref, wo_ref, w1T_ref, w1_ref, w2T_ref, w2_ref,
    wkv_ref, wkvT_ref, vec_ref, y_ref, g1_ref, back_ref, *rest
):
    piece_refs, rest = rest[:tables], rest[tables:]
    (dwq, dwo, dw1, dw2, dnp, dwkv, bias_ref, pack_ref, hk_ref, bk_ref,
     dks, dvs, hbTs, ois, hb2Ts, actss, dbTs, duss, dabTs, dqss, pbss, kvss, slp) = rest
    step = pl.program_id(0)
    blocks = [(s, b, min(16, FS - b)) for s in range(0, keys, 16) for b in range(0, FS, 16)]

    @pl.when(step == 0)
    def _():
        for ref in (dwq, dwo, dw1, dw2, dnp, dwkv):
            ref[...] = jnp.zeros_like(ref)
        for ref in (hb2Ts, actss, dbTs, duss, dabTs, dqss, dks, dvs):
            ref[1] = jnp.zeros_like(ref[1])
        for ref in (hbTs, ois):
            ref[2] = jnp.zeros_like(ref[2])
        hk_ref[:, :, D:DP] = jnp.zeros((FS, keys, DP - D), BF)
        for s, b, n in blocks:
            own = slot_ref[s // 2 : s // 2 + 8, b : b + n, :]
            own = jnp.concatenate([own[:, :, 0:D], own[:, :, D : 2 * D]], 0)
            if n < 16:
                own = jnp.concatenate([own, jnp.zeros((16, 16 - n, D), BF)], 1)
            hk_ref[b : b + n, s : s + 16, 0:D] = turn_block(perm_ref, own, 16)[0:n]
        for s in range(0, keys, 16):
            flag = slot_ref[s // 2 : s // 2 + 8, F, :].astype(F32)
            for i, at in enumerate((0, DP)):
                bias_ref[s + 8 * i : s + 8 * i + 8] = jnp.where(flag[:, at : at + 128] > 0.5, 0.0, -1e30)

    masks = half_masks()
    LW = 2 * RW
    left = lax.broadcasted_iota(jnp.int32, (1, LW), 1) < RW
    HK = H * keys
    cur, prev = lax.rem(step, 2), lax.rem(step + 1, 2)
    cur3, next3, prev3 = [lax.rem(step + i, 3) for i in range(3)]
    hb2T, acts, dbT, dus, dabT, dqs = [r.at[cur] for r in (hb2Ts, actss, dbTs, duss, dabTs, dqss)]

    def step_rows(at):
        return hk_ref[pl.ds(pl.multiple_of(at * FB, FB), FB)].reshape(FB * keys, DP)

    def keys_values(at, to):
        kvss[to] = mm(step_rows(at), wkv_ref[...]).astype(BF)

    def spreads(to, j, first):
        return [
            spread_halves(kvss[to, (2 * j + c) * keys : (2 * j + c + 1) * keys, first : first + DP], masks)
            for c in range(2)
        ]

    def attend(j, ref, qref, to, to3):
        h = ref[2 * j : 2 * j + 2].reshape(LW, DP)
        q = qref[2 * j : 2 * j + 2].reshape(LW, DP)
        ks = spreads(to, j, 0)
        hbTs[to3, :, j * LW : (j + 1) * LW] = h.T[0:D]
        yield
        st = jnp.where(left, mm_nt(ks[0], q), mm_nt(ks[1], q))
        yield
        vs = spreads(to, j, DP)
        pbs = []
        for hh in range(H):
            s = st[hh * keys : (hh + 1) * keys] + bias_ref[...]
            e = jnp.exp2(s - jnp.max(s, 0, keepdims=True))
            pbs.append((e * (1.0 / jnp.sum(e, 0, keepdims=True))).astype(BF))
            if hh % 2:
                yield
        pb = jnp.concatenate(pbs, 0)
        pbss[to, j] = pb
        pt = pb.T
        yield
        o = jnp.concatenate([mm(pt[:RW], vs[0]), mm(pt[RW:], vs[1])], 0).astype(BF)
        ois[to3, j * LW : (j + 1) * LW] = o
        yield

    @pl.when(step == 0)
    def _():
        keys_values(0, 0)
        weave([(attend(j, ht_ref, q_ref, 0, 0), 0, 1) for j in range(FB // 2)])

    def dense(i, out):
        c0 = i * 2 * LW
        g1v, b1v, g2v, b2v = [vec_ref[i] for i in range(2, 6)]
        h = ht_ref[4 * i:4 * i + 4].reshape(2 * LW, DP)
        o = ois[cur3, c0 : c0 + 2 * LW]
        aT = mm_nt(woI_ref[...], jnp.concatenate([o, h], 1))
        yield
        n2, rc2, h2, hb2 = [], [], [], []
        for t in range(2):
            n, rc = norm_t(aT[:, t * LW:(t + 1) * LW])
            hh = n * g1v + b1v
            n2.append(n.astype(BF)); rc2.append(rc); hb2.append(hh.astype(BF))
            yield
        hb2 = jnp.concatenate(hb2, 1)
        hb2T[:, c0:c0 + 2 * LW] = hb2
        hb2 = tall(hb2)
        C = CC
        u = mm(w1T_ref[0:C], hb2)
        for c in range(FF // C):
            un = mm(w1T_ref[C * c + C:C * c + 2 * C], hb2) if c + 1 < FF // C else None
            act, slope = gelu_parts(u.astype(BF))
            acts[C * c:C * c + C, c0:c0 + 2 * LW] = act
            slp[C * c:C * c + C, c0:c0 + 2 * LW] = slope
            u = un
            yield
        gT = ct_ref[4 * i:4 * i + 4].reshape(2 * LW, DP).T[0:D].astype(F32)
        z = mm(w2T_ref[...], acts[:, c0:c0 + 2 * LW])
        yield
        dbs, d3s = [], []
        ys = []
        for t in range(2):
            sl = slice(t * LW, (t + 1) * LW)
            n3, rc3 = norm_t(hb2[0:D, sl].astype(F32) + z[:, sl])
            ys.append((n3 * g2v + b2v).astype(BF))
            yield
            g = gT[:, sl]
            dnp[2] += g * n3
            dnp[3] += g
            d3 = norm_back_t(g, n3, rc3, g2v)
            dbs.append(d3.astype(BF))
            yield
        db = jnp.concatenate(dbs, 1)
        dbT[:, c0:c0 + 2 * LW] = db
        db = tall(db)
        w = mm(w2_ref[0:C], db)
        for c in range(FF // C):
            wn = mm(w2_ref[C * c + C:C * c + 2 * C], db) if c + 1 < FF // C else None
            dus[C * c:C * c + C, c0:c0 + 2 * LW] = w.astype(BF) * slp[C * c:C * c + C, c0:c0 + 2 * LW]
            w = wn
            yield
        dh = mm(w1_ref[...], dus[:, c0:c0 + 2 * LW])
        yT = tall(jnp.concatenate(ys, 1))
        y_ref[4 * i:4 * i + 4] = yT.T.reshape(4, RW, DP)
        yield
        dabs = []
        for t in range(2):
            dh2 = dbs[t].astype(F32) + dh[:, t * LW:(t + 1) * LW]
            n2f = n2[t].astype(F32)
            dnp[0] += dh2 * n2f
            dnp[1] += dh2
            dabs.append(norm_back_t(dh2, n2f, rc2[t], g1v).astype(BF))
            yield
        dab = jnp.concatenate(dabs, 1)
        dabT[:, c0:c0 + 2 * LW] = dab
        doT = mm(wo_ref[...], tall(dab)).astype(BF)
        out.extend([dab, doT])
        yield
    def back(j, doT, out):
        q, pb = q_ref[2 * j : 2 * j + 2].reshape(LW, DP), pbss[cur, j]
        ks, vs = spreads(cur, j, 0), spreads(cur, j, DP)
        do = tall(doT)
        don = do.T
        dp = jnp.where(left, mm(vs[0], do), mm(vs[1], do))
        yield
        slot_sums(dvs, j, pb, don, None)
        yield
        dss = []
        for hh in range(H):
            sl = slice(hh * keys, (hh + 1) * keys)
            p, d = pb[sl].astype(F32), dp[sl]
            dss.append((p * (d - jnp.sum(p * d, 0, keepdims=True))).astype(BF))
            if hh % 2: yield
        ds = jnp.concatenate(dss, 0)
        dst = ds.T
        yield
        slot_sums(dks, j, ds, q, 0.6931471805599453)
        yield
        dq = jnp.concatenate([mm(dst[:RW], ks[0]), mm(dst[RW:], ks[1])], 0) * SCALE
        dq = dq.astype(BF)
        dqs[j * LW:(j + 1) * LW] = dq
        out.append(dq)
        yield
    lane = lax.broadcasted_iota(jnp.int32, (1, 128), 1)
    zq = jnp.zeros((RW, 128), BF)
    def slot_sums(ref, j, w, rows, scale):
        out = [[], []]
        for t, heads in ((0, 4), (1, 2)):
            r = rows[:, 128 * t:128 * t + 128]
            both = jnp.concatenate([jnp.concatenate([r[:RW], zq], 0), jnp.concatenate([zq, r[RW:]], 0)], 1)
            full = mm(w[4 * t * keys:(4 * t + heads) * keys], both)
            for c in range(2):
                col = full[:, 128 * c:128 * c + 128]
                v = col[0:keys]
                for hh in range(1, heads):
                    v = jnp.where(lane >= E * hh, col[hh * keys:(hh + 1) * keys], v)
                out[c].append(v)
        for c in range(2):
            v = jnp.concatenate(out[c], 1)
            ref[cur, 2 * j + c] = (v if scale is None else v * scale).astype(BF)
    def finish(i, dqv, dab):
        dq = jnp.concatenate(dqv, 0)
        g1 = mm(dq, wqT_ref[...]) + tall(dab).T.astype(F32)
        g1_ref[4 * i:4 * i + 4] = g1.astype(BF).reshape(4, RW, DP)
        yield
    def chunk(i):
        out = []
        yield from dense(i, out)
        dab, doT = out
        dq = []
        for t in range(2):
            yield from back(2 * i + t, doT[:, t * LW : (t + 1) * LW], dq)
        yield from finish(i, dq, dab)

    def wgrad(at, b, b3):
        dwq[...] += mm(hbTs[b3], dqss[b])
        yield
        dwo[...] += mm(dabTs[b], ois[b3])
        yield
        for c in range(0, FF, WC):
            dw1[c : c + WC] += mm_nt(duss[b, c : c + WC], hb2Ts[b])
            yield
        for c in range(0, FF, WC):
            dw2[c : c + WC] += mm_nt(actss[b, c : c + WC], dbTs[b])
            yield
        dkv = jnp.concatenate([r[b].reshape(FB * keys, DP) for r in (dks, dvs)], 1)
        dwkv[...] += mm_tn(step_rows(at), dkv)
        yield
        back_rows = mm(dkv, wkvT_ref[...]).astype(BF).reshape(FB, keys, DP)
        bk_ref[pl.ds(pl.multiple_of(at * FB, FB), FB)] = back_rows
        yield

    def ahead():
        keys_values(jnp.minimum(step + 1, pl.num_programs(0) - 1), prev)
        yield

    NC = FB // 4
    streams = [(ahead(), 0, 1)] + [(chunk(i), i * OFF, 1) for i in range(NC)]
    streams += [(attend(j, next_ref, qnext_ref, prev, next3), AO + j * AS, 1) for j in range(FB // 2)]
    streams += [(wgrad(jnp.maximum(step - 1, 0), prev, prev3), WP, 1)]
    weave(streams)

    @pl.when(step == pl.num_programs(0) - 1)
    def _():
        for _ in wgrad(step, cur, cur3):
            pass
        for s, b, n in blocks:
            own = bk_ref[b : b + n, s : s + 16, :]
            if n < 16:
                own = jnp.concatenate([own, jnp.zeros((16 - n, 16, DP), BF)], 0)
            own = turn_block(perm_ref, own, 16)[:, 0:n, 0:D]
            back_ref[s // 2 : s // 2 + 8, b : b + n, :] = jnp.concatenate([own[0:8], own[8:16]], 2)
        at = 0
        for ref in (dw1, dw2):
            t = ref[...].astype(BF).T.astype(F32)
            for j in range(FF // 128):
                pack_ref[at : at + D] = t[:, 128 * j : 128 * j + 128]
                at += D
        pack_pair(pack_ref, at, dwq, tall(dwo[...]).T)
        pack_pair(pack_ref, at + PAIR, dwkv[:, 0:DP], dwkv[:, DP:])
        pack_norms(pack_ref, at + 2 * PAIR, [dnp[i] for i in range(4)])
        hand_out(table_ref, pack_ref, piece_refs)


def item_and_dense(table, ht, qt, ct, slots, perm, ws, vec, packed, tables, OFF=0, AO=2, AS=6, WP=4, CC=384, WC=192):
    RW = ht.shape[1]
    keys = 2 * slots.shape[0]
    M = FB * RW
    cells = pl.BlockSpec((FB, RW, DP), lambda i: (i, 0, 0))
    accs = [(D, DP), (D, DP), (FF, D), (FF, D), (4, D, 128), (DP, 2 * DP), (keys, 128), (packed, 128)]
    kept = [(3, D, M), (3, M, DP)] + [(2,) + a for a in ((D, M), (FF, M), (D, M), (FF, M), (D, M), (M, DP))]
    kept += [(2, FB // 2, H * keys, 2 * RW), (2, FB * keys, 2 * DP), (FF, M)]
    ahead = pl.BlockSpec((FB, RW, DP), lambda i: (jnp.minimum(i + 1, FS // FB - 1), 0, 0))
    flat = [slots, perm, *ws, vec]
    outs = [shape((FS, RW, DP))] * 2 + [shape(slots.shape)] + [shape((packed // tables, 128))] * tables
    return pl.pallas_call(
        functools.partial(item_kernel, RW, keys, tables, OFF, AO, AS, WP, CC, WC),
        grid=(FS // FB,),
        in_specs=[pl.BlockSpec(memory_space=pltpu.SMEM), cells, ahead, cells, ahead, cells] + [whole(a) for a in flat],
        out_specs=[cells, cells] + [whole(a) for a in outs[2:]],
        out_shape=outs,
        scratch_shapes=[pltpu.VMEM(a, F32) for a in accs]
        + [pltpu.VMEM((FS, keys, DP), BF)] * 2
        + [pltpu.VMEM((2, FB, keys, DP), BF)] * 2
        + [pltpu.VMEM(a, BF) for a in kept],
        compiler_params=params(),
        cost_estimate=cost(66),
        name="item_and_dense",
    )(table, ht, ht, qt, qt, ct, *flat)


def backward_rows(
    x_ref, n_ref, qkv_ref, p_ref, l_ref, of_ref, wqkvI_ref, wo_ref, vec_ref, cg_ref, xs, os, dqs, das, dqkv, dwo, dnp, grad_of, base_ref=None
):
    def pair(c):
        at = slice(2 * c * FP, (2 * c + 2) * FP)
        dabs = []
        for u in range(2):
            r = 2 * c + u
            xs[:, r * FP : r * FP + F] = x_ref[r]
            os[:, r * FP : (r + 1) * FP] = of_ref[r]
            g = grad_of(r)
            n = n_ref[r, 0:D, :].astype(F32)
            rc = n_ref[r, D : D + 16, :].astype(F32)[0:1]
            dnp[0] += g * n
            dnp[1] += g
            dabs.append(norm_back_t(g, n, rc, vec_ref[0]).astype(BF))
            yield
        dab = jnp.concatenate(dabs, 1)
        das[:, at] = dab
        do = mm(wo_ref[...], tall(dab))
        yield
        for u in range(2):
            r = 2 * c + u
            own = slice(u * FP, (u + 1) * FP)
            lanes_r = slice(r * FP, (r + 1) * FP)
            for j in range(H // 2):
                inv = l_ref[r, j : j + 1, :]
                parts, offs = [], []
                for t in range(2):
                    hs = slice(64 * j + 32 * t, 64 * j + 32 * t + 32)
                    d = do[hs, own] * inv[:, t * FP : (t + 1) * FP]
                    offs.append(jnp.sum(d * of_ref[r, hs, :].astype(F32), 0, keepdims=True))
                    parts.append(d.astype(BF))
                dom = two_heads(*parts)
                off = jnp.concatenate(offs, 1).astype(BF)
                dp = mm(qkv_ref[r, 2 * D + 64 * j : 2 * D + 64 * j + 64, :].T, dom)
                yield
                e = p_ref[r, :, 256 * j : 256 * j + 256]
                ds = e * (dp.astype(BF) - off)
                dv = mm_nt(dom, e)
                yield
                qm = two_heads(
                    qkv_ref[r, 64 * j : 64 * j + 32, :], qkv_ref[r, 64 * j + 32 : 64 * j + 64, :]
                )
                dk = mm_nt(qm, ds) * 0.6931471805599453
                dq = mm(qkv_ref[r, D + 64 * j : D + 64 * j + 64, :], ds)
                dq = jnp.concatenate([dq[0:32, 0:128], dq[32:64, 128:256]], 0) * SCALE
                yield
                for i, d in enumerate((dq, dk, dv)):
                    dqs[i * D + 64 * j : i * D + 64 * j + 64, lanes_r] = d.astype(BF)
        yield
        cg = mm(wqkvI_ref[...], jnp.concatenate([dqs[:, at], dab], 0))
        for u in range(2):
            own = cg[:, u * FP : u * FP + F]
            cg_ref[2 * c + u] = own if base_ref is None else own + base_ref[2 * c + u]
        yield

    def sums(at):
        dqkv[...] += mm_nt(dqs[:, at], xs[:, at])
        yield
        dwo[...] += mm_nt(os[:, at], das[:, at])
        yield

    return pair, sums


def backward_kernel(
    R, OFF, YO, x_ref, n_ref, qkv_ref, p_ref, l_ref, of_ref, g1t_ref, yt_ref, wqkvI_ref, wo_ref, vec_ref, perm_ref,
    cg_ref, y_ref, dqkv, dwo, dnp, gs, ys, xs, os, dqs, das,
):
    @pl.when(pl.program_id(0) == 0)
    def _():
        for ref in (xs, dqkv, dwo, dnp):
            ref[...] = jnp.zeros_like(ref)

    col = lax.broadcasted_iota(jnp.int32, (16, 1, 1), 0)

    def turn(ref, out, j):
        block = ref[16 * j : min(16 * j + 16, FS)]
        if block.shape[0] < 16:
            block = jnp.concatenate([block, jnp.zeros((16 - block.shape[0],) + block.shape[1:], BF)], 0)
        if 16 * j + 16 > F:
            block = jnp.where(col < F - 16 * j, block, 0).astype(BF)
        out[:, 16 * j : 16 * j + 16, :] = turn_block(perm_ref, block, 16)

    for j in range(FP // 16):
        turn(g1t_ref, gs, j)

    def outputs():
        for j in range(FP // 16):
            turn(yt_ref, ys, j)
            yield
        for r in range(R):
            y_ref[r] = ys[r].T[0:D, 0:F]
            yield

    pair, sums = backward_rows(
        x_ref, n_ref, qkv_ref, p_ref, l_ref, of_ref, wqkvI_ref, wo_ref, vec_ref, cg_ref, xs, os, dqs, das, dqkv, dwo, dnp,
        lambda r: gs[r].T[0:D].astype(F32),
    )
    streams = [(pair(c), c * OFF, 1) for c in range(R // 2)]
    streams.append((outputs(), YO, 1))
    weave(streams)
    for _ in sums(slice(0, R * FP)):
        pass


def feature_backward(x, saved, g1t, yt, wqkvI, wo, vec, perm, R=16, OFF=2, YO=3):
    rows = x.shape[0]
    nat = lambda a: pl.BlockSpec((R,) + a.shape[1:], lambda i: (i, 0, 0))
    turned = pl.BlockSpec((FS, R, DP), lambda i: (0, i, 0))
    accs = [shape((3 * D, D), F32), shape((D, D), F32), shape((2, D, FP), F32)]
    shared = [wqkvI, wo, vec, perm]
    M = R * FP
    return pl.pallas_call(
        functools.partial(backward_kernel, R, OFF, YO),
        grid=(rows // R,),
        in_specs=[nat(x)] + [nat(a) for a in saved] + [turned] * 2 + [whole(a) for a in shared],
        out_specs=[nat(x), nat(x)] + [whole(a) for a in accs],
        out_shape=[shape(x.shape, F32), shape(x.shape)] + accs,
        scratch_shapes=[pltpu.VMEM(a, BF) for a in ((R, FP, DP), (R, FP, DP), (D, M), (D, M), (3 * D, M), (D, M))],
        compiler_params=params(),
        cost_estimate=cost(60 * rows // R),
        name="feature_backward",
    )(x, *saved, g1t, yt, *shared)


def slots_back_kernel(
    SL, tables, table_ref, x_ref, n_ref, qkv_ref, p_ref, l_ref, of_ref, slot_ref, base_ref, iqkv, iwo, inp, wqkvI_ref, wo_ref, vec_ref,
    cg_ref, *rest,
):
    piece_refs, rest = rest[:tables], rest[tables:]
    pack_ref, xs, os, dqs, das, dqkv, dwo, dnp = rest
    xs[...] = jnp.zeros_like(xs)
    for ref, init in ((dqkv, iqkv), (dwo, iwo), (dnp, inp)):
        ref[...] = init[...]
    both = slot_ref[0].astype(F32)
    for i in range(1, slot_ref.shape[0]):
        both = both + slot_ref[i].astype(F32)
    z0 = jnp.zeros((FP - FS, 2 * D), F32)
    live = lax.broadcasted_iota(jnp.int32, (1, FP), 1) < F
    back = []
    for c in range(SL // 2):
        t = jnp.where(live, jnp.concatenate([both[c], z0], 0).T, 0.0)
        back += [t[0:D], t[D : 2 * D]]
    pair, sums = backward_rows(
        x_ref, n_ref, qkv_ref, p_ref, l_ref, of_ref, wqkvI_ref, wo_ref, vec_ref, cg_ref, xs, os, dqs, das, dqkv, dwo, dnp,
        lambda r: back[r], base_ref,
    )
    weave([(pair(c), 0, 1) for c in range(SL // 2)])
    for _ in sums(slice(0, SL * FP)):
        pass
    zc = jnp.zeros((D, DP - D), F32)
    three = [jnp.concatenate([dqkv[i * D : (i + 1) * D], zc], 1).T for i in range(3)]
    pack_pair(pack_ref, 0, three[0], three[1])
    pack_pair(pack_ref, PAIR, three[2], dwo)
    pack_norms(pack_ref, 2 * PAIR, [dnp[0], dnp[1]])
    hand_out(table_ref, pack_ref, piece_refs)


def slots_backward(table, x, saved, slots, prev, wqkvI, wo, vec, packed, tables):
    SL = 2 * slots.shape[1]
    nat = lambda a: pl.BlockSpec((SL,) + a.shape[1:], lambda i: (i, 0, 0))
    cg, *accs = prev
    flat = list(accs) + [wqkvI, wo, vec]
    pieces = [shape((packed // tables, 128))] * tables
    M = SL * FP
    ins = [table, x, *saved, slots, cg, *flat]
    return pl.pallas_call(
        functools.partial(slots_back_kernel, SL, tables),
        grid=(1,),
        in_specs=[pl.BlockSpec(memory_space=pltpu.SMEM), nat(x)]
        + [nat(a) for a in saved]
        + [whole(slots), nat(cg)]
        + [whole(a) for a in flat],
        out_specs=[nat(cg)] + [whole(a) for a in pieces],
        out_shape=[shape(cg.shape, F32)] + pieces,
        input_output_aliases={len(saved) + 3: 0},
        scratch_shapes=[pltpu.VMEM((packed, 128), F32)]
        + [pltpu.VMEM(a, BF) for a in ((D, M), (D, M), (3 * D, M), (D, M))]
        + [pltpu.VMEM(a.shape, F32) for a in accs],
        compiler_params=params(),
        cost_estimate=cost(8),
        name="slots_backward",
    )(*ins)


def table_sums(tables, pieces):
    sent = []
    for i, a in enumerate(pieces):
        to = [(t, (t // 2 + i // 2) % (tables // 2) * 2 + (t + i) % 2) for t in range(tables)]
        sent.append(lax.ppermute(a, "table", to) if i else a)
    return sent


def join_kernel(tables, *refs):
    out_ref = refs[-1]
    at = 0
    for group in (refs[:tables], refs[tables : 2 * tables]):
        total = group[0][...].astype(F32)
        for ref in group[1:]:
            total = total + ref[...].astype(F32)
        rows = total.shape[0] // out_ref.shape[0]
        for i in range(out_ref.shape[0]):
            out_ref[i, at : at + rows] = total[i * rows : (i + 1) * rows].astype(BF)
        at += rows


def join_tables(shards, mids, tails):
    rows = (mids[0].shape[0] + tails[0].shape[0]) // shards
    return pl.pallas_call(
        functools.partial(join_kernel, len(mids)),
        out_shape=shape((shards, rows, 128)),
        compiler_params=params(16),
        cost_estimate=cost(2),
        name="join_tables",
    )(*mids, *tails)


def sum_kernel(parts_ref, out_ref):
    total = parts_ref[0].astype(F32)
    for i in range(1, parts_ref.shape[0]):
        total = total + parts_ref[i].astype(F32)
    total = total.astype(BF)
    for i in range(out_ref.shape[0]):
        out_ref[i] = total


def sum_rows(parts):
    parts = lax.all_to_all(parts, "rows", 0, 0)
    return pl.pallas_call(
        sum_kernel,
        out_shape=shape(parts.shape),
        compiler_params=params(16),
        cost_estimate=cost(2),
        name="sum_rows",
    )(parts)


def gather_all(copies):
    tables = lax.axis_size("table")
    ny = tables // 2
    own = lax.all_to_all(copies, "rows", 0, 0)
    pieces = [own]
    for s in range(1, ny):
        pieces.append(lax.ppermute(own, "table", [(t, (t // 2 + s) % ny * 2 + t % 2) for t in range(tables)]))
    other = [lax.ppermute(a, "table", [(t, t ^ 1) for t in range(tables)]) for a in pieces]
    return [a for pair in zip(pieces, other) for a in pair]


def to_row(c):
    return jnp.broadcast_to(c, (c.shape[0], 128)).T[0:1]


def to_col(r):
    return jnp.broadcast_to(r, (128, r.shape[1])).T[:, 0:1]


def clipped(update, weight, count):
    def total(v):
        return jnp.sum(jnp.sum(v, 0, keepdims=True), 1, keepdims=True)

    rms = jnp.sqrt(total(update * update) * (1.0 / count))
    weight_rms = jnp.sqrt(total(weight * weight) * (1.0 / count))
    return update * (RATE * jnp.maximum(0.001, weight_rms) / jnp.maximum(1.0, rms / CLIP))


def optimizer_kernel(
    tables, mid_rows, *refs):
    table_ref, *refs = refs
    piece_refs, refs = refs[:tables], refs[tables:]
    mid_ref, tail_ref = refs[-2:]
    table = table_ref[0]
    ny = tables // 2
    for i, ref in enumerate(piece_refs):
        place = pair_up(table, i, ny, True)
        for out, at, end in ((mid_ref, 0, mid_rows), (tail_ref, mid_rows, ref.shape[1])):
            rows = ref.shape[0] * (end - at)
            start = pl.multiple_of(place * rows, 8)
            out[pl.ds(start, rows)] = ref[:, at:end, :].astype(F32).reshape(rows, 128)
    optimizer_steps(*refs)


def optimizer_steps(
    proj_ref, outw_ref, in_ref, hid_ref, norm_ref, sr_ref, sc_ref, mm_ref, mh_ref, ns_ref,
    proj_g, out_g, in_g, hid_g, norm_g, proj_n, out_n, in_n, hid_n, norm_n, sr_n, sc_n, mm_n, mh_n, ns_n, mid_ref, tail_ref,
):
    decay = 1.0 - STEP ** (-0.8)

    def stats(grad, col_old, row_old):
        square = grad * grad + 1e-30
        a, b = grad.shape
        over_sub = decay * row_old + (1.0 - decay) * (jnp.sum(square, 0, keepdims=True) * (1.0 / a))
        over_lane = decay * col_old + (1.0 - decay) * (jnp.sum(square, 1, keepdims=True) * (1.0 / b))
        return over_lane, over_sub

    def scaled(grad, col, row, mean):
        return grad * lax.rsqrt(col * (1.0 / mean)) * lax.rsqrt(row)

    def square_step(i, ref, at, first):
        g_ref, n_ref, w_ref, j = (proj_g, proj_n, proj_ref, i) if i < 6 else (out_g, out_n, outw_ref, i - 6)
        low = ref[at : at + D] if first else ref[at + D : at + 2 * D]
        high = ref[at + 2 * D : at + 3 * D]
        grad = jnp.concatenate([low, high[:, 0:64] if first else high[:, 64:128]], 1)
        g_ref[j] = grad
        yield
        col, row = stats(grad, to_col(sr_ref[i : i + 1, :]), sc_ref[i : i + 1, :])
        sr_n[i : i + 1, :] = to_row(col)
        sc_n[i : i + 1, :] = row
        yield
        mean = jnp.sum(col, 0, keepdims=True) * (1.0 / D)
        update = scaled(grad, col, row, mean)
        yield
        w = w_ref[j]
        n_ref[j] = w - clipped(update, w, D * D)
        yield

    def wide_step(i, at, w_ref, g_ref, n_ref):
        for j in range(6):
            g_ref[:, 128 * j : 128 * j + 128] = mid_ref[at + D * j : at + D * j + D]
            yield
        grad = g_ref[...]
        col, row = stats(grad, to_col(mm_ref[i : i + 1, :]), mh_ref[i : i + 1, :])
        mm_n[i : i + 1, :] = to_row(col)
        mh_n[i : i + 1, :] = row
        yield
        mean = jnp.sum(col, 0, keepdims=True) * (1.0 / D) if i == 0 else jnp.sum(row, 1, keepdims=True) * (1.0 / FF)
        update = scaled(grad, col, row, mean)
        yield
        w = w_ref[...]
        n_ref[...] = w - clipped(update, w, D * FF)
        yield

    steps = [wide_step(0, 0, in_ref, in_g, in_n), wide_step(1, 6 * D, hid_ref, hid_g, hid_n)]
    places = ((0, tail_ref, 0, True), (1, tail_ref, 0, False), (2, tail_ref, PAIR, True), (6, tail_ref, PAIR, False))
    places += ((3, mid_ref, 12 * D, True), (7, mid_ref, 12 * D, False))
    places += ((4, mid_ref, 12 * D + PAIR, True), (5, mid_ref, 12 * D + PAIR, False))
    steps += [square_step(*a) for a in places]
    weave([(g, WV * i, 1) for i, g in enumerate(steps)])

    pieces = []
    for ref, at, count in ((tail_ref, 2 * PAIR, 2), (mid_ref, 12 * D + 2 * PAIR, 4)):
        v = ref[at : at + 16].astype(F32)
        for i in range(count):
            pieces.append(jnp.concatenate([v[2 * i : 2 * i + 1], v[2 * i + 1 : 2 * i + 2, 0:64]], 1))
    grad = jnp.concatenate(pieces, 0)
    norm_g[...] = grad
    second = decay * ns_ref[...] + (1.0 - decay) * (grad * grad + 1e-30)
    ns_n[...] = second
    update = grad * lax.rsqrt(second)
    rms = jnp.sqrt(jnp.sum(update * update, 1, keepdims=True) * (1.0 / D))
    w = norm_ref[...]
    w_rms = jnp.sqrt(jnp.sum(w * w, 1, keepdims=True) * (1.0 / D))
    norm_n[...] = w - update * (RATE * jnp.maximum(0.001, w_rms) / jnp.maximum(1.0, rms / CLIP))


def optimizer(table, pieces, mid_rows, *state):
    proj, outw, w_in, w_outT, norms, sr, sc, ms, hs, ns = state
    shards, rows, _ = pieces[0].shape
    order = [proj, outw, w_in, w_outT, norms, proj, outw, w_in, w_outT, norms, sr, sc, ms, hs, ns]
    outs = pl.pallas_call(
        functools.partial(optimizer_kernel, len(pieces), mid_rows),
        in_specs=[pl.BlockSpec(memory_space=pltpu.SMEM)] + [whole(a) for a in (*pieces, *state)],
        out_shape=[shape(a.shape, F32) for a in order],
        scratch_shapes=[
            pltpu.VMEM((len(pieces) * shards * mid_rows, 128), F32),
            pltpu.VMEM((len(pieces) * shards * (rows - mid_rows), 128), F32),
        ],
        compiler_params=params(28),
        cost_estimate=cost(8), name="optimizer",
    )(table, *pieces, *state)
    outs = list(outs)
    for i in (3, 8):
        outs[i] = outs[i].T
    return outs


def on_device(n, cells, cotangent, train_count, key_mask, train_order, *state):
    state = list(state)
    state[3] = state[3].T
    proj, outw, w_in, w_outT, norms = state[:5]
    x = jnp.swapaxes(cells[0], 1, 2)
    cot = jnp.swapaxes(cotangent[0], 1, 2)
    rows_here = x.shape[0]
    unit = 8 * n
    tail_rows = -(-TAIL // unit) * unit
    mid_rows = -(-MID // unit) * unit
    perm = perm_matrix()
    shards, tables = lax.axis_size("rows"), lax.axis_size("table")
    table = lax.axis_index("table").astype(jnp.int32).reshape(1)
    own, wqkvT, woT, vec = slot_rows(shards, train_count, key_mask, train_order, x, proj, outw, norms)
    slots = lax.all_to_all(own, "rows", 0, 0).reshape((-1,) + own.shape[2:])
    w_in, _ = lax.optimization_barrier((w_in, own))
    wqkvI, wo, *ws = other_weights(proj, outw, w_in, w_outT)
    wkv2, wkv2T, wq2, *ws = ws
    ht, ct, qt, *saved = feature_forward(x, cot, (wqkvT, woT, vec, perm, wq2))
    yt, g1t, back, *mids = item_and_dense(table, ht, qt, ct, slots, perm, (*ws, wkv2, wkv2T), vec, mid_rows, tables)
    back = lax.all_to_all(back.reshape(own.shape), "rows", 0, 0)
    mids = table_sums(tables, mids)
    cg, y, *accs = feature_backward(x, saved, g1t, yt, wqkvI, wo, vec, perm)
    mids, accs = lax.optimization_barrier((mids, accs))
    cg, *tails = slots_backward(table, x, saved, back, (cg, *accs), wqkvI, wo, vec, tail_rows, tables)
    tails = table_sums(tables, tails)
    pieces = gather_all(sum_rows(join_tables(shards, mids, tails)))
    return (jnp.swapaxes(y, 1, 2)[None], jnp.swapaxes(cg, 1, 2)[None], *optimizer(table, pieces, mid_rows // n, *state))


def solution(mesh):
    n = int(mesh.shape["table"] * mesh.shape["rows"])
    cells = P("table", "rows", None, None)
    return jax.shard_map(
        functools.partial(on_device, n),
        mesh=mesh,
        in_specs=(cells, cells, P("table"), P("table", "rows"), P("table", "rows")) + (P(),) * 10,
        out_specs=(cells, cells) + (P(),) * 15,
        check_vma=False,
    )
```

```python
import functools

import jax
import jax.numpy as jnp
import numpy as np
from jax import lax
from jax.experimental import pallas as pl
from jax.experimental.pallas import tpu as pltpu
from jax.sharding import PartitionSpec as P

BF, F32 = jnp.bfloat16, jnp.float32
D, DP = 192, 256
H, E = 6, 32
F, FP = 119, 128
FS = 120
FF = 768
STEP = 3
CLIP = 0.3
RATE = 0.5
WV = 0
SCALE = E**-0.5
SCALE2 = SCALE * 1.4426950408889634
C0 = 0.7978845608028654
C1 = 0.044715
NT = (((1,), (1,)), ((), ()))
TN = (((0,), (0,)), ((), ()))
PAIR = 576
TAIL = 2 * PAIR + 8
MID = 2 * 6 * D + 2 * PAIR + 8


def mm(a, b):
    return jnp.dot(a, b, preferred_element_type=F32)


def mm_nt(a, b):
    return lax.dot_general(a, b, NT, preferred_element_type=F32)


def mm_tn(a, b):
    return lax.dot_general(a, b, TN, preferred_element_type=F32)


def lanes():
    return lax.broadcasted_iota(jnp.int32, (1, DP), 1)


def whole(a):
    nd = len(a.shape)
    return pl.BlockSpec(a.shape, lambda *i: (0,) * nd)


def half_masks():
    lane = lax.broadcasted_iota(jnp.int32, (1, 128), 1)
    return [jnp.where((lane >= E * h) & (lane < E * (h + 1)), 1.0, 0.0).astype(BF) for h in range(4)]


def spread_halves(w, masks):
    z = jnp.zeros((w.shape[0], 128), BF)
    lo, hi = w[:, 0:128], w[:, 128:256]
    return jnp.concatenate(
        [jnp.concatenate([lo * masks[h], z], 1) for h in range(4)]
        + [jnp.concatenate([z, hi * masks[h]], 1) for h in range(2)], 0)


def mean0(a): return jnp.sum(a, 0, keepdims=True) * (1.0 / D)


def norm_t(a):
    c = a - mean0(a)
    rc = lax.rsqrt(mean0(c * c) + 1e-5)
    return c * rc, rc


def norm_back_t(g, n, rc, gain):
    dn = g * gain
    return (dn - mean0(dn) - n * mean0(dn * n)) * rc


def tall(a):
    return jnp.concatenate([a, jnp.zeros((DP - D, a.shape[1]), a.dtype)], 0)


def gelu_parts(u):
    uu = u * u
    th = jnp.tanh(u * (BF(C0) + BF(C0 * C1) * uu))
    half = BF(0.5) + BF(0.5) * th
    act = u * half
    slope = half + act * (BF(1.0) - th) * (BF(C0) + BF(3.0 * C0 * C1) * uu)
    return act, slope


def weave(streams):
    live=[[g,s,p] for g,s,p in streams]
    turn=0
    while live:
        for it in list(live):
            if turn>=it[1]:
                for _ in range(it[2]):
                    try: next(it[0])
                    except StopIteration:
                        live.remove(it); break
        turn+=1

def shape(s, t=BF):
    return jax.ShapeDtypeStruct(s, t)


def params(mib=58):
    return pltpu.CompilerParams(vmem_limit_bytes=mib << 20)


def cost(us):
    return pl.CostEstimate(flops=int(us * 1.1e9), bytes_accessed=int(us * 1e6), transcendentals=0)


def perm_matrix():
    place = np.zeros((256, 256), np.float32)
    for f in range(16):
        for r in range(16):
            place[f * 16 + r, r * 16 + f] = 1
    return jnp.asarray(place, BF)


def padded_square(w):
    a = jnp.concatenate([w, jnp.zeros((D, DP - D), F32)], 1).astype(BF)
    a = jnp.concatenate([a, jnp.zeros((DP - D, DP), BF)], 0)
    return a, a.T


def first_weights(proj, outw, norms, wqkvT, woT, vec, nrow):
    for i in range(3):
        wqkvT[i * D : (i + 1) * D, :] = padded_square(proj[i])[1][0:D]
    woT[...] = padded_square(outw[0])[1][0:D]
    nrow[...] = jnp.zeros((8, DP), F32)
    nrow[0:6, 0:D] = norms[...]
    for i in range(6):
        vec[i] = jnp.broadcast_to(nrow[i : i + 1, :], (128, DP)).T[0:D]


def weights_kernel(proj, outw, w_in, w_outT, wqkvI, wo, wkv2, wkv2T, wq2, wq2T, wo2I, wo2, w1T, w1, w2T, w2):
    row = lax.broadcasted_iota(jnp.int32, (D, DP), 0)
    eye = jnp.where(row == lax.broadcasted_iota(jnp.int32, (D, DP), 1), 1.0, 0.0).astype(BF)
    wqkvI[...] = jnp.concatenate([proj[0], proj[1], proj[2], eye[:, 0:D].astype(F32)], 1).astype(BF)
    wo[...] = jnp.concatenate([outw[0], jnp.zeros((D, DP - D), F32)], 1).astype(BF)
    a, t = padded_square(proj[3])
    wq2[...] = a
    wq2T[...] = t
    a, t = padded_square(outw[1])
    wo2[...] = a[0:D]
    wo2I[:, 0:DP] = t[0:D]
    wo2I[:, DP : 2 * DP] = eye
    for i in range(2):
        a, t = padded_square(proj[4 + i])
        wkv2[:, i * DP : (i + 1) * DP] = a
        wkv2T[i * DP : (i + 1) * DP, :] = t
    zw = jnp.zeros((DP - D, FF), BF)
    a = w_in[...].astype(BF)
    w1[...] = a
    w1T[...] = jnp.concatenate([a, zw], 0).T
    a = w_outT[...].astype(BF)
    w2T[...] = a
    w2[...] = jnp.concatenate([a, zw], 0).T


def other_weights(proj, outw, w_in, w_outT):
    sq, half = shape((DP, DP)), shape((D, DP))
    outs = [shape((D, 4 * D)), half, shape((DP, 2 * DP)), shape((2 * DP, DP)), sq, sq]
    outs += [shape((D, 2 * DP)), half, shape((FF, DP)), shape((D, FF)), shape((D, FF)), shape((FF, DP))]
    return pl.pallas_call(
        weights_kernel,
        out_shape=outs,
        compiler_params=params(),
        cost_estimate=cost(4),
        name="other_weights",
    )(proj, outw, w_in, w_outT)


def two_heads(a, b):
    z = jnp.zeros(a.shape, a.dtype)
    return jnp.concatenate([jnp.concatenate([a, z], 1), jnp.concatenate([z, b], 1)], 0)


def feature_pair(x, wqkvT_ref, woT_ref, keep, out):
    qkv = mm(wqkvT_ref[...], x)
    q = (qkv[0:D] * SCALE2).astype(BF)
    k = qkv[D : 2 * D].astype(BF)
    v = qkv[2 * D : 3 * D].astype(BF)
    yield
    row = lax.broadcasted_iota(jnp.int32, (8, 1), 0)
    outs = []
    for u in range(2):
        own = slice(u * FP, (u + 1) * FP)
        keep("qkv", u, (q[:, own], k[:, own], v[:, own]))
        ot = []
        for j in range(H // 2):
            hs = slice(64 * j, 64 * j + 64)
            qm = two_heads(q[64 * j : 64 * j + 32, own], q[64 * j + 32 : 64 * j + 64, own])
            st = mm(k[hs, own].T, qm)
            yield
            last = jnp.where(row < F - FS + 8, st[FS - 8 : FS], -1e30)
            mx = jnp.maximum(jnp.max(st[0 : FS - 8], 0, keepdims=True), jnp.max(last, 0, keepdims=True))
            e = jnp.exp2(st[0 : FS - 8] - mx)
            last = jnp.exp2(last - mx)
            inv = 1.0 / (jnp.sum(e, 0, keepdims=True) + jnp.sum(last, 0, keepdims=True))
            e = jnp.concatenate([e, last, jnp.zeros((FP - FS, 2 * FP), F32)], 0).astype(BF)
            keep("p", (u, j), (e, inv))
            yield
            t = mm(v[hs, own], e)
            ot.append(t[0:32, 0:128] * inv[:, 0:128])
            ot.append(t[32:64, 128:256] * inv[:, 128:256])
            yield
        ot = jnp.concatenate(ot, 0).astype(BF)
        keep("o", u, ot)
        outs.append(ot)
    a = mm(woT_ref[...], tall(jnp.concatenate(outs, 1)))
    yield
    for u in range(2):
        own = slice(u * FP, (u + 1) * FP)
        out.append(norm_t(x[0:D, own].astype(F32) + a[:, own]))
        yield


def slots_kernel(
    SL, count_ref, mask_ref, order_ref, x_ref, proj_ref, outw_ref, norm_ref, out_ref, wqkvT_ref, woT_ref, vec_ref, xs, nrow
):
    xs[...] = jnp.zeros_like(xs)
    first_weights(proj_ref, outw_ref, norm_ref, wqkvT_ref, woT_ref, vec_ref, nrow)
    row = lax.broadcasted_iota(jnp.int32, (FS, 1), 0)
    lane = lax.broadcasted_iota(jnp.int32, (1, 2 * D), 1)

    def flag(r):
        order = order_ref[0, r]
        usable = (order < count_ref[0]) & ((mask_ref[0, r] == 1) | (order == 0))
        return jnp.where(usable, 1.0, 0.0)

    def pair(c):
        for u in range(2):
            xs[c, 0:D, u * FP : u * FP + F] = x_ref[2 * c + u]
        out = []
        yield from feature_pair(xs[c], wqkvT_ref, woT_ref, lambda *a: None, out)
        both = jnp.concatenate([(n * vec_ref[0] + vec_ref[1]).astype(BF) for n, _ in out], 0)
        flags = jnp.where(lane < D, flag(2 * c), flag(2 * c + 1))
        both = jnp.where(row < F, both.T[0:FS].astype(F32), flags).astype(BF)
        for i in range(out_ref.shape[0]):
            out_ref[i, c] = both
        yield

    weave([(pair(c), 0, 1) for c in range(SL // 2)])


def slot_rows(shards, count, mask, order, cells, proj, outw, norms):
    SL = mask.shape[1]
    smem = pl.BlockSpec(memory_space=pltpu.SMEM)
    part = lambda a, k: pl.BlockSpec((k,) + a.shape[1:], lambda i: (0, 0, 0))
    outs = [shape((shards, SL // 2, FS, 2 * D)), shape((3 * D, DP)), shape((D, DP)), shape((6, D, 128), F32)]
    return pl.pallas_call(
        functools.partial(slots_kernel, SL),
        grid=(1,),
        in_specs=[smem, smem, smem, part(cells, SL), part(proj, 3), part(outw, 1), whole(norms)],
        out_specs=[whole(a) for a in outs],
        out_shape=outs,
        scratch_shapes=[pltpu.VMEM((SL // 2, DP, 2 * FP), BF), pltpu.VMEM((8, DP), F32)],
        compiler_params=params(),
        cost_estimate=cost(6),
        name="slot_rows",
    )(count, mask, order, cells, proj, outw, norms)


def turn_block(perm_ref, block, R):
    return mm(perm_ref[...], block.reshape(256, block.shape[-1])).astype(BF).reshape(16, R, block.shape[-1])


def forward_kernel(
    R, OFF, x_ref, c_ref, wqkvT_ref, woT_ref, vec_ref, perm_ref, wq_ref, ht_ref, ct_ref, qt_ref, n_ref, qkv_ref, p_ref, l_ref, of_ref, xs, hs, cp, cs
):
    @pl.when(pl.program_id(0) == 0)
    def _():
        xs[...] = jnp.zeros_like(xs)
        cp[...] = jnp.zeros_like(cp)

    def pair(c):
        for u in range(2):
            xs[c, 0:D, u * FP : u * FP + F] = x_ref[2 * c + u]

        def keep(what, at, val):
            if what == "qkv":
                for i in range(3):
                    qkv_ref[2 * c + at, i * D : (i + 1) * D, :] = val[i]
            elif what == "p":
                u, j = at
                p_ref[2 * c + u, :, 256 * j : 256 * j + 256] = val[0]
                l_ref[2 * c + u, j : j + 1, :] = val[1]
            else:
                of_ref[2 * c + at] = val

        out = []
        yield from feature_pair(xs[c], wqkvT_ref, woT_ref, keep, out)
        for u in range(2):
            r = 2 * c + u
            n, rc = out[u]
            n_ref[r, 0:D, :] = n.astype(BF)
            n_ref[r, D : D + 16, :] = jnp.broadcast_to(rc, (16, FP)).astype(BF)
            h = tall((n * vec_ref[0] + vec_ref[1]).astype(BF))
            hs[r] = h.T
            yield

    def cotangents():
        for r in range(R):
            cp[r % 4, 0:D, 0:F] = c_ref[r]
            cs[r] = cp[r % 4].T
            yield
        for j in range(FP // 16):
            ct_ref[16 * j : 16 * j + 16] = turn_block(perm_ref, cs[:, 16 * j : 16 * j + 16, :], R)
            yield

    weave([(pair(c), c * OFF, 1) for c in range(R // 2)] + [(cotangents(), 4, 1)])
    for j in range(FP // 16):
        block = turn_block(perm_ref, hs[:, 16 * j : 16 * j + 16, :], R)
        ht_ref[16 * j : 16 * j + 16] = block
        q = (mm(block.reshape(16 * R, DP), wq_ref[...]) * SCALE2).astype(BF)
        qt_ref[16 * j : 16 * j + 16] = q.reshape(16, R, DP)


def feature_forward(cells, cot, ws, R=16, OFF=2):
    rows = cells.shape[0]
    nat = lambda a, b: pl.BlockSpec((R, a, b), lambda i: (i, 0, 0))
    turned = pl.BlockSpec((FP, R, DP), lambda i: (0, i, 0))
    sizes = [(D + 16, FP), (3 * D, FP), (FP, H * FP), (8, 2 * FP), (D, FP)]
    kinds = [BF, BF, BF, F32, BF]
    return pl.pallas_call(
        functools.partial(forward_kernel, R, OFF),
        grid=(rows // R,),
        in_specs=[nat(D, F), nat(D, F)] + [whole(a) for a in ws],
        out_specs=[turned] * 3 + [nat(*a) for a in sizes],
        out_shape=[shape((FP, rows, DP))] * 3 + [shape((rows,) + a, t) for a, t in zip(sizes, kinds)],
        scratch_shapes=[
            pltpu.VMEM((R // 2, DP, 2 * FP), BF),
            pltpu.VMEM((R, FP, DP), BF),
            pltpu.VMEM((4, DP, FP), BF),
            pltpu.VMEM((R, FP, DP), BF),
        ],
        compiler_params=params(),
        cost_estimate=cost(9 * rows // R),
        name="feature_forward",
    )(cells, cot, *ws)


def pair_up(table, i, ny, back=False):
    shift = ny - i // 2 if back else i // 2
    return lax.rem(table // 2 + shift, ny) * 2 + lax.rem(table + i % 2, 2)


def hand_out(table_ref, pack, piece_refs):
    tables = len(piece_refs)
    rows = pack.shape[0] // tables
    for i, ref in enumerate(piece_refs):
        place = pair_up(table_ref[0], i, tables // 2)
        ref[...] = pack[pl.ds(pl.multiple_of(place * rows, 8), rows)].astype(BF)


def pack_pair(ref, at, a, b):
    ref[at : at + D] = a[0:D, 0:128]
    ref[at + D : at + 2 * D] = b[0:D, 0:128]
    ref[at + 2 * D : at + 3 * D] = jnp.concatenate([a[0:D, 128:D], b[0:D, 128:D]], 1)


def pack_norms(ref, at, sums):
    rows = []
    for s in sums:
        if s.shape[0] == D:
            s = jnp.concatenate([s, jnp.zeros((DP - D, 128), F32)], 0).T
        v = jnp.sum(s, 0, keepdims=True)
        rows += [v[:, 0:128], v[:, 128:256]]
    rows.append(jnp.zeros((ref.shape[0] - at - len(rows), 128), F32))
    ref[at:] = jnp.concatenate(rows, 0)


def item_kernel(
    FB, RW, keys, tables, OFF, AO, AS, WP, CC, WC, table_ref, ht_ref, next_ref, q_ref, qnext_ref, ct_ref, slot_ref, perm_ref, wqT_ref, woI_ref, wo_ref, w1T_ref, w1_ref, w2T_ref, w2_ref,
    wkv_ref, wkvT_ref, vec_ref, y_ref, g1_ref, back_ref, *rest
):
    piece_refs, rest = rest[:tables], rest[tables:]
    (dwq, dwo, dw1, dw2, dnp, dwkv, bias_ref, pack_ref, hk_ref, bk_ref,
     dks, dvs, hbTs, ois, hb2Ts, actss, dbTs, duss, dabTs, dqss, pbss, kvss, slp) = rest
    step = pl.program_id(0)
    blocks = [(s, b, min(16, FS - b)) for s in range(0, keys, 16) for b in range(0, FS, 16)]

    @pl.when(step == 0)
    def _():
        for ref in (dwq, dwo, dw1, dw2, dnp, dwkv):
            ref[...] = jnp.zeros_like(ref)
        for ref in (hb2Ts, actss, dbTs, duss, dabTs, dqss, dks, dvs):
            ref[1] = jnp.zeros_like(ref[1])
        for ref in (hbTs, ois):
            ref[2] = jnp.zeros_like(ref[2])
        hk_ref[:, :, D:DP] = jnp.zeros((FS, keys, DP - D), BF)
        for s, b, n in blocks:
            own = slot_ref[s // 2 : s // 2 + 8, b : b + n, :]
            own = jnp.concatenate([own[:, :, 0:D], own[:, :, D : 2 * D]], 0)
            if n < 16:
                own = jnp.concatenate([own, jnp.zeros((16, 16 - n, D), BF)], 1)
            hk_ref[b : b + n, s : s + 16, 0:D] = turn_block(perm_ref, own, 16)[0:n]
        for s in range(0, keys, 16):
            flag = slot_ref[s // 2 : s // 2 + 8, F, :].astype(F32)
            for i, at in enumerate((0, DP)):
                bias_ref[s + 8 * i : s + 8 * i + 8] = jnp.where(flag[:, at : at + 128] > 0.5, 0.0, -1e30)

    masks = half_masks()
    LW = 2 * RW
    left = lax.broadcasted_iota(jnp.int32, (1, LW), 1) < RW
    HK = H * keys
    cur, prev = lax.rem(step, 2), lax.rem(step + 1, 2)
    cur3, next3, prev3 = [lax.rem(step + i, 3) for i in range(3)]
    hb2T, acts, dbT, dus, dabT, dqs = [r.at[cur] for r in (hb2Ts, actss, dbTs, duss, dabTs, dqss)]

    def step_rows(at):
        return hk_ref[pl.ds(pl.multiple_of(at * FB, FB), FB)].reshape(FB * keys, DP)

    def keys_values(at, to):
        kvss[to] = mm(step_rows(at), wkv_ref[...]).astype(BF)

    def spreads(to, j, first):
        return [
            spread_halves(kvss[to, (2 * j + c) * keys : (2 * j + c + 1) * keys, first : first + DP], masks)
            for c in range(2)
        ]

    def attend(j, ref, qref, to, to3):
        h = ref[2 * j : 2 * j + 2].reshape(LW, DP)
        q = qref[2 * j : 2 * j + 2].reshape(LW, DP)
        ks = spreads(to, j, 0)
        hbTs[to3, :, j * LW : (j + 1) * LW] = h.T[0:D]
        yield
        st = jnp.where(left, mm_nt(ks[0], q), mm_nt(ks[1], q))
        yield
        vs = spreads(to, j, DP)
        pbs = []
        for hh in range(H):
            s = st[hh * keys : (hh + 1) * keys] + bias_ref[...]
            e = jnp.exp2(s - jnp.max(s, 0, keepdims=True))
            pbs.append((e * (1.0 / jnp.sum(e, 0, keepdims=True))).astype(BF))
            if hh % 2:
                yield
        pb = jnp.concatenate(pbs, 0)
        pbss[to, j] = pb
        pt = pb.T
        yield
        o = jnp.concatenate([mm(pt[:RW], vs[0]), mm(pt[RW:], vs[1])], 0).astype(BF)
        ois[to3, j * LW : (j + 1) * LW] = o
        yield

    @pl.when(step == 0)
    def _():
        keys_values(0, 0)
        weave([(attend(j, ht_ref, q_ref, 0, 0), 0, 1) for j in range(FB // 2)])

    def dense(i, out):
        c0 = i * 2 * LW
        g1v, b1v, g2v, b2v = [vec_ref[i] for i in range(2, 6)]
        h = ht_ref[4 * i:4 * i + 4].reshape(2 * LW, DP)
        o = ois[cur3, c0 : c0 + 2 * LW]
        aT = mm_nt(woI_ref[...], jnp.concatenate([o, h], 1))
        yield
        n2, rc2, h2, hb2 = [], [], [], []
        for t in range(2):
            n, rc = norm_t(aT[:, t * LW:(t + 1) * LW])
            hh = n * g1v + b1v
            n2.append(n.astype(BF)); rc2.append(rc); hb2.append(hh.astype(BF))
            yield
        hb2 = jnp.concatenate(hb2, 1)
        hb2T[:, c0:c0 + 2 * LW] = hb2
        hb2 = tall(hb2)
        C = CC
        u = mm(w1T_ref[0:C], hb2)
        for c in range(FF // C):
            un = mm(w1T_ref[C * c + C:C * c + 2 * C], hb2) if c + 1 < FF // C else None
            act, slope = gelu_parts(u.astype(BF))
            acts[C * c:C * c + C, c0:c0 + 2 * LW] = act
            slp[C * c:C * c + C, c0:c0 + 2 * LW] = slope
            u = un
            yield
        gT = ct_ref[4 * i:4 * i + 4].reshape(2 * LW, DP).T[0:D].astype(F32)
        z = mm(w2T_ref[...], acts[:, c0:c0 + 2 * LW])
        yield
        dbs, d3s = [], []
        ys = []
        for t in range(2):
            sl = slice(t * LW, (t + 1) * LW)
            n3, rc3 = norm_t(hb2[0:D, sl].astype(F32) + z[:, sl])
            ys.append((n3 * g2v + b2v).astype(BF))
            yield
            g = gT[:, sl]
            dnp[2] += g * n3
            dnp[3] += g
            d3 = norm_back_t(g, n3, rc3, g2v)
            dbs.append(d3.astype(BF))
            yield
        db = jnp.concatenate(dbs, 1)
        dbT[:, c0:c0 + 2 * LW] = db
        db = tall(db)
        w = mm(w2_ref[0:C], db)
        for c in range(FF // C):
            wn = mm(w2_ref[C * c + C:C * c + 2 * C], db) if c + 1 < FF // C else None
            dus[C * c:C * c + C, c0:c0 + 2 * LW] = w.astype(BF) * slp[C * c:C * c + C, c0:c0 + 2 * LW]
            w = wn
            yield
        dh = mm(w1_ref[...], dus[:, c0:c0 + 2 * LW])
        yT = tall(jnp.concatenate(ys, 1))
        y_ref[4 * i:4 * i + 4] = yT.T.reshape(4, RW, DP)
        yield
        dabs = []
        for t in range(2):
            dh2 = dbs[t].astype(F32) + dh[:, t * LW:(t + 1) * LW]
            n2f = n2[t].astype(F32)
            dnp[0] += dh2 * n2f
            dnp[1] += dh2
            dabs.append(norm_back_t(dh2, n2f, rc2[t], g1v).astype(BF))
            yield
        dab = jnp.concatenate(dabs, 1)
        dabT[:, c0:c0 + 2 * LW] = dab
        doT = mm(wo_ref[...], tall(dab)).astype(BF)
        out.extend([dab, doT])
        yield
    def back(j, doT, out):
        q, pb = q_ref[2 * j : 2 * j + 2].reshape(LW, DP), pbss[cur, j]
        ks, vs = spreads(cur, j, 0), spreads(cur, j, DP)
        do = tall(doT)
        don = do.T
        dp = jnp.where(left, mm(vs[0], do), mm(vs[1], do))
        yield
        slot_sums(dvs, j, pb, don, None)
        yield
        dss = []
        for hh in range(H):
            sl = slice(hh * keys, (hh + 1) * keys)
            p, d = pb[sl].astype(F32), dp[sl]
            dss.append((p * (d - jnp.sum(p * d, 0, keepdims=True))).astype(BF))
            if hh % 2: yield
        ds = jnp.concatenate(dss, 0)
        dst = ds.T
        yield
        slot_sums(dks, j, ds, q, 0.6931471805599453)
        yield
        dq = jnp.concatenate([mm(dst[:RW], ks[0]), mm(dst[RW:], ks[1])], 0) * SCALE
        dq = dq.astype(BF)
        dqs[j * LW:(j + 1) * LW] = dq
        out.append(dq)
        yield
    lane = lax.broadcasted_iota(jnp.int32, (1, 128), 1)
    zq = jnp.zeros((RW, 128), BF)
    def slot_sums(ref, j, w, rows, scale):
        out = [[], []]
        for t, heads in ((0, 4), (1, 2)):
            r = rows[:, 128 * t:128 * t + 128]
            both = jnp.concatenate([jnp.concatenate([r[:RW], zq], 0), jnp.concatenate([zq, r[RW:]], 0)], 1)
            full = mm(w[4 * t * keys:(4 * t + heads) * keys], both)
            for c in range(2):
                col = full[:, 128 * c:128 * c + 128]
                v = col[0:keys]
                for hh in range(1, heads):
                    v = jnp.where(lane >= E * hh, col[hh * keys:(hh + 1) * keys], v)
                out[c].append(v)
        for c in range(2):
            v = jnp.concatenate(out[c], 1)
            ref[cur, 2 * j + c] = (v if scale is None else v * scale).astype(BF)
    def finish(i, dqv, dab):
        dq = jnp.concatenate(dqv, 0)
        g1 = mm(dq, wqT_ref[...]) + tall(dab).T.astype(F32)
        g1_ref[4 * i:4 * i + 4] = g1.astype(BF).reshape(4, RW, DP)
        yield
    def chunk(i):
        out = []
        yield from dense(i, out)
        dab, doT = out
        dq = []
        for t in range(2):
            yield from back(2 * i + t, doT[:, t * LW : (t + 1) * LW], dq)
        yield from finish(i, dq, dab)

    def wgrad(at, b, b3):
        dwq[...] += mm(hbTs[b3], dqss[b])
        yield
        dwo[...] += mm(dabTs[b], ois[b3])
        yield
        for c in range(0, FF, WC):
            dw1[c : c + WC] += mm_nt(duss[b, c : c + WC], hb2Ts[b])
            yield
        for c in range(0, FF, WC):
            dw2[c : c + WC] += mm_nt(actss[b, c : c + WC], dbTs[b])
            yield
        dkv = jnp.concatenate([r[b].reshape(FB * keys, DP) for r in (dks, dvs)], 1)
        dwkv[...] += mm_tn(step_rows(at), dkv)
        yield
        back_rows = mm(dkv, wkvT_ref[...]).astype(BF).reshape(FB, keys, DP)
        bk_ref[pl.ds(pl.multiple_of(at * FB, FB), FB)] = back_rows
        yield

    def ahead():
        keys_values(jnp.minimum(step + 1, pl.num_programs(0) - 1), prev)
        yield

    NC = FB // 4
    streams = [(ahead(), 0, 1)] + [(chunk(i), i * OFF, 1) for i in range(NC)]
    streams += [(attend(j, next_ref, qnext_ref, prev, next3), AO + j * AS, 1) for j in range(FB // 2)]
    streams += [(wgrad(jnp.maximum(step - 1, 0), prev, prev3), WP, 1)]
    weave(streams)

    @pl.when(step == pl.num_programs(0) - 1)
    def _():
        for _ in wgrad(step, cur, cur3):
            pass
        for s, b, n in blocks:
            own = bk_ref[b : b + n, s : s + 16, :]
            if n < 16:
                own = jnp.concatenate([own, jnp.zeros((16 - n, 16, DP), BF)], 0)
            own = turn_block(perm_ref, own, 16)[:, 0:n, 0:D]
            back_ref[s // 2 : s // 2 + 8, b : b + n, :] = jnp.concatenate([own[0:8], own[8:16]], 2)
        at = 0
        for ref in (dw1, dw2):
            t = ref[...].astype(BF).T.astype(F32)
            for j in range(FF // 128):
                pack_ref[at : at + D] = t[:, 128 * j : 128 * j + 128]
                at += D
        pack_pair(pack_ref, at, dwq, tall(dwo[...]).T)
        pack_pair(pack_ref, at + PAIR, dwkv[:, 0:DP], dwkv[:, DP:])
        pack_norms(pack_ref, at + 2 * PAIR, [dnp[i] for i in range(4)])
        hand_out(table_ref, pack_ref, piece_refs)


def item_and_dense(table, ht, qt, ct, slots, perm, ws, vec, packed, tables, OFF=0, CC=384, WC=192):
    RW = ht.shape[1]
    keys = 2 * slots.shape[0]
    FB, AO, AS, WP = (20, 2, 2, 2) if keys <= 32 else (8, 2, 6, 4)
    M = FB * RW
    cells = pl.BlockSpec((FB, RW, DP), lambda i: (i, 0, 0))
    accs = [(D, DP), (D, DP), (FF, D), (FF, D), (4, D, 128), (DP, 2 * DP), (keys, 128), (packed, 128)]
    kept = [(3, D, M), (3, M, DP)] + [(2,) + a for a in ((D, M), (FF, M), (D, M), (FF, M), (D, M), (M, DP))]
    kept += [(2, FB // 2, H * keys, 2 * RW), (2, FB * keys, 2 * DP), (FF, M)]
    ahead = pl.BlockSpec((FB, RW, DP), lambda i: (jnp.minimum(i + 1, FS // FB - 1), 0, 0))
    flat = [slots, perm, *ws, vec]
    outs = [shape((FS, RW, DP))] * 2 + [shape(slots.shape)] + [shape((packed // tables, 128))] * tables
    return pl.pallas_call(
        functools.partial(item_kernel, FB, RW, keys, tables, OFF, AO, AS, WP, CC, WC),
        grid=(FS // FB,),
        in_specs=[pl.BlockSpec(memory_space=pltpu.SMEM), cells, ahead, cells, ahead, cells] + [whole(a) for a in flat],
        out_specs=[cells, cells] + [whole(a) for a in outs[2:]],
        out_shape=outs,
        scratch_shapes=[pltpu.VMEM(a, F32) for a in accs]
        + [pltpu.VMEM((FS, keys, DP), BF)] * 2
        + [pltpu.VMEM((2, FB, keys, DP), BF)] * 2
        + [pltpu.VMEM(a, BF) for a in kept],
        compiler_params=params(),
        cost_estimate=cost(66),
        name="item_and_dense",
    )(table, ht, ht, qt, qt, ct, *flat)


def backward_rows(
    x_ref, n_ref, qkv_ref, p_ref, l_ref, of_ref, wqkvI_ref, wo_ref, vec_ref, cg_ref, xs, os, dqs, das, dqkv, dwo, dnp, grad_of, base_ref=None
):
    def pair(c):
        at = slice(2 * c * FP, (2 * c + 2) * FP)
        dabs = []
        for u in range(2):
            r = 2 * c + u
            xs[:, r * FP : r * FP + F] = x_ref[r]
            os[:, r * FP : (r + 1) * FP] = of_ref[r]
            g = grad_of(r)
            n = n_ref[r, 0:D, :].astype(F32)
            rc = n_ref[r, D : D + 16, :].astype(F32)[0:1]
            dnp[0] += g * n
            dnp[1] += g
            dabs.append(norm_back_t(g, n, rc, vec_ref[0]).astype(BF))
            yield
        dab = jnp.concatenate(dabs, 1)
        das[:, at] = dab
        do = mm(wo_ref[...], tall(dab))
        yield
        for u in range(2):
            r = 2 * c + u
            own = slice(u * FP, (u + 1) * FP)
            lanes_r = slice(r * FP, (r + 1) * FP)
            for j in range(H // 2):
                inv = l_ref[r, j : j + 1, :]
                parts, offs = [], []
                for t in range(2):
                    hs = slice(64 * j + 32 * t, 64 * j + 32 * t + 32)
                    d = do[hs, own] * inv[:, t * FP : (t + 1) * FP]
                    offs.append(jnp.sum(d * of_ref[r, hs, :].astype(F32), 0, keepdims=True))
                    parts.append(d.astype(BF))
                dom = two_heads(*parts)
                off = jnp.concatenate(offs, 1).astype(BF)
                dp = mm(qkv_ref[r, 2 * D + 64 * j : 2 * D + 64 * j + 64, :].T, dom)
                yield
                e = p_ref[r, :, 256 * j : 256 * j + 256]
                ds = e * (dp.astype(BF) - off)
                dv = mm_nt(dom, e)
                yield
                qm = two_heads(
                    qkv_ref[r, 64 * j : 64 * j + 32, :], qkv_ref[r, 64 * j + 32 : 64 * j + 64, :]
                )
                dk = mm_nt(qm, ds) * 0.6931471805599453
                dq = mm(qkv_ref[r, D + 64 * j : D + 64 * j + 64, :], ds)
                dq = jnp.concatenate([dq[0:32, 0:128], dq[32:64, 128:256]], 0) * SCALE
                yield
                for i, d in enumerate((dq, dk, dv)):
                    dqs[i * D + 64 * j : i * D + 64 * j + 64, lanes_r] = d.astype(BF)
        yield
        cg = mm(wqkvI_ref[...], jnp.concatenate([dqs[:, at], dab], 0))
        for u in range(2):
            own = cg[:, u * FP : u * FP + F]
            cg_ref[2 * c + u] = own if base_ref is None else own + base_ref[2 * c + u]
        yield

    def sums(at):
        dqkv[...] += mm_nt(dqs[:, at], xs[:, at])
        yield
        dwo[...] += mm_nt(os[:, at], das[:, at])
        yield

    return pair, sums


def backward_kernel(
    R, OFF, YO, x_ref, n_ref, qkv_ref, p_ref, l_ref, of_ref, g1t_ref, yt_ref, wqkvI_ref, wo_ref, vec_ref, perm_ref,
    cg_ref, y_ref, dqkv, dwo, dnp, gs, ys, xs, os, dqs, das,
):
    @pl.when(pl.program_id(0) == 0)
    def _():
        for ref in (xs, dqkv, dwo, dnp):
            ref[...] = jnp.zeros_like(ref)

    col = lax.broadcasted_iota(jnp.int32, (16, 1, 1), 0)

    def turn(ref, out, j):
        block = ref[16 * j : min(16 * j + 16, FS)]
        if block.shape[0] < 16:
            block = jnp.concatenate([block, jnp.zeros((16 - block.shape[0],) + block.shape[1:], BF)], 0)
        if 16 * j + 16 > F:
            block = jnp.where(col < F - 16 * j, block, 0).astype(BF)
        out[:, 16 * j : 16 * j + 16, :] = turn_block(perm_ref, block, 16)

    for j in range(FP // 16):
        turn(g1t_ref, gs, j)

    def outputs():
        for j in range(FP // 16):
            turn(yt_ref, ys, j)
            yield
        for r in range(R):
            y_ref[r] = ys[r].T[0:D, 0:F]
            yield

    pair, sums = backward_rows(
        x_ref, n_ref, qkv_ref, p_ref, l_ref, of_ref, wqkvI_ref, wo_ref, vec_ref, cg_ref, xs, os, dqs, das, dqkv, dwo, dnp,
        lambda r: gs[r].T[0:D].astype(F32),
    )
    streams = [(pair(c), c * OFF, 1) for c in range(R // 2)]
    streams.append((outputs(), YO, 1))
    weave(streams)
    for _ in sums(slice(0, R * FP)):
        pass


def feature_backward(x, saved, g1t, yt, wqkvI, wo, vec, perm, R=16, OFF=2, YO=3):
    rows = x.shape[0]
    nat = lambda a: pl.BlockSpec((R,) + a.shape[1:], lambda i: (i, 0, 0))
    turned = pl.BlockSpec((FS, R, DP), lambda i: (0, i, 0))
    accs = [shape((3 * D, D), F32), shape((D, D), F32), shape((2, D, FP), F32)]
    shared = [wqkvI, wo, vec, perm]
    M = R * FP
    return pl.pallas_call(
        functools.partial(backward_kernel, R, OFF, YO),
        grid=(rows // R,),
        in_specs=[nat(x)] + [nat(a) for a in saved] + [turned] * 2 + [whole(a) for a in shared],
        out_specs=[nat(x), nat(x)] + [whole(a) for a in accs],
        out_shape=[shape(x.shape, F32), shape(x.shape)] + accs,
        scratch_shapes=[pltpu.VMEM(a, BF) for a in ((R, FP, DP), (R, FP, DP), (D, M), (D, M), (3 * D, M), (D, M))],
        compiler_params=params(),
        cost_estimate=cost(60 * rows // R),
        name="feature_backward",
    )(x, *saved, g1t, yt, *shared)


def slots_back_kernel(
    SL, tables, table_ref, x_ref, n_ref, qkv_ref, p_ref, l_ref, of_ref, slot_ref, base_ref, iqkv, iwo, inp, wqkvI_ref, wo_ref, vec_ref,
    cg_ref, *rest,
):
    piece_refs, rest = rest[:tables], rest[tables:]
    pack_ref, xs, os, dqs, das, dqkv, dwo, dnp = rest
    xs[...] = jnp.zeros_like(xs)
    for ref, init in ((dqkv, iqkv), (dwo, iwo), (dnp, inp)):
        ref[...] = init[...]
    both = slot_ref[0].astype(F32)
    for i in range(1, slot_ref.shape[0]):
        both = both + slot_ref[i].astype(F32)
    z0 = jnp.zeros((FP - FS, 2 * D), F32)
    live = lax.broadcasted_iota(jnp.int32, (1, FP), 1) < F
    back = []
    for c in range(SL // 2):
        t = jnp.where(live, jnp.concatenate([both[c], z0], 0).T, 0.0)
        back += [t[0:D], t[D : 2 * D]]
    pair, sums = backward_rows(
        x_ref, n_ref, qkv_ref, p_ref, l_ref, of_ref, wqkvI_ref, wo_ref, vec_ref, cg_ref, xs, os, dqs, das, dqkv, dwo, dnp,
        lambda r: back[r], base_ref,
    )
    weave([(pair(c), 0, 1) for c in range(SL // 2)])
    for _ in sums(slice(0, SL * FP)):
        pass
    zc = jnp.zeros((D, DP - D), F32)
    three = [jnp.concatenate([dqkv[i * D : (i + 1) * D], zc], 1).T for i in range(3)]
    pack_pair(pack_ref, 0, three[0], three[1])
    pack_pair(pack_ref, PAIR, three[2], dwo)
    pack_norms(pack_ref, 2 * PAIR, [dnp[0], dnp[1]])
    hand_out(table_ref, pack_ref, piece_refs)


def slots_backward(table, x, saved, slots, prev, wqkvI, wo, vec, packed, tables):
    SL = 2 * slots.shape[1]
    nat = lambda a: pl.BlockSpec((SL,) + a.shape[1:], lambda i: (i, 0, 0))
    cg, *accs = prev
    flat = list(accs) + [wqkvI, wo, vec]
    pieces = [shape((packed // tables, 128))] * tables
    M = SL * FP
    ins = [table, x, *saved, slots, cg, *flat]
    return pl.pallas_call(
        functools.partial(slots_back_kernel, SL, tables),
        grid=(1,),
        in_specs=[pl.BlockSpec(memory_space=pltpu.SMEM), nat(x)]
        + [nat(a) for a in saved]
        + [whole(slots), nat(cg)]
        + [whole(a) for a in flat],
        out_specs=[nat(cg)] + [whole(a) for a in pieces],
        out_shape=[shape(cg.shape, F32)] + pieces,
        input_output_aliases={len(saved) + 3: 0},
        scratch_shapes=[pltpu.VMEM((packed, 128), F32)]
        + [pltpu.VMEM(a, BF) for a in ((D, M), (D, M), (3 * D, M), (D, M))]
        + [pltpu.VMEM(a.shape, F32) for a in accs],
        compiler_params=params(),
        cost_estimate=cost(8),
        name="slots_backward",
    )(*ins)


def table_sums(tables, pieces):
    sent = []
    for i, a in enumerate(pieces):
        to = [(t, (t // 2 + i // 2) % (tables // 2) * 2 + (t + i) % 2) for t in range(tables)]
        sent.append(lax.ppermute(a, "table", to) if i else a)
    return sent


def join_kernel(tables, *refs):
    out_ref = refs[-1]
    at = 0
    for group in (refs[:tables], refs[tables : 2 * tables]):
        total = group[0][...].astype(F32)
        for ref in group[1:]:
            total = total + ref[...].astype(F32)
        rows = total.shape[0] // out_ref.shape[0]
        for i in range(out_ref.shape[0]):
            out_ref[i, at : at + rows] = total[i * rows : (i + 1) * rows].astype(BF)
        at += rows


def join_tables(shards, mids, tails):
    rows = (mids[0].shape[0] + tails[0].shape[0]) // shards
    return pl.pallas_call(
        functools.partial(join_kernel, len(mids)),
        out_shape=shape((shards, rows, 128)),
        compiler_params=params(16),
        cost_estimate=cost(2),
        name="join_tables",
    )(*mids, *tails)


def sum_kernel(parts_ref, out_ref):
    total = parts_ref[0].astype(F32)
    for i in range(1, parts_ref.shape[0]):
        total = total + parts_ref[i].astype(F32)
    total = total.astype(BF)
    for i in range(out_ref.shape[0]):
        out_ref[i] = total


def sum_rows(parts):
    parts = lax.all_to_all(parts, "rows", 0, 0)
    return pl.pallas_call(
        sum_kernel,
        out_shape=shape(parts.shape),
        compiler_params=params(16),
        cost_estimate=cost(2),
        name="sum_rows",
    )(parts)


def gather_all(copies):
    tables = lax.axis_size("table")
    ny = tables // 2
    own = lax.all_to_all(copies, "rows", 0, 0)
    pieces = [own]
    for s in range(1, ny):
        pieces.append(lax.ppermute(own, "table", [(t, (t // 2 + s) % ny * 2 + t % 2) for t in range(tables)]))
    other = [lax.ppermute(a, "table", [(t, t ^ 1) for t in range(tables)]) for a in pieces]
    return [a for pair in zip(pieces, other) for a in pair]


def to_row(c):
    return jnp.broadcast_to(c, (c.shape[0], 128)).T[0:1]


def to_col(r):
    return jnp.broadcast_to(r, (128, r.shape[1])).T[:, 0:1]


def clipped(update, weight, count):
    def total(v):
        return jnp.sum(jnp.sum(v, 0, keepdims=True), 1, keepdims=True)

    rms = jnp.sqrt(total(update * update) * (1.0 / count))
    weight_rms = jnp.sqrt(total(weight * weight) * (1.0 / count))
    return update * (RATE * jnp.maximum(0.001, weight_rms) / jnp.maximum(1.0, rms / CLIP))


def optimizer_kernel(
    tables, mid_rows, *refs):
    table_ref, *refs = refs
    piece_refs, refs = refs[:tables], refs[tables:]
    mid_ref, tail_ref = refs[-2:]
    table = table_ref[0]
    ny = tables // 2
    for i, ref in enumerate(piece_refs):
        place = pair_up(table, i, ny, True)
        for out, at, end in ((mid_ref, 0, mid_rows), (tail_ref, mid_rows, ref.shape[1])):
            rows = ref.shape[0] * (end - at)
            start = pl.multiple_of(place * rows, 8)
            out[pl.ds(start, rows)] = ref[:, at:end, :].astype(F32).reshape(rows, 128)
    optimizer_steps(*refs)


def optimizer_steps(
    proj_ref, outw_ref, in_ref, hid_ref, norm_ref, sr_ref, sc_ref, mm_ref, mh_ref, ns_ref,
    proj_g, out_g, in_g, hid_g, norm_g, proj_n, out_n, in_n, hid_n, norm_n, sr_n, sc_n, mm_n, mh_n, ns_n, mid_ref, tail_ref,
):
    decay = 1.0 - STEP ** (-0.8)

    def stats(grad, col_old, row_old):
        square = grad * grad + 1e-30
        a, b = grad.shape
        over_sub = decay * row_old + (1.0 - decay) * (jnp.sum(square, 0, keepdims=True) * (1.0 / a))
        over_lane = decay * col_old + (1.0 - decay) * (jnp.sum(square, 1, keepdims=True) * (1.0 / b))
        return over_lane, over_sub

    def scaled(grad, col, row, mean):
        return grad * lax.rsqrt(col * (1.0 / mean)) * lax.rsqrt(row)

    def square_step(i, ref, at, first):
        g_ref, n_ref, w_ref, j = (proj_g, proj_n, proj_ref, i) if i < 6 else (out_g, out_n, outw_ref, i - 6)
        low = ref[at : at + D] if first else ref[at + D : at + 2 * D]
        high = ref[at + 2 * D : at + 3 * D]
        grad = jnp.concatenate([low, high[:, 0:64] if first else high[:, 64:128]], 1)
        g_ref[j] = grad
        yield
        col, row = stats(grad, to_col(sr_ref[i : i + 1, :]), sc_ref[i : i + 1, :])
        sr_n[i : i + 1, :] = to_row(col)
        sc_n[i : i + 1, :] = row
        yield
        mean = jnp.sum(col, 0, keepdims=True) * (1.0 / D)
        update = scaled(grad, col, row, mean)
        yield
        w = w_ref[j]
        n_ref[j] = w - clipped(update, w, D * D)
        yield

    def wide_step(i, at, w_ref, g_ref, n_ref):
        for j in range(6):
            g_ref[:, 128 * j : 128 * j + 128] = mid_ref[at + D * j : at + D * j + D]
            yield
        grad = g_ref[...]
        col, row = stats(grad, to_col(mm_ref[i : i + 1, :]), mh_ref[i : i + 1, :])
        mm_n[i : i + 1, :] = to_row(col)
        mh_n[i : i + 1, :] = row
        yield
        mean = jnp.sum(col, 0, keepdims=True) * (1.0 / D) if i == 0 else jnp.sum(row, 1, keepdims=True) * (1.0 / FF)
        update = scaled(grad, col, row, mean)
        yield
        w = w_ref[...]
        n_ref[...] = w - clipped(update, w, D * FF)
        yield

    steps = [wide_step(0, 0, in_ref, in_g, in_n), wide_step(1, 6 * D, hid_ref, hid_g, hid_n)]
    places = ((0, tail_ref, 0, True), (1, tail_ref, 0, False), (2, tail_ref, PAIR, True), (6, tail_ref, PAIR, False))
    places += ((3, mid_ref, 12 * D, True), (7, mid_ref, 12 * D, False))
    places += ((4, mid_ref, 12 * D + PAIR, True), (5, mid_ref, 12 * D + PAIR, False))
    steps += [square_step(*a) for a in places]
    weave([(g, WV * i, 1) for i, g in enumerate(steps)])

    pieces = []
    for ref, at, count in ((tail_ref, 2 * PAIR, 2), (mid_ref, 12 * D + 2 * PAIR, 4)):
        v = ref[at : at + 16].astype(F32)
        for i in range(count):
            pieces.append(jnp.concatenate([v[2 * i : 2 * i + 1], v[2 * i + 1 : 2 * i + 2, 0:64]], 1))
    grad = jnp.concatenate(pieces, 0)
    norm_g[...] = grad
    second = decay * ns_ref[...] + (1.0 - decay) * (grad * grad + 1e-30)
    ns_n[...] = second
    update = grad * lax.rsqrt(second)
    rms = jnp.sqrt(jnp.sum(update * update, 1, keepdims=True) * (1.0 / D))
    w = norm_ref[...]
    w_rms = jnp.sqrt(jnp.sum(w * w, 1, keepdims=True) * (1.0 / D))
    norm_n[...] = w - update * (RATE * jnp.maximum(0.001, w_rms) / jnp.maximum(1.0, rms / CLIP))


def optimizer(table, pieces, mid_rows, *state):
    proj, outw, w_in, w_outT, norms, sr, sc, ms, hs, ns = state
    shards, rows, _ = pieces[0].shape
    order = [proj, outw, w_in, w_outT, norms, proj, outw, w_in, w_outT, norms, sr, sc, ms, hs, ns]
    outs = pl.pallas_call(
        functools.partial(optimizer_kernel, len(pieces), mid_rows),
        in_specs=[pl.BlockSpec(memory_space=pltpu.SMEM)] + [whole(a) for a in (*pieces, *state)],
        out_shape=[shape(a.shape, F32) for a in order],
        scratch_shapes=[
            pltpu.VMEM((len(pieces) * shards * mid_rows, 128), F32),
            pltpu.VMEM((len(pieces) * shards * (rows - mid_rows), 128), F32),
        ],
        compiler_params=params(28),
        cost_estimate=cost(8), name="optimizer",
    )(table, *pieces, *state)
    outs = list(outs)
    for i in (3, 8):
        outs[i] = outs[i].T
    return outs


def on_device(n, cells, cotangent, train_count, key_mask, train_order, *state):
    state = list(state)
    state[3] = state[3].T
    proj, outw, w_in, w_outT, norms = state[:5]
    x = jnp.swapaxes(cells[0], 1, 2)
    cot = jnp.swapaxes(cotangent[0], 1, 2)
    rows_here = x.shape[0]
    unit = 8 * n
    tail_rows = -(-TAIL // unit) * unit
    mid_rows = -(-MID // unit) * unit
    perm = perm_matrix()
    shards, tables = lax.axis_size("rows"), lax.axis_size("table")
    table = lax.axis_index("table").astype(jnp.int32).reshape(1)
    own, wqkvT, woT, vec = slot_rows(shards, train_count, key_mask, train_order, x, proj, outw, norms)
    slots = lax.all_to_all(own, "rows", 0, 0).reshape((-1,) + own.shape[2:])
    w_in, _ = lax.optimization_barrier((w_in, own))
    wqkvI, wo, *ws = other_weights(proj, outw, w_in, w_outT)
    wkv2, wkv2T, wq2, *ws = ws
    ht, ct, qt, *saved = feature_forward(x, cot, (wqkvT, woT, vec, perm, wq2))
    yt, g1t, back, *mids = item_and_dense(table, ht, qt, ct, slots, perm, (*ws, wkv2, wkv2T), vec, mid_rows, tables)
    back = lax.all_to_all(back.reshape(own.shape), "rows", 0, 0)
    mids = table_sums(tables, mids)
    cg, y, *accs = feature_backward(x, saved, g1t, yt, wqkvI, wo, vec, perm)
    mids, accs = lax.optimization_barrier((mids, accs))
    cg, *tails = slots_backward(table, x, saved, back, (cg, *accs), wqkvI, wo, vec, tail_rows, tables)
    tails = table_sums(tables, tails)
    pieces = gather_all(sum_rows(join_tables(shards, mids, tails)))
    return (jnp.swapaxes(y, 1, 2)[None], jnp.swapaxes(cg, 1, 2)[None], *optimizer(table, pieces, mid_rows // n, *state))


def solution(mesh):
    n = int(mesh.shape["table"] * mesh.shape["rows"])
    cells = P("table", "rows", None, None)
    return jax.shard_map(
        functools.partial(on_device, n),
        mesh=mesh,
        in_specs=(cells, cells, P("table"), P("table", "rows"), P("table", "rows")) + (P(),) * 10,
        out_specs=(cells, cells) + (P(),) * 15,
        check_vma=False,
    )
```

```python
import functools

import jax
import jax.numpy as jnp
import numpy as np
from jax import lax
from jax.experimental import pallas as pl
from jax.experimental.pallas import tpu as pltpu
from jax.sharding import PartitionSpec as P

BF, F32 = jnp.bfloat16, jnp.float32
D, DP = 192, 256
H, E = 6, 32
F, FP = 119, 128
FS = 120
FF = 768
STEP = 3
CLIP = 0.3
RATE = 0.5
WV = 0
SCALE = E**-0.5
SCALE2 = SCALE * 1.4426950408889634
C0 = 0.7978845608028654
C1 = 0.044715
NT = (((1,), (1,)), ((), ()))
TN = (((0,), (0,)), ((), ()))
PAIR = 576
TAIL = 2 * PAIR + 8
MID = 2 * 6 * D + 2 * PAIR + 8


def mm(a, b):
    return jnp.dot(a, b, preferred_element_type=F32)


def mm_nt(a, b):
    return lax.dot_general(a, b, NT, preferred_element_type=F32)


def mm_tn(a, b):
    return lax.dot_general(a, b, TN, preferred_element_type=F32)


def lanes():
    return lax.broadcasted_iota(jnp.int32, (1, DP), 1)


def whole(a):
    nd = len(a.shape)
    return pl.BlockSpec(a.shape, lambda *i: (0,) * nd)


def half_masks():
    lane = lax.broadcasted_iota(jnp.int32, (1, 128), 1)
    return [jnp.where((lane >= E * h) & (lane < E * (h + 1)), 1.0, 0.0).astype(BF) for h in range(4)]


def spread_halves(w, masks):
    z = jnp.zeros((w.shape[0], 128), BF)
    lo, hi = w[:, 0:128], w[:, 128:256]
    return jnp.concatenate(
        [jnp.concatenate([lo * masks[h], z], 1) for h in range(4)]
        + [jnp.concatenate([z, hi * masks[h]], 1) for h in range(2)], 0)


def mean0(a): return jnp.sum(a, 0, keepdims=True) * (1.0 / D)


def norm_t(a):
    c = a - mean0(a)
    rc = lax.rsqrt(mean0(c * c) + 1e-5)
    return c * rc, rc


def norm_back_t(g, n, rc, gain):
    dn = g * gain
    return (dn - mean0(dn) - n * mean0(dn * n)) * rc


def tall(a):
    return jnp.concatenate([a, jnp.zeros((DP - D, a.shape[1]), a.dtype)], 0)


def gelu_parts(u):
    uu = u * u
    th = jnp.tanh(u * (BF(C0) + BF(C0 * C1) * uu))
    half = BF(0.5) + BF(0.5) * th
    act = u * half
    slope = half + act * (BF(1.0) - th) * (BF(C0) + BF(3.0 * C0 * C1) * uu)
    return act, slope


def weave(streams):
    live=[[g,s,p] for g,s,p in streams]
    turn=0
    while live:
        for it in list(live):
            if turn>=it[1]:
                for _ in range(it[2]):
                    try: next(it[0])
                    except StopIteration:
                        live.remove(it); break
        turn+=1

def shape(s, t=BF):
    return jax.ShapeDtypeStruct(s, t)


def params(mib=58):
    return pltpu.CompilerParams(vmem_limit_bytes=mib << 20)


def cost(us):
    return pl.CostEstimate(flops=int(us * 1.1e9), bytes_accessed=int(us * 1e6), transcendentals=0)


def perm_matrix():
    place = np.zeros((256, 256), np.float32)
    for f in range(16):
        for r in range(16):
            place[f * 16 + r, r * 16 + f] = 1
    return jnp.asarray(place, BF)


def padded_square(w):
    a = jnp.concatenate([w, jnp.zeros((D, DP - D), F32)], 1).astype(BF)
    a = jnp.concatenate([a, jnp.zeros((DP - D, DP), BF)], 0)
    return a, a.T


def first_weights(proj, outw, norms, wqkvT, woT, vec, nrow):
    for i in range(3):
        wqkvT[i * D : (i + 1) * D, :] = padded_square(proj[i])[1][0:D]
    woT[...] = padded_square(outw[0])[1][0:D]
    nrow[...] = jnp.zeros((8, DP), F32)
    nrow[0:6, 0:D] = norms[...]
    for i in range(6):
        vec[i] = jnp.broadcast_to(nrow[i : i + 1, :], (128, DP)).T[0:D]


def weights_kernel(proj, outw, w_in, w_outT, wqkvI, wo, wkv2, wkv2T, wq2, wq2T, wo2I, wo2, w1T, w1, w2T, w2):
    row = lax.broadcasted_iota(jnp.int32, (D, DP), 0)
    eye = jnp.where(row == lax.broadcasted_iota(jnp.int32, (D, DP), 1), 1.0, 0.0).astype(BF)
    wqkvI[...] = jnp.concatenate([proj[0], proj[1], proj[2], eye[:, 0:D].astype(F32)], 1).astype(BF)
    wo[...] = jnp.concatenate([outw[0], jnp.zeros((D, DP - D), F32)], 1).astype(BF)
    a, t = padded_square(proj[3])
    wq2[...] = a
    wq2T[...] = t
    a, t = padded_square(outw[1])
    wo2[...] = a[0:D]
    wo2I[:, 0:DP] = t[0:D]
    wo2I[:, DP : 2 * DP] = eye
    for i in range(2):
        a, t = padded_square(proj[4 + i])
        wkv2[:, i * DP : (i + 1) * DP] = a
        wkv2T[i * DP : (i + 1) * DP, :] = t
    zw = jnp.zeros((DP - D, FF), BF)
    a = w_in[...].astype(BF)
    w1[...] = a
    w1T[...] = jnp.concatenate([a, zw], 0).T
    a = w_outT[...].astype(BF)
    w2T[...] = a
    w2[...] = jnp.concatenate([a, zw], 0).T


def other_weights(proj, outw, w_in, w_outT):
    sq, half = shape((DP, DP)), shape((D, DP))
    outs = [shape((D, 4 * D)), half, shape((DP, 2 * DP)), shape((2 * DP, DP)), sq, sq]
    outs += [shape((D, 2 * DP)), half, shape((FF, DP)), shape((D, FF)), shape((D, FF)), shape((FF, DP))]
    return pl.pallas_call(
        weights_kernel,
        out_shape=outs,
        compiler_params=params(),
        cost_estimate=cost(4),
        name="other_weights",
    )(proj, outw, w_in, w_outT)


def two_heads(a, b):
    z = jnp.zeros(a.shape, a.dtype)
    return jnp.concatenate([jnp.concatenate([a, z], 1), jnp.concatenate([z, b], 1)], 0)


def feature_pair(x, wqkvT_ref, woT_ref, keep, out):
    qkv = mm(wqkvT_ref[...], x)
    q = (qkv[0:D] * SCALE2).astype(BF)
    k = qkv[D : 2 * D].astype(BF)
    v = qkv[2 * D : 3 * D].astype(BF)
    yield
    row = lax.broadcasted_iota(jnp.int32, (8, 1), 0)
    outs = []
    for u in range(2):
        own = slice(u * FP, (u + 1) * FP)
        keep("qkv", u, (q[:, own], k[:, own], v[:, own]))
        ot = []
        for j in range(H // 2):
            hs = slice(64 * j, 64 * j + 64)
            qm = two_heads(q[64 * j : 64 * j + 32, own], q[64 * j + 32 : 64 * j + 64, own])
            st = mm(k[hs, own].T, qm)
            yield
            last = jnp.where(row < F - FS + 8, st[FS - 8 : FS], -1e30)
            mx = jnp.maximum(jnp.max(st[0 : FS - 8], 0, keepdims=True), jnp.max(last, 0, keepdims=True))
            e = jnp.exp2(st[0 : FS - 8] - mx)
            last = jnp.exp2(last - mx)
            inv = 1.0 / (jnp.sum(e, 0, keepdims=True) + jnp.sum(last, 0, keepdims=True))
            e = jnp.concatenate([e, last, jnp.zeros((FP - FS, 2 * FP), F32)], 0).astype(BF)
            keep("p", (u, j), (e, inv))
            yield
            t = mm(v[hs, own], e)
            ot.append(t[0:32, 0:128] * inv[:, 0:128])
            ot.append(t[32:64, 128:256] * inv[:, 128:256])
            yield
        ot = jnp.concatenate(ot, 0).astype(BF)
        keep("o", u, ot)
        outs.append(ot)
    a = mm(woT_ref[...], tall(jnp.concatenate(outs, 1)))
    yield
    for u in range(2):
        own = slice(u * FP, (u + 1) * FP)
        out.append(norm_t(x[0:D, own].astype(F32) + a[:, own]))
        yield


def slots_kernel(
    SL, count_ref, mask_ref, order_ref, x_ref, proj_ref, outw_ref, norm_ref, out_ref, wqkvT_ref, woT_ref, vec_ref, xs, nrow
):
    xs[...] = jnp.zeros_like(xs)
    first_weights(proj_ref, outw_ref, norm_ref, wqkvT_ref, woT_ref, vec_ref, nrow)
    row = lax.broadcasted_iota(jnp.int32, (FS, 1), 0)
    lane = lax.broadcasted_iota(jnp.int32, (1, 2 * D), 1)

    def flag(r):
        order = order_ref[0, r]
        usable = (order < count_ref[0]) & ((mask_ref[0, r] == 1) | (order == 0))
        return jnp.where(usable, 1.0, 0.0)

    def pair(c):
        for u in range(2):
            xs[c, 0:D, u * FP : u * FP + F] = x_ref[2 * c + u]
        out = []
        yield from feature_pair(xs[c], wqkvT_ref, woT_ref, lambda *a: None, out)
        both = jnp.concatenate([(n * vec_ref[0] + vec_ref[1]).astype(BF) for n, _ in out], 0)
        flags = jnp.where(lane < D, flag(2 * c), flag(2 * c + 1))
        both = jnp.where(row < F, both.T[0:FS].astype(F32), flags).astype(BF)
        for i in range(out_ref.shape[0]):
            out_ref[i, c] = both
        yield

    weave([(pair(c), 0, 1) for c in range(SL // 2)])


def slot_rows(shards, count, mask, order, cells, proj, outw, norms):
    SL = mask.shape[1]
    smem = pl.BlockSpec(memory_space=pltpu.SMEM)
    part = lambda a, k: pl.BlockSpec((k,) + a.shape[1:], lambda i: (0, 0, 0))
    outs = [shape((shards, SL // 2, FS, 2 * D)), shape((3 * D, DP)), shape((D, DP)), shape((6, D, 128), F32)]
    return pl.pallas_call(
        functools.partial(slots_kernel, SL),
        grid=(1,),
        in_specs=[smem, smem, smem, part(cells, SL), part(proj, 3), part(outw, 1), whole(norms)],
        out_specs=[whole(a) for a in outs],
        out_shape=outs,
        scratch_shapes=[pltpu.VMEM((SL // 2, DP, 2 * FP), BF), pltpu.VMEM((8, DP), F32)],
        compiler_params=params(),
        cost_estimate=cost(6),
        name="slot_rows",
    )(count, mask, order, cells, proj, outw, norms)


def turn_block(perm_ref, block, R):
    return mm(perm_ref[...], block.reshape(256, block.shape[-1])).astype(BF).reshape(16, R, block.shape[-1])


def forward_kernel(
    R, OFF, x_ref, c_ref, wqkvT_ref, woT_ref, vec_ref, perm_ref, wq_ref, ht_ref, ct_ref, qt_ref, n_ref, qkv_ref, p_ref, l_ref, of_ref, xs, hs, cp, cs
):
    @pl.when(pl.program_id(0) == 0)
    def _():
        xs[...] = jnp.zeros_like(xs)
        cp[...] = jnp.zeros_like(cp)

    def pair(c):
        for u in range(2):
            xs[c, 0:D, u * FP : u * FP + F] = x_ref[2 * c + u]

        def keep(what, at, val):
            if what == "qkv":
                for i in range(3):
                    qkv_ref[2 * c + at, i * D : (i + 1) * D, :] = val[i]
            elif what == "p":
                u, j = at
                p_ref[2 * c + u, :, 256 * j : 256 * j + 256] = val[0]
                l_ref[2 * c + u, j : j + 1, :] = val[1]
            else:
                of_ref[2 * c + at] = val

        out = []
        yield from feature_pair(xs[c], wqkvT_ref, woT_ref, keep, out)
        for u in range(2):
            r = 2 * c + u
            n, rc = out[u]
            n_ref[r, 0:D, :] = n.astype(BF)
            n_ref[r, D : D + 16, :] = jnp.broadcast_to(rc, (16, FP)).astype(BF)
            h = tall((n * vec_ref[0] + vec_ref[1]).astype(BF))
            hs[r] = h.T
            yield

    def cotangents():
        for r in range(R):
            cp[r % 4, 0:D, 0:F] = c_ref[r]
            cs[r] = cp[r % 4].T
            yield
        for j in range(FP // 16):
            ct_ref[16 * j : 16 * j + 16] = turn_block(perm_ref, cs[:, 16 * j : 16 * j + 16, :], R)
            yield

    weave([(pair(c), c * OFF, 1) for c in range(R // 2)] + [(cotangents(), 4, 1)])
    for j in range(FP // 16):
        block = turn_block(perm_ref, hs[:, 16 * j : 16 * j + 16, :], R)
        ht_ref[16 * j : 16 * j + 16] = block
        q = (mm(block.reshape(16 * R, DP), wq_ref[...]) * SCALE2).astype(BF)
        qt_ref[16 * j : 16 * j + 16] = q.reshape(16, R, DP)


def feature_forward(cells, cot, ws, R=16, OFF=2):
    rows = cells.shape[0]
    nat = lambda a, b: pl.BlockSpec((R, a, b), lambda i: (i, 0, 0))
    turned = pl.BlockSpec((FP, R, DP), lambda i: (0, i, 0))
    sizes = [(D + 16, FP), (3 * D, FP), (FP, H * FP), (8, 2 * FP), (D, FP)]
    kinds = [BF, BF, BF, F32, BF]
    return pl.pallas_call(
        functools.partial(forward_kernel, R, OFF),
        grid=(rows // R,),
        in_specs=[nat(D, F), nat(D, F)] + [whole(a) for a in ws],
        out_specs=[turned] * 3 + [nat(*a) for a in sizes],
        out_shape=[shape((FP, rows, DP))] * 3 + [shape((rows,) + a, t) for a, t in zip(sizes, kinds)],
        scratch_shapes=[
            pltpu.VMEM((R // 2, DP, 2 * FP), BF),
            pltpu.VMEM((R, FP, DP), BF),
            pltpu.VMEM((4, DP, FP), BF),
            pltpu.VMEM((R, FP, DP), BF),
        ],
        compiler_params=params(),
        cost_estimate=cost(9 * rows // R),
        name="feature_forward",
    )(cells, cot, *ws)


def pair_up(table, i, ny, back=False):
    shift = ny - i // 2 if back else i // 2
    return lax.rem(table // 2 + shift, ny) * 2 + lax.rem(table + i % 2, 2)


def hand_out(table_ref, pack, piece_refs):
    tables = len(piece_refs)
    rows = pack.shape[0] // tables
    for i, ref in enumerate(piece_refs):
        place = pair_up(table_ref[0], i, tables // 2)
        ref[...] = pack[pl.ds(pl.multiple_of(place * rows, 8), rows)].astype(BF)


def pack_pair(ref, at, a, b):
    ref[at : at + D] = a[0:D, 0:128]
    ref[at + D : at + 2 * D] = b[0:D, 0:128]
    ref[at + 2 * D : at + 3 * D] = jnp.concatenate([a[0:D, 128:D], b[0:D, 128:D]], 1)


def pack_norms(ref, at, sums):
    rows = []
    for s in sums:
        if s.shape[0] == D:
            s = jnp.concatenate([s, jnp.zeros((DP - D, 128), F32)], 0).T
        v = jnp.sum(s, 0, keepdims=True)
        rows += [v[:, 0:128], v[:, 128:256]]
    rows.append(jnp.zeros((ref.shape[0] - at - len(rows), 128), F32))
    ref[at:] = jnp.concatenate(rows, 0)


def item_kernel(
    FB, RW, keys, tables, OFF, AO, AS, WP, CC, WC, table_ref, ht_ref, next_ref, q_ref, qnext_ref, ct_ref, slot_ref, perm_ref, wqT_ref, woI_ref, wo_ref, w1T_ref, w1_ref, w2T_ref, w2_ref,
    wkv_ref, wkvT_ref, vec_ref, y_ref, g1_ref, back_ref, *rest
):
    piece_refs, rest = rest[:tables], rest[tables:]
    (dwq, dwo, dw1, dw2, dnp, dwkv, bias_ref, pack_ref, hk_ref, bk_ref,
     dks, dvs, hbTs, ois, hb2Ts, actss, dbTs, duss, dabTs, dqss, pbss, kvss, slp) = rest
    step = pl.program_id(0)
    blocks = [(s, b, min(16, FS - b)) for s in range(0, keys, 16) for b in range(0, FS, 16)]

    @pl.when(step == 0)
    def _():
        for ref in (dwq, dwo, dw1, dw2, dnp, dwkv):
            ref[...] = jnp.zeros_like(ref)
        for ref in (hb2Ts, actss, dbTs, duss, dabTs, dqss, dks, dvs):
            ref[1] = jnp.zeros_like(ref[1])
        for ref in (hbTs, ois):
            ref[2] = jnp.zeros_like(ref[2])
        hk_ref[:, :, D:DP] = jnp.zeros((FS, keys, DP - D), BF)
        for s, b, n in blocks:
            own = slot_ref[s // 2 : s // 2 + 8, b : b + n, :]
            own = jnp.concatenate([own[:, :, 0:D], own[:, :, D : 2 * D]], 0)
            if n < 16:
                own = jnp.concatenate([own, jnp.zeros((16, 16 - n, D), BF)], 1)
            hk_ref[b : b + n, s : s + 16, 0:D] = turn_block(perm_ref, own, 16)[0:n]
        for s in range(0, keys, 16):
            flag = slot_ref[s // 2 : s // 2 + 8, F, :].astype(F32)
            for i, at in enumerate((0, DP)):
                bias_ref[s + 8 * i : s + 8 * i + 8] = jnp.where(flag[:, at : at + 128] > 0.5, 0.0, -1e30)

    masks = half_masks()
    LW = 2 * RW
    left = lax.broadcasted_iota(jnp.int32, (1, LW), 1) < RW
    HK = H * keys
    cur, prev = lax.rem(step, 2), lax.rem(step + 1, 2)
    cur3, next3, prev3 = [lax.rem(step + i, 3) for i in range(3)]
    hb2T, acts, dbT, dus, dabT, dqs = [r.at[cur] for r in (hb2Ts, actss, dbTs, duss, dabTs, dqss)]

    def step_rows(at):
        return hk_ref[pl.ds(pl.multiple_of(at * FB, FB), FB)].reshape(FB * keys, DP)

    def keys_values(at, to):
        kvss[to] = mm(step_rows(at), wkv_ref[...]).astype(BF)

    def spreads(to, j, first):
        return [
            spread_halves(kvss[to, (2 * j + c) * keys : (2 * j + c + 1) * keys, first : first + DP], masks)
            for c in range(2)
        ]

    def attend(j, ref, qref, to, to3):
        h = ref[2 * j : 2 * j + 2].reshape(LW, DP)
        q = qref[2 * j : 2 * j + 2].reshape(LW, DP)
        ks = spreads(to, j, 0)
        hbTs[to3, :, j * LW : (j + 1) * LW] = h.T[0:D]
        yield
        st = jnp.where(left, mm_nt(ks[0], q), mm_nt(ks[1], q))
        yield
        vs = spreads(to, j, DP)
        pbs = []
        for hh in range(H):
            s = st[hh * keys : (hh + 1) * keys] + bias_ref[...]
            e = jnp.exp2(s - jnp.max(s, 0, keepdims=True))
            pbs.append((e * (1.0 / jnp.sum(e, 0, keepdims=True))).astype(BF))
            if hh % 2:
                yield
        pb = jnp.concatenate(pbs, 0)
        pbss[to, j] = pb
        pt = pb.T
        yield
        o = jnp.concatenate([mm(pt[:RW], vs[0]), mm(pt[RW:], vs[1])], 0).astype(BF)
        ois[to3, j * LW : (j + 1) * LW] = o
        yield

    @pl.when(step == 0)
    def _():
        keys_values(0, 0)
        weave([(attend(j, ht_ref, q_ref, 0, 0), 0, 1) for j in range(FB // 2)])

    def dense(i, out):
        c0 = i * 2 * LW
        g1v, b1v, g2v, b2v = [vec_ref[i] for i in range(2, 6)]
        h = ht_ref[4 * i:4 * i + 4].reshape(2 * LW, DP)
        o = ois[cur3, c0 : c0 + 2 * LW]
        aT = mm_nt(woI_ref[...], jnp.concatenate([o, h], 1))
        yield
        n2, rc2, h2, hb2 = [], [], [], []
        for t in range(2):
            n, rc = norm_t(aT[:, t * LW:(t + 1) * LW])
            hh = n * g1v + b1v
            n2.append(n.astype(BF)); rc2.append(rc); hb2.append(hh.astype(BF))
            yield
        hb2 = jnp.concatenate(hb2, 1)
        hb2T[:, c0:c0 + 2 * LW] = hb2
        hb2 = tall(hb2)
        C = CC
        u = mm(w1T_ref[0:C], hb2)
        for c in range(FF // C):
            un = mm(w1T_ref[C * c + C:C * c + 2 * C], hb2) if c + 1 < FF // C else None
            act, slope = gelu_parts(u.astype(BF))
            acts[C * c:C * c + C, c0:c0 + 2 * LW] = act
            slp[C * c:C * c + C, c0:c0 + 2 * LW] = slope
            u = un
            yield
        gT = ct_ref[4 * i:4 * i + 4].reshape(2 * LW, DP).T[0:D].astype(F32)
        z = mm(w2T_ref[...], acts[:, c0:c0 + 2 * LW])
        yield
        dbs, d3s = [], []
        ys = []
        for t in range(2):
            sl = slice(t * LW, (t + 1) * LW)
            n3, rc3 = norm_t(hb2[0:D, sl].astype(F32) + z[:, sl])
            ys.append((n3 * g2v + b2v).astype(BF))
            yield
            g = gT[:, sl]
            dnp[2] += g * n3
            dnp[3] += g
            d3 = norm_back_t(g, n3, rc3, g2v)
            dbs.append(d3.astype(BF))
            yield
        db = jnp.concatenate(dbs, 1)
        dbT[:, c0:c0 + 2 * LW] = db
        db = tall(db)
        w = mm(w2_ref[0:C], db)
        for c in range(FF // C):
            wn = mm(w2_ref[C * c + C:C * c + 2 * C], db) if c + 1 < FF // C else None
            dus[C * c:C * c + C, c0:c0 + 2 * LW] = w.astype(BF) * slp[C * c:C * c + C, c0:c0 + 2 * LW]
            w = wn
            yield
        dh = mm(w1_ref[...], dus[:, c0:c0 + 2 * LW])
        yT = tall(jnp.concatenate(ys, 1))
        y_ref[4 * i:4 * i + 4] = yT.T.reshape(4, RW, DP)
        yield
        dabs = []
        for t in range(2):
            dh2 = dbs[t].astype(F32) + dh[:, t * LW:(t + 1) * LW]
            n2f = n2[t].astype(F32)
            dnp[0] += dh2 * n2f
            dnp[1] += dh2
            dabs.append(norm_back_t(dh2, n2f, rc2[t], g1v).astype(BF))
            yield
        dab = jnp.concatenate(dabs, 1)
        dabT[:, c0:c0 + 2 * LW] = dab
        doT = mm(wo_ref[...], tall(dab)).astype(BF)
        out.extend([dab, doT])
        yield
    def back(j, doT, out):
        q, pb = q_ref[2 * j : 2 * j + 2].reshape(LW, DP), pbss[cur, j]
        ks, vs = spreads(cur, j, 0), spreads(cur, j, DP)
        do = tall(doT)
        don = do.T
        dp = jnp.where(left, mm(vs[0], do), mm(vs[1], do))
        yield
        slot_sums(dvs, j, pb, don, None)
        yield
        dss = []
        for hh in range(H):
            sl = slice(hh * keys, (hh + 1) * keys)
            p, d = pb[sl].astype(F32), dp[sl]
            dss.append((p * (d - jnp.sum(p * d, 0, keepdims=True))).astype(BF))
            if hh % 2: yield
        ds = jnp.concatenate(dss, 0)
        dst = ds.T
        yield
        slot_sums(dks, j, ds, q, 0.6931471805599453)
        yield
        dq = jnp.concatenate([mm(dst[:RW], ks[0]), mm(dst[RW:], ks[1])], 0) * SCALE
        dq = dq.astype(BF)
        dqs[j * LW:(j + 1) * LW] = dq
        out.append(dq)
        yield
    lane = lax.broadcasted_iota(jnp.int32, (1, 128), 1)
    zq = jnp.zeros((RW, 128), BF)
    def slot_sums(ref, j, w, rows, scale):
        out = [[], []]
        for t, heads in ((0, 4), (1, 2)):
            r = rows[:, 128 * t:128 * t + 128]
            both = jnp.concatenate([jnp.concatenate([r[:RW], zq], 0), jnp.concatenate([zq, r[RW:]], 0)], 1)
            full = mm(w[4 * t * keys:(4 * t + heads) * keys], both)
            for c in range(2):
                col = full[:, 128 * c:128 * c + 128]
                v = col[0:keys]
                for hh in range(1, heads):
                    v = jnp.where(lane >= E * hh, col[hh * keys:(hh + 1) * keys], v)
                out[c].append(v)
        for c in range(2):
            v = jnp.concatenate(out[c], 1)
            ref[cur, 2 * j + c] = (v if scale is None else v * scale).astype(BF)
    def finish(i, dqv, dab):
        dq = jnp.concatenate(dqv, 0)
        g1 = mm(dq, wqT_ref[...]) + tall(dab).T.astype(F32)
        g1_ref[4 * i:4 * i + 4] = g1.astype(BF).reshape(4, RW, DP)
        yield
    def chunk(i):
        out = []
        yield from dense(i, out)
        dab, doT = out
        dq = []
        for t in range(2):
            yield from back(2 * i + t, doT[:, t * LW : (t + 1) * LW], dq)
        yield from finish(i, dq, dab)

    def wgrad(at, b, b3):
        dwq[...] += mm(hbTs[b3], dqss[b])
        yield
        dwo[...] += mm(dabTs[b], ois[b3])
        yield
        for c in range(0, FF, WC):
            dw1[c : c + WC] += mm_nt(duss[b, c : c + WC], hb2Ts[b])
            yield
        for c in range(0, FF, WC):
            dw2[c : c + WC] += mm_nt(actss[b, c : c + WC], dbTs[b])
            yield
        dkv = jnp.concatenate([r[b].reshape(FB * keys, DP) for r in (dks, dvs)], 1)
        dwkv[...] += mm_tn(step_rows(at), dkv)
        yield
        back_rows = mm(dkv, wkvT_ref[...]).astype(BF).reshape(FB, keys, DP)
        bk_ref[pl.ds(pl.multiple_of(at * FB, FB), FB)] = back_rows
        yield

    def ahead():
        keys_values(jnp.minimum(step + 1, pl.num_programs(0) - 1), prev)
        yield

    NC = FB // 4
    streams = [(ahead(), 0, 1)] + [(chunk(i), i * OFF, 1) for i in range(NC)]
    streams += [(attend(j, next_ref, qnext_ref, prev, next3), AO + j * AS, 1) for j in range(FB // 2)]
    streams += [(wgrad(jnp.maximum(step - 1, 0), prev, prev3), WP, 1)]
    weave(streams)

    @pl.when(step == pl.num_programs(0) - 1)
    def _():
        for _ in wgrad(step, cur, cur3):
            pass
        for s, b, n in blocks:
            own = bk_ref[b : b + n, s : s + 16, :]
            if n < 16:
                own = jnp.concatenate([own, jnp.zeros((16 - n, 16, DP), BF)], 0)
            own = turn_block(perm_ref, own, 16)[:, 0:n, 0:D]
            back_ref[s // 2 : s // 2 + 8, b : b + n, :] = jnp.concatenate([own[0:8], own[8:16]], 2)
        at = 0
        for ref in (dw1, dw2):
            t = ref[...].astype(BF).T.astype(F32)
            for j in range(FF // 128):
                pack_ref[at : at + D] = t[:, 128 * j : 128 * j + 128]
                at += D
        pack_pair(pack_ref, at, dwq, tall(dwo[...]).T)
        pack_pair(pack_ref, at + PAIR, dwkv[:, 0:DP], dwkv[:, DP:])
        pack_norms(pack_ref, at + 2 * PAIR, [dnp[i] for i in range(4)])
        hand_out(table_ref, pack_ref, piece_refs)


def item_and_dense(table, ht, qt, ct, slots, perm, ws, vec, packed, tables, OFF=0, CC=384, WC=384):
    RW = ht.shape[1]
    keys = 2 * slots.shape[0]
    FB, AO, AS, WP = (20, 2, 2, 2) if keys <= 32 else (8, 2, 6, 4)
    M = FB * RW
    cells = pl.BlockSpec((FB, RW, DP), lambda i: (i, 0, 0))
    accs = [(D, DP), (D, DP), (FF, D), (FF, D), (4, D, 128), (DP, 2 * DP), (keys, 128), (packed, 128)]
    kept = [(3, D, M), (3, M, DP)] + [(2,) + a for a in ((D, M), (FF, M), (D, M), (FF, M), (D, M), (M, DP))]
    kept += [(2, FB // 2, H * keys, 2 * RW), (2, FB * keys, 2 * DP), (FF, M)]
    ahead = pl.BlockSpec((FB, RW, DP), lambda i: (jnp.minimum(i + 1, FS // FB - 1), 0, 0))
    flat = [slots, perm, *ws, vec]
    outs = [shape((FS, RW, DP))] * 2 + [shape(slots.shape)] + [shape((packed // tables, 128))] * tables
    return pl.pallas_call(
        functools.partial(item_kernel, FB, RW, keys, tables, OFF, AO, AS, WP, CC, WC),
        grid=(FS // FB,),
        in_specs=[pl.BlockSpec(memory_space=pltpu.SMEM), cells, ahead, cells, ahead, cells] + [whole(a) for a in flat],
        out_specs=[cells, cells] + [whole(a) for a in outs[2:]],
        out_shape=outs,
        scratch_shapes=[pltpu.VMEM(a, F32) for a in accs]
        + [pltpu.VMEM((FS, keys, DP), BF)] * 2
        + [pltpu.VMEM((2, FB, keys, DP), BF)] * 2
        + [pltpu.VMEM(a, BF) for a in kept],
        compiler_params=params(),
        cost_estimate=cost(66),
        name="item_and_dense",
    )(table, ht, ht, qt, qt, ct, *flat)


def backward_rows(
    x_ref, n_ref, qkv_ref, p_ref, l_ref, of_ref, wqkvI_ref, wo_ref, vec_ref, cg_ref, xs, os, dqs, das, dqkv, dwo, dnp, grad_of, base_ref=None
):
    def pair(c):
        at = slice(2 * c * FP, (2 * c + 2) * FP)
        dabs = []
        for u in range(2):
            r = 2 * c + u
            xs[:, r * FP : r * FP + F] = x_ref[r]
            os[:, r * FP : (r + 1) * FP] = of_ref[r]
            g = grad_of(r)
            n = n_ref[r, 0:D, :].astype(F32)
            rc = n_ref[r, D : D + 16, :].astype(F32)[0:1]
            dnp[0] += g * n
            dnp[1] += g
            dabs.append(norm_back_t(g, n, rc, vec_ref[0]).astype(BF))
            yield
        dab = jnp.concatenate(dabs, 1)
        das[:, at] = dab
        do = mm(wo_ref[...], tall(dab))
        yield
        for u in range(2):
            r = 2 * c + u
            own = slice(u * FP, (u + 1) * FP)
            lanes_r = slice(r * FP, (r + 1) * FP)
            for j in range(H // 2):
                inv = l_ref[r, j : j + 1, :]
                parts, offs = [], []
                for t in range(2):
                    hs = slice(64 * j + 32 * t, 64 * j + 32 * t + 32)
                    d = do[hs, own] * inv[:, t * FP : (t + 1) * FP]
                    offs.append(jnp.sum(d * of_ref[r, hs, :].astype(F32), 0, keepdims=True))
                    parts.append(d.astype(BF))
                dom = two_heads(*parts)
                off = jnp.concatenate(offs, 1).astype(BF)
                dp = mm(qkv_ref[r, 2 * D + 64 * j : 2 * D + 64 * j + 64, :].T, dom)
                yield
                e = p_ref[r, :, 256 * j : 256 * j + 256]
                ds = e * (dp.astype(BF) - off)
                dv = mm_nt(dom, e)
                yield
                qm = two_heads(
                    qkv_ref[r, 64 * j : 64 * j + 32, :], qkv_ref[r, 64 * j + 32 : 64 * j + 64, :]
                )
                dk = mm_nt(qm, ds) * 0.6931471805599453
                dq = mm(qkv_ref[r, D + 64 * j : D + 64 * j + 64, :], ds)
                dq = jnp.concatenate([dq[0:32, 0:128], dq[32:64, 128:256]], 0) * SCALE
                yield
                for i, d in enumerate((dq, dk, dv)):
                    dqs[i * D + 64 * j : i * D + 64 * j + 64, lanes_r] = d.astype(BF)
        yield
        cg = mm(wqkvI_ref[...], jnp.concatenate([dqs[:, at], dab], 0))
        for u in range(2):
            own = cg[:, u * FP : u * FP + F]
            cg_ref[2 * c + u] = own if base_ref is None else own + base_ref[2 * c + u]
        yield

    def sums(at):
        dqkv[...] += mm_nt(dqs[:, at], xs[:, at])
        yield
        dwo[...] += mm_nt(os[:, at], das[:, at])
        yield

    return pair, sums


def backward_kernel(
    R, OFF, YO, x_ref, n_ref, qkv_ref, p_ref, l_ref, of_ref, g1t_ref, yt_ref, wqkvI_ref, wo_ref, vec_ref, perm_ref,
    cg_ref, y_ref, dqkv, dwo, dnp, gs, ys, xs, os, dqs, das,
):
    @pl.when(pl.program_id(0) == 0)
    def _():
        for ref in (xs, dqkv, dwo, dnp):
            ref[...] = jnp.zeros_like(ref)

    col = lax.broadcasted_iota(jnp.int32, (16, 1, 1), 0)

    def turn(ref, out, j):
        block = ref[16 * j : min(16 * j + 16, FS)]
        if block.shape[0] < 16:
            block = jnp.concatenate([block, jnp.zeros((16 - block.shape[0],) + block.shape[1:], BF)], 0)
        if 16 * j + 16 > F:
            block = jnp.where(col < F - 16 * j, block, 0).astype(BF)
        out[:, 16 * j : 16 * j + 16, :] = turn_block(perm_ref, block, 16)

    for j in range(FP // 16):
        turn(g1t_ref, gs, j)

    def outputs():
        for j in range(FP // 16):
            turn(yt_ref, ys, j)
            yield
        for r in range(R):
            y_ref[r] = ys[r].T[0:D, 0:F]
            yield

    pair, sums = backward_rows(
        x_ref, n_ref, qkv_ref, p_ref, l_ref, of_ref, wqkvI_ref, wo_ref, vec_ref, cg_ref, xs, os, dqs, das, dqkv, dwo, dnp,
        lambda r: gs[r].T[0:D].astype(F32),
    )
    streams = [(pair(c), c * OFF, 1) for c in range(R // 2)]
    streams.append((outputs(), YO, 1))
    weave(streams)
    for _ in sums(slice(0, R * FP)):
        pass


def feature_backward(x, saved, g1t, yt, wqkvI, wo, vec, perm, R=16, OFF=2, YO=3):
    rows = x.shape[0]
    nat = lambda a: pl.BlockSpec((R,) + a.shape[1:], lambda i: (i, 0, 0))
    turned = pl.BlockSpec((FS, R, DP), lambda i: (0, i, 0))
    accs = [shape((3 * D, D), F32), shape((D, D), F32), shape((2, D, FP), F32)]
    shared = [wqkvI, wo, vec, perm]
    M = R * FP
    return pl.pallas_call(
        functools.partial(backward_kernel, R, OFF, YO),
        grid=(rows // R,),
        in_specs=[nat(x)] + [nat(a) for a in saved] + [turned] * 2 + [whole(a) for a in shared],
        out_specs=[nat(x), nat(x)] + [whole(a) for a in accs],
        out_shape=[shape(x.shape, F32), shape(x.shape)] + accs,
        scratch_shapes=[pltpu.VMEM(a, BF) for a in ((R, FP, DP), (R, FP, DP), (D, M), (D, M), (3 * D, M), (D, M))],
        compiler_params=params(),
        cost_estimate=cost(60 * rows // R),
        name="feature_backward",
    )(x, *saved, g1t, yt, *shared)


def slots_back_kernel(
    SL, tables, table_ref, x_ref, n_ref, qkv_ref, p_ref, l_ref, of_ref, slot_ref, base_ref, iqkv, iwo, inp, wqkvI_ref, wo_ref, vec_ref,
    cg_ref, *rest,
):
    piece_refs, rest = rest[:tables], rest[tables:]
    pack_ref, xs, os, dqs, das, dqkv, dwo, dnp = rest
    xs[...] = jnp.zeros_like(xs)
    for ref, init in ((dqkv, iqkv), (dwo, iwo), (dnp, inp)):
        ref[...] = init[...]
    both = slot_ref[0].astype(F32)
    for i in range(1, slot_ref.shape[0]):
        both = both + slot_ref[i].astype(F32)
    z0 = jnp.zeros((FP - FS, 2 * D), F32)
    live = lax.broadcasted_iota(jnp.int32, (1, FP), 1) < F
    back = []
    for c in range(SL // 2):
        t = jnp.where(live, jnp.concatenate([both[c], z0], 0).T, 0.0)
        back += [t[0:D], t[D : 2 * D]]
    pair, sums = backward_rows(
        x_ref, n_ref, qkv_ref, p_ref, l_ref, of_ref, wqkvI_ref, wo_ref, vec_ref, cg_ref, xs, os, dqs, das, dqkv, dwo, dnp,
        lambda r: back[r], base_ref,
    )
    weave([(pair(c), 0, 1) for c in range(SL // 2)])
    for _ in sums(slice(0, SL * FP)):
        pass
    zc = jnp.zeros((D, DP - D), F32)
    three = [jnp.concatenate([dqkv[i * D : (i + 1) * D], zc], 1).T for i in range(3)]
    pack_pair(pack_ref, 0, three[0], three[1])
    pack_pair(pack_ref, PAIR, three[2], dwo)
    pack_norms(pack_ref, 2 * PAIR, [dnp[0], dnp[1]])
    hand_out(table_ref, pack_ref, piece_refs)


def slots_backward(table, x, saved, slots, prev, wqkvI, wo, vec, packed, tables):
    SL = 2 * slots.shape[1]
    nat = lambda a: pl.BlockSpec((SL,) + a.shape[1:], lambda i: (i, 0, 0))
    cg, *accs = prev
    flat = list(accs) + [wqkvI, wo, vec]
    pieces = [shape((packed // tables, 128))] * tables
    M = SL * FP
    ins = [table, x, *saved, slots, cg, *flat]
    return pl.pallas_call(
        functools.partial(slots_back_kernel, SL, tables),
        grid=(1,),
        in_specs=[pl.BlockSpec(memory_space=pltpu.SMEM), nat(x)]
        + [nat(a) for a in saved]
        + [whole(slots), nat(cg)]
        + [whole(a) for a in flat],
        out_specs=[nat(cg)] + [whole(a) for a in pieces],
        out_shape=[shape(cg.shape, F32)] + pieces,
        input_output_aliases={len(saved) + 3: 0},
        scratch_shapes=[pltpu.VMEM((packed, 128), F32)]
        + [pltpu.VMEM(a, BF) for a in ((D, M), (D, M), (3 * D, M), (D, M))]
        + [pltpu.VMEM(a.shape, F32) for a in accs],
        compiler_params=params(),
        cost_estimate=cost(8),
        name="slots_backward",
    )(*ins)


def table_sums(tables, pieces):
    sent = []
    for i, a in enumerate(pieces):
        to = [(t, (t // 2 + i // 2) % (tables // 2) * 2 + (t + i) % 2) for t in range(tables)]
        sent.append(lax.ppermute(a, "table", to) if i else a)
    return sent


def join_kernel(tables, *refs):
    out_ref = refs[-1]
    at = 0
    for group in (refs[:tables], refs[tables : 2 * tables]):
        total = group[0][...].astype(F32)
        for ref in group[1:]:
            total = total + ref[...].astype(F32)
        rows = total.shape[0] // out_ref.shape[0]
        for i in range(out_ref.shape[0]):
            out_ref[i, at : at + rows] = total[i * rows : (i + 1) * rows].astype(BF)
        at += rows


def join_tables(shards, mids, tails):
    rows = (mids[0].shape[0] + tails[0].shape[0]) // shards
    return pl.pallas_call(
        functools.partial(join_kernel, len(mids)),
        out_shape=shape((shards, rows, 128)),
        compiler_params=params(16),
        cost_estimate=cost(2),
        name="join_tables",
    )(*mids, *tails)


def sum_kernel(parts_ref, out_ref):
    total = parts_ref[0].astype(F32)
    for i in range(1, parts_ref.shape[0]):
        total = total + parts_ref[i].astype(F32)
    total = total.astype(BF)
    for i in range(out_ref.shape[0]):
        out_ref[i] = total


def sum_rows(parts):
    parts = lax.all_to_all(parts, "rows", 0, 0)
    return pl.pallas_call(
        sum_kernel,
        out_shape=shape(parts.shape),
        compiler_params=params(16),
        cost_estimate=cost(2),
        name="sum_rows",
    )(parts)


def gather_all(copies):
    tables = lax.axis_size("table")
    ny = tables // 2
    own = lax.all_to_all(copies, "rows", 0, 0)
    pieces = [own]
    for s in range(1, ny):
        pieces.append(lax.ppermute(own, "table", [(t, (t // 2 + s) % ny * 2 + t % 2) for t in range(tables)]))
    other = [lax.ppermute(a, "table", [(t, t ^ 1) for t in range(tables)]) for a in pieces]
    return [a for pair in zip(pieces, other) for a in pair]


def to_row(c):
    return jnp.broadcast_to(c, (c.shape[0], 128)).T[0:1]


def to_col(r):
    return jnp.broadcast_to(r, (128, r.shape[1])).T[:, 0:1]


def clipped(update, weight, count):
    def total(v):
        return jnp.sum(jnp.sum(v, 0, keepdims=True), 1, keepdims=True)

    rms = jnp.sqrt(total(update * update) * (1.0 / count))
    weight_rms = jnp.sqrt(total(weight * weight) * (1.0 / count))
    return update * (RATE * jnp.maximum(0.001, weight_rms) / jnp.maximum(1.0, rms / CLIP))


def optimizer_kernel(
    tables, mid_rows, *refs):
    table_ref, *refs = refs
    piece_refs, refs = refs[:tables], refs[tables:]
    mid_ref, tail_ref = refs[-2:]
    table = table_ref[0]
    ny = tables // 2
    for i, ref in enumerate(piece_refs):
        place = pair_up(table, i, ny, True)
        for out, at, end in ((mid_ref, 0, mid_rows), (tail_ref, mid_rows, ref.shape[1])):
            rows = ref.shape[0] * (end - at)
            start = pl.multiple_of(place * rows, 8)
            out[pl.ds(start, rows)] = ref[:, at:end, :].astype(F32).reshape(rows, 128)
    optimizer_steps(*refs)


def optimizer_steps(
    proj_ref, outw_ref, in_ref, hid_ref, norm_ref, sr_ref, sc_ref, mm_ref, mh_ref, ns_ref,
    proj_g, out_g, in_g, hid_g, norm_g, proj_n, out_n, in_n, hid_n, norm_n, sr_n, sc_n, mm_n, mh_n, ns_n, mid_ref, tail_ref,
):
    decay = 1.0 - STEP ** (-0.8)

    def stats(grad, col_old, row_old):
        square = grad * grad + 1e-30
        a, b = grad.shape
        over_sub = decay * row_old + (1.0 - decay) * (jnp.sum(square, 0, keepdims=True) * (1.0 / a))
        over_lane = decay * col_old + (1.0 - decay) * (jnp.sum(square, 1, keepdims=True) * (1.0 / b))
        return over_lane, over_sub

    def scaled(grad, col, row, mean):
        return grad * lax.rsqrt(col * (1.0 / mean)) * lax.rsqrt(row)

    def square_step(i, ref, at, first):
        g_ref, n_ref, w_ref, j = (proj_g, proj_n, proj_ref, i) if i < 6 else (out_g, out_n, outw_ref, i - 6)
        low = ref[at : at + D] if first else ref[at + D : at + 2 * D]
        high = ref[at + 2 * D : at + 3 * D]
        grad = jnp.concatenate([low, high[:, 0:64] if first else high[:, 64:128]], 1)
        g_ref[j] = grad
        yield
        col, row = stats(grad, to_col(sr_ref[i : i + 1, :]), sc_ref[i : i + 1, :])
        sr_n[i : i + 1, :] = to_row(col)
        sc_n[i : i + 1, :] = row
        yield
        mean = jnp.sum(col, 0, keepdims=True) * (1.0 / D)
        update = scaled(grad, col, row, mean)
        yield
        w = w_ref[j]
        n_ref[j] = w - clipped(update, w, D * D)
        yield

    def wide_step(i, at, w_ref, g_ref, n_ref):
        for j in range(6):
            g_ref[:, 128 * j : 128 * j + 128] = mid_ref[at + D * j : at + D * j + D]
            yield
        grad = g_ref[...]
        col, row = stats(grad, to_col(mm_ref[i : i + 1, :]), mh_ref[i : i + 1, :])
        mm_n[i : i + 1, :] = to_row(col)
        mh_n[i : i + 1, :] = row
        yield
        mean = jnp.sum(col, 0, keepdims=True) * (1.0 / D) if i == 0 else jnp.sum(row, 1, keepdims=True) * (1.0 / FF)
        update = scaled(grad, col, row, mean)
        yield
        w = w_ref[...]
        n_ref[...] = w - clipped(update, w, D * FF)
        yield

    steps = [wide_step(0, 0, in_ref, in_g, in_n), wide_step(1, 6 * D, hid_ref, hid_g, hid_n)]
    places = ((0, tail_ref, 0, True), (1, tail_ref, 0, False), (2, tail_ref, PAIR, True), (6, tail_ref, PAIR, False))
    places += ((3, mid_ref, 12 * D, True), (7, mid_ref, 12 * D, False))
    places += ((4, mid_ref, 12 * D + PAIR, True), (5, mid_ref, 12 * D + PAIR, False))
    steps += [square_step(*a) for a in places]
    weave([(g, WV * i, 1) for i, g in enumerate(steps)])

    pieces = []
    for ref, at, count in ((tail_ref, 2 * PAIR, 2), (mid_ref, 12 * D + 2 * PAIR, 4)):
        v = ref[at : at + 16].astype(F32)
        for i in range(count):
            pieces.append(jnp.concatenate([v[2 * i : 2 * i + 1], v[2 * i + 1 : 2 * i + 2, 0:64]], 1))
    grad = jnp.concatenate(pieces, 0)
    norm_g[...] = grad
    second = decay * ns_ref[...] + (1.0 - decay) * (grad * grad + 1e-30)
    ns_n[...] = second
    update = grad * lax.rsqrt(second)
    rms = jnp.sqrt(jnp.sum(update * update, 1, keepdims=True) * (1.0 / D))
    w = norm_ref[...]
    w_rms = jnp.sqrt(jnp.sum(w * w, 1, keepdims=True) * (1.0 / D))
    norm_n[...] = w - update * (RATE * jnp.maximum(0.001, w_rms) / jnp.maximum(1.0, rms / CLIP))


def optimizer(table, pieces, mid_rows, *state):
    proj, outw, w_in, w_outT, norms, sr, sc, ms, hs, ns = state
    shards, rows, _ = pieces[0].shape
    order = [proj, outw, w_in, w_outT, norms, proj, outw, w_in, w_outT, norms, sr, sc, ms, hs, ns]
    outs = pl.pallas_call(
        functools.partial(optimizer_kernel, len(pieces), mid_rows),
        in_specs=[pl.BlockSpec(memory_space=pltpu.SMEM)] + [whole(a) for a in (*pieces, *state)],
        out_shape=[shape(a.shape, F32) for a in order],
        scratch_shapes=[
            pltpu.VMEM((len(pieces) * shards * mid_rows, 128), F32),
            pltpu.VMEM((len(pieces) * shards * (rows - mid_rows), 128), F32),
        ],
        compiler_params=params(28),
        cost_estimate=cost(8), name="optimizer",
    )(table, *pieces, *state)
    outs = list(outs)
    for i in (3, 8):
        outs[i] = outs[i].T
    return outs


def on_device(n, cells, cotangent, train_count, key_mask, train_order, *state):
    state = list(state)
    state[3] = state[3].T
    proj, outw, w_in, w_outT, norms = state[:5]
    x = jnp.swapaxes(cells[0], 1, 2)
    cot = jnp.swapaxes(cotangent[0], 1, 2)
    rows_here = x.shape[0]
    unit = 8 * n
    tail_rows = -(-TAIL // unit) * unit
    mid_rows = -(-MID // unit) * unit
    perm = perm_matrix()
    shards, tables = lax.axis_size("rows"), lax.axis_size("table")
    table = lax.axis_index("table").astype(jnp.int32).reshape(1)
    own, wqkvT, woT, vec = slot_rows(shards, train_count, key_mask, train_order, x, proj, outw, norms)
    slots = lax.all_to_all(own, "rows", 0, 0).reshape((-1,) + own.shape[2:])
    w_in, _ = lax.optimization_barrier((w_in, own))
    wqkvI, wo, *ws = other_weights(proj, outw, w_in, w_outT)
    wkv2, wkv2T, wq2, *ws = ws
    ht, ct, qt, *saved = feature_forward(x, cot, (wqkvT, woT, vec, perm, wq2))
    yt, g1t, back, *mids = item_and_dense(table, ht, qt, ct, slots, perm, (*ws, wkv2, wkv2T), vec, mid_rows, tables)
    back = lax.all_to_all(back.reshape(own.shape), "rows", 0, 0)
    mids = table_sums(tables, mids)
    cg, y, *accs = feature_backward(x, saved, g1t, yt, wqkvI, wo, vec, perm)
    mids, accs = lax.optimization_barrier((mids, accs))
    cg, *tails = slots_backward(table, x, saved, back, (cg, *accs), wqkvI, wo, vec, tail_rows, tables)
    tails = table_sums(tables, tails)
    pieces = gather_all(sum_rows(join_tables(shards, mids, tails)))
    return (jnp.swapaxes(y, 1, 2)[None], jnp.swapaxes(cg, 1, 2)[None], *optimizer(table, pieces, mid_rows // n, *state))


def solution(mesh):
    n = int(mesh.shape["table"] * mesh.shape["rows"])
    cells = P("table", "rows", None, None)
    return jax.shard_map(
        functools.partial(on_device, n),
        mesh=mesh,
        in_specs=(cells, cells, P("table"), P("table", "rows"), P("table", "rows")) + (P(),) * 10,
        out_specs=(cells, cells) + (P(),) * 15,
        check_vma=False,
    )
```
